32 devices in a mesh: seq: 32 (over z, y, x, core).
Axes of the slice: x: 2, y: 2, z: 4, core: 2. Of those that a mesh axis runs over, the one named last changes fastest.
Arguments:
- tokens: bfloat16 [2, 16384, 1024], P(None, 'seq'), may hold values from -6 to 6
- seq_starts: int32 [2, 16384], P(None, 'seq'), may hold values from 0 to 15360, as said below
- seq_lengths: int32 [2, 16384], P(None, 'seq'), may hold values from 1 to 16384, as said below
- gain_in: float32 [1024], replicated, may hold values from 0.25 to 1.75
- gain_mlp: float32 [1024], replicated, may hold values from 0.25 to 1.75
- w_in: bfloat16 [1024, 3584], replicated, may hold values from -0.1875 to 0.1875
- w_out: bfloat16 [1024, 1024], replicated, may hold values from -0.1875 to 0.1875
- w_gate_up: bfloat16 [1024, 5632], replicated, may hold values from -0.1875 to 0.1875
- w_down: bfloat16 [2816, 1024], replicated, may hold values from -0.109375 to 0.109375
- cotangent: bfloat16 [2, 16384, 1024], P(None, 'seq'), may hold values from -6 to 6
Outputs:
- mixed_out: bfloat16 [2, 16384, 1024], P(None, 'seq')
- grad_tokens: float32 [2, 16384, 1024], P(None, 'seq')
- grad_gain_in: float32 [1024], P('seq')
- grad_gain_mlp: float32 [1024], P('seq')
- grad_w_in: float32 [1024, 3584], P('seq')
- grad_w_out: float32 [1024, 1024], P('seq')
- grad_w_gate_up: float32 [1024, 5632], P('seq')
- grad_w_down: float32 [2816, 1024], P('seq')
The draws below stay inside these ranges and needn't reach their ends.
Inputs may be any that keep to these rules, and one draw needn't show every extreme that they name: `seq_starts`: tokens of one sequence occupy a run of positions beginning at this value, which never falls along a row and is a multiple of 64. Row 0 holds a single sequence filling the whole row. Every other row holds sequences of 1024 to 8192 tokens, each followed by padding up to a multiple of 64 positions, and ends with a sequence of exactly 1024 tokens that starts at 15360; the sequence before that one may be cut short. `seq_lengths`: the same for all tokens of a sequence; positions from start + length up to the next sequence's start are padding, fewer than 64 of them.
All inputs are finite; a program needn't handle non-finite values.
Results may differ from the reference program's by a relative error of at most 0.017.
Values may be sent and summed in bfloat16 or wider, within the bound.
A program may use at most 896 MiB of HBM per device.

```python
import jax
import jax.numpy as jnp
from jax import lax

D = 1024
HEADS = 16
FEAT = 16
FF = 2816
WINDOW = 64
BUCKET = 64
MIN_LEN = 1024
MAX_LEN = 8192
ROWS = 2
TOK_ROW = 512
HEAD = 64
PHI = 273
PROJ = 3584
ROW_LEN = 16384
N_SEQ = 32


def row_layout(key):
    places = jnp.arange(ROW_LEN, dtype=jnp.int32)
    final_start = ROW_LEN - MIN_LEN
    starts_list = [jnp.zeros((ROW_LEN,), jnp.int32)]
    lengths_list = [jnp.full((ROW_LEN,), ROW_LEN, jnp.int32)]
    doc_count = ROW_LEN // MIN_LEN + 1
    for row_index in range(1, ROWS):
        doc_lengths = jax.random.randint(jax.random.fold_in(key, row_index), (doc_count,), MIN_LEN, MAX_LEN + 1, dtype=jnp.int32)
        buckets = (doc_lengths + BUCKET - 1) // BUCKET * BUCKET
        doc_starts = jnp.cumsum(buckets) - buckets
        owner = (doc_starts[None, :] <= places[:, None]).astype(jnp.int32)
        following = jnp.concatenate([owner[:, 1:], jnp.zeros((ROW_LEN, 1), jnp.int32)], axis=1)
        chosen = owner - following
        own_start = jnp.sum(chosen * doc_starts[None, :], axis=1)
        own_length = jnp.minimum(jnp.sum(chosen * doc_lengths[None, :], axis=1), final_start - own_start)
        in_final = places >= final_start
        own_start = jnp.where(in_final, final_start, own_start)
        own_length = jnp.where(in_final, MIN_LEN, own_length)
        starts_list.append(own_start)
        lengths_list.append(own_length)
    return (jnp.stack(starts_list).astype(jnp.int32), jnp.stack(lengths_list).astype(jnp.int32))


def draw_seq_starts(key, part):
    starts, unused = row_layout(key)
    return starts


def draw_seq_lengths(key, part):
    unused, lengths = row_layout(key)
    return lengths


def raised(array, own_key, source, target, parts, factor):
    def block_of(dim):
        return (jnp.arange(array.shape[dim]) // (array.shape[dim] // parts)).reshape((-1,) + (1,) * (array.ndim - 1 - dim))

    near = jax.random.permutation(own_key, parts)[block_of(target)]
    second = (block_of(target) + parts // 2) % parts
    return jnp.where((block_of(source) == near) | (block_of(source) == second), factor * array, array)


def block_levels(key, dims, shards, least, high):
    level = 1.0
    for dim, parts in shards:
        heights = jax.random.uniform(jax.random.fold_in(jax.random.fold_in(key, 6), dim), (parts,), jnp.float32, least / len(shards), high / len(shards))
        level = level * jnp.repeat(jnp.exp(heights), dims[dim] // parts).reshape((-1,) + (1,) * (len(dims) - 1 - dim))
    return level


def gaussian(rng, shape, width, limit, shards=(), kind=jnp.bfloat16):
    values = width * jax.random.normal(rng, shape, jnp.float32)
    if shards:
        values = values * block_levels(rng, shape, shards, -0.22, 0.18)
    return jnp.clip(values, -limit, limit).astype(kind)


def heavy_noise(key, shape, spread, reach, cuts, heavy, held_as=jnp.bfloat16):
    entries = spread * jax.random.normal(key, shape, jnp.float32)
    if cuts:
        entries = entries * block_levels(key, shape, cuts, -0.22, 0.18)
    return jnp.clip(raised(entries, jax.random.fold_in(key, 3), *heavy), -reach, reach).astype(held_as)


def setup_inputs(seed: int = 0) -> dict:
    key_of = jax.random.split(jax.random.key(seed), 11)
    tokens = heavy_noise(key_of[0], (ROWS, ROW_LEN, D), 1.0, 6.0, ((1, 32),), (1, 2, 32, 2.75))
    seq_starts = draw_seq_starts(jax.random.fold_in(key_of[10], 71), 0)
    seq_lengths = draw_seq_lengths(jax.random.fold_in(key_of[10], 71), 0)
    gain_in = jnp.clip(1.0 + 0.15 * jax.random.normal(key_of[3], (D,), jnp.float32), 0.25, 1.75)
    gain_mlp = jnp.clip(1.0 + 0.15 * jax.random.normal(key_of[4], (D,), jnp.float32), 0.25, 1.75)
    w_in = gaussian(key_of[5], (D, PROJ), D ** -0.5, 0.1875)
    w_out = gaussian(key_of[6], (D, D), D ** -0.5, 0.1875)
    w_gate_up = gaussian(key_of[7], (D, 2 * FF), D ** -0.5, 0.1875)
    w_down = gaussian(key_of[8], (FF, D), FF ** -0.5, 0.109375)
    cotangent = gaussian(key_of[9], (ROWS, ROW_LEN, D), 1.0, 6.0, ((1, 32),))
    return dict(tokens=tokens, seq_starts=seq_starts, seq_lengths=seq_lengths, gain_in=gain_in, gain_mlp=gain_mlp, w_in=w_in, w_out=w_out, w_gate_up=w_gate_up, w_down=w_down, cotangent=cotangent)


EPSILON = 1e-06
PRECISE = lax.Precision.HIGHEST

@jax.custom_vjp
def low(v):
    return lax.optimization_barrier(v.astype(jnp.bfloat16)).astype(jnp.float32)

@jax.custom_vjp
def low_back(v):
    return v

def low_keep(v):
    return (low(v), None)

def low_pass(kept, grad):
    return (grad,)

def back_keep(v):
    return (v, None)

def back_low(kept, grad):
    return (low(grad),)
low.defvjp(low_keep, low_pass)
low_back.defvjp(back_keep, back_low)

def product(left, right):
    return jnp.dot(left, right, precision=PRECISE, preferred_element_type=jnp.float32)

def rms_scale(value, gain):
    return value * lax.rsqrt(lax.optimization_barrier(jnp.mean(value * value, axis=-1, keepdims=True)) + EPSILON) * gain

def features(vectors):
    feat_width = vectors.shape[-1]
    outer_part = (vectors[..., :, None] * vectors[..., None, :]).reshape(vectors.shape[:-1] + (feat_width * feat_width,))
    constant = jnp.ones(vectors.shape[:-1] + (1,), jnp.float32)
    return jnp.concatenate([constant, vectors * feat_width ** (-0.25), outer_part * (2.0 * feat_width) ** (-0.5)], axis=-1)

def block_step(carried, inputs):
    state_in, key_tail, value_tail = carried
    q_lin, k_lin, q_win, k_win, values, starts, lengths, block_begin = inputs
    block_len = q_lin.shape[0]
    places = block_begin + jnp.arange(block_len, dtype=jnp.int32)
    key_places = block_begin - WINDOW + jnp.arange(block_len + WINDOW, dtype=jnp.int32)
    seq_ends = starts + lengths
    inner_mask = (starts[:, None] <= places[None, :]) & (places[None, :] <= places[:, None]) & (places[None, :] < seq_ends[:, None])
    near_mask = (starts[:, None] <= key_places[None, :]) & (key_places[None, :] <= places[:, None])
    near_mask = near_mask & (key_places[None, :] >= places[:, None] - WINDOW) & (key_places[None, :] < seq_ends[:, None])
    scores = low_back(jnp.einsum('ihf,jhf->hij', q_lin, k_lin, precision=PRECISE) * FEAT ** (-0.5))
    weights = jnp.where(inner_mask[None], 1.0 + scores + 0.5 * scores * scores, 0.0)
    numerator = jnp.einsum('hij,jhe->ihe', low(weights), values, precision=PRECISE)
    earlier_mask = (starts < block_begin)[:, None, None]
    inter = jnp.einsum('ihp,hpe->ihe', features(q_lin), state_in, precision=PRECISE)
    numerator = low_back(numerator + jnp.where(earlier_mask, inter, 0.0))
    linear_out = numerator * lax.rsqrt(lax.optimization_barrier(jnp.mean(numerator * numerator, axis=-1, keepdims=True)) + EPSILON)
    keys_all = jnp.concatenate([key_tail, k_win], axis=0)
    values_all = jnp.concatenate([value_tail, values], axis=0)
    logits = low_back(jnp.einsum('ihe,jhe->hij', q_win, keys_all, precision=PRECISE) * HEAD ** (-0.5))
    attn_probs = jax.nn.softmax(jnp.where(near_mask[None], logits, -1e+30), axis=-1)
    windowed = jnp.einsum('hij,jhe->ihe', low(attn_probs), values_all, precision=PRECISE)
    last_start = starts[-1]
    owned_mask = ((starts == last_start) & (places < seq_ends)).astype(jnp.float32)[:, None, None]
    state_local = jnp.einsum('jhp,jhe->hpe', features(k_lin) * owned_mask, values, precision=PRECISE)
    reset_flag = (last_start >= block_begin).astype(jnp.float32)
    state_out = state_local + (1.0 - reset_flag) * state_in
    mixed_block = (linear_out + windowed).reshape(block_len, HEADS * HEAD)
    return ((state_out, k_win[-WINDOW:], values[-WINDOW:]), mixed_block)

def attend_row(q_lin, k_lin, q_win, k_win, values, starts, lengths):
    inputs = (q_lin.reshape(N_SEQ, TOK_ROW, HEADS, FEAT), k_lin.reshape(N_SEQ, TOK_ROW, HEADS, FEAT), q_win.reshape(N_SEQ, TOK_ROW, HEADS, HEAD), k_win.reshape(N_SEQ, TOK_ROW, HEADS, HEAD), values.reshape(N_SEQ, TOK_ROW, HEADS, HEAD), starts.reshape(N_SEQ, TOK_ROW), lengths.reshape(N_SEQ, TOK_ROW), jnp.arange(N_SEQ, dtype=jnp.int32) * TOK_ROW)
    initial = (jnp.zeros((HEADS, PHI, HEAD), jnp.float32), jnp.zeros((WINDOW, HEADS, HEAD), jnp.float32), jnp.zeros((WINDOW, HEADS, HEAD), jnp.float32))
    unused, blocks = lax.scan(jax.checkpoint(block_step), initial, inputs)
    return blocks.reshape(ROW_LEN, D)

def reference(tokens, seq_starts, seq_lengths, gain_in, gain_mlp, w_in, w_out, w_gate_up, w_down, cotangent):
    lin_cols = HEADS * FEAT

    def forward(stream, g_first, g_second, m_in, m_out, m_gate_up, m_down):
        normed = low(rms_scale(stream, g_first))
        projected = product(normed.reshape(-1, D), m_in).reshape(ROWS, ROW_LEN, PROJ)
        q_lin = low_back(low(projected[..., :lin_cols]))
        k_lin = low_back(low(projected[..., lin_cols:2 * lin_cols]))
        q_win = low_back(low(projected[..., 2 * lin_cols:2 * lin_cols + D]))
        k_win = low_back(low(projected[..., 2 * lin_cols + D:2 * lin_cols + 2 * D]))
        values = low_back(low(projected[..., 2 * lin_cols + 2 * D:]))
        mixed_rows = []
        for row_index in range(ROWS):
            mixed_rows.append(attend_row(q_lin[row_index], k_lin[row_index], q_win[row_index], k_win[row_index], values[row_index], seq_starts[row_index], seq_lengths[row_index]))
        mixed = low_back(low(jnp.stack(mixed_rows)))
        branch = low_back(product(mixed.reshape(-1, D), m_out)).reshape(ROWS, ROW_LEN, D)
        resid = stream + branch
        hnorm = low(rms_scale(resid, g_second))
        gate_up = low_back(product(hnorm.reshape(-1, D), m_gate_up))
        hidden = low(jax.nn.silu(gate_up[:, :FF]) * gate_up[:, FF:])
        result = resid.reshape(-1, D) + product(hidden, m_down)
        return result.reshape(ROWS, ROW_LEN, D)
    primal = (tokens.astype(jnp.float32), gain_in, gain_mlp, w_in.astype(jnp.float32), w_out.astype(jnp.float32), w_gate_up.astype(jnp.float32), w_down.astype(jnp.float32))
    result, pullback = jax.vjp(forward, *primal)
    grads = pullback(cotangent.astype(jnp.float32))
    return (result.astype(jnp.bfloat16), grads[0], grads[1], grads[2], grads[3], grads[4], grads[5], grads[6])
```

```python
import functools
import jax
import jax.numpy as jnp
from jax import lax
from jax.experimental import pallas as pl
from jax.experimental.pallas import tpu as pltpu
from jax.sharding import PartitionSpec as P
F32=jnp.float32; BF=jnp.bfloat16
EPSILON=1e-6
MIB=1<<20

def nn(a,b): return lax.dot_general(a,b,(((1,),(0,)),((),())),preferred_element_type=F32)
def nt(a,b): return lax.dot_general(a,b,(((1,),(1,)),((),())),preferred_element_type=F32)
def tn(a,b): return lax.dot_general(a,b,(((0,),(0,)),((),())),preferred_element_type=F32)

def mlp_kernel(core_ref, mixed, tokens, cot, w_out, gain, wg, wu, wd,
               result, grad_resid, grad_mixed, gain_part, keep_gu, send_gu, keep_d, send_d, keep_o, send_o,
               resid, acc, dh, hn, hn_t, hid, dgate, dup, *, steps, chunk):
    step = pl.program_id(0)
    toks = mixed.shape[0]
    width = mixed.shape[1]
    count = toks // chunk
    first = core_ref[0] == 0

    def rows(n):
        return pl.ds(pl.multiple_of(n * chunk, chunk), chunk)

    @pl.when(step == 0)
    def _():
        def one(n, carry):
            r = rows(n)
            res = tokens[r, :].astype(F32) + nn(mixed[r, :], w_out[...])
            scale = lax.rsqrt(jnp.mean(res * res, axis=-1, keepdims=True) + EPSILON)
            h = (res * scale * gain[...]).astype(BF)
            resid[r, :] = res
            acc[r, :] = res
            dh[r, :] = jnp.zeros((chunk, width), F32)
            hn[r, :] = h
            return carry
        lax.fori_loop(0, count, one, 0)
        for n in range(count):
            hn_t[:, n * chunk:(n + 1) * chunk] = hn[n * chunk:(n + 1) * chunk, :].T

    def forward(n, carry):
        r = rows(n)
        h = hn[r, :]
        gate = nn(h, wg[...])
        up = nn(h, wu[...])
        dhid = nt(cot[r, :], wd[...])
        sig = 1.0 / (1.0 + jnp.exp(-gate))
        silu = gate * sig
        hidden = (silu * up).astype(BF)
        d_gate = (dhid * up * (sig + silu * (1.0 - sig))).astype(BF)
        d_up = (dhid * silu).astype(BF)
        hid[r, :] = hidden
        dgate[r, :] = d_gate
        dup[r, :] = d_up
        acc[r, :] += nn(hidden, wd[...])
        dh[r, :] += nt(d_gate, wg[...]) + nt(d_up, wu[...])
        return carry
    lax.fori_loop(0, count, forward, 0, unroll=2)

    half = width // 2
    grad_d = tn(hid[...], cot[...])
    left, right = grad_d[:, :half].astype(BF), grad_d[:, half:].astype(BF)
    keep_d[...] = jnp.where(first, left, right)
    send_d[...] = jnp.where(first, right, left)

    def weights(n, carry):
        r = rows(n)
        gg = nn(hn_t[r, :], dgate[...]).astype(BF)
        gu = nn(hn_t[r, :], dup[...]).astype(BF)
        keep_gu[r, :] = jnp.where(first, gg, gu)
        send_gu[r, :] = jnp.where(first, gu, gg)
        return carry
    lax.fori_loop(0, width // chunk, weights, 0, unroll=2)

    @pl.when(step == steps - 1)
    def _():
        gain_part[...] = jnp.zeros_like(gain_part)
        def one(n, carry):
            r = rows(n)
            res = resid[r, :]
            scale = lax.rsqrt(jnp.mean(res * res, axis=-1, keepdims=True) + EPSILON)
            grad = dh[r, :]
            gain_part[...] += jnp.sum(grad * res * scale, axis=0, keepdims=True)
            c = grad * gain[...]
            back = cot[r, :].astype(F32) + scale * c - res * (scale * scale * scale * jnp.mean(c * res, axis=-1, keepdims=True))
            result[r, :] = acc[r, :].astype(BF)
            grad_resid[r, :] = back
            b = back.astype(BF)
            hn[r, :] = b
            grad_mixed[r, :] = nt(b, w_out[...]).astype(BF)
            return carry
        lax.fori_loop(0, count, one, 0)
        for n in range(count):
            hn_t[:, n * chunk:(n + 1) * chunk] = mixed[n * chunk:(n + 1) * chunk, :].T
        def outer(n, carry):
            r = rows(n)
            go = nn(hn_t[r, :], hn[...])
            l, rr = go[:, :half].astype(BF), go[:, half:].astype(BF)
            keep_o[r, :] = jnp.where(first, l, rr)
            send_o[r, :] = jnp.where(first, rr, l)
            return carry
        lax.fori_loop(0, width // chunk, outer, 0)

def mlp(core, mixed, tokens, cot, w_out, gain, w_gate_up, w_down, tile=256, chunk=256):
    toks, width = mixed.shape
    ff = w_down.shape[0]
    steps = ff // tile
    half = width // 2
    whole = lambda s, c: (0, 0)
    one = dict(pipeline_mode=pl.Buffered(1))
    full = lambda shape: pl.BlockSpec(shape, whole, **one)
    out = pl.pallas_call(
        functools.partial(mlp_kernel, steps=steps, chunk=chunk),
        grid_spec=pltpu.PrefetchScalarGridSpec(
            num_scalar_prefetch=1, grid=(steps,),
            in_specs=[full((toks, width)), full((toks, width)), full((toks, width)), full((width, width)), full((1, width)),
                      pl.BlockSpec((width, tile), lambda s, c: (0, s)),
                      pl.BlockSpec((width, tile), lambda s, c: (0, s + steps)),
                      pl.BlockSpec((tile, width), lambda s, c: (s, 0))],
            out_specs=[full((toks, width)), full((toks, width)), full((toks, width)), full((1, width)),
                       pl.BlockSpec((width, tile), lambda s, c: (0, s)), pl.BlockSpec((width, tile), lambda s, c: (0, s)),
                       pl.BlockSpec((tile, half), lambda s, c: (s, 0)), pl.BlockSpec((tile, half), lambda s, c: (s, 0)),
                       full((width, half)), full((width, half))],
            scratch_shapes=[pltpu.VMEM((toks, width), F32)] * 3 + [pltpu.VMEM((toks, width), BF), pltpu.VMEM((width, toks), BF)]
                         + [pltpu.VMEM((toks, tile), BF)] * 3),
        out_shape=[jax.ShapeDtypeStruct((toks, width), BF), jax.ShapeDtypeStruct((toks, width), F32), jax.ShapeDtypeStruct((toks, width), BF),
                   jax.ShapeDtypeStruct((1, width), F32),
                   jax.ShapeDtypeStruct((width, ff), BF), jax.ShapeDtypeStruct((width, ff), BF),
                   jax.ShapeDtypeStruct((ff, half), BF), jax.ShapeDtypeStruct((ff, half), BF),
                   jax.ShapeDtypeStruct((width, half), BF), jax.ShapeDtypeStruct((width, half), BF)],
        compiler_params=pltpu.CompilerParams(vmem_limit_bytes=60 * MIB, dimension_semantics=("arbitrary",)),
        cost_estimate=pl.CostEstimate(flops=2 * toks * width * (9 * ff + 3 * width), bytes_accessed=60 * MIB, transcendentals=toks * ff),
        name="mlp",
    )(core, mixed, tokens, cot, w_out, gain.reshape(1, width), w_gate_up, w_gate_up, w_down)
    return out

HEADS=16; FEAT=16; WINDOW=64; ROWS_PHI=160

def lane_mask(width, size, which, dtype=BF):
    lanes = lax.broadcasted_iota(jnp.int32, (1, width), 1)
    return (lanes // size == which).astype(dtype)

def features_t(x):
    feat, toks = x.shape
    both = jnp.concatenate([x, x], axis=0)
    parts = [x * x * (2.0 * feat) ** -0.5]
    xs = x * feat ** -0.5
    for d in range(1, feat // 2):
        parts.append(xs * both[d:d + feat])
    parts.append(x * feat ** -0.25)
    parts.append(xs[:feat // 2] * x[feat // 2:])
    row = lax.broadcasted_iota(jnp.int32, (8, toks), 0)
    parts.append((row == 0).astype(F32))
    return jnp.concatenate(parts, axis=0)

def features_back_t(x, g):
    feat, toks = x.shape
    half = feat // 2
    both = jnp.concatenate([x, x], axis=0)
    total = g[:feat] * x * (2.0 * (2.0 * feat) ** -0.5)
    mixed = jnp.zeros((feat, toks), F32)
    for d in range(1, half):
        gd = g[d * feat:(d + 1) * feat]
        mixed = mixed + gd * both[d:d + feat]
        gx = gd * x
        mixed = mixed + jnp.concatenate([gx[feat - d:], gx[:feat - d]], axis=0)
    g8 = g[(half + 1) * feat:(half + 1) * feat + half]
    mixed = mixed + jnp.concatenate([g8 * x[half:], g8 * x[:half]], axis=0)
    return total + mixed * feat ** -0.5 + g[half * feat:(half + 1) * feat] * feat ** -0.25

def states_of(x_t, y, group):
    out = None
    size = y.shape[1] // 4
    for h in range(4):
        x = x_t[pl.ds(pl.multiple_of(group * 4 * FEAT + h * FEAT, FEAT), FEAT), :]
        s = nn(features_t(x).astype(BF), y * lane_mask(4 * size, size, h))
        out = s if out is None else out + s
    return out

def state_kernel(k, v, owned, out, k_t):
    g = pl.program_id(1)
    @pl.when(g == 0)
    def _():
        k_t[...] = k[...].astype(F32).T
    out[0, 0] = states_of(k_t, v[...] * owned[...].astype(BF), g)

def spec_tok(rows_len, width):
    return pl.BlockSpec((rows_len, width), lambda r, g: (r, g))
def spec_col(rows_len, first):
    return pl.BlockSpec((rows_len, 256), lambda r, g: (r, first + g))
def spec_all(rows_len, width):
    return pl.BlockSpec((rows_len, width), lambda r, g: (r, 0))
SPEC_STATE = pl.BlockSpec((1, 1, ROWS_PHI, 256), lambda r, g: (r, g, 0, 0))
PARAMS = pltpu.CompilerParams(vmem_limit_bytes=56 * MIB, dimension_semantics=("arbitrary", "arbitrary"))

def local_states(first, owned, rows, length):
    groups = HEADS // 4
    return pl.pallas_call(
        state_kernel, grid=(rows, groups),
        in_specs=[spec_all(length, 256), spec_col(length, 1), spec_all(length, 1)],
        out_specs=SPEC_STATE,
        out_shape=jax.ShapeDtypeStruct((rows, groups, ROWS_PHI, 256), F32),
        scratch_shapes=[pltpu.VMEM((256, length), F32)],
        compiler_params=PARAMS, name="state",
        cost_estimate=pl.CostEstimate(flops=rows*groups*4*2*ROWS_PHI*256*length, bytes_accessed=6*MIB, transcendentals=0),
    )(first, first, owned)

def intra_kernel(q, k, v, low, end, out, mask, *, length):
    g = pl.program_id(1)
    half = length // 2
    @pl.when(g == 0)
    def _():
        i = lax.broadcasted_iota(jnp.int32, (length, length), 0)
        j = lax.broadcasted_iota(jnp.int32, (length, length), 1)
        mask[...] = ((j >= low[...]) & (j <= i) & (j < end[...])).astype(BF)
    qv, kv, vv = q[...], k[...], v[...]
    top = bottom = None
    for h in range(4):
        km = kv * lane_mask(HEADS * FEAT, FEAT, g * 4 + h)
        vm = vv * lane_mask(256, 64, h)
        u0 = 1.0 + nt(qv[:half], km[:half]) * FEAT ** -0.5
        a0 = (0.5 + 0.5 * u0 * u0).astype(BF) * mask[:half, :half]
        u1 = 1.0 + nt(qv[half:], km) * FEAT ** -0.5
        a1 = (0.5 + 0.5 * u1 * u1).astype(BF) * mask[half:, :]
        o0, o1 = nn(a0, vm[:half]), nn(a1, vm)
        top = o0 if top is None else top + o0
        bottom = o1 if bottom is None else bottom + o1
    out[:half, :] = top
    out[half:, :] = bottom

def intra(first, second, low, end, rows, length):
    groups = HEADS // 4
    return pl.pallas_call(
        functools.partial(intra_kernel, length=length), grid=(rows, groups),
        in_specs=[spec_all(length, 256), spec_all(length, 256), spec_col(length, 1), spec_all(length, 1), spec_all(length, 1)],
        out_specs=spec_tok(length, 256),
        out_shape=jax.ShapeDtypeStruct((rows * length, 1024), F32),
        scratch_shapes=[pltpu.VMEM((length, length), BF)],
        compiler_params=PARAMS, name="intra",
        cost_estimate=pl.CostEstimate(flops=rows*HEADS*2*6*256*256*256, bytes_accessed=8*MIB, transcendentals=0),
    )(second, first, first, low, end)

def window_mask_t(low, high):
    key = lax.broadcasted_iota(jnp.int32, (2 * WINDOW, 4 * WINDOW), 0)
    query = lax.broadcasted_iota(jnp.int32, (2 * WINDOW, 4 * WINDOW), 1) % WINDOW
    return (key >= query) & (key <= query + WINDOW) & (key >= low) & (key < high)

def stacked(x):
    return jnp.concatenate([x * lane_mask(256, 64, h) for h in range(4)], axis=0)

def unstacked(x):
    total = None
    for h in range(4):
        part = x[h * WINDOW:(h + 1) * WINDOW] * lane_mask(256, 64, h, F32)
        total = part if total is None else total + part
    return total

def window_kernel(low, high, q, k, v, hk, hv, out, ka, va, *, length, per_row):
    r = pl.program_id(0)
    ka[:WINDOW, :] = hk[...]
    ka[WINDOW:, :] = k[...]
    va[:WINDOW, :] = hv[...]
    va[WINDOW:, :] = v[...]
    for n in range(length // WINDOW):
        keys = ka[n * WINDOW:(n + 2) * WINDOW, :]
        vals = va[n * WINDOW:(n + 2) * WINDOW, :]
        s = nt(stacked(q[n * WINDOW:(n + 1) * WINDOW, :]), keys) * 64 ** -0.5
        key = lax.broadcasted_iota(jnp.int32, (4 * WINDOW, 2 * WINDOW), 1)
        query = lax.broadcasted_iota(jnp.int32, (4 * WINDOW, 2 * WINDOW), 0) % WINDOW
        ok = (key >= query) & (key <= query + WINDOW) & (key >= low[r * per_row + n]) & (key < high[r * per_row + n])
        s = jnp.where(ok, s, -1e30)
        p = jnp.exp(s - jnp.max(s, axis=1, keepdims=True))
        p = (p / jnp.sum(p, axis=1, keepdims=True)).astype(BF)
        out[n * WINDOW:(n + 1) * WINDOW, :] = unstacked(nn(p, vals))

def smem_spec():
    return pl.BlockSpec(memory_space=pltpu.SMEM)

def window(low, high, first, second, hk, hv, rows, length):
    groups = HEADS // 4
    return pl.pallas_call(
        functools.partial(window_kernel, length=length, per_row=length // WINDOW), grid=(rows, groups),
        in_specs=[smem_spec(), smem_spec(), spec_col(length, 1), spec_col(length, 5), spec_col(length, 1), spec_tok(WINDOW, 256), spec_tok(WINDOW, 256)],
        out_specs=spec_tok(length, 256),
        out_shape=jax.ShapeDtypeStruct((rows * length, 1024), F32),
        scratch_shapes=[pltpu.VMEM((length + WINDOW, 256), BF)] * 2,
        compiler_params=PARAMS, name="window",
        cost_estimate=pl.CostEstimate(flops=rows*HEADS*2*4*length*128*256, bytes_accessed=8*MIB, transcendentals=0),
    )(low, high, second, second, first, hk, hv)

def window_back_kernel(low, high, q, k, v, hk, hv, go, dq, dk, dv, dhk, dhv, ka, va, dka, dva, *, length, per_row):
    r = pl.program_id(0)
    ka[:WINDOW, :] = hk[...]
    ka[WINDOW:, :] = k[...]
    va[:WINDOW, :] = hv[...]
    va[WINDOW:, :] = v[...]
    carry_k = carry_v = None
    for n in range(length // WINDOW):
        keys = ka[n * WINDOW:(n + 2) * WINDOW, :]
        vals = va[n * WINDOW:(n + 2) * WINDOW, :]
        qs = stacked(q[n * WINDOW:(n + 1) * WINDOW, :])
        gs = stacked(go[n * WINDOW:(n + 1) * WINDOW, :])
        s = nt(keys, qs) * 64 ** -0.5
        s = jnp.where(window_mask_t(low[r * per_row + n], high[r * per_row + n]), s, -1e30)
        p = jnp.exp(s - jnp.max(s, axis=0, keepdims=True))
        p = p * (1.0 / jnp.sum(p, axis=0, keepdims=True))
        gp = nt(vals, gs)
        ds = (p * (gp - jnp.sum(p * gp, axis=0, keepdims=True)) * 64 ** -0.5).astype(BF)
        dk_n = nn(ds, qs)
        dv_n = nn(p.astype(BF), gs)
        dq[n * WINDOW:(n + 1) * WINDOW, :] = unstacked(tn(ds, keys)).astype(BF)
        if n == 0:
            dhk[...] = dk_n[:WINDOW].astype(BF)
            dhv[...] = dv_n[:WINDOW].astype(BF)
        else:
            dk[(n - 1) * WINDOW:n * WINDOW, :] = (carry_k + dk_n[:WINDOW]).astype(dk.dtype)
            dv[(n - 1) * WINDOW:n * WINDOW, :] = carry_v + dv_n[:WINDOW]
        carry_k, carry_v = dk_n[WINDOW:], dv_n[WINDOW:]
    dk[length - WINDOW:, :] = carry_k.astype(dk.dtype)
    dv[length - WINDOW:, :] = carry_v

def window_back(low, high, first, second, hk, hv, go, rows, length):
    groups = HEADS // 4
    total = rows * length
    return pl.pallas_call(
        functools.partial(window_back_kernel, length=length, per_row=length // WINDOW), grid=(rows, groups),
        in_specs=[smem_spec(), smem_spec(), spec_col(length, 1), spec_col(length, 5), spec_col(length, 1), spec_tok(WINDOW, 256), spec_tok(WINDOW, 256), spec_tok(length, 256)],
        out_specs=[spec_tok(length, 256)] * 3 + [spec_tok(WINDOW, 256)] * 2,
        out_shape=[jax.ShapeDtypeStruct((total, 1024), BF), jax.ShapeDtypeStruct((total, 1024), F32), jax.ShapeDtypeStruct((total, 1024), F32),
                   jax.ShapeDtypeStruct((rows * WINDOW, 1024), BF), jax.ShapeDtypeStruct((rows * WINDOW, 1024), BF)],
        scratch_shapes=[pltpu.VMEM((length + WINDOW, 256), BF)] * 2 + [pltpu.VMEM((8, 256), F32)] * 2,
        compiler_params=PARAMS, name="window_back",
        cost_estimate=pl.CostEstimate(flops=rows*HEADS*2*10*length*128*256, bytes_accessed=16*MIB, transcendentals=0),
    )(low, high, second, second, first, hk, hv, go)

def piece_mean(x):
    a = lax.broadcasted_iota(jnp.int32, (256, 256), 0) // 64
    b = lax.broadcasted_iota(jnp.int32, (256, 256), 1) // 64
    ones = jnp.where(a == b, 1.0 / 64, 0.0).astype(BF)
    high = x.astype(BF)
    return nn(high, ones) + nn((x - high.astype(F32)).astype(BF), ones)

def through_state(x_t, state, group):
    state_t = state.T.astype(BF)
    parts = []
    for h in range(4):
        x = x_t[pl.ds(pl.multiple_of(group * 4 * FEAT + h * FEAT, FEAT), FEAT), :]
        parts.append(nn(state_t[h * 64:(h + 1) * 64], features_t(x).astype(BF)))
    return jnp.concatenate(parts, axis=0).T

def mix_kernel(q, state, local, windowed, early, numer, mixed, q_t):
    g = pl.program_id(1)
    @pl.when(g == 0)
    def _():
        q_t[...] = q[...].astype(F32).T
    num = local[...] + through_state(q_t, state[0, 0].astype(F32), g) * early[...]
    rho = lax.rsqrt(piece_mean(num * num) + EPSILON)
    numer[...] = num
    mixed[...] = (num * rho + windowed[...]).astype(BF)

def mix(q, state, local, windowed, early, rows, length):
    groups = HEADS // 4
    total = rows * length
    return pl.pallas_call(
        mix_kernel, grid=(rows, groups),
        in_specs=[spec_all(length, 256), SPEC_STATE, spec_tok(length, 256), spec_tok(length, 256), spec_all(length, 1)],
        out_specs=[spec_tok(length, 256)] * 2,
        out_shape=[jax.ShapeDtypeStruct((total, 1024), F32), jax.ShapeDtypeStruct((total, 1024), BF)],
        scratch_shapes=[pltpu.VMEM((256, length), F32)],
        compiler_params=PARAMS, name="mix",
        cost_estimate=pl.CostEstimate(flops=rows*HEADS*2*1024*256*256, bytes_accessed=18*MIB, transcendentals=0),
    )(q, state, local, windowed, early)

def numer_back_kernel(q, numer, gm, early, grad_numer, grad_state, q_t):
    g = pl.program_id(1)
    @pl.when(g == 0)
    def _():
        q_t[...] = q[...].astype(F32).T
    num = numer[...]
    rho = lax.rsqrt(piece_mean(num * num) + EPSILON)
    lin = num * rho
    gl = gm[...].astype(F32)
    gn = (rho * (gl - lin * piece_mean(gl * lin))).astype(BF)
    grad_numer[...] = gn
    grad_state[0, 0] = states_of(q_t, gn * early[...].astype(BF), g)

def numer_back(q, numer, gm, early, rows, length):
    groups = HEADS // 4
    total = rows * length
    return pl.pallas_call(
        numer_back_kernel, grid=(rows, groups),
        in_specs=[spec_all(length, 256), spec_tok(length, 256), spec_tok(length, 256), spec_all(length, 1)],
        out_specs=[spec_tok(length, 256), SPEC_STATE],
        out_shape=[jax.ShapeDtypeStruct((total, 1024), BF), jax.ShapeDtypeStruct((rows, groups, ROWS_PHI, 256), F32)],
        scratch_shapes=[pltpu.VMEM((256, length), F32)],
        compiler_params=PARAMS, name="numer_back",
        cost_estimate=pl.CostEstimate(flops=rows*HEADS*2*1024*256*256, bytes_accessed=10*MIB, transcendentals=0),
    )(q, numer, gm, early)

def intra_back_kernel(q, k, v, gn, dv_in, low, end, early_r, state, dq, dk_t, dv, mask, q_t, k_t, dq_t, *, length):
    g = pl.program_id(1)
    half = length // 2
    @pl.when(g == 0)
    def _():
        j = lax.broadcasted_iota(jnp.int32, (length, length), 0)
        i = lax.broadcasted_iota(jnp.int32, (length, length), 1)
        mask[...] = ((j >= low[0]) & (j <= i) & (j < end[0])).astype(BF)
        q_t[...] = q[...].astype(F32).T
        k_t[...] = k[...].astype(F32).T
    qv, kv, vv, gv = q[...], k[...], v[...], gn[...]
    st = state[0, 0].astype(BF)
    top = dv_in[:half, :]
    bottom = dv_in[half:, :]
    for h in range(4):
        at = pl.ds(pl.multiple_of(g * 4 * FEAT + h * FEAT, FEAT), FEAT)
        km = kv * lane_mask(HEADS * FEAT, FEAT, g * 4 + h)
        vm = vv * lane_mask(256, 64, h)
        gm = gv * lane_mask(256, 64, h)
        qx, kx = q_t[at, :], k_t[at, :]
        qb, kb = qx.astype(BF), kx.astype(BF)
        u0 = 1.0 + nt(km[:half], qv) * FEAT ** -0.5
        u1 = 1.0 + nt(km[half:], qv[half:]) * FEAT ** -0.5
        ga0 = nt(vm[:half], gv)
        ga1 = nt(vm[half:], gv[half:])
        m0, m1 = mask[:half, :], mask[half:, half:]
        a0 = (0.5 + 0.5 * u0 * u0).astype(BF) * m0
        a1 = (0.5 + 0.5 * u1 * u1).astype(BF) * m1
        ds0 = (ga0 * u0 * FEAT ** -0.5).astype(BF) * m0
        ds1 = (ga1 * u1 * FEAT ** -0.5).astype(BF) * m1
        top = top + nn(a0, gm)
        bottom = bottom + nn(a1, gm[half:])
        dk_t[0, at, :half] = nt(qb, ds0)
        dk_t[0, at, half:] = nt(qb[:, half:], ds1)
        d = nn(kb[:, :half], ds0)
        d = d + jnp.concatenate([jnp.zeros((FEAT, half), F32), nn(kb[:, half:], ds1)], axis=1)
        gphi = nt(st * lane_mask(256, 64, h), gv) * early_r[0]
        dq_t[at, :] = d + features_back_t(qx, gphi)
    dv[:half, :] = top
    dv[half:, :] = bottom
    @pl.when(g == pl.num_programs(1) - 1)
    def _():
        dq[...] = dq_t[...].T.astype(BF)

def intra_back(first, second, gn, dv_in, low, end, early_r, state, rows, length):
    groups = HEADS // 4
    total = rows * length
    return pl.pallas_call(
        functools.partial(intra_back_kernel, length=length), grid=(rows, groups),
        in_specs=[spec_all(length, 256), spec_all(length, 256), spec_col(length, 1), spec_tok(length, 256), spec_tok(length, 256),
                  pl.BlockSpec((1, 1, length), lambda r, g: (r, 0, 0)),
                  pl.BlockSpec((1, 1, length), lambda r, g: (r, 0, 0)), pl.BlockSpec((1, 1, length), lambda r, g: (r, 0, 0)), SPEC_STATE],
        out_specs=[spec_all(length, 256), pl.BlockSpec((1, 256, length), lambda r, g: (r, 0, 0)), spec_tok(length, 256)],
        out_shape=[jax.ShapeDtypeStruct((total, 256), BF), jax.ShapeDtypeStruct((rows, 256, length), F32), jax.ShapeDtypeStruct((total, 1024), F32)],
        scratch_shapes=[pltpu.VMEM((length, length), BF)] + [pltpu.VMEM((256, length), F32)] * 3,
        compiler_params=PARAMS, name="intra_back",
        cost_estimate=pl.CostEstimate(flops=rows*HEADS*2*15*256*256*256, bytes_accessed=14*MIB, transcendentals=0),
    )(second, first, first, gn, dv_in, low, end, early_r, state)

def state_back_kernel(k, v, dk_in, dv_in, dhv, owned_r, owned_c, state, dk, dv, k_t, dk_t, *, length):
    g = pl.program_id(1)
    @pl.when(g == 0)
    def _():
        k_t[...] = k[...].astype(F32).T
    st = state[0, 0].astype(F32)
    sb = st.astype(BF)
    vv = v[...]
    dvs = through_state(k_t, st, g) * owned_c[...]
    tail = length - WINDOW
    dv[:tail, :] = (dv_in[:tail, :] + dvs[:tail]).astype(BF)
    dv[tail:, :] = (dv_in[tail:, :] + dvs[tail:] + dhv[...].astype(F32)).astype(BF)
    for h in range(4):
        at = pl.ds(pl.multiple_of(g * 4 * FEAT + h * FEAT, FEAT), FEAT)
        gphi = nt(sb * lane_mask(256, 64, h), vv) * owned_r[0]
        dk_t[at, :] = dk_in[0, at, :] + features_back_t(k_t[at, :], gphi)
    @pl.when(g == pl.num_programs(1) - 1)
    def _():
        dk[...] = dk_t[...].T.astype(BF)

def state_back(first, dk_in, dv_in, dhv, owned_r, owned_c, state, rows, length):
    groups = HEADS // 4
    total = rows * length
    return pl.pallas_call(
        functools.partial(state_back_kernel, length=length), grid=(rows, groups),
        in_specs=[spec_all(length, 256), spec_col(length, 1), pl.BlockSpec((1, 256, length), lambda r, g: (r, 0, 0)), spec_tok(length, 256),
                  spec_tok(WINDOW, 256), pl.BlockSpec((1, 1, length), lambda r, g: (r, 0, 0)), spec_all(length, 1), SPEC_STATE],
        out_specs=[spec_all(length, 256), spec_tok(length, 256)],
        out_shape=[jax.ShapeDtypeStruct((total, 256), BF), jax.ShapeDtypeStruct((total, 1024), BF)],
        scratch_shapes=[pltpu.VMEM((256, length), F32)] * 2,
        compiler_params=PARAMS, name="state_back",
        cost_estimate=pl.CostEstimate(flops=rows*HEADS*2*1024*256*256, bytes_accessed=14*MIB, transcendentals=0),
    )(first, first, dk_in, dv_in, dhv, owned_r, owned_c, state)


def proj_kernel(tokens, gain, w, normed, out):
    @pl.when(pl.program_id(0) == 0)
    def _():
        x = tokens[...].astype(F32)
        normed[...] = (x * lax.rsqrt(jnp.mean(x * x, axis=-1, keepdims=True) + EPSILON) * gain[...]).astype(BF)
    out[...] = nn(normed[...], w[...]).astype(BF)

def proj_more_kernel(normed, w, out):
    out[...] = nn(normed[...], w[...]).astype(BF)

def project(tokens, gain, w_in):
    toks, width = tokens.shape
    tiles = w_in.shape[1] // 256
    lin = HEADS * FEAT // 256
    heads = width // 256
    whole = lambda s: (0, 0)
    one = dict(pipeline_mode=pl.Buffered(1))
    params = pltpu.CompilerParams(vmem_limit_bytes=56 * MIB, dimension_semantics=("arbitrary",))
    count = 1 + heads
    normed, first = pl.pallas_call(
        proj_kernel, grid=(count,),
        in_specs=[pl.BlockSpec((toks, width), whole, **one), pl.BlockSpec((1, width), whole),
                  pl.BlockSpec((width, 256), lambda s: (0, jnp.where(s == 0, 1, tiles - count + s)))],
        out_specs=[pl.BlockSpec((toks, width), whole, **one), pl.BlockSpec((toks, 256), lambda s: (0, s))],
        out_shape=[jax.ShapeDtypeStruct((toks, width), BF), jax.ShapeDtypeStruct((toks, 256 * count), BF)],
        compiler_params=params, name="project_keys",
        cost_estimate=pl.CostEstimate(flops=2 * toks * width * 256 * count, bytes_accessed=10 * MIB, transcendentals=0),
    )(tokens, gain.reshape(1, width), w_in)
    rest = tiles - count
    second = pl.pallas_call(
        proj_more_kernel, grid=(rest,),
        in_specs=[pl.BlockSpec((toks, width), whole, **one), pl.BlockSpec((width, 256), lambda s: (0, jnp.where(s == 0, 0, s + 1)))],
        out_specs=pl.BlockSpec((toks, 256), lambda s: (0, s)),
        out_shape=jax.ShapeDtypeStruct((toks, 256 * rest), BF),
        compiler_params=params, name="project_rest",
        cost_estimate=pl.CostEstimate(flops=2 * toks * width * 256 * rest, bytes_accessed=12 * MIB, transcendentals=0),
    )(normed, w_in)
    return normed, first, second

def swap(x, bit, count):
    return lax.ppermute(x, "seq", [(i, i ^ (1 << bit)) for i in range(count)])

def pick(x, index, axis):
    return lax.dynamic_index_in_dim(x, index, axis, False)

def scan_states(local, table, me, count, backward):
    bits = count.bit_length() - 1
    core = me % 2
    flags = pick(table, core, 1)
    place = jnp.arange(count, dtype=jnp.int32)
    chip = me - core
    order = jnp.arange(1, bits, dtype=jnp.int32)
    base = (me >> (order + 1)) << (order + 1)
    middle = base + (1 << order)
    upper = ((me >> order) & 1) == 1
    def flagged(low, high):
        inside = (place[None, :] >= low[:, None]) & (place[None, :] < high[:, None])
        return jnp.max(jnp.where(inside, flags[None, :], 0.0), axis=1)
    if backward:
        cut = 1.0 - flagged(base, middle)
        stop = 1.0 - flagged(jnp.full_like(base, chip + 2), middle)
        own, other = jnp.where(upper, cut, 1.0), jnp.where(upper, 1.0, cut)
        into = jnp.where(upper, 0.0, stop)
    else:
        cut = 1.0 - flagged(middle, base + (2 << order))
        stop = 1.0 - flagged(middle, jnp.full_like(base, chip))
        own, other = jnp.where(upper, 1.0, cut), jnp.where(upper, cut, 1.0)
        into = jnp.where(upper, stop, 0.0)
    f0 = pick(flags, chip, 0)
    f1 = pick(flags, chip + 1, 0)
    mine = pick(local, core, 0)
    theirs = swap(pick(local, 1 - core, 0).astype(BF), 0, count).astype(F32)
    at0 = jnp.where(core == 0, mine, theirs)
    at1 = jnp.where(core == 0, theirs, mine)
    total = (at0 + (1.0 - f0) * at1 if backward else at1 + (1.0 - f1) * at0).astype(BF)
    entering = jnp.zeros_like(mine)
    for b in range(1, bits):
        received = swap(total, b, count).astype(F32)
        entering = entering + into[b - 1] * received
        if b < bits - 1:
            total = (own[b - 1] * total.astype(F32) + other[b - 1] * received).astype(BF)
    if backward:
        x1, x0 = entering, at1 + (1.0 - f1) * entering
    else:
        x0, x1 = entering, at0 + (1.0 - f0) * entering
    x0, x1 = x0.astype(BF), x1.astype(BF)
    keep = jnp.where(core == 0, x0, x1)
    back = swap(jnp.where(core == 0, x1, x0), 0, count)
    return jnp.stack([jnp.where(core == 0, keep, back), jnp.where(core == 0, back, keep)])

def halve(keep, received, me, count, order):
    left = list(range(count.bit_length() - 2, 0, -1))
    for b in order:
        at = left.index(b)
        left.remove(b)
        mine = (me >> b) & 1
        def part(x, which):
            x = x.reshape((1 << at, 2, -1) + x.shape[1:])
            x = pick(x, which, 1)
            return x.reshape((-1,) + x.shape[2:])
        send = part(keep, 1 - mine) + part(received, 1 - mine)
        keep = part(keep, mine) + part(received, mine)
        received = swap(send, b, count)
    return keep[0].astype(F32) + received[0].astype(F32)

def finish(rows, me, count):
    core = me % 2
    each = rows.shape[0] // 2
    own = lax.dynamic_slice_in_dim(rows, core * each, each, 0)
    got = swap(lax.dynamic_slice_in_dim(rows, (1 - core) * each, each, 0), 0, count)
    return jnp.where(core == 0, own, got), jnp.where(core == 0, got, own)

def chips_first(x, chips):
    return x.reshape(chips, x.shape[0] // chips, x.shape[1])

def reduced(keep, send, me, count, order):
    chips = count // 2
    got = swap(send, 0, count)
    return finish(halve(chips_first(keep, chips), chips_first(got, chips), me, count, order), me, count)

def gain_sum(part, me):
    all_parts = lax.all_gather(part, "seq")
    each = part.shape[0] // all_parts.shape[0]
    return jnp.sum(lax.dynamic_slice_in_dim(all_parts, me * each, each, 1), axis=0)

def shards(tokens, seq_starts, seq_lengths, gain_in, gain_mlp, w_in, w_out, w_gate_up, w_down, cotangent):
    rows, length, width = tokens.shape
    count = lax.axis_size("seq")
    bits = count.bit_length() - 1
    order_a = list(range(1, bits))
    order_b = [2, 1] + list(range(3, bits))
    me = lax.axis_index("seq")
    core = me % 2
    total = rows * length
    begin = me * length
    ends = seq_starts + seq_lengths
    places = begin + jnp.arange(length, dtype=jnp.int32)
    last = seq_starts[:, -1:]
    reset = (last[:, 0] >= begin).astype(F32)
    early = (seq_starts < begin).astype(F32)
    owned = ((seq_starts == last) & (places[None, :] < ends)).astype(F32)
    low, end = seq_starts - begin, ends - begin
    column = lambda x: x.reshape(total, 1)
    line = lambda x: x.reshape(rows, 1, length)
    block_at = places[None, ::WINDOW] - WINDOW
    low_w = (seq_starts[:, ::WINDOW] - block_at).reshape(-1)
    high_w = (ends[:, ::WINDOW] - block_at).reshape(-1)
    table = lax.all_gather(reset, "seq")

    x = tokens.reshape(total, width)
    cot = cotangent.reshape(total, width)
    normed, first, second = project(x, gain_in, w_in)
    local_state = local_states(first, column(owned), rows, length)
    state_in = scan_states(local_state, table, me, count, False)

    tails = lambda a, at: a.reshape(rows, length, -1)[:, -WINDOW:, at:at + width]
    forward = [(i, i + 1) for i in range(count - 1)]
    backward = [(i + 1, i) for i in range(count - 1)]
    halo = lax.ppermute(jnp.stack([tails(second, 256 + width), tails(first, 256)]), "seq", forward)
    halo = halo.reshape(2, rows * WINDOW, width)
    local = intra(first, second, column(low), column(end), rows, length)
    windowed = window(low_w, high_w, first, second, halo[0], halo[1], rows, length)
    numer, mixed = mix(second, state_in, local, windowed, column(early), rows, length)
    (result, grad_resid, grad_mixed, gain_mlp_part, keep_gu, send_gu, keep_d, send_d, keep_o, send_o) = mlp(
        core.reshape(1), mixed, x, cot, w_out, gain_mlp, w_gate_up, w_down)
    part_gain_mlp = gain_sum(gain_mlp_part[0], me)
    grad_numer, grad_state_in = numer_back(second, numer, grad_mixed, column(early), rows, length)
    grad_state = scan_states(grad_state_in, table, me, count, True)
    part_gate_up = jnp.concatenate(reduced(keep_gu, send_gu, me, count, order_a), axis=1)
    part_down = jnp.concatenate(reduced(keep_d, send_d, me, count, order_b), axis=1)
    part_out = jnp.concatenate(reduced(keep_o, send_o, me, count, order_b), axis=1)

    dq_win, dk_win, dv_win, dhk, dhv = window_back(low_w, high_w, first, second, halo[0], halo[1], grad_mixed, rows, length)
    returned = lax.ppermute(jnp.stack([dhk, dhv]), "seq", backward).reshape(2, rows, WINDOW, width)
    dq_lin, dk_t, dv_part = intra_back(first, second, grad_numer, dv_win, line(low), line(end), line(early), state_in, rows, length)
    dk_lin, dv = state_back(first, dk_t, dv_part, returned[1].reshape(rows * WINDOW, width), line(owned), column(owned), grad_state, rows, length)
    dk_win = dk_win.reshape(rows, length, width)
    dk_win = jnp.concatenate([dk_win[:, :-WINDOW], dk_win[:, -WINDOW:] + returned[0].astype(F32)], axis=1).astype(BF).reshape(total, width)
    lin = HEADS * FEAT

    grad_projected = jnp.concatenate([dq_lin, dk_lin, dq_win, dk_win, dv], axis=1)
    grad_w = jnp.dot(normed.T, grad_projected, preferred_element_type=F32).astype(BF)
    half = grad_w.shape[1] // 2
    keep_i = lax.dynamic_slice_in_dim(grad_w, core * half, half, 1)
    send_i = lax.dynamic_slice_in_dim(grad_w, (1 - core) * half, half, 1)
    part_in = jnp.concatenate(reduced(keep_i, send_i, me, count, order_b), axis=1)
    grad_normed = jnp.dot(grad_projected, w_in.T, preferred_element_type=F32)
    stream = x.astype(F32)
    scale = lax.rsqrt(jnp.mean(stream * stream, axis=-1, keepdims=True) + EPSILON)
    part_gain_in = gain_sum(jnp.sum(grad_normed * stream * scale, axis=0), me)
    c = grad_normed * gain_in
    grad_tokens = grad_resid + scale * c - stream * (scale * scale * scale * jnp.mean(c * stream, axis=-1, keepdims=True))
    return (result.reshape(rows, length, width), grad_tokens.reshape(rows, length, width), part_gain_in, part_gain_mlp,
            part_in, part_out, part_gate_up, part_down)

def solution(mesh):
    split = P(None, "seq", None)
    placed = (split, P(None, "seq"), P(None, "seq"), P(), P(), P(), P(), P(), P(), split)
    return jax.shard_map(shards, mesh=mesh, in_specs=placed,
        out_specs=(split, split, P("seq"), P("seq"), P("seq", None), P("seq", None), P("seq", None), P("seq", None)),
        check_vma=False)
```

```python
import functools
import jax
import jax.numpy as jnp
from jax import lax
from jax.experimental import pallas as pl
from jax.experimental.pallas import tpu as pltpu
from jax.sharding import PartitionSpec as P
F32=jnp.float32; BF=jnp.bfloat16
EPSILON=1e-6
MIB=1<<20

def nn(a,b): return lax.dot_general(a,b,(((1,),(0,)),((),())),preferred_element_type=F32)
def nt(a,b): return lax.dot_general(a,b,(((1,),(1,)),((),())),preferred_element_type=F32)
def tn(a,b): return lax.dot_general(a,b,(((0,),(0,)),((),())),preferred_element_type=F32)

def parted(x, first, each):
    x = x.reshape(x.shape[0] // (2 * each), 2, each, x.shape[1])
    a, b = x[:, 0].reshape(-1, x.shape[3]), x[:, 1].reshape(-1, x.shape[3])
    return jnp.where(first, a, b).astype(BF), jnp.where(first, b, a).astype(BF)

def mlp_kernel(core_ref, mixed, tokens, cot, w_out, gain, wg, wu, wd,
               result, grad_resid, grad_mixed, keep_g, send_g, keep_u, send_u, keep_d, send_d, keep_o, send_o,
               resid, acc, dh, hn, hn_t, hid, dgate, dup, *, steps, chunk, each):
    step = pl.program_id(0)
    toks = mixed.shape[0]
    width = mixed.shape[1]
    count = toks // chunk
    first = core_ref[0] == 0

    def rows(n):
        return pl.ds(pl.multiple_of(n * chunk, chunk), chunk)

    @pl.when(step == 0)
    def _():
        def one(n, carry):
            r = rows(n)
            res = tokens[r, :].astype(F32) + nn(mixed[r, :], w_out[...])
            scale = lax.rsqrt(jnp.mean(res * res, axis=-1, keepdims=True) + EPSILON)
            h = (res * scale * gain[...]).astype(BF)
            resid[r, :] = res
            acc[r, :] = res
            dh[r, :] = jnp.zeros((chunk, width), F32)
            hn[r, :] = h
            return carry
        lax.fori_loop(0, count, one, 0)
        for n in range(count):
            hn_t[:, n * chunk:(n + 1) * chunk] = hn[n * chunk:(n + 1) * chunk, :].T

    def forward(n, carry):
        r = rows(n)
        h = hn[r, :]
        gate = nn(h, wg[...])
        up = nn(h, wu[...])
        dhid = nt(cot[r, :], wd[...])
        sig = 1.0 / (1.0 + jnp.exp(-gate))
        silu = gate * sig
        hidden = (silu * up).astype(BF)
        d_gate = (dhid * up * (sig + silu * (1.0 - sig))).astype(BF)
        d_up = (dhid * silu).astype(BF)
        hid[r, :] = hidden
        dgate[r, :] = d_gate
        dup[r, :] = d_up
        acc[r, :] += nn(hidden, wd[...])
        dh[r, :] += nt(d_gate, wg[...]) + nt(d_up, wu[...])
        return carry
    lax.fori_loop(0, count, forward, 0, unroll=2)

    half = width // 2
    grad_d = tn(hid[...], cot[...])
    left, right = grad_d[:, :half].astype(BF), grad_d[:, half:].astype(BF)
    keep_d[...] = jnp.where(first, left, right)
    send_d[...] = jnp.where(first, right, left)

    def weights(n, carry):
        r = rows(n)
        o = pl.ds(pl.multiple_of(n * (chunk // 2), chunk // 2), chunk // 2)
        keep_g[o, :], send_g[o, :] = parted(nn(hn_t[r, :], dgate[...]), first, each)
        keep_u[o, :], send_u[o, :] = parted(nn(hn_t[r, :], dup[...]), first, each)
        return carry
    lax.fori_loop(0, width // chunk, weights, 0, unroll=2)

    @pl.when(step == steps - 1)
    def _():
        def one(n, carry):
            r = rows(n)
            res = resid[r, :]
            scale = lax.rsqrt(jnp.mean(res * res, axis=-1, keepdims=True) + EPSILON)
            grad = dh[r, :]
            c = grad * gain[...]
            back = cot[r, :].astype(F32) + scale * c - res * (scale * scale * scale * jnp.mean(c * res, axis=-1, keepdims=True))
            result[r, :] = acc[r, :].astype(BF)
            grad_resid[r, :] = back
            b = back.astype(BF)
            hn[r, :] = b
            grad_mixed[r, :] = nt(b, w_out[...]).astype(BF)
            return carry
        lax.fori_loop(0, count, one, 0)
        for n in range(count):
            hn_t[:, n * chunk:(n + 1) * chunk] = mixed[n * chunk:(n + 1) * chunk, :].T
        def outer(n, carry):
            r = rows(n)
            o = pl.ds(pl.multiple_of(n * (chunk // 2), chunk // 2), chunk // 2)
            keep_o[o, :], send_o[o, :] = parted(nn(hn_t[r, :], hn[...]), first, each)
            return carry
        lax.fori_loop(0, width // chunk, outer, 0)


VMEM = 64 * MIB
COST = dict(project_keys=6.8, state=7.4, project_rest=10, begun=2, joined=2.5, ended=3, intra=7.2, window=8.5, mix=10, mlp=88, numer_back=12,
    window_back=13, intra_back=14, sum_first=10.6, sum_second=6.4, state_back=0.1, weight_grad_early=0.1, weight_grad_late=0.1, input_grad_first=0.1, input_grad=0.1, in_first=3, in_second=3, quarters=3.5, tail=1.8, gathered=2.3, plain=2.0, sum_third=3.6)
HEADS=16; FEAT=16; WINDOW=64; ROWS_PHI=160; FLAG_ROW=153

class Order:
    last = None

def call(kernel, name, grid, ins, outs, scratch=(), flops=0, moved=10 * MIB, deps=(), into=None, alias=None, scalars=(), through=()):
    arrays, specs = [a for a, _ in ins], [s for _, s in ins]
    count, ahead = len(arrays), len(scalars)
    into = list(into or ())
    deps = list(deps)
    if Order.last is not None and not any(Order.last is a for a in into + deps + arrays):
        deps.append(Order.last)
    extra = deps + into + list(through)
    aliases = {ahead + count + len(deps) + n: n for n in range(len(into))}
    aliases.update({ahead + i: o for i, o in (alias or {}).items()})
    aliases.update({ahead + count + len(deps) + len(into) + n: len(outs) + n for n in range(len(through))})
    results = len(outs)
    outs = list(outs) + [(a.shape, a.dtype, pl.BlockSpec(memory_space=pl.ANY)) for a in through]
    def body(*refs):
        begin = ahead + count + len(extra)
        kernel(*refs[:ahead + count], *refs[begin:begin + results], *refs[begin + len(outs):])
    out = pl.pallas_call(
        body, grid_spec=pltpu.PrefetchScalarGridSpec(num_scalar_prefetch=ahead, grid=grid,
            in_specs=specs + [pl.BlockSpec(memory_space=pl.ANY)] * len(extra), out_specs=[s for _, _, s in outs], scratch_shapes=list(scratch)),
        out_shape=[jax.ShapeDtypeStruct(shape, dtype) for shape, dtype, _ in outs],
        input_output_aliases=aliases, name=name,
        compiler_params=pltpu.CompilerParams(vmem_limit_bytes=VMEM, dimension_semantics=("arbitrary",) * len(grid)),
        cost_estimate=pl.CostEstimate(flops=int(COST.get(name, 2.0) * 1e9), bytes_accessed=1000, transcendentals=0),
    )(*scalars, *arrays, *extra)
    Order.last = out[0]
    return out

def lane_mask(width, size, which, dtype=BF):
    lanes = lax.broadcasted_iota(jnp.int32, (1, width), 1)
    return (lanes // size == which).astype(dtype)

def spread(values, length):
    block = lax.broadcasted_iota(jnp.int32, (1, length), 1) // WINDOW
    out = jnp.zeros((1, length), jnp.int32)
    for n, value in enumerate(values):
        out = jnp.where(block == n, value, out)
    return out

def scalars(ref, row, length):
    per_row = length // WINDOW
    return [ref[row * per_row + n] for n in range(per_row)]

def early_line(low, row, length):
    return (spread(scalars(low, row, length), length) < 0).astype(F32)

def owned_line(low, high, row, length):
    lows = scalars(low, row, length)
    place = lax.broadcasted_iota(jnp.int32, (1, length), 1)
    same = spread(lows, length) == lows[-1]
    return (same & (place < spread(scalars(high, row, length), length))).astype(F32)

def features_t(x):
    feat, toks = x.shape
    both = jnp.concatenate([x, x], axis=0)
    parts = [x * x * (2.0 * feat) ** -0.5]
    xs = x * feat ** -0.5
    for d in range(1, feat // 2):
        parts.append(xs * both[d:d + feat])
    parts.append(x * feat ** -0.25)
    parts.append(xs[:feat // 2] * x[feat // 2:])
    row = lax.broadcasted_iota(jnp.int32, (8, toks), 0)
    parts.append((row == 0).astype(F32))
    return jnp.concatenate(parts, axis=0)

def features_back_t(x, g):
    feat, toks = x.shape
    half = feat // 2
    both = jnp.concatenate([x, x], axis=0)
    total = g[:feat] * x * (2.0 * (2.0 * feat) ** -0.5)
    mixed = jnp.zeros((feat, toks), F32)
    for d in range(1, half):
        gd = g[d * feat:(d + 1) * feat]
        mixed = mixed + gd * both[d:d + feat]
        gx = gd * x
        mixed = mixed + jnp.concatenate([gx[feat - d:], gx[:feat - d]], axis=0)
    g8 = g[(half + 1) * feat:(half + 1) * feat + half]
    mixed = mixed + jnp.concatenate([g8 * x[half:], g8 * x[:half]], axis=0)
    return total + mixed * feat ** -0.5 + g[half * feat:(half + 1) * feat] * feat ** -0.25

def head_rows(group, h):
    return pl.ds(pl.multiple_of(group * 4 * FEAT + h * FEAT, FEAT), FEAT)

def states_of(x_t, y, group, line, flag):
    row = lax.broadcasted_iota(jnp.int32, (ROWS_PHI, 256), 0)
    out = jnp.where(row == FLAG_ROW, flag, 0.0)
    for h in range(4):
        out = out + nn((features_t(x_t[head_rows(group, h), :]) * line).astype(BF), y * lane_mask(256, 64, h))
    return out

def put_state(state, core, mine, send):
    r, g = pl.program_id(0), pl.program_id(1)
    @pl.when(r == core[0])
    def _():
        mine[g] = state
    @pl.when(r != core[0])
    def _():
        send[g] = state.astype(BF)

def state_outs():
    shape = (GROUPS, ROWS_PHI, 256)
    spec = pl.BlockSpec(shape, lambda r, g: (0, 0, 0))
    return [(shape, F32, spec), (shape, BF, spec)]

def state_kernel(core, low, high, k, v, mine, send, k_t, line, *, length):
    r, g = pl.program_id(0), pl.program_id(1)
    @pl.when(g == 0)
    def _():
        k_t[...] = k[...].astype(F32).T
        line[...] = owned_line(low, high, r, length)
    flag = (low[(r + 1) * (length // WINDOW) - 1] >= 0).astype(F32)
    put_state(states_of(k_t, v[...], g, line[...], flag), core, mine, send)

def spec_col(length, first=0, row=0):
    return pl.BlockSpec((length, 256), lambda r, g: (r + row, first + g))
def spec_all(length, row=0):
    return pl.BlockSpec((length, 256), lambda r, g: (r + row, 0))
SPEC_STATE = pl.BlockSpec((1, ROWS_PHI, 256), lambda r, g: (g, 0, 0))
def spec_t(length, row=0):
    return pl.BlockSpec((1, 256, length), lambda r, g: (r + row, 0, 0))
SMEM = pl.BlockSpec(memory_space=pltpu.SMEM)
GROUPS = HEADS // 4

def local_states(core, low, high, k, v, rows, length):
    return call(functools.partial(state_kernel, length=length), "state", (rows, GROUPS),
        [(core, SMEM), (low, SMEM), (high, SMEM), (k, spec_all(length)), (v, spec_col(length))], state_outs(),
        [pltpu.VMEM((256, length), F32), pltpu.VMEM((1, length), F32)], flops=rows * HEADS * 2 * ROWS_PHI * 256 * length)

def intra_kernel(low, high, q, k, v, out, mask, *, length, row):
    g = pl.program_id(1)
    half = length // 2
    @pl.when(g == 0)
    def _():
        lows, highs = scalars(low, row, length), scalars(high, row, length)
        for n in range(length // WINDOW):
            i = lax.broadcasted_iota(jnp.int32, (WINDOW, length), 0) + n * WINDOW
            j = lax.broadcasted_iota(jnp.int32, (WINDOW, length), 1)
            mask[n * WINDOW:(n + 1) * WINDOW, :] = ((j >= lows[n]) & (j <= i) & (j < highs[n])).astype(BF)
    qv, kv, vv = q[...], k[...], v[...]
    top = bottom = None
    for h in range(4):
        km = kv * lane_mask(HEADS * FEAT, FEAT, g * 4 + h)
        vm = vv * lane_mask(256, 64, h)
        u0 = 1.0 + nt(qv[:half], km[:half]) * FEAT ** -0.5
        a0 = (0.5 + 0.5 * u0 * u0).astype(BF) * mask[:half, :half]
        u1 = 1.0 + nt(qv[half:], km) * FEAT ** -0.5
        a1 = (0.5 + 0.5 * u1 * u1).astype(BF) * mask[half:, :]
        o0, o1 = nn(a0, vm[:half]), nn(a1, vm)
        top = o0 if top is None else top + o0
        bottom = o1 if bottom is None else bottom + o1
    out[:half, :] = top
    out[half:, :] = bottom

def intra(low, high, p, rows, length, row, deps=(), into=None):
    return call(functools.partial(intra_kernel, length=length, row=row), "intra", (1, GROUPS),
        [(low, SMEM), (high, SMEM), (p.q_lin, spec_all(length, row)), (p.k_lin, spec_all(length, row)), (p.v, spec_col(length, 0, row))],
        [((rows * length, 1024), F32, spec_col(length, 0, row))],
        [pltpu.VMEM((length, length), BF)], flops=HEADS * 2 * 6 * 256 ** 3, deps=deps, into=into)

def stacked(x):
    return jnp.concatenate([x * lane_mask(256, 64, h) for h in range(4)], axis=0)

def unstacked(x):
    total = None
    for h in range(4):
        part = x[h * WINDOW:(h + 1) * WINDOW] * lane_mask(256, 64, h, F32)
        total = part if total is None else total + part
    return total

def window_kernel(low, high, q, k, v, hk, hv, out, ka, va, *, length, row):
    per_row = length // WINDOW
    ka[:WINDOW, :] = hk[...]
    ka[WINDOW:, :] = k[...]
    va[:WINDOW, :] = hv[...]
    va[WINDOW:, :] = v[...]
    for n in range(per_row):
        shift = (1 - n) * WINDOW
        keys = ka[n * WINDOW:(n + 2) * WINDOW, :]
        vals = va[n * WINDOW:(n + 2) * WINDOW, :]
        s = nt(stacked(q[n * WINDOW:(n + 1) * WINDOW, :]), keys) * 64 ** -0.5
        key = lax.broadcasted_iota(jnp.int32, (4 * WINDOW, 2 * WINDOW), 1)
        query = lax.broadcasted_iota(jnp.int32, (4 * WINDOW, 2 * WINDOW), 0) % WINDOW
        at = row * per_row + n
        ok = (key >= query) & (key <= query + WINDOW) & (key >= low[at] + shift) & (key < high[at] + shift)
        s = jnp.where(ok, s, -1e30)
        p = jnp.exp(s - jnp.max(s, axis=1, keepdims=True))
        p = (p / jnp.sum(p, axis=1, keepdims=True)).astype(BF)
        out[n * WINDOW:(n + 1) * WINDOW, :] = unstacked(nn(p, vals))

def window_ins(low, high, p, halo, length, row):
    tail = lambda part: pl.BlockSpec((None, WINDOW, 256), lambda r, g: (part, r + row, g))
    return [(low, SMEM), (high, SMEM), (p.qk_win, spec_col(length, 0, row)), (p.qk_win, spec_col(length, GROUPS, row)), (p.v, spec_col(length, 0, row)),
            (halo, tail(0)), (halo, tail(1))]

def window(low, high, p, halo, rows, length, row, deps=(), into=None):
    return call(functools.partial(window_kernel, length=length, row=row), "window", (1, GROUPS),
        window_ins(low, high, p, halo, length, row),
        [((rows * length, 1024), F32, spec_col(length, 0, row))],
        [pltpu.VMEM((length + WINDOW, 256), BF)] * 2, flops=HEADS * 2 * 4 * length * 128 * 256, deps=deps, into=into)

def window_back_block(low, high, row, n, per_row, q, keys, vals, go):
    shift = (1 - n) * WINDOW
    at = row * per_row + n
    qs, gs = stacked(q), stacked(go)
    s = nt(keys, qs) * 64 ** -0.5
    key = lax.broadcasted_iota(jnp.int32, (2 * WINDOW, 4 * WINDOW), 0)
    query = lax.broadcasted_iota(jnp.int32, (2 * WINDOW, 4 * WINDOW), 1) % WINDOW
    ok = (key >= query) & (key <= query + WINDOW) & (key >= low[at] + shift) & (key < high[at] + shift)
    s = jnp.where(ok, s, -1e30)
    p = jnp.exp(s - jnp.max(s, axis=0, keepdims=True))
    p = p * (1.0 / jnp.sum(p, axis=0, keepdims=True))
    gp = nt(vals, gs)
    ds = (p * (gp - jnp.sum(p * gp, axis=0, keepdims=True)) * 64 ** -0.5).astype(BF)
    return unstacked(tn(ds, keys)).astype(BF), nn(ds, qs), nn(p.astype(BF), gs)

def window_back_first_kernel(low, high, q, k, v, hk, hv, go, q1, k1, v1, hk1, hv1, go1, dq, dk, dv, dh, q_kept, k_kept, v_kept, ka, va, *, length):
    per_row = length // WINDOW
    ka[:WINDOW, :] = hk[...]
    ka[WINDOW:, :] = k[...]
    va[:WINDOW, :] = hv[...]
    va[WINDOW:, :] = v[...]
    carry_k = carry_v = None
    for n in range(per_row):
        rows = slice(n * WINDOW, (n + 1) * WINDOW)
        both = slice(n * WINDOW, (n + 2) * WINDOW)
        dq[rows, :], dk_n, dv_n = window_back_block(low, high, 0, n, per_row, q[rows, :], ka[both, :], va[both, :], go[rows, :])
        if n == 0:
            dh[0, :WINDOW] = dk_n[:WINDOW].astype(BF)
            dh[1, :WINDOW] = dv_n[:WINDOW].astype(BF)
        else:
            dk[(n - 1) * WINDOW:n * WINDOW, :] = (carry_k + dk_n[:WINDOW]).astype(BF)
            dv[(n - 1) * WINDOW:n * WINDOW, :] = carry_v + dv_n[:WINDOW]
        carry_k, carry_v = dk_n[WINDOW:], dv_n[WINDOW:]
    dk[length - WINDOW:, :] = carry_k.astype(BF)
    dv[length - WINDOW:, :] = carry_v
    keys = jnp.concatenate([hk1[...], k1[...]], axis=0)
    vals = jnp.concatenate([hv1[...], v1[...]], axis=0)
    q_kept[...], dk_n, dv_n = window_back_block(low, high, 1, 0, per_row, q1[...], keys, vals, go1[...])
    dh[0, WINDOW:] = dk_n[:WINDOW].astype(BF)
    dh[1, WINDOW:] = dv_n[:WINDOW].astype(BF)
    k_kept[...] = dk_n[WINDOW:]
    v_kept[...] = dv_n[WINDOW:]

def window_back_second_kernel(low, high, q, k, v, go, q_kept, k_kept, v_kept, dq, dk, dv, *, length):
    per_row = length // WINDOW
    dq[:WINDOW, :] = q_kept[...]
    carry_k, carry_v = k_kept[...], v_kept[...]
    for n in range(1, per_row):
        rows = slice(n * WINDOW, (n + 1) * WINDOW)
        both = slice((n - 1) * WINDOW, (n + 1) * WINDOW)
        dq[rows, :], dk_n, dv_n = window_back_block(low, high, 1, n, per_row, q[rows, :], k[both, :], v[both, :], go[rows, :])
        dk[(n - 1) * WINDOW:n * WINDOW, :] = (carry_k + dk_n[:WINDOW]).astype(BF)
        dv[(n - 1) * WINDOW:n * WINDOW, :] = carry_v + dv_n[:WINDOW]
        carry_k, carry_v = dk_n[WINDOW:], dv_n[WINDOW:]
    dk[length - WINDOW:, :] = carry_k.astype(BF)
    dv[length - WINDOW:, :] = carry_v

def window_back_outs(total, length, row):
    spec = spec_col(length, 0, row)
    return [((total, 1024), BF, spec), ((total, 1024), BF, spec), ((total, 1024), F32, spec)]

def window_back_first(low, high, p, halo, go, rows, length):
    total, per_row = rows * length, length // WINDOW
    block = lambda first=0: pl.BlockSpec((WINDOW, 256), lambda r, g: (per_row, first + g))
    tail = lambda part: pl.BlockSpec((None, WINDOW, 256), lambda r, g: (part, 1, g))
    small = spec_col(WINDOW)
    got = call(functools.partial(window_back_first_kernel, length=length), "window_back", (1, GROUPS),
        window_ins(low, high, p, halo, length, 0) + [(go, spec_col(length)), (p.qk_win, block()), (p.qk_win, block(GROUPS)), (p.v, block()), (halo, tail(0)), (halo, tail(1)), (go, block())],
        window_back_outs(total, length, 0) + [((2, rows * WINDOW, 1024), BF, pl.BlockSpec((2, rows * WINDOW, 256), lambda r, g: (0, 0, g))),
         ((WINDOW, 1024), BF, small), ((WINDOW, 1024), F32, small), ((WINDOW, 1024), F32, small)],
        [pltpu.VMEM((length + WINDOW, 256), BF)] * 2)
    return got[:3], got[3], got[4:]

def window_back_second(low, high, p, go, into, kept, rows, length):
    small = spec_col(WINDOW)
    return call(functools.partial(window_back_second_kernel, length=length), "window_back", (1, GROUPS),
        [(low, SMEM), (high, SMEM), (p.qk_win, spec_col(length, 0, 1)), (p.qk_win, spec_col(length, GROUPS, 1)), (p.v, spec_col(length, 0, 1)), (go, spec_col(length, 0, 1))]
        + [(k, small) for k in kept], window_back_outs(rows * length, length, 1), into=into)

def piece_mean(x):
    a = lax.broadcasted_iota(jnp.int32, (256, 256), 0) // 64
    b = lax.broadcasted_iota(jnp.int32, (256, 256), 1) // 64
    ones = jnp.where(a == b, 1.0 / 64, 0.0).astype(BF)
    high = x.astype(BF)
    return nn(high, ones) + nn((x - high.astype(F32)).astype(BF), ones)

def through_state(x_t, state, group, line):
    state_t = state.T.astype(BF)
    parts = []
    for h in range(4):
        parts.append(nn(state_t[h * 64:(h + 1) * 64], features_t(x_t[head_rows(group, h), :]).astype(BF)))
    return (jnp.concatenate(parts, axis=0) * line).T

def state_for(row, core, kept, received):
    return jnp.where(row == core[0], kept[0].astype(F32), received[0].astype(F32))

def mix_kernel(core, low, q, kept, received, local, windowed, numer, mixed, q_t, line, *, length):
    r, g = pl.program_id(0), pl.program_id(1)
    @pl.when(g == 0)
    def _():
        q_t[...] = q[...].astype(F32).T
        line[...] = early_line(low, r, length)
    num = local[...] + through_state(q_t, state_for(r, core, kept, received), g, line[...])
    rho = lax.rsqrt(piece_mean(num * num) + EPSILON)
    numer[...] = num
    mixed[...] = (num * rho + windowed[...]).astype(BF)

def mix(core, low, p, state, local, windowed, rows, length, deps=()):
    total = rows * length
    return call(functools.partial(mix_kernel, length=length), "mix", (rows, GROUPS),
        [(core, SMEM), (low, SMEM), (p.q_lin, spec_all(length)), (state[0], SPEC_STATE), (state[1], SPEC_STATE), (local, spec_col(length)), (windowed, spec_col(length))],
        [((total, 1024), F32, spec_col(length)), ((total, 1024), BF, spec_col(length))],
        [pltpu.VMEM((256, length), F32), pltpu.VMEM((1, length), F32)], flops=rows * HEADS * 2 * 512 * 256 * 256, deps=deps)

def numer_back_kernel(core, low, q, numer, gm, grad_numer, mine, send, q_t, line, *, length):
    r, g = pl.program_id(0), pl.program_id(1)
    @pl.when(g == 0)
    def _():
        q_t[...] = q[...].astype(F32).T
        line[...] = early_line(low, r, length)
    num = numer[...]
    rho = lax.rsqrt(piece_mean(num * num) + EPSILON)
    lin = num * rho
    gl = gm[...].astype(F32)
    gn = (rho * (gl - lin * piece_mean(gl * lin))).astype(BF)
    grad_numer[...] = gn
    flag = (low[(r + 1) * (length // WINDOW) - 1] >= 0).astype(F32)
    put_state(states_of(q_t, gn, g, line[...], flag), core, mine, send)

def numer_back(core, low, p, numer, gm, rows, length, deps=()):
    total = rows * length
    return call(functools.partial(numer_back_kernel, length=length), "numer_back", (rows, GROUPS),
        [(core, SMEM), (low, SMEM), (p.q_lin, spec_all(length)), (numer, spec_col(length)), (gm, spec_col(length))],
        [((total, 1024), BF, spec_col(length))] + state_outs(),
        [pltpu.VMEM((256, length), F32), pltpu.VMEM((1, length), F32)], flops=rows * HEADS * 2 * 512 * 256 * 256, deps=deps)

def intra_back_kernel(core, low, high, q, k, v, gn, dv_in, kept, received, dq, dk_t, dv, mask, q_t, k_t, dq_t, early, *, length, row):
    g = pl.program_id(1)
    half = length // 2
    @pl.when(g == 0)
    def _():
        lows, highs = spread(scalars(low, row, length), length), spread(scalars(high, row, length), length)
        j = lax.broadcasted_iota(jnp.int32, (length, length), 0)
        i = lax.broadcasted_iota(jnp.int32, (length, length), 1)
        mask[...] = ((j >= lows) & (j <= i) & (j < highs)).astype(BF)
        early[...] = (lows < 0).astype(F32)
        q_t[...] = q[...].astype(F32).T
        k_t[...] = k[...].astype(F32).T
    qv, kv, vv, gv = q[...], k[...], v[...], gn[...]
    st = state_for(row, core, kept, received).astype(BF)
    top = dv_in[:half, :]
    bottom = dv_in[half:, :]
    for h in range(4):
        at = head_rows(g, h)
        km = kv * lane_mask(HEADS * FEAT, FEAT, g * 4 + h)
        vm = vv * lane_mask(256, 64, h)
        gm = gv * lane_mask(256, 64, h)
        qx, kx = q_t[at, :], k_t[at, :]
        qb, kb = qx.astype(BF), kx.astype(BF)
        u0 = 1.0 + nt(km[:half], qv) * FEAT ** -0.5
        u1 = 1.0 + nt(km[half:], qv[half:]) * FEAT ** -0.5
        ga0 = nt(vm[:half], gv)
        ga1 = nt(vm[half:], gv[half:])
        m0, m1 = mask[:half, :], mask[half:, half:]
        a0 = (0.5 + 0.5 * u0 * u0).astype(BF) * m0
        a1 = (0.5 + 0.5 * u1 * u1).astype(BF) * m1
        ds0 = (ga0 * u0 * FEAT ** -0.5).astype(BF) * m0
        ds1 = (ga1 * u1 * FEAT ** -0.5).astype(BF) * m1
        top = top + nn(a0, gm)
        bottom = bottom + nn(a1, gm[half:])
        dk_t[0, at, :half] = nt(qb, ds0)
        dk_t[0, at, half:] = nt(qb[:, half:], ds1)
        d = nn(kb[:, :half], ds0)
        d = d + jnp.concatenate([jnp.zeros((FEAT, half), F32), nn(kb[:, half:], ds1)], axis=1)
        gphi = nt(st * lane_mask(256, 64, h), gv) * early[...]
        dq_t[at, :] = d + features_back_t(qx, gphi)
    dv[:half, :] = top
    dv[half:, :] = bottom
    @pl.when(g == pl.num_programs(1) - 1)
    def _():
        dq[...] = dq_t[...].T.astype(BF)

def intra_back(core, low, high, p, gn, dv_in, state, rows, length, row, deps=(), into=None):
    total = rows * length
    return call(functools.partial(intra_back_kernel, length=length, row=row), "intra_back", (1, GROUPS),
        [(core, SMEM), (low, SMEM), (high, SMEM), (p.q_lin, spec_all(length, row)), (p.k_lin, spec_all(length, row)), (p.v, spec_col(length, 0, row)),
         (gn, spec_col(length, 0, row)), (dv_in, spec_col(length, 0, row)), (state[0], SPEC_STATE), (state[1], SPEC_STATE)],
        [((total, 256), BF, spec_all(length, row)), ((rows, 256, length), F32, spec_t(length, row)), ((total, 1024), F32, spec_col(length, 0, row))],
        [pltpu.VMEM((length, length), BF)] + [pltpu.VMEM((256, length), F32)] * 3 + [pltpu.VMEM((1, length), F32)],
        flops=HEADS * 2 * 15 * 256 ** 3, deps=deps, into=into)

def state_back_kernel(core, low, high, k, v, dk_in, dv_in, dhv, kept, received, dk, dv, k_t, dk_t, line, *, length):
    r, g = pl.program_id(0), pl.program_id(1)
    @pl.when(g == 0)
    def _():
        k_t[...] = k[...].astype(F32).T
        line[...] = owned_line(low, high, r, length)
    st = state_for(r, core, kept, received)
    sb = st.astype(BF)
    vv = v[...]
    dvs = through_state(k_t, st, g, line[...])
    tail = length - WINDOW
    dv[:tail, :] = (dv_in[:tail, :] + dvs[:tail]).astype(BF)
    dv[tail:, :] = (dv_in[tail:, :] + dvs[tail:] + dhv[...].astype(F32)).astype(BF)
    for h in range(4):
        at = head_rows(g, h)
        gphi = nt(sb * lane_mask(256, 64, h), vv) * line[...]
        dk_t[at, :] = dk_in[0, at, :] + features_back_t(k_t[at, :], gphi)
    @pl.when(g == pl.num_programs(1) - 1)
    def _():
        dk[...] = dk_t[...].T.astype(BF)

def state_back(core, low, high, p, dk_in, dv_in, returned, state, rows, length, deps=()):
    total = rows * length
    tail = pl.BlockSpec((None, WINDOW, 256), lambda r, g: (1, r, g))
    return call(functools.partial(state_back_kernel, length=length), "state_back", (rows, GROUPS),
        [(core, SMEM), (low, SMEM), (high, SMEM), (p.k_lin, spec_all(length)), (p.v, spec_col(length)), (dk_in, spec_t(length)), (dv_in, spec_col(length)),
         (returned, tail), (state[0], SPEC_STATE), (state[1], SPEC_STATE)],
        [((total, 256), BF, spec_all(length)), ((total, 1024), BF, spec_col(length))],
        [pltpu.VMEM((256, length), F32)] * 2 + [pltpu.VMEM((1, length), F32)], flops=rows * HEADS * 2 * 512 * 256 * 256, deps=deps)

def tail_kernel(x, got, out):
    out[...] = (x[...].astype(F32) + got[...].astype(F32)).astype(BF)

def tail_added(x, returned, rows, length):
    per_row = length // WINDOW
    end = pl.BlockSpec((WINDOW, x.shape[1]), lambda r: ((r + 1) * per_row - 1, 0))
    return call(tail_kernel, "tail", (rows,), [(x, end), (returned, pl.BlockSpec((None, WINDOW, x.shape[1]), lambda r: (0, r, 0)))],
        [(x.shape, BF, end)], flops=10, moved=MIB, alias={0: 0})[0]


ONE = dict(pipeline_mode=pl.Buffered(1))
def resident(shape):
    return pl.BlockSpec(shape, lambda *s: (0,) * len(shape), **ONE)

class Projected:
    pass

def keys_kernel(tokens, gain, wk, wv, normed, k, v):
    @pl.when(pl.program_id(0) == 0)
    def _():
        x = tokens[...].astype(F32)
        normed[...] = (x * lax.rsqrt(jnp.mean(x * x, axis=-1, keepdims=True) + EPSILON) * gain[...]).astype(BF)
        k[...] = nn(normed[...], wk[...]).astype(BF)
    v[...] = nn(normed[...], wv[...]).astype(BF)

def rest_kernel(normed, part, wq, w, q, out, normed_t):
    @pl.when(pl.program_id(0) == 0)
    def _():
        q[...] = nn(normed[...], wq[...]).astype(BF)
    normed_t[...] = part[...].T
    out[...] = nn(normed[...], w[...]).astype(BF)

def project_keys(p, tokens, gain, w_in):
    toks, width = tokens.shape
    lin = HEADS * FEAT
    first = (w_in.shape[1] - width) // 512
    p.normed, p.k_lin, p.v = call(keys_kernel, "project_keys", (width // 512,),
        [(tokens, resident((toks, width))), (gain.reshape(1, width), resident((1, width))), (w_in, pl.BlockSpec((width, lin), lambda s: (0, 1), **ONE)),
         (w_in, pl.BlockSpec((width, 512), lambda s: (0, first + s)))],
        [((toks, width), BF, resident((toks, width))), ((toks, lin), BF, resident((toks, lin))), ((toks, width), BF, pl.BlockSpec((toks, 512), lambda s: (0, s)))],
        flops=2 * toks * width * (width + lin))

def project_rest(p, w_in, deps=()):
    toks, width = p.normed.shape
    lin = HEADS * FEAT
    count = 2 * width // 512
    piece = toks // count
    p.q_lin, p.qk_win, p.normed_t = call(rest_kernel, "project_rest", (count,),
        [(p.normed, resident((toks, width))), (p.normed, pl.BlockSpec((piece, width), lambda s: (s, 0))), (w_in, pl.BlockSpec((width, lin), lambda s: (0, 0), **ONE)),
         (w_in, pl.BlockSpec((width, 512), lambda s: (0, 2 * lin // 512 + s)))],
        [((toks, lin), BF, resident((toks, lin))), ((toks, 2 * width), BF, pl.BlockSpec((toks, 512), lambda s: (0, s))),
         ((width, toks), BF, pl.BlockSpec((width, piece), lambda s: (0, s)))],
        flops=2 * toks * width * (2 * width + lin), deps=deps)

def mlp(core, mixed, tokens, cot, w_out, gain, w_gate_up, w_down, count, tile=256, chunk=256):
    toks, width = mixed.shape
    ff = w_down.shape[0]
    steps = ff // tile
    half = width // 2
    big = resident((toks, width))
    across = pl.BlockSpec((half, tile), lambda s: (0, s))
    down = pl.BlockSpec((tile, half), lambda s: (s, 0))
    return call(functools.partial(mlp_kernel, steps=steps, chunk=chunk, each=width // count), "mlp", (steps,),
        [(core, SMEM), (mixed, big), (tokens, big), (cot, big), (w_out, resident((width, width))), (gain.reshape(1, width), resident((1, width))),
         (w_gate_up, pl.BlockSpec((width, tile), lambda s: (0, s))), (w_gate_up, pl.BlockSpec((width, tile), lambda s: (0, s + steps))),
         (w_down, pl.BlockSpec((tile, width), lambda s: (s, 0)))],
        [((toks, width), BF, big), ((toks, width), F32, big), ((toks, width), BF, big)] + [((half, ff), BF, across)] * 4
        + [((ff, half), BF, down)] * 2 + [((half, width), BF, resident((half, width)))] * 2,
        [pltpu.VMEM((toks, width), F32)] * 3 + [pltpu.VMEM((toks, width), BF), pltpu.VMEM((width, toks), BF)] + [pltpu.VMEM((toks, tile), BF)] * 3,
        flops=2 * toks * width * (9 * ff + 3 * width), moved=60 * MIB)

def weight_kernel(core, normed_t, *refs, counts, each):
    parts, (keep, send) = refs[:len(counts)], refs[len(counts):]
    step = pl.program_id(0)
    first = core[0] == 0
    begin = 0
    for ref, count in zip(parts, counts):
        @pl.when((step >= begin) & (step < begin + count))
        def _(ref=ref):
            keep[...], send[...] = parted(nn(normed_t[...], ref[...]), first, each)
        begin += count

def weight_grad(core, normed_t, parts, count, name, deps=()):
    width, toks = normed_t.shape
    counts = [p.shape[1] // 256 for p in parts]
    begins = [sum(counts[:n]) for n in range(len(counts))]
    def spec(begin, size):
        return pl.BlockSpec((toks, 256), lambda s: (0, jnp.clip(s - begin, 0, size - 1)))
    half = width // 2
    out = ((half, 256 * sum(counts)), BF, pl.BlockSpec((half, 256), lambda s: (0, s)))
    return call(functools.partial(weight_kernel, counts=counts, each=width // count), name, (sum(counts),),
        [(core, SMEM), (normed_t, resident((width, toks)))] + [(p, spec(b, n)) for p, b, n in zip(parts, begins, counts)],
        [out, out], flops=2 * width * toks * 256 * sum(counts), deps=deps)

def input_kernel(dq_lin, dk_lin, dq_win, dk_win, dv, w, tokens, gain, resid, out):
    begin, grad = 0, None
    for ref in (dq_lin, dk_lin, dq_win, dk_win, dv):
        size = ref.shape[1]
        term = nt(ref[...], w[:, begin:begin + size])
        grad = term if grad is None else grad + term
        begin += size
    x = tokens[...].astype(F32)
    scale = lax.rsqrt(jnp.mean(x * x, axis=-1, keepdims=True) + EPSILON)
    c = grad * gain[...]
    out[...] = resid[...] + scale * c - x * (scale * scale * scale * jnp.mean(c * x, axis=-1, keepdims=True))

def input_grad(parts, w_in, tokens, gain, resid, part, ways, name, deps=(), into=None):
    toks, width = tokens.shape
    piece = toks // ways
    by_rows = lambda columns: pl.BlockSpec((piece, columns), lambda s: (part, 0), **ONE)
    return call(input_kernel, name, (1,),
        [(p, by_rows(p.shape[1])) for p in parts] + [(w_in, resident(w_in.shape)), (tokens, by_rows(width)), (gain.reshape(1, width), resident((1, width))), (resid, by_rows(width))],
        [((toks, width), F32, by_rows(width))], flops=2 * piece * width * w_in.shape[1], deps=deps, into=into)

def swap(x, bit, count):
    return lax.ppermute(x, "seq", [(i, i ^ (1 << bit)) for i in range(count)])

def over(near, far):
    return near + (1.0 - near[FLAG_ROW:FLAG_ROW + 1, :]) * far

def begun_kernel(core, mine, received, total, *, backward):
    first = core[0] == 0
    for n in range(mine.shape[0]):
        m, r = mine[n], received[n].astype(F32)
        at0, at1 = jnp.where(first, m, r), jnp.where(first, r, m)
        total[n] = (over(at0, at1) if backward else over(at1, at0)).astype(BF)

def joined_kernel(ahead, total, received, new_total):
    here = ahead[0] == 1
    for n in range(total.shape[0]):
        t, r = total[n].astype(F32), received[n].astype(F32)
        new_total[n] = over(jnp.where(here, t, r), jnp.where(here, r, t)).astype(BF)

def ended_kernel(core, ahead, mine, *refs, backward):
    received, (kept, send) = refs[:-2], refs[-2:]
    first = core[0] == 0
    own = first ^ backward
    for n in range(mine.shape[0]):
        m, r = mine[n], received[0][n].astype(F32)
        base = jnp.where(own, m, r)
        e = jnp.zeros_like(m)
        for k, ref in enumerate(received[1:]):
            e = jnp.where(ahead[k] == 1, over(e, ref[n].astype(F32)), e)
        o = over(base, e)
        kept[n] = jnp.where(own, e, o).astype(BF)
        send[n] = jnp.where(own, o, e).astype(BF)

class Scan:
    def __init__(self, mine, send, me, count, backward):
        self.me, self.count, self.backward, self.mine = me, count, backward, mine
        self.received = [swap(send, 0, count)]
        self.bit, self.last = 0, count.bit_length() - 2
        self.core = (me % 2).reshape(1)
        self.ahead = ((me >> jnp.arange(1, self.last + 1, dtype=jnp.int32)) & 1) ^ (1 if backward else 0)
    def _call(self, kernel, name, flags, arrays, outs, through=()):
        shape = self.mine.shape
        whole = pl.BlockSpec(shape, lambda: (0, 0, 0))
        return call(kernel, name, (), [(f, SMEM) for f in flags] + [(a, whole) for a in arrays], [(shape, BF, whole)] * outs, flops=10, moved=MIB, through=through)
    def step(self, through=()):
        if self.bit == 0:
            self.total, *self.through = self._call(functools.partial(begun_kernel, backward=self.backward), "begun", [self.core], [self.mine, self.received[0]], 1, through)
        elif self.bit < self.last:
            self.total, = self._call(joined_kernel, "joined", [self.ahead[self.bit - 1:self.bit]], [self.total, self.received[-1]], 1)
        else:
            self.kept, self.total = self._call(functools.partial(ended_kernel, backward=self.backward), "ended", [self.core, self.ahead], [self.mine] + self.received, 2)
        self.bit += 1
        self.received.append(swap(self.total, self.bit if self.bit <= self.last else 0, self.count))
    def done(self):
        return self.kept, self.received[-1]

def padded(rows):
    return -(-rows // 16) * 16

class Piece:
    def __init__(self, arrays, first=0, size=None, rows=None):
        self.arrays = arrays
        self.first, self.size = first, size or arrays[0].shape[2]
        self.rows = rows or arrays[0].shape[1]
        self.height = self.size // 256 * padded(self.rows)

def add_kernel(*refs, plan, count, scalars):
    refs = refs[scalars:]
    ins, outs = refs[:-count], refs[-count:]
    for target, parts, at, height, rows, columns in plan:
        for k, sources in enumerate(parts):
            total = None
            for s in sources:
                term = ins[s][...].astype(F32)
                total = term if total is None else total + term
            total = total.astype(BF)
            pad = padded(rows)
            for c in range(columns // 256):
                outs[target + k][:, :, at + c * pad:at + c * pad + rows, :] = total[..., c * 256:(c + 1) * 256]

def add_up(groups, ways, name, most=4, deps=()):
    grid = min([most] + [outer for _, outer, _, _ in groups])
    ins, outs, plan = [], [], []
    for n, (pieces, outer, inner, own) in enumerate(groups):
        per = outer // grid
        at = 0
        for piece in pieces:
            parts = []
            for k in range(ways):
                sources = []
                for array in piece.arrays:
                    _, rows, columns = array.shape
                    def index(a, *own_refs, n=n, k=k, block=piece.first // piece.size):
                        return (a, own_refs[n][0] ^ k if ways > 1 else 0, 0, 0, block)
                    sources.append(len(ins))
                    ins.append((array.reshape(outer, ways, inner, rows, columns), pl.BlockSpec((per, None, inner, rows, piece.size), index)))
                parts.append(sources)
            plan.append((n * ways, parts, at, piece.height, piece.rows, piece.size))
            at += piece.height
        outs += [((outer, inner, at, 256), BF, pl.BlockSpec((per, inner, at, 256), lambda a, *own_refs: (a, 0, 0, 0)))] * ways
    got = call(functools.partial(add_kernel, plan=plan, count=len(outs), scalars=len(groups)), name, (grid,), ins, outs, flops=10, moved=20 * MIB,
        scalars=[own.reshape(1) for _, _, _, own in groups], deps=deps)
    got = [x.reshape((-1,) + x.shape[2:]) for x in got]
    return [got[n * ways:(n + 1) * ways] for n in range(len(groups))]

def chips_first(x, chips):
    return x.reshape(chips, x.shape[0] // chips, x.shape[1])

class MlpSum:
    def __init__(self, pairs, me, count):
        self.me, self.count, self.chips = me, count, count // 2
        self.pairs = [(chips_first(k, self.chips), chips_first(swap(s, 0, count), self.chips)) for k, s in pairs]
        self.bit = 0
    def step(self, deps=()):
        me, chips = self.me, self.chips
        bits = self.count.bit_length() - 1
        self.bit += 1
        if self.bit == 1:
            g, u, d, o = self.pairs
            half = lambda x, n: Piece(x, n * (x[0].shape[2] // 2), x[0].shape[2] // 2)
            pieces = [Piece(g), half(d, 0), half(o, 0)], [Piece(u), half(d, 1), half(o, 1)]
            self.layout = [(p.rows, p.size) for ps in pieces for p in ps]
            (ka, sa), (kb, sb) = add_up([(pieces[0], chips // 2, 1, (me >> 1) & 1), (pieces[1], chips // 4, 2, (me >> 2) & 1)], 2, "sum_first", deps=deps)
            self.a, self.b = [ka, swap(sa, 1, self.count)], [kb, swap(sb, 2, self.count)]
        elif self.bit == 2:
            (ka, sa), (kb, sb) = add_up([([Piece(self.a)], chips // 4, 1, (me >> 2) & 1), ([Piece(self.b)], chips // 4, 1, (me >> 1) & 1)], 2, "sum_second")
            self.a, self.b = [ka, swap(sa, 2, self.count)], [kb, swap(sb, 1, self.count)]
        else:
            (both,), = add_up([([Piece(self.a), Piece(self.b)], chips // 4, 1, me)], 1, "sum_third", 2)
            own = (1 << 3) - 1
            groups = [[i for i in range(self.count) if i & own == low] for low in range(own + 1)]
            self.all = [lax.psum_scatter(both, "seq", scatter_dimension=0, axis_index_groups=groups, tiled=True)]

def quarters(pieces, bit, me, count):
    flip = lambda x, k: lax.ppermute(x, "seq", [(i, i ^ (k << bit)) for i in range(count)])
    parts, = add_up([(pieces, (count // 2) >> (bit + 1), 1, (me >> bit) & 3)], 4, "quarters", 2)
    return [parts[0]] + [flip(parts[k], k) for k in (3, 2, 1)]

class InSum:
    def __init__(self, me, count):
        self.me, self.count, self.chips = me, count, count // 2
        self.bit = 1
    def first(self, keep, send, columns):
        arrays = chips_first(keep, self.chips), chips_first(swap(send, 0, self.count), self.chips)
        return arrays, columns
    def second(self, arrays, columns):
        me, chips = self.me, self.chips
        a, b = ([Piece(arrays, first, size) for first, size in c] for c in columns)
        (ka, sa), (kb, sb) = add_up([(a, chips // 2, 1, (me >> 1) & 1), (b, chips // 4, 2, (me >> 2) & 1)], 2, "in_first")
        return [ka, swap(sa, 1, self.count)], [kb, swap(sb, 2, self.count)]
    def third(self, *parts):
        me, chips = self.me, self.chips
        a, b = ([Piece(p[n]) for p in parts] for n in (0, 1))
        (ka, sa), (kb, sb) = add_up([(a, chips // 4, 1, (me >> 2) & 1), (b, chips // 4, 1, (me >> 1) & 1)], 2, "in_second")
        self.arrays = [Piece([ka, swap(sa, 2, self.count)]), Piece([kb, swap(sb, 1, self.count)])]
        self.bit = 3
    def rest(self):
        while self.bit < self.count.bit_length() - 1:
            got = quarters(self.arrays, self.bit, self.me, self.count)
            self.arrays = [Piece(got)]
            self.bit += 2
        return got

def finish(rows, me, count):
    core = me % 2
    each = rows.shape[0] // 2
    own = lax.dynamic_slice_in_dim(rows, core * each, each, 0)
    got = swap(lax.dynamic_slice_in_dim(rows, (1 - core) * each, each, 0), 0, count)
    return jnp.concatenate([jnp.where(core == 0, own, got), jnp.where(core == 0, got, own)], axis=1)

def gathered_kernel(place, weights, gain, *refs, layout, rows):
    arrays, (out, gain_out) = refs[:-2], refs[-2:]
    total = None
    for n, at in enumerate(layout):
        g = None
        for ref in arrays:
            term = ref[0, at:at + rows, :].astype(F32)
            g = term if g is None else g + term
        out[:, n * 256:(n + 1) * 256] = g
        t = g * weights[:, n * 256:(n + 1) * 256].astype(F32)
        total = t if total is None else total + t
    gain_out[...] = jnp.sum(total, axis=1, keepdims=True) / gain[...]

def gathered(arrays, layout, weights, gain, me, count):
    each, columns = weights.shape[0] // count, weights.shape[1]
    if each < 16:
        weights, gain = lax.dynamic_slice_in_dim(weights, me * each, each, 0), lax.dynamic_slice_in_dim(gain, me * each, each, 0)
        me = jnp.zeros((), jnp.int32)
    mine = pl.BlockSpec((each, columns), lambda s, place: (place[0], 0))
    one = pl.BlockSpec((each, 1), lambda s, place: (place[0], 0))
    out, gain_out = call(functools.partial(gathered_kernel, layout=layout, rows=each), "gathered", (1,),
        [(weights, mine), (gain.reshape(-1, 1), one)] + [(a, resident(a.shape)) for a in arrays],
        [((each, columns), F32, resident((each, columns))), ((each, 1), F32, resident((each, 1)))], flops=10, moved=MIB, scalars=[me.reshape(1)])
    return out, gain_out.reshape(each)

def plain_kernel(*refs, pieces, shapes):
    arrays, outs = refs[:-len(shapes)], refs[-len(shapes):]
    for out, first, rows, column in pieces:
        g = None
        for ref in arrays:
            term = ref[0, first:first + rows, :].astype(F32)
            g = term if g is None else g + term
        outs[out][:, column:column + 256] = g

def plain(arrays, pieces, shapes):
    return call(functools.partial(plain_kernel, pieces=pieces, shapes=shapes), "plain", (1,), [(a, resident(a.shape)) for a in arrays],
        [(s, F32, resident(s)) for s in shapes], flops=10, moved=MIB)

def shards(tokens, seq_starts, seq_lengths, gain_in, gain_mlp, w_in, w_out, w_gate_up, w_down, cotangent):
    Order.last = None
    rows, length, width = tokens.shape
    count = lax.axis_size("seq")
    bits = count.bit_length() - 1
    order_a = list(range(1, bits))
    order_b = [2, 1] + list(range(3, bits))
    order_c = [3, 1, 2] + list(range(4, bits))
    me = lax.axis_index("seq")
    core = (me % 2).reshape(1)
    total = rows * length
    begin = me * length
    low = (seq_starts[:, ::WINDOW] - begin).reshape(-1)
    high = low + seq_lengths[:, ::WINDOW].reshape(-1)

    x = tokens.reshape(total, width)
    cot = cotangent.reshape(total, width)
    p = Projected()
    project_keys(p, x, gain_in, w_in)
    scan = Scan(*local_states(core, low, high, p.k_lin, p.v, rows, length), me, count, False)
    project_rest(p, w_in)
    tails = lambda a, at: a.reshape(rows, length, -1)[:, -WINDOW:, at:at + width]
    forward = [(i, i + 1) for i in range(count - 1)]
    backward = [(i + 1, i) for i in range(count - 1)]
    halo = lax.ppermute(jnp.stack([tails(p.qk_win, width), tails(p.v, 0)]), "seq", forward).reshape(2, rows * WINDOW, width)
    scan.step()
    local = intra(low, high, p, rows, length, 0)
    scan.step()
    local, = intra(low, high, p, rows, length, 1, into=local)
    scan.step()
    windowed = window(low, high, p, halo, rows, length, 0)
    scan.step()
    windowed, = window(low, high, p, halo, rows, length, 1, into=windowed)
    while scan.bit < bits:
        scan.step()
    state_in = scan.done()
    numer, mixed = mix(core, low, p, state_in, local, windowed, rows, length)

    (result, grad_resid, grad_mixed, keep_g, send_g, keep_u, send_u, keep_d, send_d, keep_o, send_o) = mlp(
        core, mixed, x, cot, w_out, gain_mlp, w_gate_up, w_down, count)
    grad_numer, *grad_state_in = numer_back(core, low, p, numer, grad_mixed, rows, length)
    scan = Scan(*grad_state_in, me, count, True)

    scan.step(through=(send_g, send_u, send_d, send_o))
    mlp_sum = MlpSum(list(zip((keep_g, keep_u, keep_d, keep_o), scan.through)), me, count)
    back, dh, kept = window_back_first(low, high, p, halo, grad_mixed, rows, length)
    returned = lax.ppermute(dh, "seq", backward)
    scan.step()
    mlp_sum.step(deps=(returned,))
    scan.step()
    dq_win, dk_win, dv_win = window_back_second(low, high, p, grad_mixed, back, kept, rows, length)
    scan.step()
    inner = intra_back(core, low, high, p, grad_numer, dv_win, state_in, rows, length, 0)
    while scan.bit < bits:
        scan.step()
    inner = intra_back(core, low, high, p, grad_numer, dv_win, state_in, rows, length, 1, into=inner)
    dq_lin, dk_t, dv_part = inner
    mlp_sum.step()
    dk_win = tail_added(dk_win, returned, rows, length)
    lin = HEADS * FEAT
    in_sum = InSum(me, count)
    early = in_sum.first(*weight_grad(core, p.normed_t, [dq_win, dk_win, dq_lin], count, "weight_grad_early"), (((0, width), (2 * width, lin)), ((width, width),)))
    dk_lin, dv = state_back(core, low, high, p, dk_t, dv_part, returned, scan.done(), rows, length)
    mlp_sum.step()
    late = in_sum.first(*weight_grad(core, p.normed_t, [dv, dk_lin], count, "weight_grad_late"), (((0, width // 2),), ((width // 2, width // 2), (width, lin))))
    parts = [dq_lin, dk_lin, dq_win, dk_win, dv]
    early = in_sum.second(*early)
    grad_tokens = input_grad(parts, w_in, x, gain_in, grad_resid, 0, 4, "input_grad_first")
    late = in_sum.second(*late)
    grad_tokens = input_grad(parts, w_in, x, gain_in, grad_resid, 1, 4, "input_grad", into=grad_tokens)
    in_sum.third(early, late)
    grad_tokens, = input_grad(parts, w_in, x, gain_in, grad_resid, 1, 2, "input_grad", into=grad_tokens)
    in_got = in_sum.rest()
    ff, each, chip = w_down.shape[0], width // count, w_down.shape[0] // (count // 2)
    pad = padded(each)
    height = ff // 256 * pad
    second = height + padded(chip) + 2 * pad
    part_gate_up, part_gain_mlp = gathered(mlp_sum.all, [n * pad for n in range(ff // 256)] + [second + n * pad for n in range(ff // 256)],
        w_gate_up, gain_mlp, me, count)
    down, part_out = plain(mlp_sum.all, [(0, height, chip, 0), (0, second + height, chip, 256)]
        + [(1, height + padded(chip) + n * pad + (second - 2 * pad if n >= 2 else 0), each, n * 256) for n in range(4)],
        [(chip, width // 2), (each, width)])
    part_down = finish(down, me, count)
    wide, piece = width // 256, list(range(3 * width // 256 + 2 * lin // 256))
    q_win, q_lin, v_a, k_win, v_b, k_lin = (piece[wide * n // 2 + m:wide * (n + c) // 2 + m + k] for n, m, c, k in
        ((0, 0, 2, 0), (2, 0, 0, 1), (2, 1, 1, 0), (3, 1, 2, 0), (5, 1, 1, 0), (6, 1, 0, 1)))
    part_in, part_gain_in = gathered(in_got, [n * pad for n in q_lin + k_lin + q_win + k_win + v_a + v_b], w_in, gain_in, me, count)
    return (result.reshape(rows, length, width), grad_tokens.reshape(rows, length, width), part_gain_in, part_gain_mlp,
            part_in, part_out, part_gate_up, part_down)

def solution(mesh):
    split = P(None, "seq", None)
    placed = (split, P(None, "seq"), P(None, "seq"), P(), P(), P(), P(), P(), P(), split)
    return jax.shard_map(shards, mesh=mesh, in_specs=placed,
        out_specs=(split, split, P("seq"), P("seq"), P("seq", None), P("seq", None), P("seq", None), P("seq", None)),
        check_vma=False)
```

```python
import functools
import jax
import jax.numpy as jnp
from jax import lax
from jax.experimental import pallas as pl
from jax.experimental.pallas import tpu as pltpu
from jax.sharding import PartitionSpec as P
F32=jnp.float32; BF=jnp.bfloat16
EPSILON=1e-6
MIB=1<<20

def nn(a,b): return lax.dot_general(a,b,(((1,),(0,)),((),())),preferred_element_type=F32)
def nt(a,b): return lax.dot_general(a,b,(((1,),(1,)),((),())),preferred_element_type=F32)
def tn(a,b): return lax.dot_general(a,b,(((0,),(0,)),((),())),preferred_element_type=F32)

def parted(x, first, each):
    x = x.reshape(x.shape[0] // (2 * each), 2, each, x.shape[1])
    a, b = x[:, 0].reshape(-1, x.shape[3]), x[:, 1].reshape(-1, x.shape[3])
    return jnp.where(first, a, b).astype(BF), jnp.where(first, b, a).astype(BF)

def mlp_kernel(core_ref, mixed, tokens, cot, w_out, gain, wg, wu, wd,
               result, grad_resid, grad_mixed, keep_g, send_g, keep_u, send_u, keep_d, send_d, keep_o, send_o,
               resid, acc, dh, hn, hn_t, hid, dgu, wgu, *, steps, chunk, each):
    step = pl.program_id(0)
    toks = mixed.shape[0]
    width = mixed.shape[1]
    count = toks // chunk
    first = core_ref[0] == 0

    def rows(n):
        return pl.ds(pl.multiple_of(n * chunk, chunk), chunk)

    @pl.when(step == 0)
    def _():
        def one(n, carry):
            r = rows(n)
            res = tokens[r, :].astype(F32) + nn(mixed[r, :], w_out[...])
            scale = lax.rsqrt(jnp.mean(res * res, axis=-1, keepdims=True) + EPSILON)
            h = (res * scale * gain[...]).astype(BF)
            resid[r, :] = res
            acc[r, :] = res
            dh[r, :] = jnp.zeros((chunk, width), F32)
            hn[r, :] = h
            return carry
        lax.fori_loop(0, count, one, 0)
        for n in range(count):
            hn_t[:, n * chunk:(n + 1) * chunk] = hn[n * chunk:(n + 1) * chunk, :].T

    tile = wg.shape[1]
    wgu[:, :tile] = wg[...]
    wgu[:, tile:] = wu[...]

    def forward(n, carry):
        r = rows(n)
        h = hn[r, :]
        both = nn(h, wgu[...])
        gate, up = both[:, :tile], both[:, tile:]
        dhid = nt(cot[r, :], wd[...])
        sig = 1.0 / (1.0 + jnp.exp(-gate))
        silu = gate * sig
        hidden = (silu * up).astype(BF)
        d_gate = (dhid * up * (sig + silu * (1.0 - sig))).astype(BF)
        d_up = (dhid * silu).astype(BF)
        hid[r, :] = hidden
        dgu[r, :tile] = d_gate
        dgu[r, tile:] = d_up
        acc[r, :] += nn(hidden, wd[...])
        dh[r, :] += nt(dgu[r, :], wgu[...])
        return carry
    lax.fori_loop(0, count, forward, 0, unroll=2)

    half = width // 2
    grad_d = tn(hid[...], cot[...])
    left, right = grad_d[:, :half].astype(BF), grad_d[:, half:].astype(BF)
    keep_d[...] = jnp.where(first, left, right)
    send_d[...] = jnp.where(first, right, left)

    def weights(n, carry):
        r = rows(n)
        o = pl.ds(pl.multiple_of(n * (chunk // 2), chunk // 2), chunk // 2)
        grad = nn(hn_t[r, :], dgu[...])
        keep_g[o, :], send_g[o, :] = parted(grad[:, :tile], first, each)
        keep_u[o, :], send_u[o, :] = parted(grad[:, tile:], first, each)
        return carry
    lax.fori_loop(0, width // chunk, weights, 0, unroll=2)

    @pl.when(step == steps - 1)
    def _():
        def one(n, carry):
            r = rows(n)
            res = resid[r, :]
            scale = lax.rsqrt(jnp.mean(res * res, axis=-1, keepdims=True) + EPSILON)
            grad = dh[r, :]
            c = grad * gain[...]
            back = cot[r, :].astype(F32) + scale * c - res * (scale * scale * scale * jnp.mean(c * res, axis=-1, keepdims=True))
            result[r, :] = acc[r, :].astype(BF)
            grad_resid[r, :] = back
            b = back.astype(BF)
            hn[r, :] = b
            grad_mixed[r, :] = nt(b, w_out[...]).astype(BF)
            return carry
        lax.fori_loop(0, count, one, 0)
        for n in range(count):
            hn_t[:, n * chunk:(n + 1) * chunk] = mixed[n * chunk:(n + 1) * chunk, :].T
        def outer(n, carry):
            r = rows(n)
            o = pl.ds(pl.multiple_of(n * (chunk // 2), chunk // 2), chunk // 2)
            keep_o[o, :], send_o[o, :] = parted(nn(hn_t[r, :], hn[...]), first, each)
            return carry
        lax.fori_loop(0, width // chunk, outer, 0)


HEADS=16; FEAT=16; WINDOW=64; ROWS_PHI=160; FLAG_ROW=153
VMEM = 64 * MIB
GROUPS = HEADS // 4
EACH = 2
STEPS = GROUPS // EACH

def groups():
    return [(pl.program_id(1) * EACH + s, slice(s * 256, (s + 1) * 256)) for s in range(EACH)]

COST = dict(project_keys=6.8, state=7.4, project_rest=10, begun=2, joined=2.5, ended=3, intra=7.2, window=8.5, mix=10, mlp=88, numer_back=12,
    window_back=13, intra_back=14, sum_first=10.6, sum_second=6.4, state_back=0.1, weight_grad_early=0.1, weight_grad_late=0.1, input_grad_first=0.1, input_grad=0.1, in_first=3, in_second=3, quarters=3.5, tail=1.8, gathered=2.3, plain=2.0, sum_more=3)

class Order:
    last = None

def call(kernel, name, grid, ins, outs, scratch=(), flops=0, moved=10 * MIB, deps=(), into=None, alias=None, scalars=(), through=()):
    arrays, specs = [a for a, _ in ins], [s for _, s in ins]
    count, ahead = len(arrays), len(scalars)
    into = list(into or ())
    deps = list(deps)
    if Order.last is not None and not any(Order.last is a for a in into + deps + arrays):
        deps.append(Order.last)
    extra = deps + into + list(through)
    aliases = {ahead + count + len(deps) + n: n for n in range(len(into))}
    aliases.update({ahead + i: o for i, o in (alias or {}).items()})
    aliases.update({ahead + count + len(deps) + len(into) + n: len(outs) + n for n in range(len(through))})
    results = len(outs)
    outs = list(outs) + [(a.shape, a.dtype, pl.BlockSpec(memory_space=pl.ANY)) for a in through]
    def body(*refs):
        begin = ahead + count + len(extra)
        kernel(*refs[:ahead + count], *refs[begin:begin + results], *refs[begin + len(outs):])
    out = pl.pallas_call(
        body, grid_spec=pltpu.PrefetchScalarGridSpec(num_scalar_prefetch=ahead, grid=grid,
            in_specs=specs + [pl.BlockSpec(memory_space=pl.ANY)] * len(extra), out_specs=[s for _, _, s in outs], scratch_shapes=list(scratch)),
        out_shape=[jax.ShapeDtypeStruct(shape, dtype) for shape, dtype, _ in outs],
        input_output_aliases=aliases, name=name,
        compiler_params=pltpu.CompilerParams(vmem_limit_bytes=VMEM, dimension_semantics=("arbitrary",) * len(grid)),
        cost_estimate=pl.CostEstimate(flops=int(COST.get(name, 2.0) * 1e9), bytes_accessed=1000, transcendentals=0),
    )(*scalars, *arrays, *extra)
    Order.last = out[0]
    return out

def lane_mask(width, size, which, dtype=BF):
    lanes = lax.broadcasted_iota(jnp.int32, (1, width), 1)
    return ((lanes >> (size.bit_length() - 1)) == which).astype(dtype)

def spread(values, length):
    block = lax.broadcasted_iota(jnp.int32, (1, length), 1) >> 6
    out = jnp.zeros((1, length), jnp.int32)
    for n, value in enumerate(values):
        out = jnp.where(block == n, value, out)
    return out

def scalars(ref, row, length):
    per_row = length // WINDOW
    return [ref[row * per_row + n] for n in range(per_row)]

def early_line(low, row, length):
    return (spread(scalars(low, row, length), length) < 0).astype(F32)

def owned_line(low, high, row, length):
    lows = scalars(low, row, length)
    place = lax.broadcasted_iota(jnp.int32, (1, length), 1)
    same = spread(lows, length) == lows[-1]
    return (same & (place < spread(scalars(high, row, length), length))).astype(F32)

TURNS = FEAT // 2

def turn(d):
    row = lax.broadcasted_iota(jnp.int32, (HEADS * FEAT, HEADS * FEAT), 0)
    entry = lax.broadcasted_iota(jnp.int32, (HEADS * FEAT, HEADS * FEAT), 1)
    return (((row & -FEAT) | ((row + d) & (FEAT - 1))) == entry).astype(BF)

def turned_scratch(length):
    return pltpu.VMEM((TURNS, HEADS * FEAT, length), BF)

def turn_all(x, x_t, turned, line):
    flipped = x.astype(F32).T
    flat = (flipped if line is None else flipped * line).astype(BF)
    x_t[...] = flat
    for d in range(1, TURNS + 1):
        turned[d - 1] = nn(turn(d), flat).astype(BF)

def features_t(x_t, turned, at, line):
    half = FEAT // 2
    x = x_t[at, :]
    parts = [x * x * jnp.bfloat16((2.0 * FEAT) ** -0.5)]
    xs = x * jnp.bfloat16(FEAT ** -0.5)
    for d in range(1, half):
        parts.append(xs * turned[d - 1, at, :])
    parts.append(x * jnp.bfloat16(FEAT ** -0.25))
    row = lax.broadcasted_iota(jnp.int32, x.shape, 0)
    parts.append(jnp.where(row < half, xs * turned[half - 1, at, :], jnp.where(row == half, line, 0.0).astype(BF)))
    return jnp.concatenate(parts, axis=0)

def features_back_t(x_t, turned, at, g, pulled):
    half = FEAT // 2
    x = x_t[at, :]
    total = g[:FEAT] * x.astype(F32) * (2.0 * (2.0 * FEAT) ** -0.5) + g[half * FEAT:(half + 1) * FEAT] * FEAT ** -0.25
    mixed = jnp.zeros(x.shape, F32)
    xs = x * jnp.bfloat16(FEAT ** -0.5)
    row = lax.broadcasted_iota(jnp.int32, x.shape, 0)
    gb = g.astype(BF)
    for d in range(1, half + 1):
        if d < half:
            gd = gb[d * FEAT:(d + 1) * FEAT]
        else:
            gd = jnp.where(row < half, gb[(half + 1) * FEAT:(half + 2) * FEAT], jnp.bfloat16(0))
        mixed = mixed + (gd * turned[d - 1, at, :]).astype(F32)
        pulled[d - 1, at, :] = gd * xs
    return total + mixed * FEAT ** -0.5

def turned_back(pulled):
    total = None
    for d in range(1, TURNS + 1):
        term = nn(turn(-d), pulled[d - 1])
        total = term if total is None else total + term
    return total

def head_rows(group, h):
    return pl.ds(pl.multiple_of(group * 4 * FEAT + h * FEAT, FEAT), FEAT)

def states_of(x_t, turned, y, group, line, flag):
    row = lax.broadcasted_iota(jnp.int32, (ROWS_PHI, 256), 0)
    out = jnp.where(row == FLAG_ROW, flag, 0.0)
    for h in range(4):
        out = out + nn(features_t(x_t, turned, head_rows(group, h), line), y * lane_mask(256, 64, h))
    return out

def put_state(g, state, core, mine, send):
    r = pl.program_id(0)
    @pl.when(r == core[0])
    def _():
        mine[g] = state
    @pl.when(r != core[0])
    def _():
        send[g] = state.astype(BF)

def state_outs():
    shape = (GROUPS, ROWS_PHI, 256)
    spec = pl.BlockSpec(shape, lambda r, g: (0, 0, 0))
    return [(shape, F32, spec), (shape, BF, spec)]

def state_kernel(core, low, high, k, v, mine, send, k_t, line, turned, *, length):
    r, g = pl.program_id(0), pl.program_id(1)
    @pl.when(g == 0)
    def _():
        line[...] = owned_line(low, high, r, length)
        turn_all(k[...], k_t, turned, line[...])
    flag = (low[(r + 1) * (length // WINDOW) - 1] >= 0).astype(F32)
    for g, at in groups():
        put_state(g, states_of(k_t, turned, v[:, at], g, line[...], flag), core, mine, send)

def spec_col(length, first=0, row=0):
    return pl.BlockSpec((length, 256 * EACH), lambda r, g: (r + row, first // EACH + g))
def spec_all(length, row=0):
    return pl.BlockSpec((length, 256), lambda r, g: (r + row, 0))
SPEC_STATE = pl.BlockSpec((EACH, ROWS_PHI, 256), lambda r, g: (g, 0, 0))
def spec_t(length, row=0):
    return pl.BlockSpec((1, 256, length), lambda r, g: (r + row, 0, 0))
SMEM = pl.BlockSpec(memory_space=pltpu.SMEM)
def local_states(core, low, high, k, v, rows, length):
    return call(functools.partial(state_kernel, length=length), "state", (rows, STEPS),
        [(core, SMEM), (low, SMEM), (high, SMEM), (k, spec_all(length)), (v, spec_col(length))], state_outs(),
        [pltpu.VMEM((256, length), BF), pltpu.VMEM((1, length), F32), turned_scratch(length)])

def intra_kernel(low, high, q, k, v, out, mask, *, length, row):
    g = pl.program_id(1)
    half = length // 2
    @pl.when(g == 0)
    def _():
        lows, highs = scalars(low, row, length), scalars(high, row, length)
        for n in range(length // WINDOW):
            i = lax.broadcasted_iota(jnp.int32, (WINDOW, length), 0) + n * WINDOW
            j = lax.broadcasted_iota(jnp.int32, (WINDOW, length), 1)
            mask[n * WINDOW:(n + 1) * WINDOW, :] = ((j >= lows[n]) & (j <= i) & (j < highs[n])).astype(BF)
    qv, kv = q[...] * jnp.bfloat16(FEAT ** -0.5), k[...]
    for g, at in groups():
        vv = v[:, at] * jnp.bfloat16(0.5)
        top = bottom = None
        for h in range(4):
            km = kv * lane_mask(HEADS * FEAT, FEAT, g * 4 + h)
            vm = vv * lane_mask(256, 64, h)
            u0 = 1.0 + nt(qv[:half], km[:half])
            a0 = (1.0 + u0 * u0).astype(BF) * mask[:half, :half]
            u1 = 1.0 + nt(qv[half:], km)
            a1 = (1.0 + u1 * u1).astype(BF) * mask[half:, :]
            o0, o1 = nn(a0, vm[:half]), nn(a1, vm)
            top = o0 if top is None else top + o0
            bottom = o1 if bottom is None else bottom + o1
        out[:half, at] = top.astype(BF)
        out[half:, at] = bottom.astype(BF)

def intra(low, high, p, rows, length, row, deps=(), into=None):
    return call(functools.partial(intra_kernel, length=length, row=row), "intra", (1, STEPS),
        [(low, SMEM), (high, SMEM), (p.q_lin, spec_all(length, row)), (p.k_lin, spec_all(length, row)), (p.v, spec_col(length, 0, row))],
        [((rows * length, 1024), BF, spec_col(length, 0, row))],
        [pltpu.VMEM((length, length), BF)], flops=HEADS * 2 * 6 * 256 ** 3, deps=deps, into=into)

def stacked(x, scale=1.0):
    return jnp.concatenate([x * (lane_mask(256, 64, h) * jnp.bfloat16(scale)) for h in range(4)], axis=0)

def unstacked(x, scale=1.0):
    total = None
    for h in range(4):
        part = x[h * WINDOW:(h + 1) * WINDOW] * (lane_mask(256, 64, h, F32) * scale)
        total = part if total is None else total + part
    return total

def window_probs(low, high, at, shift, keys, qs):
    s = nt(keys, qs)
    key = lax.broadcasted_iota(jnp.int32, (2 * WINDOW, 4 * WINDOW), 0)
    query = lax.broadcasted_iota(jnp.int32, (2 * WINDOW, 4 * WINDOW), 1) & (WINDOW - 1)
    ok = (key >= jnp.maximum(query, low[at] + shift)) & (key < jnp.minimum(query + (WINDOW + 1), high[at] + shift))
    s = jnp.where(ok, s, -1e30)
    p = jnp.exp(s - jnp.max(s, axis=0, keepdims=True))
    return p * (1.0 / jnp.sum(p, axis=0, keepdims=True))

def window_kernel(low, high, q, k, v, hk, hv, out, ka, va, *, length, row):
    per_row = length // WINDOW
    ka[:WINDOW, :] = hk[...]
    ka[WINDOW:, :] = k[...]
    va[:WINDOW, :] = hv[...]
    va[WINDOW:, :] = v[...]
    for g, at in groups():
        for n in range(per_row):
            own, both = slice(n * WINDOW, (n + 1) * WINDOW), slice(n * WINDOW, (n + 2) * WINDOW)
            p = window_probs(low, high, row * per_row + n, (1 - n) * WINDOW, ka[both, at], stacked(q[own, at], 64 ** -0.5))
            out[own, at] = unstacked(tn(p.astype(BF), va[both, at])).astype(BF)

def window_ins(low, high, p, halo, length, row):
    tail = lambda part: pl.BlockSpec((None, WINDOW, 256 * EACH), lambda r, g: (part, r + row, g))
    return [(low, SMEM), (high, SMEM), (p.qk_win, spec_col(length, 0, row)), (p.qk_win, spec_col(length, GROUPS, row)), (p.v, spec_col(length, 0, row)),
            (halo, tail(0)), (halo, tail(1))]

def window(low, high, p, halo, rows, length, row, deps=(), into=None):
    return call(functools.partial(window_kernel, length=length, row=row), "window", (1, STEPS),
        window_ins(low, high, p, halo, length, row),
        [((rows * length, 1024), BF, spec_col(length, 0, row))],
        [pltpu.VMEM((length + WINDOW, 256 * EACH), BF)] * 2, flops=HEADS * 2 * 4 * length * 128 * 256, deps=deps, into=into)

def window_back_block(low, high, row, n, per_row, q, keys, vals, go):
    qs, gs = stacked(q, 64 ** -0.5), stacked(go)
    p = window_probs(low, high, row * per_row + n, (1 - n) * WINDOW, keys, qs)
    gp = nt(vals, gs)
    ds = (p * (gp - jnp.sum(p * gp, axis=0, keepdims=True))).astype(BF)
    return unstacked(tn(ds, keys), 64 ** -0.5).astype(BF), nn(ds, qs), nn(p.astype(BF), gs)

def window_back_first_kernel(low, high, q, k, v, hk, hv, go, q1, k1, v1, hk1, hv1, go1, dq, dk, dv, dh, q_kept, k_kept, v_kept, ka, va, *, length):
    per_row = length // WINDOW
    ka[:WINDOW, :] = hk[...]
    ka[WINDOW:, :] = k[...]
    va[:WINDOW, :] = hv[...]
    va[WINDOW:, :] = v[...]
    for _, at in groups():
        carry_k = carry_v = None
        for n in range(per_row):
            rows = slice(n * WINDOW, (n + 1) * WINDOW)
            both = slice(n * WINDOW, (n + 2) * WINDOW)
            dq[rows, at], dk_n, dv_n = window_back_block(low, high, 0, n, per_row, q[rows, at], ka[both, at], va[both, at], go[rows, at])
            if n == 0:
                dh[0, :WINDOW, at] = dk_n[:WINDOW].astype(BF)
                dh[1, :WINDOW, at] = dv_n[:WINDOW].astype(BF)
            else:
                dk[(n - 1) * WINDOW:n * WINDOW, at] = (carry_k + dk_n[:WINDOW]).astype(BF)
                dv[(n - 1) * WINDOW:n * WINDOW, at] = (carry_v + dv_n[:WINDOW]).astype(BF)
            carry_k, carry_v = dk_n[WINDOW:], dv_n[WINDOW:]
        dk[length - WINDOW:, at] = carry_k.astype(BF)
        dv[length - WINDOW:, at] = carry_v.astype(BF)
        keys = jnp.concatenate([hk1[:, at], k1[:, at]], axis=0)
        vals = jnp.concatenate([hv1[:, at], v1[:, at]], axis=0)
        q_kept[:, at], dk_n, dv_n = window_back_block(low, high, 1, 0, per_row, q1[:, at], keys, vals, go1[:, at])
        dh[0, WINDOW:, at] = dk_n[:WINDOW].astype(BF)
        dh[1, WINDOW:, at] = dv_n[:WINDOW].astype(BF)
        k_kept[:, at] = dk_n[WINDOW:]
        v_kept[:, at] = dv_n[WINDOW:]

def window_back_second_kernel(low, high, q, k, v, go, q_kept, k_kept, v_kept, dq, dk, dv, *, length):
    per_row = length // WINDOW
    dq[:WINDOW, :] = q_kept[...]
    for _, at in groups():
        carry_k, carry_v = k_kept[:, at], v_kept[:, at]
        for n in range(1, per_row):
            rows = slice(n * WINDOW, (n + 1) * WINDOW)
            both = slice((n - 1) * WINDOW, (n + 1) * WINDOW)
            dq[rows, at], dk_n, dv_n = window_back_block(low, high, 1, n, per_row, q[rows, at], k[both, at], v[both, at], go[rows, at])
            dk[(n - 1) * WINDOW:n * WINDOW, at] = (carry_k + dk_n[:WINDOW]).astype(BF)
            dv[(n - 1) * WINDOW:n * WINDOW, at] = (carry_v + dv_n[:WINDOW]).astype(BF)
            carry_k, carry_v = dk_n[WINDOW:], dv_n[WINDOW:]
        dk[length - WINDOW:, at] = carry_k.astype(BF)
        dv[length - WINDOW:, at] = carry_v.astype(BF)

def window_back_outs(total, length, row):
    spec = spec_col(length, 0, row)
    return [((total, 1024), BF, spec)] * 3

def window_back_first(low, high, p, halo, go, rows, length):
    total, per_row = rows * length, length // WINDOW
    block = lambda first=0: pl.BlockSpec((WINDOW, 256 * EACH), lambda r, g: (per_row, first // EACH + g))
    tail = lambda part: pl.BlockSpec((None, WINDOW, 256 * EACH), lambda r, g: (part, 1, g))
    small = spec_col(WINDOW)
    got = call(functools.partial(window_back_first_kernel, length=length), "window_back", (1, STEPS),
        window_ins(low, high, p, halo, length, 0) + [(go, spec_col(length)), (p.qk_win, block()), (p.qk_win, block(GROUPS)), (p.v, block()), (halo, tail(0)), (halo, tail(1)), (go, block())],
        window_back_outs(total, length, 0) + [((2, rows * WINDOW, 1024), BF, pl.BlockSpec((2, rows * WINDOW, 256 * EACH), lambda r, g: (0, 0, g))),
         ((WINDOW, 1024), BF, small), ((WINDOW, 1024), F32, small), ((WINDOW, 1024), F32, small)],
        [pltpu.VMEM((length + WINDOW, 256 * EACH), BF)] * 2)
    return got[:3], got[3], got[4:]

def window_back_second(low, high, p, go, into, kept, rows, length):
    small = spec_col(WINDOW)
    return call(functools.partial(window_back_second_kernel, length=length), "window_back", (1, STEPS),
        [(low, SMEM), (high, SMEM), (p.qk_win, spec_col(length, 0, 1)), (p.qk_win, spec_col(length, GROUPS, 1)), (p.v, spec_col(length, 0, 1)), (go, spec_col(length, 0, 1))]
        + [(k, small) for k in kept], window_back_outs(rows * length, length, 1), into=into)

def piece_mean(x):
    a = lax.broadcasted_iota(jnp.int32, (256, 256), 0) >> 6
    b = lax.broadcasted_iota(jnp.int32, (256, 256), 1) >> 6
    ones = jnp.where(a == b, 1.0 / 64, 0.0).astype(BF)
    high = x.astype(BF)
    return nn(high, ones) + nn((x - high.astype(F32)).astype(BF), ones)

def through_state(x_t, turned, state, group, line):
    state_t = state.T.astype(BF)
    parts = []
    for h in range(4):
        parts.append(nn(state_t[h * 64:(h + 1) * 64], features_t(x_t, turned, head_rows(group, h), line)))
    return jnp.concatenate(parts, axis=0).T

def state_for(row, core, kept, received, n):
    return jnp.where(row == core[0], kept[n].astype(F32), received[n].astype(F32))

def mix_kernel(core, low, q, kept, received, local, windowed, numer, mixed, q_t, line, turned, *, length):
    r, g = pl.program_id(0), pl.program_id(1)
    @pl.when(g == 0)
    def _():
        line[...] = early_line(low, r, length)
        turn_all(q[...], q_t, turned, line[...])
    for n, (group, at) in enumerate(groups()):
        num = local[:, at].astype(F32) + through_state(q_t, turned, state_for(r, core, kept, received, n), group, line[...])
        rho = lax.rsqrt(piece_mean(num * num) + EPSILON)
        numer[:, at] = num.astype(BF)
        mixed[:, at] = (num * rho + windowed[:, at].astype(F32)).astype(BF)

def mix(core, low, p, state, local, windowed, rows, length, deps=()):
    total = rows * length
    return call(functools.partial(mix_kernel, length=length), "mix", (rows, STEPS),
        [(core, SMEM), (low, SMEM), (p.q_lin, spec_all(length)), (state[0], SPEC_STATE), (state[1], SPEC_STATE), (local, spec_col(length)), (windowed, spec_col(length))],
        [((total, 1024), BF, spec_col(length)), ((total, 1024), BF, spec_col(length))],
        [pltpu.VMEM((256, length), BF), pltpu.VMEM((1, length), F32), turned_scratch(length)], deps=deps)

def numer_back_kernel(core, low, q, numer, gm, grad_numer, mine, send, q_t, line, turned, *, length):
    r, g = pl.program_id(0), pl.program_id(1)
    @pl.when(g == 0)
    def _():
        line[...] = early_line(low, r, length)
        turn_all(q[...], q_t, turned, line[...])
    flag = (low[(r + 1) * (length // WINDOW) - 1] >= 0).astype(F32)
    for group, at in groups():
        num = numer[:, at].astype(F32)
        rho = lax.rsqrt(piece_mean(num * num) + EPSILON)
        lin = num * rho
        gl = gm[:, at].astype(F32)
        gn = (rho * (gl - lin * piece_mean(gl * lin))).astype(BF)
        grad_numer[:, at] = gn
        put_state(group, states_of(q_t, turned, gn, group, line[...], flag), core, mine, send)

def numer_back(core, low, p, numer, gm, rows, length, deps=()):
    total = rows * length
    return call(functools.partial(numer_back_kernel, length=length), "numer_back", (rows, STEPS),
        [(core, SMEM), (low, SMEM), (p.q_lin, spec_all(length)), (numer, spec_col(length)), (gm, spec_col(length))],
        [((total, 1024), BF, spec_col(length))] + state_outs(),
        [pltpu.VMEM((256, length), BF), pltpu.VMEM((1, length), F32), turned_scratch(length)], deps=deps)

def intra_back_kernel(core, low, high, q, k, v, gn, dv_in, kept, received, dq, dk_t, dv, mask, q_t, k_t, dq_t, early, turned, pulled, *, length, row):
    g = pl.program_id(1)
    half = length // 2
    @pl.when(g == 0)
    def _():
        lows, highs = spread(scalars(low, row, length), length), spread(scalars(high, row, length), length)
        j = lax.broadcasted_iota(jnp.int32, (length, length), 0)
        i = lax.broadcasted_iota(jnp.int32, (length, length), 1)
        mask[...] = ((j >= lows) & (j <= i) & (j < highs)).astype(BF)
        early[...] = (lows < 0).astype(F32)
        turn_all(q[...], q_t, turned, None)
        k_t[...] = k[...].astype(F32).T.astype(BF)
    quarter = FEAT ** -0.5
    qv, kv = q[...] * jnp.bfloat16(quarter), k[...]
    for n, (group, cols) in enumerate(groups()):
        vv, gv = v[:, cols], gn[:, cols]
        st = state_for(row, core, kept, received, n).astype(BF)
        top = dv_in[:half, cols].astype(F32)
        bottom = dv_in[half:, cols].astype(F32)
        for h in range(4):
            at = head_rows(group, h)
            km = kv * lane_mask(HEADS * FEAT, FEAT, group * 4 + h)
            vm = vv * lane_mask(256, 64, h)
            gm = gv * (lane_mask(256, 64, h) * jnp.bfloat16(0.5))
            qx, kx = q_t[at, :], k_t[at, :]
            qb, kb = qx * jnp.bfloat16(quarter), kx * jnp.bfloat16(quarter)
            u0 = 1.0 + nt(km[:half], qv)
            u1 = 1.0 + nt(km[half:], qv[half:])
            ga0 = nt(vm[:half], gv)
            ga1 = nt(vm[half:], gv[half:])
            m0, m1 = mask[:half, :], mask[half:, half:]
            a0 = (1.0 + u0 * u0).astype(BF) * m0
            a1 = (1.0 + u1 * u1).astype(BF) * m1
            ds0 = (ga0 * u0).astype(BF) * m0
            ds1 = (ga1 * u1).astype(BF) * m1
            top = top + nn(a0, gm)
            bottom = bottom + nn(a1, gm[half:])
            dk_t[0, at, :half] = nt(qb, ds0)
            dk_t[0, at, half:] = nt(qb[:, half:], ds1)
            d = nn(kb[:, :half], ds0)
            d = d + jnp.concatenate([jnp.zeros((FEAT, half), F32), nn(kb[:, half:], ds1)], axis=1)
            gphi = nt(st * lane_mask(256, 64, h), gv)
            dq_t[at, :] = d + features_back_t(q_t, turned, at, gphi * early[...], pulled)
        dv[:half, cols] = top.astype(BF)
        dv[half:, cols] = bottom.astype(BF)
    @pl.when(g == pl.num_programs(1) - 1)
    def _():
        dq[...] = (dq_t[...] + turned_back(pulled)).T.astype(BF)

def intra_back(core, low, high, p, gn, dv_in, state, rows, length, row, deps=(), into=None):
    total = rows * length
    return call(functools.partial(intra_back_kernel, length=length, row=row), "intra_back", (1, STEPS),
        [(core, SMEM), (low, SMEM), (high, SMEM), (p.q_lin, spec_all(length, row)), (p.k_lin, spec_all(length, row)), (p.v, spec_col(length, 0, row)),
         (gn, spec_col(length, 0, row)), (dv_in, spec_col(length, 0, row)), (state[0], SPEC_STATE), (state[1], SPEC_STATE)],
        [((total, 256), BF, spec_all(length, row)), ((rows, 256, length), F32, spec_t(length, row)), ((total, 1024), BF, spec_col(length, 0, row))],
        [pltpu.VMEM((length, length), BF)] + [pltpu.VMEM((256, length), BF)] * 2 + [pltpu.VMEM((256, length), F32), pltpu.VMEM((1, length), F32)] + [turned_scratch(length)] * 2,
        flops=HEADS * 2 * 15 * 256 ** 3, deps=deps, into=into)

def state_back_kernel(core, low, high, k, v, dk_in, dv_in, dhv, kept, received, dk, dv, k_t, dk_t, line, turned, pulled, *, length):
    r, g = pl.program_id(0), pl.program_id(1)
    @pl.when(g == 0)
    def _():
        line[...] = owned_line(low, high, r, length)
        turn_all(k[...], k_t, turned, line[...])
    tail = length - WINDOW
    for n, (group, cols) in enumerate(groups()):
        st = state_for(r, core, kept, received, n)
        sb = st.astype(BF)
        vv = v[:, cols]
        total = dv_in[:, cols].astype(F32) + through_state(k_t, turned, st, group, line[...])
        dv[:tail, cols] = total[:tail].astype(BF)
        dv[tail:, cols] = (total[tail:] + dhv[:, cols].astype(F32)).astype(BF)
        for h in range(4):
            at = head_rows(group, h)
            gphi = nt(sb * lane_mask(256, 64, h), vv)
            dk_t[at, :] = dk_in[0, at, :] + features_back_t(k_t, turned, at, gphi * line[...], pulled)
    @pl.when(g == pl.num_programs(1) - 1)
    def _():
        dk[...] = (dk_t[...] + turned_back(pulled)).T.astype(BF)

def state_back(core, low, high, p, dk_in, dv_in, returned, state, rows, length, deps=()):
    total = rows * length
    tail = pl.BlockSpec((None, WINDOW, 256 * EACH), lambda r, g: (1, r, g))
    return call(functools.partial(state_back_kernel, length=length), "state_back", (rows, STEPS),
        [(core, SMEM), (low, SMEM), (high, SMEM), (p.k_lin, spec_all(length)), (p.v, spec_col(length)), (dk_in, spec_t(length)), (dv_in, spec_col(length)),
         (returned, tail), (state[0], SPEC_STATE), (state[1], SPEC_STATE)],
        [((total, 256), BF, spec_all(length)), ((total, 1024), BF, spec_col(length))],
        [pltpu.VMEM((256, length), BF), pltpu.VMEM((256, length), F32), pltpu.VMEM((1, length), F32)] + [turned_scratch(length)] * 2, deps=deps)

def tail_kernel(x, got, out):
    out[...] = (x[...].astype(F32) + got[...].astype(F32)).astype(BF)

def tail_added(x, returned, rows, length, deps=()):
    per_row = length // WINDOW
    end = pl.BlockSpec((WINDOW, x.shape[1]), lambda r: ((r + 1) * per_row - 1, 0))
    return call(tail_kernel, "tail", (rows,), [(x, end), (returned, pl.BlockSpec((None, WINDOW, x.shape[1]), lambda r: (0, r, 0)))],
        [(x.shape, BF, end)], flops=10, moved=MIB, alias={0: 0}, deps=deps)[0]


ONE = dict(pipeline_mode=pl.Buffered(1))
def resident(shape):
    return pl.BlockSpec(shape, lambda *s: (0,) * len(shape), **ONE)

class Projected:
    pass

def keys_kernel(tokens, gain, wk, wv, normed, k, v):
    @pl.when(pl.program_id(0) == 0)
    def _():
        x = tokens[...].astype(F32)
        normed[...] = (x * lax.rsqrt(jnp.mean(x * x, axis=-1, keepdims=True) + EPSILON) * gain[...]).astype(BF)
        k[...] = nn(normed[...], wk[...]).astype(BF)
    v[...] = nn(normed[...], wv[...]).astype(BF)

def rest_kernel(normed, part, wq, w, q, out, normed_t):
    @pl.when(pl.program_id(0) == 0)
    def _():
        q[...] = nn(normed[...], wq[...]).astype(BF)
    normed_t[...] = part[...].T
    out[...] = nn(normed[...], w[...]).astype(BF)

def project_keys(p, tokens, gain, w_in):
    toks, width = tokens.shape
    lin = HEADS * FEAT
    first = (w_in.shape[1] - width) // 512
    p.normed, p.k_lin, p.v = call(keys_kernel, "project_keys", (width // 512,),
        [(tokens, resident((toks, width))), (gain.reshape(1, width), resident((1, width))), (w_in, pl.BlockSpec((width, lin), lambda s: (0, 1), **ONE)),
         (w_in, pl.BlockSpec((width, 512), lambda s: (0, first + s)))],
        [((toks, width), BF, resident((toks, width))), ((toks, lin), BF, resident((toks, lin))), ((toks, width), BF, pl.BlockSpec((toks, 512), lambda s: (0, s)))],
        flops=2 * toks * width * (width + lin))

def project_rest(p, w_in, deps=()):
    toks, width = p.normed.shape
    lin = HEADS * FEAT
    count = 2 * width // 512
    piece = toks // count
    p.q_lin, p.qk_win, p.normed_t = call(rest_kernel, "project_rest", (count,),
        [(p.normed, resident((toks, width))), (p.normed, pl.BlockSpec((piece, width), lambda s: (s, 0))), (w_in, pl.BlockSpec((width, lin), lambda s: (0, 0), **ONE)),
         (w_in, pl.BlockSpec((width, 512), lambda s: (0, 2 * lin // 512 + s)))],
        [((toks, lin), BF, resident((toks, lin))), ((toks, 2 * width), BF, pl.BlockSpec((toks, 512), lambda s: (0, s))),
         ((width, toks), BF, pl.BlockSpec((width, piece), lambda s: (0, s)))],
        flops=2 * toks * width * (2 * width + lin), deps=deps)

def mlp(core, mixed, tokens, cot, w_out, gain, w_gate_up, w_down, count, tile=256, chunk=1024):
    toks, width = mixed.shape
    ff = w_down.shape[0]
    steps = ff // tile
    half = width // 2
    big = resident((toks, width))
    across = pl.BlockSpec((half, tile), lambda s: (0, s))
    down = pl.BlockSpec((tile, half), lambda s: (s, 0))
    return call(functools.partial(mlp_kernel, steps=steps, chunk=chunk, each=width // count), "mlp", (steps,),
        [(core, SMEM), (mixed, big), (tokens, big), (cot, big), (w_out, resident((width, width))), (gain.reshape(1, width), resident((1, width))),
         (w_gate_up, pl.BlockSpec((width, tile), lambda s: (0, s))), (w_gate_up, pl.BlockSpec((width, tile), lambda s: (0, s + steps))),
         (w_down, pl.BlockSpec((tile, width), lambda s: (s, 0)))],
        [((toks, width), BF, big), ((toks, width), F32, big), ((toks, width), BF, big)] + [((half, ff), BF, across)] * 4
        + [((ff, half), BF, down)] * 2 + [((half, width), BF, resident((half, width)))] * 2,
        [pltpu.VMEM((toks, width), F32)] * 3 + [pltpu.VMEM((toks, width), BF), pltpu.VMEM((width, toks), BF), pltpu.VMEM((toks, tile), BF),
         pltpu.VMEM((toks, 2 * tile), BF), pltpu.VMEM((width, 2 * tile), BF)],
        flops=2 * toks * width * (9 * ff + 3 * width), moved=60 * MIB)

def weight_kernel(core, normed_t, *refs, counts, each):
    parts, (keep, send) = refs[:len(counts)], refs[len(counts):]
    step = pl.program_id(0)
    first = core[0] == 0
    begin = 0
    for ref, count in zip(parts, counts):
        @pl.when((step >= begin) & (step < begin + count))
        def _(ref=ref):
            keep[...], send[...] = parted(nn(normed_t[...], ref[...]), first, each)
        begin += count

def weight_grad(core, normed_t, parts, count, name, deps=()):
    width, toks = normed_t.shape
    counts = [p.shape[1] // 256 for p in parts]
    begins = [sum(counts[:n]) for n in range(len(counts))]
    def spec(begin, size):
        return pl.BlockSpec((toks, 256), lambda s: (0, jnp.clip(s - begin, 0, size - 1)))
    half = width // 2
    out = ((half, 256 * sum(counts)), BF, pl.BlockSpec((half, 256), lambda s: (0, s)))
    return call(functools.partial(weight_kernel, counts=counts, each=width // count), name, (sum(counts),),
        [(core, SMEM), (normed_t, resident((width, toks)))] + [(p, spec(b, n)) for p, b, n in zip(parts, begins, counts)],
        [out, out], flops=2 * width * toks * 256 * sum(counts), deps=deps)

def input_kernel(dq_lin, dk_lin, dq_win, dk_win, dv, w, tokens, gain, resid, out):
    begin, grad = 0, None
    for ref in (dq_lin, dk_lin, dq_win, dk_win, dv):
        size = ref.shape[1]
        term = nt(ref[...], w[:, begin:begin + size])
        grad = term if grad is None else grad + term
        begin += size
    x = tokens[...].astype(F32)
    scale = lax.rsqrt(jnp.mean(x * x, axis=-1, keepdims=True) + EPSILON)
    c = grad * gain[...]
    out[...] = resid[...] + scale * c - x * (scale * scale * scale * jnp.mean(c * x, axis=-1, keepdims=True))

def input_grad(parts, w_in, tokens, gain, resid, part, ways, name, deps=(), into=None):
    toks, width = tokens.shape
    piece = toks // ways
    by_rows = lambda columns: pl.BlockSpec((piece, columns), lambda s: (part, 0), **ONE)
    return call(input_kernel, name, (1,),
        [(p, by_rows(p.shape[1])) for p in parts] + [(w_in, resident(w_in.shape)), (tokens, by_rows(width)), (gain.reshape(1, width), resident((1, width))), (resid, by_rows(width))],
        [((toks, width), F32, by_rows(width))], flops=2 * piece * width * w_in.shape[1], deps=deps, into=into)

def swap(x, bit, count):
    return lax.ppermute(x, "seq", [(i, i ^ (1 << bit)) for i in range(count)])

def over(near, far):
    return near + (1.0 - near[FLAG_ROW:FLAG_ROW + 1, :]) * far

def begun_kernel(core, mine, received, total, *, backward):
    first = core[0] == 0
    for n in range(mine.shape[0]):
        m, r = mine[n], received[n].astype(F32)
        at0, at1 = jnp.where(first, m, r), jnp.where(first, r, m)
        total[n] = (over(at0, at1) if backward else over(at1, at0)).astype(BF)

def joined_kernel(ahead, total, received, new_total):
    here = ahead[0] == 1
    for n in range(total.shape[0]):
        t, r = total[n].astype(F32), received[n].astype(F32)
        new_total[n] = over(jnp.where(here, t, r), jnp.where(here, r, t)).astype(BF)

def ended_kernel(core, ahead, mine, *refs, backward):
    received, (kept, send) = refs[:-2], refs[-2:]
    first = core[0] == 0
    own = first ^ backward
    for n in range(mine.shape[0]):
        m, r = mine[n], received[0][n].astype(F32)
        base = jnp.where(own, m, r)
        e = jnp.zeros_like(m)
        for k, ref in enumerate(received[1:]):
            e = jnp.where(ahead[k] == 1, over(e, ref[n].astype(F32)), e)
        o = over(base, e)
        kept[n] = jnp.where(own, e, o).astype(BF)
        send[n] = jnp.where(own, o, e).astype(BF)

class Scan:
    def __init__(self, mine, send, me, count, backward):
        self.me, self.count, self.backward, self.mine = me, count, backward, mine
        self.received = [swap(send, 0, count)]
        self.bit, self.last = 0, count.bit_length() - 2
        self.core = (me % 2).reshape(1)
        self.ahead = ((me >> jnp.arange(1, self.last + 1, dtype=jnp.int32)) & 1) ^ (1 if backward else 0)
    def _call(self, kernel, name, flags, arrays, outs, through=()):
        shape = self.mine.shape
        whole = pl.BlockSpec(shape, lambda: (0, 0, 0))
        return call(kernel, name, (), [(f, SMEM) for f in flags] + [(a, whole) for a in arrays], [(shape, BF, whole)] * outs, flops=10, moved=MIB, through=through)
    def step(self, through=()):
        if self.bit == 0:
            self.total, *self.through = self._call(functools.partial(begun_kernel, backward=self.backward), "begun", [self.core], [self.mine, self.received[0]], 1, through)
        elif self.bit < self.last:
            self.total, = self._call(joined_kernel, "joined", [self.ahead[self.bit - 1:self.bit]], [self.total, self.received[-1]], 1)
        else:
            self.kept, self.total = self._call(functools.partial(ended_kernel, backward=self.backward), "ended", [self.core, self.ahead], [self.mine] + self.received, 2)
        self.bit += 1
        self.received.append(swap(self.total, self.bit if self.bit <= self.last else 0, self.count))
    def done(self):
        return self.kept, self.received[-1]

def padded(rows):
    return -(-rows // 16) * 16

class Piece:
    def __init__(self, arrays, first=0, size=None, rows=None):
        self.arrays = arrays
        self.first, self.size = first, size or arrays[0].shape[2]
        self.rows = rows or arrays[0].shape[1]
        self.height = self.size // 256 * padded(self.rows)

def add_kernel(*refs, plan, count, scalars):
    refs = refs[scalars:]
    ins, outs = refs[:-count], refs[-count:]
    for target, parts, at, height, rows, columns in plan:
        for k, sources in enumerate(parts):
            total = None
            for s in sources:
                term = ins[s][...].astype(F32)
                total = term if total is None else total + term
            total = total.astype(BF)
            pad = padded(rows)
            for c in range(columns // 256):
                outs[target + k][:, :, at + c * pad:at + c * pad + rows, :] = total[..., c * 256:(c + 1) * 256]

def add_up(groups, ways, name, most=4, deps=()):
    grid = min([most] + [outer for _, outer, _, _ in groups])
    ins, outs, plan = [], [], []
    for n, (pieces, outer, inner, own) in enumerate(groups):
        per = outer // grid
        at = 0
        for piece in pieces:
            parts = []
            for k in range(ways):
                sources = []
                for array in piece.arrays:
                    _, rows, columns = array.shape
                    def index(a, *own_refs, n=n, k=k, block=piece.first // piece.size):
                        return (a, own_refs[n][0] ^ k if ways > 1 else 0, 0, 0, block)
                    sources.append(len(ins))
                    ins.append((array.reshape(outer, ways, inner, rows, columns), pl.BlockSpec((per, None, inner, rows, piece.size), index)))
                parts.append(sources)
            plan.append((n * ways, parts, at, piece.height, piece.rows, piece.size))
            at += piece.height
        outs += [((outer, inner, at, 256), BF, pl.BlockSpec((per, inner, at, 256), lambda a, *own_refs: (a, 0, 0, 0)))] * ways
    got = call(functools.partial(add_kernel, plan=plan, count=len(outs), scalars=len(groups)), name, (grid,), ins, outs, flops=10, moved=20 * MIB,
        scalars=[own.reshape(1) for _, _, _, own in groups], deps=deps)
    got = [x.reshape((-1,) + x.shape[2:]) for x in got]
    return [got[n * ways:(n + 1) * ways] for n in range(len(groups))]

def chips_first(x, chips):
    return x.reshape(chips, x.shape[0] // chips, x.shape[1])

class MlpSum:
    def __init__(self, pairs, me, count):
        self.me, self.count, self.chips = me, count, count // 2
        self.pairs = [(chips_first(k, self.chips), chips_first(swap(s, 0, count), self.chips)) for k, s in pairs]
        self.bit = 0
    def step(self, deps=()):
        me, chips = self.me, self.chips
        bits = self.count.bit_length() - 1
        self.bit += 1
        if self.bit == 1:
            g, u, d, o = self.pairs
            half = lambda x, n: Piece(x, n * (x[0].shape[2] // 2), x[0].shape[2] // 2)
            pieces = [Piece(g), half(d, 0), half(o, 0)], [Piece(u), half(d, 1), half(o, 1)]
            self.layout = [(p.rows, p.size) for ps in pieces for p in ps]
            (ka, sa), (kb, sb) = add_up([(pieces[0], chips // 2, 1, (me >> 1) & 1), (pieces[1], chips // 4, 2, (me >> 2) & 1)], 2, "sum_first", deps=deps)
            self.a, self.b = [ka, swap(sa, 1, self.count)], [kb, swap(sb, 2, self.count)]
        elif self.bit == 2:
            (ka, sa), (kb, sb) = add_up([([Piece(self.a)], chips // 4, 1, (me >> 2) & 1), ([Piece(self.b)], chips // 4, 1, (me >> 1) & 1)], 2, "sum_second")
            self.a, self.b = [ka, swap(sa, 2, self.count)], [kb, swap(sb, 1, self.count)]
        else:
            pieces = [Piece(self.a), Piece(self.b)] if self.bit == 3 else [Piece(self.all)]
            (k, s), = add_up([(pieces, chips >> self.bit, 1, (me >> self.bit) & 1)], 2, "sum_more")
            self.all = [k, swap(s, self.bit, self.count)]

def quarters(pieces, bit, me, count):
    flip = lambda x, k: lax.ppermute(x, "seq", [(i, i ^ (k << bit)) for i in range(count)])
    parts, = add_up([(pieces, (count // 2) >> (bit + 1), 1, (me >> bit) & 3)], 4, "quarters", 2)
    return [parts[0]] + [flip(parts[k], k) for k in (3, 2, 1)]

class InSum:
    def __init__(self, me, count):
        self.me, self.count, self.chips = me, count, count // 2
        self.bit = 1
    def first(self, keep, send, columns):
        arrays = chips_first(keep, self.chips), chips_first(swap(send, 0, self.count), self.chips)
        return arrays, columns
    def second(self, arrays, columns):
        me, chips = self.me, self.chips
        a, b = ([Piece(arrays, first, size) for first, size in c] for c in columns)
        (ka, sa), (kb, sb) = add_up([(a, chips // 2, 1, (me >> 1) & 1), (b, chips // 4, 2, (me >> 2) & 1)], 2, "in_first")
        return [ka, swap(sa, 1, self.count)], [kb, swap(sb, 2, self.count)]
    def third(self, *parts):
        me, chips = self.me, self.chips
        a, b = ([Piece(p[n]) for p in parts] for n in (0, 1))
        (ka, sa), (kb, sb) = add_up([(a, chips // 4, 1, (me >> 2) & 1), (b, chips // 4, 1, (me >> 1) & 1)], 2, "in_second")
        self.arrays = [Piece([ka, swap(sa, 2, self.count)]), Piece([kb, swap(sb, 1, self.count)])]
        self.bit = 3
    def rest(self):
        while self.bit < self.count.bit_length() - 1:
            got = quarters(self.arrays, self.bit, self.me, self.count)
            self.arrays = [Piece(got)]
            self.bit += 2
        return got

def finish(rows, me, count):
    core = me % 2
    each = rows.shape[0] // 2
    own = lax.dynamic_slice_in_dim(rows, core * each, each, 0)
    got = swap(lax.dynamic_slice_in_dim(rows, (1 - core) * each, each, 0), 0, count)
    return jnp.concatenate([jnp.where(core == 0, own, got), jnp.where(core == 0, got, own)], axis=1)

def gathered_kernel(place, weights, gain, *refs, layout, rows):
    arrays, (out, gain_out) = refs[:-2], refs[-2:]
    total = None
    for n, at in enumerate(layout):
        g = None
        for ref in arrays:
            term = ref[0, at:at + rows, :].astype(F32)
            g = term if g is None else g + term
        out[:, n * 256:(n + 1) * 256] = g
        t = g * weights[:, n * 256:(n + 1) * 256].astype(F32)
        total = t if total is None else total + t
    gain_out[...] = jnp.sum(total, axis=1, keepdims=True) / gain[...]

def gathered(arrays, layout, weights, gain, me, count):
    each, columns = weights.shape[0] // count, weights.shape[1]
    if each < 16:
        weights, gain = lax.dynamic_slice_in_dim(weights, me * each, each, 0), lax.dynamic_slice_in_dim(gain, me * each, each, 0)
        me = jnp.zeros((), jnp.int32)
    mine = pl.BlockSpec((each, columns), lambda s, place: (place[0], 0))
    one = pl.BlockSpec((each, 1), lambda s, place: (place[0], 0))
    out, gain_out = call(functools.partial(gathered_kernel, layout=layout, rows=each), "gathered", (1,),
        [(weights, mine), (gain.reshape(-1, 1), one)] + [(a, resident(a.shape)) for a in arrays],
        [((each, columns), F32, resident((each, columns))), ((each, 1), F32, resident((each, 1)))], flops=10, moved=MIB, scalars=[me.reshape(1)])
    return out, gain_out.reshape(each)

def plain_kernel(*refs, pieces, shapes):
    arrays, outs = refs[:-len(shapes)], refs[-len(shapes):]
    for out, first, rows, column in pieces:
        g = None
        for ref in arrays:
            term = ref[0, first:first + rows, :].astype(F32)
            g = term if g is None else g + term
        outs[out][:, column:column + 256] = g

def plain(arrays, pieces, shapes):
    return call(functools.partial(plain_kernel, pieces=pieces, shapes=shapes), "plain", (1,), [(a, resident(a.shape)) for a in arrays],
        [(s, F32, resident(s)) for s in shapes], flops=10, moved=MIB)

def shards(tokens, seq_starts, seq_lengths, gain_in, gain_mlp, w_in, w_out, w_gate_up, w_down, cotangent):
    Order.last = None
    rows, length, width = tokens.shape
    count = lax.axis_size("seq")
    bits = count.bit_length() - 1
    order_a = list(range(1, bits))
    order_b = [2, 1] + list(range(3, bits))
    order_c = [3, 1, 2] + list(range(4, bits))
    me = lax.axis_index("seq")
    core = (me % 2).reshape(1)
    total = rows * length
    begin = me * length
    low = (seq_starts[:, ::WINDOW] - begin).reshape(-1)
    high = low + seq_lengths[:, ::WINDOW].reshape(-1)

    x = tokens.reshape(total, width)
    cot = cotangent.reshape(total, width)
    p = Projected()
    project_keys(p, x, gain_in, w_in)
    scan = Scan(*local_states(core, low, high, p.k_lin, p.v, rows, length), me, count, False)
    project_rest(p, w_in)
    tails = lambda a, at: a.reshape(rows, length, -1)[:, -WINDOW:, at:at + width]
    forward = [(i, i + 1) for i in range(count - 1)]
    backward = [(i + 1, i) for i in range(count - 1)]
    halo = lax.ppermute(jnp.stack([tails(p.qk_win, width), tails(p.v, 0)]), "seq", forward).reshape(2, rows * WINDOW, width)
    scan.step()
    local = intra(low, high, p, rows, length, 0)
    scan.step()
    local, = intra(low, high, p, rows, length, 1, into=local)
    scan.step()
    windowed = window(low, high, p, halo, rows, length, 0)
    scan.step()
    windowed, = window(low, high, p, halo, rows, length, 1, into=windowed)
    while scan.bit < bits:
        scan.step()
    state_in = scan.done()
    numer, mixed = mix(core, low, p, state_in, local, windowed, rows, length)

    (result, grad_resid, grad_mixed, keep_g, send_g, keep_u, send_u, keep_d, send_d, keep_o, send_o) = mlp(
        core, mixed, x, cot, w_out, gain_mlp, w_gate_up, w_down, count)
    grad_numer, *grad_state_in = numer_back(core, low, p, numer, grad_mixed, rows, length)
    scan = Scan(*grad_state_in, me, count, True)

    scan.step(through=(send_g, send_u, send_d, send_o))
    mlp_sum = MlpSum(list(zip((keep_g, keep_u, keep_d, keep_o), scan.through)), me, count)
    back, dh, kept = window_back_first(low, high, p, halo, grad_mixed, rows, length)
    returned = lax.ppermute(dh, "seq", backward)
    scan.step()
    mlp_sum.step(deps=(returned,))
    scan.step()
    dq_win, dk_win, dv_win = window_back_second(low, high, p, grad_mixed, back, kept, rows, length)
    scan.step()
    inner = intra_back(core, low, high, p, grad_numer, dv_win, state_in, rows, length, 0)
    while scan.bit < bits:
        scan.step()
    inner = intra_back(core, low, high, p, grad_numer, dv_win, state_in, rows, length, 1, into=inner)
    dq_lin, dk_t, dv_part = inner
    mlp_sum.step()
    dk_win = tail_added(dk_win, returned, rows, length, deps=(scan.received[-1],))
    lin = HEADS * FEAT
    in_sum = InSum(me, count)
    early = in_sum.first(*weight_grad(core, p.normed_t, [dq_win, dk_win, dq_lin], count, "weight_grad_early"), (((0, width), (2 * width, lin)), ((width, width),)))
    dk_lin, dv = state_back(core, low, high, p, dk_t, dv_part, returned, scan.done(), rows, length)
    mlp_sum.step()
    late = in_sum.first(*weight_grad(core, p.normed_t, [dv, dk_lin], count, "weight_grad_late"), (((0, width // 2),), ((width // 2, width // 2), (width, lin))))
    parts = [dq_lin, dk_lin, dq_win, dk_win, dv]
    early = in_sum.second(*early)
    grad_tokens = input_grad(parts, w_in, x, gain_in, grad_resid, 0, 4, "input_grad_first")
    late = in_sum.second(*late)
    while mlp_sum.bit < bits - 1:
        mlp_sum.step()
    grad_tokens = input_grad(parts, w_in, x, gain_in, grad_resid, 1, 4, "input_grad", into=grad_tokens)
    in_sum.third(early, late)
    grad_tokens, = input_grad(parts, w_in, x, gain_in, grad_resid, 1, 2, "input_grad", into=grad_tokens)
    ff, each, chip = w_down.shape[0], width // count, w_down.shape[0] // (count // 2)
    pad = padded(each)
    height = ff // 256 * pad
    second = height + padded(chip) + 2 * pad
    part_gate_up, part_gain_mlp = gathered(mlp_sum.all, [n * pad for n in range(ff // 256)] + [second + n * pad for n in range(ff // 256)],
        w_gate_up, gain_mlp, me, count)
    in_got = in_sum.rest()
    down, part_out = plain(mlp_sum.all, [(0, height, chip, 0), (0, second + height, chip, 256)]
        + [(1, height + padded(chip) + n * pad + (second - 2 * pad if n >= 2 else 0), each, n * 256) for n in range(4)],
        [(chip, width // 2), (each, width)])
    part_down = finish(down, me, count)
    wide, piece = width // 256, list(range(3 * width // 256 + 2 * lin // 256))
    q_win, q_lin, v_a, k_win, v_b, k_lin = (piece[wide * n // 2 + m:wide * (n + c) // 2 + m + k] for n, m, c, k in
        ((0, 0, 2, 0), (2, 0, 0, 1), (2, 1, 1, 0), (3, 1, 2, 0), (5, 1, 1, 0), (6, 1, 0, 1)))
    part_in, part_gain_in = gathered(in_got, [n * pad for n in q_lin + k_lin + q_win + k_win + v_a + v_b], w_in, gain_in, me, count)
    return (result.reshape(rows, length, width), grad_tokens.reshape(rows, length, width), part_gain_in, part_gain_mlp,
            part_in, part_out, part_gate_up, part_down)

def solution(mesh):
    split = P(None, "seq", None)
    placed = (split, P(None, "seq"), P(None, "seq"), P(), P(), P(), P(), P(), P(), split)
    return jax.shard_map(shards, mesh=mesh, in_specs=placed,
        out_specs=(split, split, P("seq"), P("seq"), P("seq", None), P("seq", None), P("seq", None), P("seq", None)),
        check_vma=False)
```

```python
import functools
import jax
import jax.numpy as jnp
from jax import lax
from jax.experimental import pallas as pl
from jax.experimental.pallas import tpu as pltpu
from jax.sharding import PartitionSpec as P
F32=jnp.float32; BF=jnp.bfloat16
EPSILON=1e-6
MIB=1<<20

def nn(a,b): return lax.dot_general(a,b,(((1,),(0,)),((),())),preferred_element_type=F32)
def nt(a,b): return lax.dot_general(a,b,(((1,),(1,)),((),())),preferred_element_type=F32)
def tn(a,b): return lax.dot_general(a,b,(((0,),(0,)),((),())),preferred_element_type=F32)

def parted(x, first, each):
    x = x.reshape(x.shape[0] // (2 * each), 2, each, x.shape[1])
    a, b = x[:, 0].reshape(-1, x.shape[3]), x[:, 1].reshape(-1, x.shape[3])
    return jnp.where(first, a, b).astype(BF), jnp.where(first, b, a).astype(BF)

def mlp_kernel(core_ref, mixed, tokens, cot, w_out, gain, wg, wu, wd,
               result, grad_resid, grad_mixed, keep_g, send_g, keep_u, send_u, keep_d, send_d, keep_o, send_o,
               resid, acc, dh, hn, hn_t, hid, dgu, wgu, *, steps, chunk, each):
    step = pl.program_id(0)
    toks = mixed.shape[0]
    width = mixed.shape[1]
    count = toks // chunk
    first = core_ref[0] == 0

    def rows(n):
        return pl.ds(pl.multiple_of(n * chunk, chunk), chunk)

    @pl.when(step == 0)
    def _():
        def one(n, carry):
            r = rows(n)
            res = tokens[r, :].astype(F32) + nn(mixed[r, :], w_out[...])
            scale = lax.rsqrt(jnp.mean(res * res, axis=-1, keepdims=True) + EPSILON)
            h = (res * scale * gain[...]).astype(BF)
            resid[r, :] = res
            acc[r, :] = res
            dh[r, :] = jnp.zeros((chunk, width), F32)
            hn[r, :] = h
            return carry
        lax.fori_loop(0, count, one, 0)
        for n in range(count):
            hn_t[:, n * chunk:(n + 1) * chunk] = hn[n * chunk:(n + 1) * chunk, :].T

    tile = wg.shape[1]
    wgu[:, :tile] = wg[...]
    wgu[:, tile:] = wu[...]

    def forward(n, carry):
        r = rows(n)
        h = hn[r, :]
        both = nn(h, wgu[...])
        gate, up = both[:, :tile], both[:, tile:]
        dhid = nt(cot[r, :], wd[...])
        sig = 1.0 / (1.0 + jnp.exp(-gate))
        silu = gate * sig
        hidden = (silu * up).astype(BF)
        d_gate = (dhid * up * (sig + silu * (1.0 - sig))).astype(BF)
        d_up = (dhid * silu).astype(BF)
        hid[r, :] = hidden
        dgu[r, :tile] = d_gate
        dgu[r, tile:] = d_up
        acc[r, :] += nn(hidden, wd[...])
        dh[r, :] += nt(dgu[r, :], wgu[...])
        return carry
    lax.fori_loop(0, count, forward, 0, unroll=2)

    half = width // 2
    grad_d = tn(hid[...], cot[...])
    left, right = grad_d[:, :half].astype(BF), grad_d[:, half:].astype(BF)
    keep_d[...] = jnp.where(first, left, right)
    send_d[...] = jnp.where(first, right, left)

    def weights(n, carry):
        r = rows(n)
        o = pl.ds(pl.multiple_of(n * (chunk // 2), chunk // 2), chunk // 2)
        grad = nn(hn_t[r, :], dgu[...])
        keep_g[o, :], send_g[o, :] = parted(grad[:, :tile], first, each)
        keep_u[o, :], send_u[o, :] = parted(grad[:, tile:], first, each)
        return carry
    lax.fori_loop(0, width // chunk, weights, 0, unroll=2)

    @pl.when(step == steps - 1)
    def _():
        def one(n, carry):
            r = rows(n)
            res = resid[r, :]
            scale = lax.rsqrt(jnp.mean(res * res, axis=-1, keepdims=True) + EPSILON)
            grad = dh[r, :]
            c = grad * gain[...]
            back = cot[r, :].astype(F32) + scale * c - res * (scale * scale * scale * jnp.mean(c * res, axis=-1, keepdims=True))
            result[r, :] = acc[r, :].astype(BF)
            grad_resid[r, :] = back
            b = back.astype(BF)
            hn[r, :] = b
            grad_mixed[r, :] = nt(b, w_out[...]).astype(BF)
            return carry
        lax.fori_loop(0, count, one, 0)
        for n in range(count):
            hn_t[:, n * chunk:(n + 1) * chunk] = mixed[n * chunk:(n + 1) * chunk, :].T
        def outer(n, carry):
            r = rows(n)
            o = pl.ds(pl.multiple_of(n * (chunk // 2), chunk // 2), chunk // 2)
            keep_o[o, :], send_o[o, :] = parted(nn(hn_t[r, :], hn[...]), first, each)
            return carry
        lax.fori_loop(0, width // chunk, outer, 0)


HEADS=16; FEAT=16; WINDOW=64; ROWS_PHI=160; FLAG_ROW=153
VMEM = 64 * MIB
GROUPS = HEADS // 4
EACH = 2
STEPS = GROUPS // EACH

def groups():
    return [(pl.program_id(1) * EACH + s, slice(s * 256, (s + 1) * 256)) for s in range(EACH)]

COST = dict(project_keys=6.8, state=7.4, project_rest=10, begun=2, joined=2.5, ended=3, intra=7.2, window=8.5, mix=10, mlp=88, numer_back=12,
    window_back=13, intra_back=14, sum_first=10.6, sum_second=6.4, state_back=0.1, weight_grad_early=0.1, weight_grad_late=0.1, input_grad_first=0.1, input_grad=0.1, in_first=3, in_second=3, quarters=3.5, tail=1.8, gathered=2.3, plain=2.0, sum_more=3)

class Order:
    last = None

def call(kernel, name, grid, ins, outs, scratch=(), flops=0, moved=10 * MIB, deps=(), into=None, alias=None, scalars=(), through=()):
    arrays, specs = [a for a, _ in ins], [s for _, s in ins]
    count, ahead = len(arrays), len(scalars)
    into = list(into or ())
    deps = list(deps)
    if Order.last is not None and not any(Order.last is a for a in into + deps + arrays):
        deps.append(Order.last)
    extra = deps + into + list(through)
    aliases = {ahead + count + len(deps) + n: n for n in range(len(into))}
    aliases.update({ahead + i: o for i, o in (alias or {}).items()})
    aliases.update({ahead + count + len(deps) + len(into) + n: len(outs) + n for n in range(len(through))})
    results = len(outs)
    outs = list(outs) + [(a.shape, a.dtype, pl.BlockSpec(memory_space=pl.ANY)) for a in through]
    def body(*refs):
        begin = ahead + count + len(extra)
        kernel(*refs[:ahead + count], *refs[begin:begin + results], *refs[begin + len(outs):])
    out = pl.pallas_call(
        body, grid_spec=pltpu.PrefetchScalarGridSpec(num_scalar_prefetch=ahead, grid=grid,
            in_specs=specs + [pl.BlockSpec(memory_space=pl.ANY)] * len(extra), out_specs=[s for _, _, s in outs], scratch_shapes=list(scratch)),
        out_shape=[jax.ShapeDtypeStruct(shape, dtype) for shape, dtype, _ in outs],
        input_output_aliases=aliases, name=name,
        compiler_params=pltpu.CompilerParams(vmem_limit_bytes=VMEM, dimension_semantics=("arbitrary",) * len(grid)),
        cost_estimate=pl.CostEstimate(flops=int(COST.get(name, 2.0) * 1e9), bytes_accessed=1000, transcendentals=0),
    )(*scalars, *arrays, *extra)
    Order.last = out[0]
    return out

def lane_mask(width, size, which, dtype=BF):
    lanes = lax.broadcasted_iota(jnp.int32, (1, width), 1)
    return ((lanes >> (size.bit_length() - 1)) == which).astype(dtype)

def spread(values, length):
    block = lax.broadcasted_iota(jnp.int32, (1, length), 1) >> 6
    out = jnp.zeros((1, length), jnp.int32)
    for n, value in enumerate(values):
        out = jnp.where(block == n, value, out)
    return out

def scalars(ref, row, length):
    per_row = length // WINDOW
    return [ref[row * per_row + n] for n in range(per_row)]

def early_line(low, row, length):
    return (spread(scalars(low, row, length), length) < 0).astype(F32)

def owned_line(low, high, row, length):
    lows = scalars(low, row, length)
    place = lax.broadcasted_iota(jnp.int32, (1, length), 1)
    same = spread(lows, length) == lows[-1]
    return (same & (place < spread(scalars(high, row, length), length))).astype(F32)

TURNS = FEAT // 2

def turn(d):
    row = lax.broadcasted_iota(jnp.int32, (HEADS * FEAT, HEADS * FEAT), 0)
    entry = lax.broadcasted_iota(jnp.int32, (HEADS * FEAT, HEADS * FEAT), 1)
    return (((row & -FEAT) | ((row + d) & (FEAT - 1))) == entry).astype(BF)

def turned_scratch(length):
    return pltpu.VMEM((TURNS, HEADS * FEAT, length), BF)

def turn_all(x, x_t, turned, line):
    flipped = x.astype(F32).T
    flat = (flipped if line is None else flipped * line).astype(BF)
    x_t[...] = flat
    for d in range(1, TURNS + 1):
        turned[d - 1] = nn(turn(d), flat).astype(BF)

def features_t(x_t, turned, at, line):
    half = FEAT // 2
    x = x_t[at, :]
    parts = [x * x * jnp.bfloat16((2.0 * FEAT) ** -0.5)]
    xs = x * jnp.bfloat16(FEAT ** -0.5)
    for d in range(1, half):
        parts.append(xs * turned[d - 1, at, :])
    parts.append(x * jnp.bfloat16(FEAT ** -0.25))
    row = lax.broadcasted_iota(jnp.int32, x.shape, 0)
    parts.append(jnp.where(row < half, xs * turned[half - 1, at, :], jnp.where(row == half, line, 0.0).astype(BF)))
    return jnp.concatenate(parts, axis=0)

def features_back_t(x_t, turned, at, g, pulled):
    half = FEAT // 2
    x = x_t[at, :]
    total = g[:FEAT] * x.astype(F32) * (2.0 * (2.0 * FEAT) ** -0.5) + g[half * FEAT:(half + 1) * FEAT] * FEAT ** -0.25
    mixed = jnp.zeros(x.shape, F32)
    xs = x * jnp.bfloat16(FEAT ** -0.5)
    row = lax.broadcasted_iota(jnp.int32, x.shape, 0)
    gb = g.astype(BF)
    for d in range(1, half + 1):
        if d < half:
            gd = gb[d * FEAT:(d + 1) * FEAT]
        else:
            gd = jnp.where(row < half, gb[(half + 1) * FEAT:(half + 2) * FEAT], jnp.bfloat16(0))
        mixed = mixed + (gd * turned[d - 1, at, :]).astype(F32)
        pulled[d - 1, at, :] = gd * xs
    return total + mixed * FEAT ** -0.5

def turned_back(pulled):
    total = None
    for d in range(1, TURNS + 1):
        term = nn(turn(-d), pulled[d - 1])
        total = term if total is None else total + term
    return total

def head_rows(group, h):
    return pl.ds(pl.multiple_of(group * 4 * FEAT + h * FEAT, FEAT), FEAT)

def states_of(x_t, turned, y, group, line, flag):
    row = lax.broadcasted_iota(jnp.int32, (ROWS_PHI, 256), 0)
    out = jnp.where(row == FLAG_ROW, flag, 0.0)
    phi = jnp.concatenate([features_t(x_t, turned, head_rows(group, h), line) for h in range(4)], axis=0)
    every = nn(phi, y)
    for h in range(4):
        out = out + every[h * ROWS_PHI:(h + 1) * ROWS_PHI] * lane_mask(256, 64, h, F32)
    return out

def put_state(g, state, core, mine, send):
    r = pl.program_id(0)
    @pl.when(r == core[0])
    def _():
        mine[g] = state
    @pl.when(r != core[0])
    def _():
        send[g] = state.astype(BF)

def state_outs():
    shape = (GROUPS, ROWS_PHI, 256)
    spec = pl.BlockSpec(shape, lambda r, g: (0, 0, 0))
    return [(shape, F32, spec), (shape, BF, spec)]

def state_kernel(core, low, high, k, v, mine, send, k_t, line, turned, *, length):
    r, g = pl.program_id(0), pl.program_id(1)
    @pl.when(g == 0)
    def _():
        line[...] = owned_line(low, high, r, length)
        turn_all(k[...], k_t, turned, line[...])
    flag = (low[(r + 1) * (length // WINDOW) - 1] >= 0).astype(F32)
    for g, at in groups():
        put_state(g, states_of(k_t, turned, v[:, at], g, line[...], flag), core, mine, send)

def spec_col(length, first=0, row=0):
    return pl.BlockSpec((length, 256 * EACH), lambda r, g: (r + row, first // EACH + g))
def spec_all(length, row=0):
    return pl.BlockSpec((length, 256), lambda r, g: (r + row, 0))
SPEC_STATE = pl.BlockSpec((EACH, ROWS_PHI, 256), lambda r, g: (g, 0, 0))
def spec_t(length, row=0):
    return pl.BlockSpec((1, 256, length), lambda r, g: (r + row, 0, 0))
SMEM = pl.BlockSpec(memory_space=pltpu.SMEM)
def local_states(core, low, high, k, v, rows, length):
    return call(functools.partial(state_kernel, length=length), "state", (rows, STEPS),
        [(core, SMEM), (low, SMEM), (high, SMEM), (k, spec_all(length)), (v, spec_col(length))], state_outs(),
        [pltpu.VMEM((256, length), BF), pltpu.VMEM((1, length), F32), turned_scratch(length)])

def intra_kernel(low, high, q, k, v, out, mask, *, length, row):
    g = pl.program_id(1)
    half = length // 2
    @pl.when(g == 0)
    def _():
        lows, highs = scalars(low, row, length), scalars(high, row, length)
        for n in range(length // WINDOW):
            i = lax.broadcasted_iota(jnp.int32, (WINDOW, length), 0) + n * WINDOW
            j = lax.broadcasted_iota(jnp.int32, (WINDOW, length), 1)
            mask[n * WINDOW:(n + 1) * WINDOW, :] = ((j >= lows[n]) & (j <= i) & (j < highs[n])).astype(BF)
    qv, kv = q[...] * jnp.bfloat16(FEAT ** -0.5), k[...]
    for g, at in groups():
        vv = v[:, at] * jnp.bfloat16(0.5)
        top = bottom = None
        for h in range(4):
            km = kv * lane_mask(HEADS * FEAT, FEAT, g * 4 + h)
            vm = vv * lane_mask(256, 64, h)
            u0 = 1.0 + nt(qv[:half], km[:half])
            a0 = (1.0 + u0 * u0).astype(BF) * mask[:half, :half]
            u1 = 1.0 + nt(qv[half:], km)
            a1 = (1.0 + u1 * u1).astype(BF) * mask[half:, :]
            o0, o1 = nn(a0, vm[:half]), nn(a1, vm)
            top = o0 if top is None else top + o0
            bottom = o1 if bottom is None else bottom + o1
        out[:half, at] = top.astype(BF)
        out[half:, at] = bottom.astype(BF)

def intra(low, high, p, rows, length, row, deps=(), into=None):
    return call(functools.partial(intra_kernel, length=length, row=row), "intra", (1, STEPS),
        [(low, SMEM), (high, SMEM), (p.q_lin, spec_all(length, row)), (p.k_lin, spec_all(length, row)), (p.v, spec_col(length, 0, row))],
        [((rows * length, 1024), BF, spec_col(length, 0, row))],
        [pltpu.VMEM((length, length), BF)], flops=HEADS * 2 * 6 * 256 ** 3, deps=deps, into=into)

def stacked(x, scale=1.0):
    return jnp.concatenate([x * (lane_mask(256, 64, h) * jnp.bfloat16(scale)) for h in range(4)], axis=0)

def unstacked(x, scale=1.0):
    total = None
    for h in range(4):
        part = x[h * WINDOW:(h + 1) * WINDOW] * (lane_mask(256, 64, h, F32) * scale)
        total = part if total is None else total + part
    return total

def window_probs(low, high, at, shift, keys, qs):
    s = nt(keys, qs)
    key = lax.broadcasted_iota(jnp.int32, (2 * WINDOW, 4 * WINDOW), 0)
    query = lax.broadcasted_iota(jnp.int32, (2 * WINDOW, 4 * WINDOW), 1) & (WINDOW - 1)
    ok = (key >= jnp.maximum(query, low[at] + shift)) & (key < jnp.minimum(query + (WINDOW + 1), high[at] + shift))
    s = jnp.where(ok, s, -1e30)
    p = jnp.exp(s - jnp.max(s, axis=0, keepdims=True))
    return p * (1.0 / jnp.sum(p, axis=0, keepdims=True))

def window_kernel(low, high, q, k, v, hk, hv, out, ka, va, *, length, row):
    per_row = length // WINDOW
    ka[:WINDOW, :] = hk[...]
    ka[WINDOW:, :] = k[...]
    va[:WINDOW, :] = hv[...]
    va[WINDOW:, :] = v[...]
    for g, at in groups():
        for n in range(per_row):
            own, both = slice(n * WINDOW, (n + 1) * WINDOW), slice(n * WINDOW, (n + 2) * WINDOW)
            p = window_probs(low, high, row * per_row + n, (1 - n) * WINDOW, ka[both, at], stacked(q[own, at], 64 ** -0.5))
            out[own, at] = unstacked(tn(p.astype(BF), va[both, at])).astype(BF)

def window_ins(low, high, p, halo, length, row):
    tail = lambda part: pl.BlockSpec((None, WINDOW, 256 * EACH), lambda r, g: (part, r + row, g))
    return [(low, SMEM), (high, SMEM), (p.qk_win, spec_col(length, 0, row)), (p.qk_win, spec_col(length, GROUPS, row)), (p.v, spec_col(length, 0, row)),
            (halo, tail(0)), (halo, tail(1))]

def window(low, high, p, halo, rows, length, row, deps=(), into=None):
    return call(functools.partial(window_kernel, length=length, row=row), "window", (1, STEPS),
        window_ins(low, high, p, halo, length, row),
        [((rows * length, 1024), BF, spec_col(length, 0, row))],
        [pltpu.VMEM((length + WINDOW, 256 * EACH), BF)] * 2, flops=HEADS * 2 * 4 * length * 128 * 256, deps=deps, into=into)

def window_back_block(low, high, row, n, per_row, q, keys, vals, go):
    qs, gs = stacked(q, 64 ** -0.5), stacked(go)
    p = window_probs(low, high, row * per_row + n, (1 - n) * WINDOW, keys, qs)
    gp = nt(vals, gs)
    ds = (p * (gp - jnp.sum(p * gp, axis=0, keepdims=True))).astype(BF)
    return unstacked(tn(ds, keys), 64 ** -0.5).astype(BF), nn(ds, qs), nn(p.astype(BF), gs)

def window_back_first_kernel(low, high, q, k, v, hk, hv, go, q1, k1, v1, hk1, hv1, go1, dq, dk, dv, dh, q_kept, k_kept, v_kept, ka, va, *, length):
    per_row = length // WINDOW
    ka[:WINDOW, :] = hk[...]
    ka[WINDOW:, :] = k[...]
    va[:WINDOW, :] = hv[...]
    va[WINDOW:, :] = v[...]
    for _, at in groups():
        carry_k = carry_v = None
        for n in range(per_row):
            rows = slice(n * WINDOW, (n + 1) * WINDOW)
            both = slice(n * WINDOW, (n + 2) * WINDOW)
            dq[rows, at], dk_n, dv_n = window_back_block(low, high, 0, n, per_row, q[rows, at], ka[both, at], va[both, at], go[rows, at])
            if n == 0:
                dh[0, :WINDOW, at] = dk_n[:WINDOW].astype(BF)
                dh[1, :WINDOW, at] = dv_n[:WINDOW].astype(BF)
            else:
                dk[(n - 1) * WINDOW:n * WINDOW, at] = (carry_k + dk_n[:WINDOW]).astype(BF)
                dv[(n - 1) * WINDOW:n * WINDOW, at] = (carry_v + dv_n[:WINDOW]).astype(BF)
            carry_k, carry_v = dk_n[WINDOW:], dv_n[WINDOW:]
        dk[length - WINDOW:, at] = carry_k.astype(BF)
        dv[length - WINDOW:, at] = carry_v.astype(BF)
        keys = jnp.concatenate([hk1[:, at], k1[:, at]], axis=0)
        vals = jnp.concatenate([hv1[:, at], v1[:, at]], axis=0)
        q_kept[:, at], dk_n, dv_n = window_back_block(low, high, 1, 0, per_row, q1[:, at], keys, vals, go1[:, at])
        dh[0, WINDOW:, at] = dk_n[:WINDOW].astype(BF)
        dh[1, WINDOW:, at] = dv_n[:WINDOW].astype(BF)
        k_kept[:, at] = dk_n[WINDOW:]
        v_kept[:, at] = dv_n[WINDOW:]

def window_back_second_kernel(low, high, q, k, v, go, q_kept, k_kept, v_kept, dq, dk, dv, *, length):
    per_row = length // WINDOW
    dq[:WINDOW, :] = q_kept[...]
    for _, at in groups():
        carry_k, carry_v = k_kept[:, at], v_kept[:, at]
        for n in range(1, per_row):
            rows = slice(n * WINDOW, (n + 1) * WINDOW)
            both = slice((n - 1) * WINDOW, (n + 1) * WINDOW)
            dq[rows, at], dk_n, dv_n = window_back_block(low, high, 1, n, per_row, q[rows, at], k[both, at], v[both, at], go[rows, at])
            dk[(n - 1) * WINDOW:n * WINDOW, at] = (carry_k + dk_n[:WINDOW]).astype(BF)
            dv[(n - 1) * WINDOW:n * WINDOW, at] = (carry_v + dv_n[:WINDOW]).astype(BF)
            carry_k, carry_v = dk_n[WINDOW:], dv_n[WINDOW:]
        dk[length - WINDOW:, at] = carry_k.astype(BF)
        dv[length - WINDOW:, at] = carry_v.astype(BF)

def window_back_outs(total, length, row):
    spec = spec_col(length, 0, row)
    return [((total, 1024), BF, spec)] * 3

def window_back_first(low, high, p, halo, go, rows, length):
    total, per_row = rows * length, length // WINDOW
    block = lambda first=0: pl.BlockSpec((WINDOW, 256 * EACH), lambda r, g: (per_row, first // EACH + g))
    tail = lambda part: pl.BlockSpec((None, WINDOW, 256 * EACH), lambda r, g: (part, 1, g))
    small = spec_col(WINDOW)
    got = call(functools.partial(window_back_first_kernel, length=length), "window_back", (1, STEPS),
        window_ins(low, high, p, halo, length, 0) + [(go, spec_col(length)), (p.qk_win, block()), (p.qk_win, block(GROUPS)), (p.v, block()), (halo, tail(0)), (halo, tail(1)), (go, block())],
        window_back_outs(total, length, 0) + [((2, rows * WINDOW, 1024), BF, pl.BlockSpec((2, rows * WINDOW, 256 * EACH), lambda r, g: (0, 0, g))),
         ((WINDOW, 1024), BF, small), ((WINDOW, 1024), F32, small), ((WINDOW, 1024), F32, small)],
        [pltpu.VMEM((length + WINDOW, 256 * EACH), BF)] * 2)
    return got[:3], got[3], got[4:]

def window_back_second(low, high, p, go, into, kept, rows, length):
    small = spec_col(WINDOW)
    return call(functools.partial(window_back_second_kernel, length=length), "window_back", (1, STEPS),
        [(low, SMEM), (high, SMEM), (p.qk_win, spec_col(length, 0, 1)), (p.qk_win, spec_col(length, GROUPS, 1)), (p.v, spec_col(length, 0, 1)), (go, spec_col(length, 0, 1))]
        + [(k, small) for k in kept], window_back_outs(rows * length, length, 1), into=into)

def piece_mean(x):
    a = lax.broadcasted_iota(jnp.int32, (256, 256), 0) >> 6
    b = lax.broadcasted_iota(jnp.int32, (256, 256), 1) >> 6
    ones = jnp.where(a == b, 1.0 / 64, 0.0).astype(BF)
    high = x.astype(BF)
    return nn(high, ones) + nn((x - high.astype(F32)).astype(BF), ones)

def through_state(x_t, turned, state, group, line):
    state_t = state.T.astype(BF)
    parts = []
    for h in range(4):
        parts.append(nn(state_t[h * 64:(h + 1) * 64], features_t(x_t, turned, head_rows(group, h), line)))
    return jnp.concatenate(parts, axis=0).T

def state_for(row, core, kept, received, n):
    return jnp.where(row == core[0], kept[n].astype(F32), received[n].astype(F32))

def mix_kernel(core, low, q, kept, received, local, windowed, numer, mixed, q_t, line, turned, *, length):
    r, g = pl.program_id(0), pl.program_id(1)
    @pl.when(g == 0)
    def _():
        line[...] = early_line(low, r, length)
        turn_all(q[...], q_t, turned, line[...])
    for n, (group, at) in enumerate(groups()):
        num = local[:, at].astype(F32) + through_state(q_t, turned, state_for(r, core, kept, received, n), group, line[...])
        rho = lax.rsqrt(piece_mean(num * num) + EPSILON)
        numer[:, at] = num.astype(BF)
        mixed[:, at] = (num * rho + windowed[:, at].astype(F32)).astype(BF)

def mix(core, low, p, state, local, windowed, rows, length, deps=()):
    total = rows * length
    return call(functools.partial(mix_kernel, length=length), "mix", (rows, STEPS),
        [(core, SMEM), (low, SMEM), (p.q_lin, spec_all(length)), (state[0], SPEC_STATE), (state[1], SPEC_STATE), (local, spec_col(length)), (windowed, spec_col(length))],
        [((total, 1024), BF, spec_col(length)), ((total, 1024), BF, spec_col(length))],
        [pltpu.VMEM((256, length), BF), pltpu.VMEM((1, length), F32), turned_scratch(length)], deps=deps)

def numer_back_kernel(core, low, q, numer, gm, grad_numer, mine, send, q_t, line, turned, *, length):
    r, g = pl.program_id(0), pl.program_id(1)
    @pl.when(g == 0)
    def _():
        line[...] = early_line(low, r, length)
        turn_all(q[...], q_t, turned, line[...])
    flag = (low[(r + 1) * (length // WINDOW) - 1] >= 0).astype(F32)
    for group, at in groups():
        num = numer[:, at].astype(F32)
        rho = lax.rsqrt(piece_mean(num * num) + EPSILON)
        lin = num * rho
        gl = gm[:, at].astype(F32)
        gn = (rho * (gl - lin * piece_mean(gl * lin))).astype(BF)
        grad_numer[:, at] = gn
        put_state(group, states_of(q_t, turned, gn, group, line[...], flag), core, mine, send)

def numer_back(core, low, p, numer, gm, rows, length, deps=()):
    total = rows * length
    return call(functools.partial(numer_back_kernel, length=length), "numer_back", (rows, STEPS),
        [(core, SMEM), (low, SMEM), (p.q_lin, spec_all(length)), (numer, spec_col(length)), (gm, spec_col(length))],
        [((total, 1024), BF, spec_col(length))] + state_outs(),
        [pltpu.VMEM((256, length), BF), pltpu.VMEM((1, length), F32), turned_scratch(length)], deps=deps)

def intra_back_kernel(core, low, high, q, k, v, gn, dv_in, kept, received, dq, dk_t, dv, mask, q_t, k_t, dq_t, early, turned, pulled, *, length, row):
    g = pl.program_id(1)
    half = length // 2
    @pl.when(g == 0)
    def _():
        lows, highs = spread(scalars(low, row, length), length), spread(scalars(high, row, length), length)
        j = lax.broadcasted_iota(jnp.int32, (length, length), 0)
        i = lax.broadcasted_iota(jnp.int32, (length, length), 1)
        mask[...] = ((j >= lows) & (j <= i) & (j < highs)).astype(BF)
        early[...] = (lows < 0).astype(F32)
        turn_all(q[...], q_t, turned, None)
        k_t[...] = k[...].astype(F32).T.astype(BF)
    quarter = FEAT ** -0.5
    qv, kv = q[...] * jnp.bfloat16(quarter), k[...]
    for n, (group, cols) in enumerate(groups()):
        vv, gv = v[:, cols], gn[:, cols]
        st = state_for(row, core, kept, received, n).astype(BF)
        top = dv_in[:half, cols].astype(F32)
        bottom = dv_in[half:, cols].astype(F32)
        km = [kv * lane_mask(HEADS * FEAT, FEAT, group * 4 + h) for h in range(4)]
        vm = [vv * lane_mask(256, 64, h) for h in range(4)]
        u0 = nt(jnp.concatenate([x[:half] for x in km], axis=0), qv)
        u1 = nt(jnp.concatenate([x[half:] for x in km], axis=0), qv[half:])
        ga0 = nt(jnp.concatenate([x[:half] for x in vm], axis=0), gv)
        ga1 = nt(jnp.concatenate([x[half:] for x in vm], axis=0), gv[half:])
        gphi = nt(jnp.concatenate([st * lane_mask(256, 64, h) for h in range(4)], axis=0), gv) * early[...]
        m0, m1 = mask[:half, :], mask[half:, half:]
        for h in range(4):
            at = head_rows(group, h)
            mine = slice(h * half, (h + 1) * half)
            gm = gv * (lane_mask(256, 64, h) * jnp.bfloat16(0.5))
            qb, kb = q_t[at, :] * jnp.bfloat16(quarter), k_t[at, :] * jnp.bfloat16(quarter)
            w0, w1 = 1.0 + u0[mine], 1.0 + u1[mine]
            a0 = (1.0 + w0 * w0).astype(BF) * m0
            a1 = (1.0 + w1 * w1).astype(BF) * m1
            ds0 = (ga0[mine] * w0).astype(BF) * m0
            ds1 = (ga1[mine] * w1).astype(BF) * m1
            top = top + nn(a0, gm)
            bottom = bottom + nn(a1, gm[half:])
            dk_t[0, at, :half] = nt(qb, ds0)
            dk_t[0, at, half:] = nt(qb[:, half:], ds1)
            d = nn(kb[:, :half], ds0)
            d = d + jnp.concatenate([jnp.zeros((FEAT, half), F32), nn(kb[:, half:], ds1)], axis=1)
            dq_t[at, :] = d + features_back_t(q_t, turned, at, gphi[h * ROWS_PHI:(h + 1) * ROWS_PHI], pulled)
        dv[:half, cols] = top.astype(BF)
        dv[half:, cols] = bottom.astype(BF)
    @pl.when(g == pl.num_programs(1) - 1)
    def _():
        dq[...] = (dq_t[...] + turned_back(pulled)).T.astype(BF)

def intra_back(core, low, high, p, gn, dv_in, state, rows, length, row, deps=(), into=None):
    total = rows * length
    return call(functools.partial(intra_back_kernel, length=length, row=row), "intra_back", (1, STEPS),
        [(core, SMEM), (low, SMEM), (high, SMEM), (p.q_lin, spec_all(length, row)), (p.k_lin, spec_all(length, row)), (p.v, spec_col(length, 0, row)),
         (gn, spec_col(length, 0, row)), (dv_in, spec_col(length, 0, row)), (state[0], SPEC_STATE), (state[1], SPEC_STATE)],
        [((total, 256), BF, spec_all(length, row)), ((rows, 256, length), F32, spec_t(length, row)), ((total, 1024), BF, spec_col(length, 0, row))],
        [pltpu.VMEM((length, length), BF)] + [pltpu.VMEM((256, length), BF)] * 2 + [pltpu.VMEM((256, length), F32), pltpu.VMEM((1, length), F32)] + [turned_scratch(length)] * 2,
        flops=HEADS * 2 * 15 * 256 ** 3, deps=deps, into=into)

def state_back_kernel(core, low, high, k, v, dk_in, dv_in, dhv, kept, received, dk, dv, k_t, dk_t, line, turned, pulled, *, length):
    r, g = pl.program_id(0), pl.program_id(1)
    @pl.when(g == 0)
    def _():
        line[...] = owned_line(low, high, r, length)
        turn_all(k[...], k_t, turned, line[...])
    tail = length - WINDOW
    for n, (group, cols) in enumerate(groups()):
        st = state_for(r, core, kept, received, n)
        sb = st.astype(BF)
        vv = v[:, cols]
        total = dv_in[:, cols].astype(F32) + through_state(k_t, turned, st, group, line[...])
        dv[:tail, cols] = total[:tail].astype(BF)
        dv[tail:, cols] = (total[tail:] + dhv[:, cols].astype(F32)).astype(BF)
        gphi = nt(jnp.concatenate([sb * lane_mask(256, 64, h) for h in range(4)], axis=0), vv) * line[...]
        for h in range(4):
            at = head_rows(group, h)
            dk_t[at, :] = dk_in[0, at, :] + features_back_t(k_t, turned, at, gphi[h * ROWS_PHI:(h + 1) * ROWS_PHI], pulled)
    @pl.when(g == pl.num_programs(1) - 1)
    def _():
        dk[...] = (dk_t[...] + turned_back(pulled)).T.astype(BF)

def state_back(core, low, high, p, dk_in, dv_in, returned, state, rows, length, deps=()):
    total = rows * length
    tail = pl.BlockSpec((None, WINDOW, 256 * EACH), lambda r, g: (1, r, g))
    return call(functools.partial(state_back_kernel, length=length), "state_back", (rows, STEPS),
        [(core, SMEM), (low, SMEM), (high, SMEM), (p.k_lin, spec_all(length)), (p.v, spec_col(length)), (dk_in, spec_t(length)), (dv_in, spec_col(length)),
         (returned, tail), (state[0], SPEC_STATE), (state[1], SPEC_STATE)],
        [((total, 256), BF, spec_all(length)), ((total, 1024), BF, spec_col(length))],
        [pltpu.VMEM((256, length), BF), pltpu.VMEM((256, length), F32), pltpu.VMEM((1, length), F32)] + [turned_scratch(length)] * 2, deps=deps)

def tail_kernel(x, got, out):
    out[...] = (x[...].astype(F32) + got[...].astype(F32)).astype(BF)

def tail_added(x, returned, rows, length, deps=()):
    per_row = length // WINDOW
    end = pl.BlockSpec((WINDOW, x.shape[1]), lambda r: ((r + 1) * per_row - 1, 0))
    return call(tail_kernel, "tail", (rows,), [(x, end), (returned, pl.BlockSpec((None, WINDOW, x.shape[1]), lambda r: (0, r, 0)))],
        [(x.shape, BF, end)], flops=10, moved=MIB, alias={0: 0}, deps=deps)[0]


ONE = dict(pipeline_mode=pl.Buffered(1))
def resident(shape):
    return pl.BlockSpec(shape, lambda *s: (0,) * len(shape), **ONE)

class Projected:
    pass

def put_tails(tails, x, rows):
    length = x.shape[0] // rows
    for r in range(rows):
        tails[r * WINDOW:(r + 1) * WINDOW, :] = x[(r + 1) * length - WINDOW:(r + 1) * length, :]

def keys_kernel(tokens, gain, wk, wv, normed, k, v, tails, *, rows):
    @pl.when(pl.program_id(0) == 0)
    def _():
        x = tokens[...].astype(F32)
        normed[...] = (x * lax.rsqrt(jnp.mean(x * x, axis=-1, keepdims=True) + EPSILON) * gain[...]).astype(BF)
        k[...] = nn(normed[...], wk[...]).astype(BF)
    v[...] = nn(normed[...], wv[...]).astype(BF)
    put_tails(tails, v, rows)

def queries_kernel(normed, w, out):
    out[...] = nn(normed[...], w[...]).astype(BF)

def rest_kernel(normed, part, w, tails, out, normed_t, *, rows):
    normed_t[...] = part[...].T
    out[...] = nn(normed[...], w[...]).astype(BF)
    put_tails(tails, out, rows)

def project_keys(p, tokens, gain, w_in, rows):
    toks, width = tokens.shape
    lin = HEADS * FEAT
    first = (w_in.shape[1] - width) // 512
    p.normed, p.k_lin, p.v, p.tails = call(functools.partial(keys_kernel, rows=rows), "project_keys", (width // 512,),
        [(tokens, resident((toks, width))), (gain.reshape(1, width), resident((1, width))), (w_in, pl.BlockSpec((width, lin), lambda s: (0, 1), **ONE)),
         (w_in, pl.BlockSpec((width, 512), lambda s: (0, first + s)))],
        [((toks, width), BF, resident((toks, width))), ((toks, lin), BF, resident((toks, lin))), ((toks, width), BF, pl.BlockSpec((toks, 512), lambda s: (0, s))),
         ((2, rows * WINDOW, width), BF, pl.BlockSpec((None, rows * WINDOW, 512), lambda s: (1, 0, s)))])

def project_queries(p, w_in):
    toks, width = p.normed.shape
    lin = HEADS * FEAT
    p.q_lin, = call(queries_kernel, "project_queries", (1,),
        [(p.normed, resident((toks, width))), (w_in, pl.BlockSpec((width, lin), lambda s: (0, 0), **ONE))],
        [((toks, lin), BF, resident((toks, lin)))])

def project_rest(p, w_in, rows):
    toks, width = p.normed.shape
    lin = HEADS * FEAT
    count = 2 * width // 512
    piece = toks // count
    p.tails, p.qk_win, p.normed_t = call(functools.partial(rest_kernel, rows=rows), "project_rest", (count,),
        [(p.normed, resident((toks, width))), (p.normed, pl.BlockSpec((piece, width), lambda s: (s, 0))),
         (w_in, pl.BlockSpec((width, 512), lambda s: (0, 2 * lin // 512 + s)))],
        [((2, rows * WINDOW, width), BF, pl.BlockSpec((None, rows * WINDOW, 512), lambda s: (0, 0, jnp.maximum(s - count // 2, 0)))),
         ((toks, 2 * width), BF, pl.BlockSpec((toks, 512), lambda s: (0, s))), ((width, toks), BF, pl.BlockSpec((width, piece), lambda s: (0, s)))],
        into=(p.tails,))

def mlp(core, mixed, tokens, cot, w_out, gain, w_gate_up, w_down, count, tile=256, chunk=1024):
    toks, width = mixed.shape
    ff = w_down.shape[0]
    steps = ff // tile
    half = width // 2
    big = resident((toks, width))
    across = pl.BlockSpec((half, tile), lambda s: (0, s))
    down = pl.BlockSpec((tile, half), lambda s: (s, 0))
    return call(functools.partial(mlp_kernel, steps=steps, chunk=chunk, each=width // count), "mlp", (steps,),
        [(core, SMEM), (mixed, big), (tokens, big), (cot, big), (w_out, resident((width, width))), (gain.reshape(1, width), resident((1, width))),
         (w_gate_up, pl.BlockSpec((width, tile), lambda s: (0, s))), (w_gate_up, pl.BlockSpec((width, tile), lambda s: (0, s + steps))),
         (w_down, pl.BlockSpec((tile, width), lambda s: (s, 0)))],
        [((toks, width), BF, big), ((toks, width), F32, big), ((toks, width), BF, big)] + [((half, ff), BF, across)] * 4
        + [((ff, half), BF, down)] * 2 + [((half, width), BF, resident((half, width)))] * 2,
        [pltpu.VMEM((toks, width), F32)] * 3 + [pltpu.VMEM((toks, width), BF), pltpu.VMEM((width, toks), BF), pltpu.VMEM((toks, tile), BF),
         pltpu.VMEM((toks, 2 * tile), BF), pltpu.VMEM((width, 2 * tile), BF)],
        flops=2 * toks * width * (9 * ff + 3 * width), moved=60 * MIB)

def weight_kernel(core, normed_t, *refs, counts, each):
    parts, (keep, send) = refs[:len(counts)], refs[len(counts):]
    step = pl.program_id(0)
    first = core[0] == 0
    begin = 0
    for ref, count in zip(parts, counts):
        @pl.when((step >= begin) & (step < begin + count))
        def _(ref=ref):
            columns = ref.shape[1]
            keep[:, :columns], send[:, :columns] = parted(nn(normed_t[...], ref[...]), first, each)
        begin += count

def weight_grad(core, normed_t, parts, count, name, deps=()):
    width, toks = normed_t.shape
    counts = [max(p.shape[1] // 512, 1) for p in parts]
    begins = [sum(counts[:n]) for n in range(len(counts))]
    def spec(part, begin, size):
        return pl.BlockSpec((toks, min(part.shape[1], 512)), lambda s: (0, jnp.clip(s - begin, 0, size - 1)))
    half = width // 2
    out = ((half, 512 * sum(counts)), BF, pl.BlockSpec((half, 512), lambda s: (0, s)))
    return call(functools.partial(weight_kernel, counts=counts, each=width // count), name, (sum(counts),),
        [(core, SMEM), (normed_t, resident((width, toks)))] + [(p, spec(p, b, n)) for p, b, n in zip(parts, begins, counts)],
        [out, out], deps=deps)

def input_kernel(dq_lin, dk_lin, dq_win, dk_win, dv, w, tokens, gain, resid, out):
    begin, grad = 0, None
    for ref in (dq_lin, dk_lin, dq_win, dk_win, dv):
        size = ref.shape[1]
        term = nt(ref[...], w[:, begin:begin + size])
        grad = term if grad is None else grad + term
        begin += size
    x = tokens[...].astype(F32)
    scale = lax.rsqrt(jnp.mean(x * x, axis=-1, keepdims=True) + EPSILON)
    c = grad * gain[...]
    out[...] = resid[...] + scale * c - x * (scale * scale * scale * jnp.mean(c * x, axis=-1, keepdims=True))

def input_grad(parts, w_in, tokens, gain, resid, part, ways, name, deps=(), into=None):
    toks, width = tokens.shape
    piece = toks // ways
    by_rows = lambda columns: pl.BlockSpec((piece, columns), lambda s: (part, 0), **ONE)
    return call(input_kernel, name, (1,),
        [(p, by_rows(p.shape[1])) for p in parts] + [(w_in, resident(w_in.shape)), (tokens, by_rows(width)), (gain.reshape(1, width), resident((1, width))), (resid, by_rows(width))],
        [((toks, width), F32, by_rows(width))], flops=2 * piece * width * w_in.shape[1], deps=deps, into=into)

def swap(x, bit, count):
    return lax.ppermute(x, "seq", [(i, i ^ (1 << bit)) for i in range(count)])

def over(near, far):
    return near + (1.0 - near[FLAG_ROW:FLAG_ROW + 1, :]) * far

def begun_kernel(core, mine, received, total, *, backward):
    first = core[0] == 0
    for n in range(mine.shape[0]):
        m, r = mine[n], received[n].astype(F32)
        at0, at1 = jnp.where(first, m, r), jnp.where(first, r, m)
        total[n] = (over(at0, at1) if backward else over(at1, at0)).astype(BF)

def joined_kernel(ahead, total, received, new_total):
    here = ahead[0] == 1
    for n in range(total.shape[0]):
        t, r = total[n].astype(F32), received[n].astype(F32)
        new_total[n] = over(jnp.where(here, t, r), jnp.where(here, r, t)).astype(BF)

def ended_kernel(core, ahead, mine, *refs, backward):
    received, (kept, send) = refs[:-2], refs[-2:]
    first = core[0] == 0
    own = first ^ backward
    for n in range(mine.shape[0]):
        m, r = mine[n], received[0][n].astype(F32)
        base = jnp.where(own, m, r)
        e = jnp.zeros_like(m)
        for k, ref in enumerate(received[1:]):
            e = jnp.where(ahead[k] == 1, over(e, ref[n].astype(F32)), e)
        o = over(base, e)
        kept[n] = jnp.where(own, e, o).astype(BF)
        send[n] = jnp.where(own, o, e).astype(BF)

class Scan:
    def __init__(self, mine, send, me, count, backward):
        self.me, self.count, self.backward, self.mine = me, count, backward, mine
        self.received = [swap(send, 0, count)]
        self.bit, self.last = 0, count.bit_length() - 2
        self.core = (me % 2).reshape(1)
        self.ahead = ((me >> jnp.arange(1, self.last + 1, dtype=jnp.int32)) & 1) ^ (1 if backward else 0)
    def _call(self, kernel, name, flags, arrays, outs, through=()):
        shape = self.mine.shape
        whole = pl.BlockSpec(shape, lambda: (0, 0, 0))
        return call(kernel, name, (), [(f, SMEM) for f in flags] + [(a, whole) for a in arrays], [(shape, BF, whole)] * outs, flops=10, moved=MIB, through=through)
    def step(self, through=()):
        if self.bit == 0:
            self.total, *self.through = self._call(functools.partial(begun_kernel, backward=self.backward), "begun", [self.core], [self.mine, self.received[0]], 1, through)
        elif self.bit < self.last:
            self.total, *self.through = self._call(joined_kernel, "joined", [self.ahead[self.bit - 1:self.bit]], [self.total, self.received[-1]], 1, through)
        else:
            self.kept, self.total = self._call(functools.partial(ended_kernel, backward=self.backward), "ended", [self.core, self.ahead], [self.mine] + self.received, 2)
        self.bit += 1
        self.received.append(swap(self.total, self.bit if self.bit <= self.last else 0, self.count))
    def done(self):
        return self.kept, self.received[-1]

def padded(rows):
    return -(-rows // 16) * 16

class Piece:
    def __init__(self, arrays, first=0, size=None, rows=None):
        self.arrays = arrays
        self.first, self.size = first, size or arrays[0].shape[2]
        self.rows = rows or arrays[0].shape[1]
        self.height = self.size // 256 * padded(self.rows)

def add_kernel(*refs, plan, count, scalars):
    refs = refs[scalars:]
    ins, outs = refs[:-count], refs[-count:]
    for target, parts, at, height, rows, columns in plan:
        for k, sources in enumerate(parts):
            total = None
            for s in sources:
                term = ins[s][...].astype(F32)
                total = term if total is None else total + term
            total = total.astype(BF)
            pad = padded(rows)
            for c in range(columns // 256):
                outs[target + k][:, :, at + c * pad:at + c * pad + rows, :] = total[..., c * 256:(c + 1) * 256]

def add_up(groups, ways, name, most=4, deps=()):
    grid = min([most] + [outer for _, outer, _, _ in groups])
    ins, outs, plan = [], [], []
    for n, (pieces, outer, inner, own) in enumerate(groups):
        per = outer // grid
        at = 0
        for piece in pieces:
            parts = []
            for k in range(ways):
                sources = []
                for array in piece.arrays:
                    _, rows, columns = array.shape
                    def index(a, *own_refs, n=n, k=k, block=piece.first // piece.size):
                        return (a, own_refs[n][0] ^ k if ways > 1 else 0, 0, 0, block)
                    sources.append(len(ins))
                    ins.append((array.reshape(outer, ways, inner, rows, columns), pl.BlockSpec((per, None, inner, rows, piece.size), index)))
                parts.append(sources)
            plan.append((n * ways, parts, at, piece.height, piece.rows, piece.size))
            at += piece.height
        outs += [((outer, inner, at, 256), BF, pl.BlockSpec((per, inner, at, 256), lambda a, *own_refs: (a, 0, 0, 0)))] * ways
    got = call(functools.partial(add_kernel, plan=plan, count=len(outs), scalars=len(groups)), name, (grid,), ins, outs, flops=10, moved=20 * MIB,
        scalars=[own.reshape(1) for _, _, _, own in groups], deps=deps)
    got = [x.reshape((-1,) + x.shape[2:]) for x in got]
    return [got[n * ways:(n + 1) * ways] for n in range(len(groups))]

def chips_first(x, chips):
    return x.reshape(chips, x.shape[0] // chips, x.shape[1])

class MlpSum:
    def __init__(self, pairs, me, count):
        self.me, self.count, self.chips = me, count, count // 2
        self.pairs = [(chips_first(k, self.chips), chips_first(swap(s, 0, count), self.chips)) for k, s in pairs]
        self.bit = 0
    def start(self, sends):
        self.a.append(swap(sends[0], 1, self.count))
        self.b.append(swap(sends[1], 2, self.count))
    def step(self, deps=()):
        me, chips = self.me, self.chips
        bits = self.count.bit_length() - 1
        self.bit += 1
        if self.bit == 1:
            g, u, d, o = self.pairs
            half = lambda x, n: Piece(x, n * (x[0].shape[2] // 2), x[0].shape[2] // 2)
            pieces = [Piece(g), half(d, 0), half(o, 0)], [Piece(u), half(d, 1), half(o, 1)]
            self.layout = [(p.rows, p.size) for ps in pieces for p in ps]
            (ka, sa), (kb, sb) = add_up([(pieces[0], chips // 2, 1, (me >> 1) & 1), (pieces[1], chips // 4, 2, (me >> 2) & 1)], 2, "sum_first", deps=deps)
            self.a, self.b, self.sends = [ka], [kb], (sa, sb)
        elif self.bit == 2:
            (ka, sa), (kb, sb) = add_up([([Piece(self.a)], chips // 4, 1, (me >> 2) & 1), ([Piece(self.b)], chips // 4, 1, (me >> 1) & 1)], 2, "sum_second")
            self.a, self.b = [ka, swap(sa, 2, self.count)], [kb, swap(sb, 1, self.count)]
        else:
            pieces = [Piece(self.a), Piece(self.b)] if self.bit == 3 else [Piece(self.all)]
            (k, s), = add_up([(pieces, chips >> self.bit, 1, (me >> self.bit) & 1)], 2, "sum_more")
            self.all = [k, swap(s, self.bit, self.count)]

def quarters(pieces, bit, me, count):
    flip = lambda x, k: lax.ppermute(x, "seq", [(i, i ^ (k << bit)) for i in range(count)])
    parts, = add_up([(pieces, (count // 2) >> (bit + 1), 1, (me >> bit) & 3)], 4, "quarters", 2)
    return [parts[0]] + [flip(parts[k], k) for k in (3, 2, 1)]

class InSum:
    def __init__(self, me, count):
        self.me, self.count, self.chips = me, count, count // 2
        self.bit = 1
    def first(self, keep, send, columns):
        arrays = chips_first(keep, self.chips), chips_first(swap(send, 0, self.count), self.chips)
        return arrays, columns
    def second(self, arrays, columns):
        me, chips = self.me, self.chips
        a, b = ([Piece(arrays, first, size) for first, size in c] for c in columns)
        (ka, sa), (kb, sb) = add_up([(a, chips // 2, 1, (me >> 1) & 1), (b, chips // 4, 2, (me >> 2) & 1)], 2, "in_first")
        return [ka, swap(sa, 1, self.count)], [kb, swap(sb, 2, self.count)]
    def third(self, *parts):
        me, chips = self.me, self.chips
        a, b = ([Piece(p[n]) for p in parts] for n in (0, 1))
        (ka, sa), (kb, sb) = add_up([(a, chips // 4, 1, (me >> 2) & 1), (b, chips // 4, 1, (me >> 1) & 1)], 2, "in_second")
        self.arrays = [Piece([ka, swap(sa, 2, self.count)]), Piece([kb, swap(sb, 1, self.count)])]
        self.bit = 3
    def rest(self):
        while self.bit < self.count.bit_length() - 1:
            got = quarters(self.arrays, self.bit, self.me, self.count)
            self.arrays = [Piece(got)]
            self.bit += 2
        return got

def finish(rows, me, count):
    core = me % 2
    each = rows.shape[0] // 2
    own = lax.dynamic_slice_in_dim(rows, core * each, each, 0)
    got = swap(lax.dynamic_slice_in_dim(rows, (1 - core) * each, each, 0), 0, count)
    return jnp.concatenate([jnp.where(core == 0, own, got), jnp.where(core == 0, got, own)], axis=1)

def gathered_kernel(place, weights, *refs, layout, rows):
    arrays, (out, gain_out) = refs[:-2], refs[-2:]
    total = None
    for n, at in enumerate(layout):
        g = None
        for ref in arrays:
            term = ref[0, at:at + rows, :].astype(F32)
            g = term if g is None else g + term
        out[:, n * 256:(n + 1) * 256] = g
        t = g * weights[:, n * 256:(n + 1) * 256].astype(F32)
        total = t if total is None else total + t
    gain_out[...] = jnp.sum(total, axis=1, keepdims=True)

def gathered(arrays, layout, weights, gain, me, count):
    each, columns = weights.shape[0] // count, weights.shape[1]
    own_gain = lax.dynamic_slice_in_dim(gain, me * each, each, 0)
    if each < 16:
        weights, me = lax.dynamic_slice_in_dim(weights, me * each, each, 0), jnp.zeros((), jnp.int32)
    mine = pl.BlockSpec((each, columns), lambda s, place: (place[0], 0))
    out, gain_out = call(functools.partial(gathered_kernel, layout=layout, rows=each), "gathered", (1,),
        [(weights, mine)] + [(a, resident(a.shape)) for a in arrays],
        [((each, columns), F32, resident((each, columns))), ((each, 1), F32, resident((each, 1)))], scalars=[me.reshape(1)])
    return out, gain_out.reshape(each) / own_gain

def plain_kernel(*refs, pieces, shapes):
    arrays, outs = refs[:-len(shapes)], refs[-len(shapes):]
    for out, first, rows, column in pieces:
        g = None
        for ref in arrays:
            term = ref[0, first:first + rows, :].astype(F32)
            g = term if g is None else g + term
        outs[out][:, column:column + 256] = g

def plain(arrays, pieces, shapes):
    return call(functools.partial(plain_kernel, pieces=pieces, shapes=shapes), "plain", (1,), [(a, resident(a.shape)) for a in arrays],
        [(s, F32, resident(s)) for s in shapes], flops=10, moved=MIB)

def shards(tokens, seq_starts, seq_lengths, gain_in, gain_mlp, w_in, w_out, w_gate_up, w_down, cotangent):
    Order.last = None
    rows, length, width = tokens.shape
    count = lax.axis_size("seq")
    bits = count.bit_length() - 1
    order_a = list(range(1, bits))
    order_b = [2, 1] + list(range(3, bits))
    order_c = [3, 1, 2] + list(range(4, bits))
    me = lax.axis_index("seq")
    core = (me % 2).reshape(1)
    total = rows * length
    begin = me * length
    low = (seq_starts[:, ::WINDOW] - begin).reshape(-1)
    high = low + seq_lengths[:, ::WINDOW].reshape(-1)

    x = tokens.reshape(total, width)
    cot = cotangent.reshape(total, width)
    p = Projected()
    project_keys(p, x, gain_in, w_in, rows)
    scan = Scan(*local_states(core, low, high, p.k_lin, p.v, rows, length), me, count, False)
    project_queries(p, w_in)
    scan.step()
    project_rest(p, w_in, rows)
    forward = [(i, i + 1) for i in range(count - 1)]
    backward = [(i + 1, i) for i in range(count - 1)]
    halo = lax.ppermute(p.tails, "seq", forward)
    scan.step()
    local = intra(low, high, p, rows, length, 0)
    scan.step()
    local, = intra(low, high, p, rows, length, 1, into=local)
    scan.step()
    windowed = window(low, high, p, halo, rows, length, 0)
    windowed, = window(low, high, p, halo, rows, length, 1, into=windowed)
    while scan.bit < bits:
        scan.step()
    state_in = scan.done()
    numer, mixed = mix(core, low, p, state_in, local, windowed, rows, length)

    (result, grad_resid, grad_mixed, keep_g, send_g, keep_u, send_u, keep_d, send_d, keep_o, send_o) = mlp(
        core, mixed, x, cot, w_out, gain_mlp, w_gate_up, w_down, count)
    grad_numer, *grad_state_in = numer_back(core, low, p, numer, grad_mixed, rows, length)
    scan = Scan(*grad_state_in, me, count, True)

    mlp_sum = MlpSum([(keep_g, send_g), (keep_u, send_u), (keep_d, send_d), (keep_o, send_o)], me, count)
    scan.step()
    mlp_sum.step()
    scan.step(through=mlp_sum.sends)
    mlp_sum.start(scan.through)
    back, dh, kept = window_back_first(low, high, p, halo, grad_mixed, rows, length)
    scan.step()
    returned = lax.ppermute(dh, "seq", backward)
    dq_win, dk_win, dv_win = window_back_second(low, high, p, grad_mixed, back, kept, rows, length)
    scan.step()
    inner = intra_back(core, low, high, p, grad_numer, dv_win, state_in, rows, length, 0)
    while scan.bit < bits:
        scan.step()
    inner = intra_back(core, low, high, p, grad_numer, dv_win, state_in, rows, length, 1, into=inner)
    dq_lin, dk_t, dv_part = inner
    mlp_sum.step()
    dk_win = tail_added(dk_win, returned, rows, length, deps=(scan.received[-1],))
    lin = HEADS * FEAT
    in_sum = InSum(me, count)
    early = in_sum.first(*weight_grad(core, p.normed_t, [dq_win, dk_win, dq_lin], count, "weight_grad_early"), (((0, width), (2 * width, lin)), ((width, width),)))
    dk_lin, dv = state_back(core, low, high, p, dk_t, dv_part, returned, scan.done(), rows, length)
    mlp_sum.step()
    late = in_sum.first(*weight_grad(core, p.normed_t, [dv, dk_lin], count, "weight_grad_late"), (((0, width // 2),), ((width // 2, width // 2), (width, lin))))
    parts = [dq_lin, dk_lin, dq_win, dk_win, dv]
    early = in_sum.second(*early)
    grad_tokens = input_grad(parts, w_in, x, gain_in, grad_resid, 0, 2, "input_grad_first")
    late = in_sum.second(*late)
    while mlp_sum.bit < bits - 1:
        mlp_sum.step()
    in_sum.third(early, late)
    grad_tokens, = input_grad(parts, w_in, x, gain_in, grad_resid, 1, 2, "input_grad", into=grad_tokens)
    in_got = in_sum.rest()
    ff, each, chip = w_down.shape[0], width // count, w_down.shape[0] // (count // 2)
    pad = padded(each)
    height = ff // 256 * pad
    second = height + padded(chip) + 2 * pad
    part_gate_up, part_gain_mlp = gathered(mlp_sum.all, [n * pad for n in range(ff // 256)] + [second + n * pad for n in range(ff // 256)],
        w_gate_up, gain_mlp, me, count)
    down, part_out = plain(mlp_sum.all, [(0, height, chip, 0), (0, second + height, chip, 256)]
        + [(1, height + padded(chip) + n * pad + (second - 2 * pad if n >= 2 else 0), each, n * 256) for n in range(4)],
        [(chip, width // 2), (each, width)])
    part_down = finish(down, me, count)
    wide, piece = width // 256, list(range(3 * width // 256 + 2 * lin // 256))
    q_win, q_lin, v_a, k_win, v_b, k_lin = (piece[wide * n // 2 + m:wide * (n + c) // 2 + m + k] for n, m, c, k in
        ((0, 0, 2, 0), (2, 0, 0, 1), (2, 1, 1, 0), (3, 1, 2, 0), (5, 1, 1, 0), (6, 1, 0, 1)))
    part_in, part_gain_in = gathered(in_got, [n * pad for n in q_lin + k_lin + q_win + k_win + v_a + v_b], w_in, gain_in, me, count)
    return (result.reshape(rows, length, width), grad_tokens.reshape(rows, length, width), part_gain_in, part_gain_mlp,
            part_in, part_out, part_gate_up, part_down)

def solution(mesh):
    split = P(None, "seq", None)
    placed = (split, P(None, "seq"), P(None, "seq"), P(), P(), P(), P(), P(), P(), split)
    return jax.shard_map(shards, mesh=mesh, in_specs=placed,
        out_specs=(split, split, P("seq"), P("seq"), P("seq", None), P("seq", None), P("seq", None), P("seq", None)),
        check_vma=False)
```

```python
import functools
import jax
import jax.numpy as jnp
from jax import lax
from jax.experimental import pallas as pl
from jax.experimental.pallas import tpu as pltpu
from jax.sharding import PartitionSpec as P
F32=jnp.float32; BF=jnp.bfloat16
EPSILON=1e-6
MIB=1<<20

def nn(a,b): return lax.dot_general(a,b,(((1,),(0,)),((),())),preferred_element_type=F32)
def nt(a,b): return lax.dot_general(a,b,(((1,),(1,)),((),())),preferred_element_type=F32)
def tn(a,b): return lax.dot_general(a,b,(((0,),(0,)),((),())),preferred_element_type=F32)

def parted(x, first, each):
    x = x.reshape(x.shape[0] // (2 * each), 2, each, x.shape[1])
    a, b = x[:, 0].reshape(-1, x.shape[3]), x[:, 1].reshape(-1, x.shape[3])
    return jnp.where(first, a, b).astype(BF), jnp.where(first, b, a).astype(BF)

def mlp_kernel(core_ref, mixed, tokens, cot, w_out, gain, wg, wu, wd,
               result, grad_resid, grad_mixed, keep_g, send_g, keep_u, send_u, keep_d, send_d, keep_o, send_o,
               resid, acc, dh, hn, hn_t, hid, dgu, wgu, *, steps, chunk, each):
    step = pl.program_id(0)
    toks = mixed.shape[0]
    width = mixed.shape[1]
    count = toks // chunk
    first = core_ref[0] == 0

    def rows(n):
        return pl.ds(pl.multiple_of(n * chunk, chunk), chunk)

    @pl.when(step == 0)
    def _():
        def one(n, carry):
            r = rows(n)
            res = tokens[r, :].astype(F32) + nn(mixed[r, :], w_out[...])
            scale = lax.rsqrt(jnp.mean(res * res, axis=-1, keepdims=True) + EPSILON)
            h = (res * scale * gain[...]).astype(BF)
            resid[r, :] = res
            acc[r, :] = res
            dh[r, :] = jnp.zeros((chunk, width), F32)
            hn[r, :] = h
            return carry
        lax.fori_loop(0, count, one, 0)
        for n in range(count):
            hn_t[:, n * chunk:(n + 1) * chunk] = hn[n * chunk:(n + 1) * chunk, :].T

    tile = wg.shape[1]
    wgu[:, :tile] = wg[...]
    wgu[:, tile:] = wu[...]

    def forward(n, carry):
        r = rows(n)
        h = hn[r, :]
        both = nn(h, wgu[...])
        gate, up = both[:, :tile], both[:, tile:]
        dhid = nt(cot[r, :], wd[...])
        sig = 1.0 / (1.0 + jnp.exp(-gate))
        silu = gate * sig
        hidden = (silu * up).astype(BF)
        d_gate = (dhid * up * (sig + silu * (1.0 - sig))).astype(BF)
        d_up = (dhid * silu).astype(BF)
        hid[r, :] = hidden
        dgu[r, :tile] = d_gate
        dgu[r, tile:] = d_up
        acc[r, :] += nn(hidden, wd[...])
        dh[r, :] += nt(dgu[r, :], wgu[...])
        return carry
    lax.fori_loop(0, count, forward, 0, unroll=2)

    half = width // 2
    grad_d = tn(hid[...], cot[...])
    left, right = grad_d[:, :half].astype(BF), grad_d[:, half:].astype(BF)
    keep_d[...] = jnp.where(first, left, right)
    send_d[...] = jnp.where(first, right, left)

    def weights(n, carry):
        r = rows(n)
        o = pl.ds(pl.multiple_of(n * (chunk // 2), chunk // 2), chunk // 2)
        grad = nn(hn_t[r, :], dgu[...])
        keep_g[o, :], send_g[o, :] = parted(grad[:, :tile], first, each)
        keep_u[o, :], send_u[o, :] = parted(grad[:, tile:], first, each)
        return carry
    lax.fori_loop(0, width // chunk, weights, 0, unroll=2)

    @pl.when(step == steps - 1)
    def _():
        def one(n, carry):
            r = rows(n)
            res = resid[r, :]
            scale = lax.rsqrt(jnp.mean(res * res, axis=-1, keepdims=True) + EPSILON)
            grad = dh[r, :]
            c = grad * gain[...]
            back = cot[r, :].astype(F32) + scale * c - res * (scale * scale * scale * jnp.mean(c * res, axis=-1, keepdims=True))
            result[r, :] = acc[r, :].astype(BF)
            grad_resid[r, :] = back
            b = back.astype(BF)
            hn[r, :] = b
            grad_mixed[r, :] = nt(b, w_out[...]).astype(BF)
            return carry
        lax.fori_loop(0, count, one, 0)
        for n in range(count):
            hn_t[:, n * chunk:(n + 1) * chunk] = mixed[n * chunk:(n + 1) * chunk, :].T
        def outer(n, carry):
            r = rows(n)
            o = pl.ds(pl.multiple_of(n * (chunk // 2), chunk // 2), chunk // 2)
            keep_o[o, :], send_o[o, :] = parted(nn(hn_t[r, :], hn[...]), first, each)
            return carry
        lax.fori_loop(0, width // chunk, outer, 0)


HEADS=16; FEAT=16; WINDOW=64; ROWS_PHI=160; FLAG_ROW=153
VMEM = 64 * MIB
GROUPS = HEADS // 4
EACH = 2
STEPS = GROUPS // EACH

def groups():
    return [(pl.program_id(1) * EACH + s, slice(s * 256, (s + 1) * 256)) for s in range(EACH)]

COST = dict(project_keys=6.8, state=7.4, project_rest=10, begun=2, joined=2.5, ended=3, intra=7.2, window=12, mix=10, mlp=88, numer_back=12,
    window_back=13, intra_back=25, sum_first=10.6, sum_second=6.4, state_back=0.1, weight_grad_early=0.1, weight_grad_late=0.1, input_grad_first=0.1, input_grad=0.1, in_first=3, in_second=3, quarters=3.5, tail=1.8, gathered=0.1, plain=0.1, sum_more=3)

class Order:
    last = None

def call(kernel, name, grid, ins, outs, scratch=(), flops=0, moved=10 * MIB, deps=(), into=None, alias=None, scalars=(), through=()):
    arrays, specs = [a for a, _ in ins], [s for _, s in ins]
    count, ahead = len(arrays), len(scalars)
    into = list(into or ())
    deps = list(deps)
    if Order.last is not None and not any(Order.last is a for a in into + deps + arrays):
        deps.append(Order.last)
    extra = deps + into + list(through)
    aliases = {ahead + count + len(deps) + n: n for n in range(len(into))}
    aliases.update({ahead + i: o for i, o in (alias or {}).items()})
    aliases.update({ahead + count + len(deps) + len(into) + n: len(outs) + n for n in range(len(through))})
    results = len(outs)
    outs = list(outs) + [(a.shape, a.dtype, pl.BlockSpec(memory_space=pl.ANY)) for a in through]
    def body(*refs):
        begin = ahead + count + len(extra)
        kernel(*refs[:ahead + count], *refs[begin:begin + results], *refs[begin + len(outs):])
    out = pl.pallas_call(
        body, grid_spec=pltpu.PrefetchScalarGridSpec(num_scalar_prefetch=ahead, grid=grid,
            in_specs=specs + [pl.BlockSpec(memory_space=pl.ANY)] * len(extra), out_specs=[s for _, _, s in outs], scratch_shapes=list(scratch)),
        out_shape=[jax.ShapeDtypeStruct(shape, dtype) for shape, dtype, _ in outs],
        input_output_aliases=aliases, name=name,
        compiler_params=pltpu.CompilerParams(vmem_limit_bytes=VMEM, dimension_semantics=("arbitrary",) * len(grid)),
        cost_estimate=pl.CostEstimate(flops=int(COST.get(name, 2.0) * 1e9), bytes_accessed=1000, transcendentals=0),
    )(*scalars, *arrays, *extra)
    Order.last = out[0]
    return out

def lane_mask(width, size, which, dtype=BF):
    lanes = lax.broadcasted_iota(jnp.int32, (1, width), 1)
    return ((lanes >> (size.bit_length() - 1)) == which).astype(dtype)

def spread(values, length):
    block = lax.broadcasted_iota(jnp.int32, (1, length), 1) >> 6
    out = jnp.zeros((1, length), jnp.int32)
    for n, value in enumerate(values):
        out = jnp.where(block == n, value, out)
    return out

def scalars(ref, row, length):
    per_row = length // WINDOW
    return [ref[row * per_row + n] for n in range(per_row)]

def early_line(low, row, length):
    return (spread(scalars(low, row, length), length) < 0).astype(F32)

def owned_line(low, high, row, length):
    lows = scalars(low, row, length)
    place = lax.broadcasted_iota(jnp.int32, (1, length), 1)
    same = spread(lows, length) == lows[-1]
    return (same & (place < spread(scalars(high, row, length), length))).astype(F32)

TURNS = FEAT // 2

def turn(d):
    row = lax.broadcasted_iota(jnp.int32, (HEADS * FEAT, HEADS * FEAT), 0)
    entry = lax.broadcasted_iota(jnp.int32, (HEADS * FEAT, HEADS * FEAT), 1)
    return (((row & -FEAT) | ((row + d) & (FEAT - 1))) == entry).astype(BF)

def turned_scratch(length):
    return pltpu.VMEM((TURNS, HEADS * FEAT, length), BF)

def turn_all(x, x_t, turned, line):
    flipped = x.astype(F32).T
    flat = (flipped if line is None else flipped * line).astype(BF)
    x_t[...] = flat
    for d in range(1, TURNS + 1):
        turned[d - 1] = nn(turn(d), flat).astype(BF)

def features_t(x_t, turned, at, line):
    half = FEAT // 2
    x = x_t[at, :]
    parts = [x * x * jnp.bfloat16((2.0 * FEAT) ** -0.5)]
    xs = x * jnp.bfloat16(FEAT ** -0.5)
    for d in range(1, half):
        parts.append(xs * turned[d - 1, at, :])
    parts.append(x * jnp.bfloat16(FEAT ** -0.25))
    row = lax.broadcasted_iota(jnp.int32, x.shape, 0)
    parts.append(jnp.where(row < half, xs * turned[half - 1, at, :], jnp.where(row == half, line, 0.0).astype(BF)))
    return jnp.concatenate(parts, axis=0)

def features_back_t(x_t, turned, at, g, pulled):
    half = FEAT // 2
    x = x_t[at, :]
    total = g[:FEAT] * x.astype(F32) * (2.0 * (2.0 * FEAT) ** -0.5) + g[half * FEAT:(half + 1) * FEAT] * FEAT ** -0.25
    mixed = jnp.zeros(x.shape, F32)
    xs = x * jnp.bfloat16(FEAT ** -0.5)
    row = lax.broadcasted_iota(jnp.int32, x.shape, 0)
    gb = g.astype(BF)
    for d in range(1, half + 1):
        if d < half:
            gd = gb[d * FEAT:(d + 1) * FEAT]
        else:
            gd = jnp.where(row < half, gb[(half + 1) * FEAT:(half + 2) * FEAT], jnp.bfloat16(0))
        mixed = mixed + (gd * turned[d - 1, at, :]).astype(F32)
        pulled[d - 1, at, :] = gd * xs
    return total + mixed * FEAT ** -0.5

def turned_back(pulled):
    total = None
    for d in range(1, TURNS + 1):
        term = nn(turn(-d), pulled[d - 1])
        total = term if total is None else total + term
    return total

def head_rows(group, h):
    return pl.ds(pl.multiple_of(group * 4 * FEAT + h * FEAT, FEAT), FEAT)

def states_of(x_t, turned, y, group, line, flag):
    row = lax.broadcasted_iota(jnp.int32, (ROWS_PHI, 256), 0)
    out = jnp.where(row == FLAG_ROW, flag, 0.0)
    phi = jnp.concatenate([features_t(x_t, turned, head_rows(group, h), line) for h in range(4)], axis=0)
    every = nn(phi, y)
    for h in range(4):
        out = out + every[h * ROWS_PHI:(h + 1) * ROWS_PHI] * lane_mask(256, 64, h, F32)
    return out

def put_state(g, state, core, mine, send):
    r = pl.program_id(0)
    @pl.when(r == core[0])
    def _():
        mine[g] = state
    @pl.when(r != core[0])
    def _():
        send[g] = state.astype(BF)

def state_outs():
    shape = (GROUPS, ROWS_PHI, 256)
    spec = pl.BlockSpec(shape, lambda r, g: (0, 0, 0))
    return [(shape, F32, spec), (shape, BF, spec)]

def state_kernel(core, low, high, k, v, mine, send, k_t, line, turned, *, length):
    r, g = pl.program_id(0), pl.program_id(1)
    @pl.when(g == 0)
    def _():
        line[...] = owned_line(low, high, r, length)
        turn_all(k[...], k_t, turned, line[...])
    flag = (low[(r + 1) * (length // WINDOW) - 1] >= 0).astype(F32)
    for g, at in groups():
        put_state(g, states_of(k_t, turned, v[:, at], g, line[...], flag), core, mine, send)

def spec_col(length, first=0, row=0):
    return pl.BlockSpec((length, 256 * EACH), lambda r, g: (r + row, first // EACH + g))
def spec_all(length, row=0):
    return pl.BlockSpec((length, 256), lambda r, g: (r + row, 0))
SPEC_STATE = pl.BlockSpec((EACH, ROWS_PHI, 256), lambda r, g: (g, 0, 0))
def spec_t(length, row=0):
    return pl.BlockSpec((1, 256, length), lambda r, g: (r + row, 0, 0))
SMEM = pl.BlockSpec(memory_space=pltpu.SMEM)
def local_states(core, low, high, k, v, rows, length):
    return call(functools.partial(state_kernel, length=length), "state", (rows, STEPS),
        [(core, SMEM), (low, SMEM), (high, SMEM), (k, spec_all(length)), (v, spec_col(length))], state_outs(),
        [pltpu.VMEM((256, length), BF), pltpu.VMEM((1, length), F32), turned_scratch(length)])

def intra_kernel(low, high, q, k, v, out, mask, *, length, row):
    g = pl.program_id(1)
    half = length // 2
    @pl.when(g == 0)
    def _():
        lows, highs = scalars(low, row, length), scalars(high, row, length)
        for n in range(length // WINDOW):
            i = lax.broadcasted_iota(jnp.int32, (WINDOW, length), 0) + n * WINDOW
            j = lax.broadcasted_iota(jnp.int32, (WINDOW, length), 1)
            mask[n * WINDOW:(n + 1) * WINDOW, :] = ((j >= lows[n]) & (j <= i) & (j < highs[n])).astype(BF)
    qv, kv = q[...] * jnp.bfloat16(FEAT ** -0.5), k[...]
    for g, at in groups():
        vv = v[:, at] * jnp.bfloat16(0.5)
        top = bottom = None
        for h in range(4):
            km = kv * lane_mask(HEADS * FEAT, FEAT, g * 4 + h)
            vm = vv * lane_mask(256, 64, h)
            u0 = 1.0 + nt(qv[:half], km[:half])
            a0 = (1.0 + u0 * u0).astype(BF) * mask[:half, :half]
            u1 = 1.0 + nt(qv[half:], km)
            a1 = (1.0 + u1 * u1).astype(BF) * mask[half:, :]
            o0, o1 = nn(a0, vm[:half]), nn(a1, vm)
            top = o0 if top is None else top + o0
            bottom = o1 if bottom is None else bottom + o1
        out[:half, at] = top.astype(BF)
        out[half:, at] = bottom.astype(BF)

def intra(low, high, p, rows, length, row, deps=(), into=None):
    return call(functools.partial(intra_kernel, length=length, row=row), "intra", (1, STEPS),
        [(low, SMEM), (high, SMEM), (p.q_lin, spec_all(length, row)), (p.k_lin, spec_all(length, row)), (p.v, spec_col(length, 0, row))],
        [((rows * length, 1024), BF, spec_col(length, 0, row))],
        [pltpu.VMEM((length, length), BF)], flops=HEADS * 2 * 6 * 256 ** 3, deps=deps, into=into)

def stacked(x, scale=1.0):
    return jnp.concatenate([x * (lane_mask(256, 64, h) * jnp.bfloat16(scale)) for h in range(4)], axis=0)

def unstacked(x, scale=1.0):
    total = None
    for h in range(4):
        part = x[h * WINDOW:(h + 1) * WINDOW] * (lane_mask(256, 64, h, F32) * scale)
        total = part if total is None else total + part
    return total

def window_probs(low, high, at, shift, keys, qs):
    s = nt(keys, qs)
    key = lax.broadcasted_iota(jnp.int32, (2 * WINDOW, 4 * WINDOW), 0)
    query = lax.broadcasted_iota(jnp.int32, (2 * WINDOW, 4 * WINDOW), 1) & (WINDOW - 1)
    ok = (key >= jnp.maximum(query, low[at] + shift)) & (key < jnp.minimum(query + (WINDOW + 1), high[at] + shift))
    s = jnp.where(ok, s, -1e30)
    p = jnp.exp(s - jnp.max(s, axis=0, keepdims=True))
    return p * (1.0 / jnp.sum(p, axis=0, keepdims=True))

def window_kernel(low, high, q, k, v, hk, hv, out, ka, va, *, length):
    row = pl.program_id(0)
    per_row = length // WINDOW
    ka[:WINDOW, :] = hk[...]
    ka[WINDOW:, :] = k[...]
    va[:WINDOW, :] = hv[...]
    va[WINDOW:, :] = v[...]
    for g, at in groups():
        for n in range(per_row):
            own, both = slice(n * WINDOW, (n + 1) * WINDOW), slice(n * WINDOW, (n + 2) * WINDOW)
            p = window_probs(low, high, row * per_row + n, (1 - n) * WINDOW, ka[both, at], stacked(q[own, at], 64 ** -0.5))
            out[own, at] = unstacked(tn(p.astype(BF), va[both, at])).astype(BF)

def window_ins(low, high, p, halo, length, row):
    tail = lambda part: pl.BlockSpec((None, WINDOW, 256 * EACH), lambda r, g: (part, r + row, g))
    return [(low, SMEM), (high, SMEM), (p.qk_win, spec_col(length, 0, row)), (p.qk_win, spec_col(length, GROUPS, row)), (p.v, spec_col(length, 0, row)),
            (halo, tail(0)), (halo, tail(1))]

def window(low, high, p, halo, rows, length):
    return call(functools.partial(window_kernel, length=length), "window", (rows, STEPS), window_ins(low, high, p, halo, length, 0),
        [((rows * length, 1024), BF, spec_col(length))], [pltpu.VMEM((length + WINDOW, 256 * EACH), BF)] * 2)

def window_back_block(low, high, row, n, per_row, q, keys, vals, go):
    qs, gs = stacked(q, 64 ** -0.5), stacked(go)
    p = window_probs(low, high, row * per_row + n, (1 - n) * WINDOW, keys, qs)
    gp = nt(vals, gs)
    ds = (p * (gp - jnp.sum(p * gp, axis=0, keepdims=True))).astype(BF)
    return unstacked(tn(ds, keys), 64 ** -0.5).astype(BF), nn(ds, qs), nn(p.astype(BF), gs)

def window_back_first_kernel(low, high, q, k, v, hk, hv, go, q1, k1, v1, hk1, hv1, go1, dq, dk, dv, dh, q_kept, k_kept, v_kept, ka, va, *, length):
    per_row = length // WINDOW
    ka[:WINDOW, :] = hk[...]
    ka[WINDOW:, :] = k[...]
    va[:WINDOW, :] = hv[...]
    va[WINDOW:, :] = v[...]
    for _, at in groups():
        carry_k = carry_v = None
        for n in range(per_row):
            rows = slice(n * WINDOW, (n + 1) * WINDOW)
            both = slice(n * WINDOW, (n + 2) * WINDOW)
            dq[rows, at], dk_n, dv_n = window_back_block(low, high, 0, n, per_row, q[rows, at], ka[both, at], va[both, at], go[rows, at])
            if n == 0:
                dh[0, :WINDOW, at] = dk_n[:WINDOW].astype(BF)
                dh[1, :WINDOW, at] = dv_n[:WINDOW].astype(BF)
            else:
                dk[(n - 1) * WINDOW:n * WINDOW, at] = (carry_k + dk_n[:WINDOW]).astype(BF)
                dv[(n - 1) * WINDOW:n * WINDOW, at] = (carry_v + dv_n[:WINDOW]).astype(BF)
            carry_k, carry_v = dk_n[WINDOW:], dv_n[WINDOW:]
        dk[length - WINDOW:, at] = carry_k.astype(BF)
        dv[length - WINDOW:, at] = carry_v.astype(BF)
        keys = jnp.concatenate([hk1[:, at], k1[:, at]], axis=0)
        vals = jnp.concatenate([hv1[:, at], v1[:, at]], axis=0)
        q_kept[:, at], dk_n, dv_n = window_back_block(low, high, 1, 0, per_row, q1[:, at], keys, vals, go1[:, at])
        dh[0, WINDOW:, at] = dk_n[:WINDOW].astype(BF)
        dh[1, WINDOW:, at] = dv_n[:WINDOW].astype(BF)
        k_kept[:, at] = dk_n[WINDOW:]
        v_kept[:, at] = dv_n[WINDOW:]

def window_back_second_kernel(low, high, q, k, v, go, q_kept, k_kept, v_kept, dq, dk, dv, *, length):
    per_row = length // WINDOW
    dq[:WINDOW, :] = q_kept[...]
    for _, at in groups():
        carry_k, carry_v = k_kept[:, at], v_kept[:, at]
        for n in range(1, per_row):
            rows = slice(n * WINDOW, (n + 1) * WINDOW)
            both = slice((n - 1) * WINDOW, (n + 1) * WINDOW)
            dq[rows, at], dk_n, dv_n = window_back_block(low, high, 1, n, per_row, q[rows, at], k[both, at], v[both, at], go[rows, at])
            dk[(n - 1) * WINDOW:n * WINDOW, at] = (carry_k + dk_n[:WINDOW]).astype(BF)
            dv[(n - 1) * WINDOW:n * WINDOW, at] = (carry_v + dv_n[:WINDOW]).astype(BF)
            carry_k, carry_v = dk_n[WINDOW:], dv_n[WINDOW:]
        dk[length - WINDOW:, at] = carry_k.astype(BF)
        dv[length - WINDOW:, at] = carry_v.astype(BF)

def window_back_outs(total, length, row):
    spec = spec_col(length, 0, row)
    return [((total, 1024), BF, spec)] * 3

def window_back_first(low, high, p, halo, go, rows, length):
    total, per_row = rows * length, length // WINDOW
    block = lambda first=0: pl.BlockSpec((WINDOW, 256 * EACH), lambda r, g: (per_row, first // EACH + g))
    tail = lambda part: pl.BlockSpec((None, WINDOW, 256 * EACH), lambda r, g: (part, 1, g))
    small = spec_col(WINDOW)
    got = call(functools.partial(window_back_first_kernel, length=length), "window_back", (1, STEPS),
        window_ins(low, high, p, halo, length, 0) + [(go, spec_col(length)), (p.qk_win, block()), (p.qk_win, block(GROUPS)), (p.v, block()), (halo, tail(0)), (halo, tail(1)), (go, block())],
        window_back_outs(total, length, 0) + [((2, rows * WINDOW, 1024), BF, pl.BlockSpec((2, rows * WINDOW, 256 * EACH), lambda r, g: (0, 0, g))),
         ((WINDOW, 1024), BF, small), ((WINDOW, 1024), F32, small), ((WINDOW, 1024), F32, small)],
        [pltpu.VMEM((length + WINDOW, 256 * EACH), BF)] * 2)
    return got[:3], got[3], got[4:]

def window_back_second(low, high, p, go, into, kept, rows, length):
    small = spec_col(WINDOW)
    return call(functools.partial(window_back_second_kernel, length=length), "window_back", (1, STEPS),
        [(low, SMEM), (high, SMEM), (p.qk_win, spec_col(length, 0, 1)), (p.qk_win, spec_col(length, GROUPS, 1)), (p.v, spec_col(length, 0, 1)), (go, spec_col(length, 0, 1))]
        + [(k, small) for k in kept], window_back_outs(rows * length, length, 1), into=into)

def piece_mean(x):
    a = lax.broadcasted_iota(jnp.int32, (256, 256), 0) >> 6
    b = lax.broadcasted_iota(jnp.int32, (256, 256), 1) >> 6
    ones = jnp.where(a == b, 1.0 / 64, 0.0).astype(BF)
    high = x.astype(BF)
    return nn(high, ones)

def through_state(x_t, turned, state, group, line):
    state_t = state.T.astype(BF)
    parts = []
    for h in range(4):
        parts.append(nn(state_t[h * 64:(h + 1) * 64], features_t(x_t, turned, head_rows(group, h), line)))
    return jnp.concatenate(parts, axis=0).T

def state_for(row, core, kept, received, n):
    return jnp.where(row == core[0], kept[n].astype(F32), received[n].astype(F32))

def mix_kernel(core, low, q, kept, received, local, windowed, numer, mixed, q_t, line, turned, *, length):
    r, g = pl.program_id(0), pl.program_id(1)
    @pl.when(g == 0)
    def _():
        line[...] = early_line(low, r, length)
        turn_all(q[...], q_t, turned, line[...])
    for n, (group, at) in enumerate(groups()):
        num = local[:, at].astype(F32) + through_state(q_t, turned, state_for(r, core, kept, received, n), group, line[...])
        rho = lax.rsqrt(piece_mean(num * num) + EPSILON)
        numer[:, at] = num.astype(BF)
        mixed[:, at] = (num * rho + windowed[:, at].astype(F32)).astype(BF)

def mix(core, low, p, state, local, windowed, rows, length, deps=()):
    total = rows * length
    return call(functools.partial(mix_kernel, length=length), "mix", (rows, STEPS),
        [(core, SMEM), (low, SMEM), (p.q_lin, spec_all(length)), (state[0], SPEC_STATE), (state[1], SPEC_STATE), (local, spec_col(length)), (windowed, spec_col(length))],
        [((total, 1024), BF, spec_col(length)), ((total, 1024), BF, spec_col(length))],
        [pltpu.VMEM((256, length), BF), pltpu.VMEM((1, length), F32), turned_scratch(length)], deps=deps)

def numer_back_kernel(core, low, q, numer, gm, grad_numer, mine, send, q_t, line, turned, *, length):
    r, g = pl.program_id(0), pl.program_id(1)
    @pl.when(g == 0)
    def _():
        line[...] = early_line(low, r, length)
        turn_all(q[...], q_t, turned, line[...])
    flag = (low[(r + 1) * (length // WINDOW) - 1] >= 0).astype(F32)
    for group, at in groups():
        num = numer[:, at].astype(F32)
        rho = lax.rsqrt(piece_mean(num * num) + EPSILON)
        lin = num * rho
        gl = gm[:, at].astype(F32)
        gn = (rho * (gl - lin * piece_mean(gl * lin))).astype(BF)
        grad_numer[:, at] = gn
        put_state(group, states_of(q_t, turned, gn, group, line[...], flag), core, mine, send)

def numer_back(core, low, p, numer, gm, rows, length, deps=()):
    total = rows * length
    return call(functools.partial(numer_back_kernel, length=length), "numer_back", (rows, STEPS),
        [(core, SMEM), (low, SMEM), (p.q_lin, spec_all(length)), (numer, spec_col(length)), (gm, spec_col(length))],
        [((total, 1024), BF, spec_col(length))] + state_outs(),
        [pltpu.VMEM((256, length), BF), pltpu.VMEM((1, length), F32), turned_scratch(length)], deps=deps)

def intra_back_kernel(core, low, high, q, k, v, gn, dv_in, kept, received, dq, dk_t, dv, mask, q_t, k_t, dq_t, early, turned, pulled, *, length):
    row, g = pl.program_id(0), pl.program_id(1)
    half = length // 2
    @pl.when(g == 0)
    def _():
        lows, highs = spread(scalars(low, row, length), length), spread(scalars(high, row, length), length)
        j = lax.broadcasted_iota(jnp.int32, (length, length), 0)
        i = lax.broadcasted_iota(jnp.int32, (length, length), 1)
        mask[...] = ((j >= lows) & (j <= i) & (j < highs)).astype(BF)
        early[...] = (lows < 0).astype(F32)
        turn_all(q[...], q_t, turned, None)
        k_t[...] = k[...].astype(F32).T.astype(BF)
    quarter = FEAT ** -0.5
    qv, kv = q[...] * jnp.bfloat16(quarter), k[...]
    for n, (group, cols) in enumerate(groups()):
        vv, gv = v[:, cols], gn[:, cols]
        st = state_for(row, core, kept, received, n).astype(BF)
        top = dv_in[:half, cols].astype(F32)
        bottom = dv_in[half:, cols].astype(F32)
        km = [kv * lane_mask(HEADS * FEAT, FEAT, group * 4 + h) for h in range(4)]
        vm = [vv * lane_mask(256, 64, h) for h in range(4)]
        u0 = nt(jnp.concatenate([x[:half] for x in km], axis=0), qv)
        u1 = nt(jnp.concatenate([x[half:] for x in km], axis=0), qv[half:])
        ga0 = nt(jnp.concatenate([x[:half] for x in vm], axis=0), gv)
        ga1 = nt(jnp.concatenate([x[half:] for x in vm], axis=0), gv[half:])
        gphi = nt(jnp.concatenate([st * lane_mask(256, 64, h) for h in range(4)], axis=0), gv) * early[...]
        m0, m1 = mask[:half, :], mask[half:, half:]
        for h in range(4):
            at = head_rows(group, h)
            mine = slice(h * half, (h + 1) * half)
            gm = gv * (lane_mask(256, 64, h) * jnp.bfloat16(0.5))
            qb, kb = q_t[at, :] * jnp.bfloat16(quarter), k_t[at, :] * jnp.bfloat16(quarter)
            w0, w1 = 1.0 + u0[mine], 1.0 + u1[mine]
            a0 = (1.0 + w0 * w0).astype(BF) * m0
            a1 = (1.0 + w1 * w1).astype(BF) * m1
            ds0 = (ga0[mine] * w0).astype(BF) * m0
            ds1 = (ga1[mine] * w1).astype(BF) * m1
            top = top + nn(a0, gm)
            bottom = bottom + nn(a1, gm[half:])
            dk_t[0, at, :half] = nt(qb, ds0)
            dk_t[0, at, half:] = nt(qb[:, half:], ds1)
            d = nn(kb[:, :half], ds0)
            d = d + jnp.concatenate([jnp.zeros((FEAT, half), F32), nn(kb[:, half:], ds1)], axis=1)
            dq_t[at, :] = d + features_back_t(q_t, turned, at, gphi[h * ROWS_PHI:(h + 1) * ROWS_PHI], pulled)
        dv[:half, cols] = top.astype(BF)
        dv[half:, cols] = bottom.astype(BF)
    @pl.when(g == pl.num_programs(1) - 1)
    def _():
        dq[...] = (dq_t[...] + turned_back(pulled)).T.astype(BF)

def intra_back(core, low, high, p, gn, dv_in, state, rows, length):
    total = rows * length
    return call(functools.partial(intra_back_kernel, length=length), "intra_back", (rows, STEPS),
        [(core, SMEM), (low, SMEM), (high, SMEM), (p.q_lin, spec_all(length)), (p.k_lin, spec_all(length)), (p.v, spec_col(length)),
         (gn, spec_col(length)), (dv_in, spec_col(length)), (state[0], SPEC_STATE), (state[1], SPEC_STATE)],
        [((total, 256), BF, spec_all(length)), ((rows, 256, length), F32, spec_t(length)), ((total, 1024), BF, spec_col(length))],
        [pltpu.VMEM((length, length), BF)] + [pltpu.VMEM((256, length), BF)] * 2 + [pltpu.VMEM((256, length), F32), pltpu.VMEM((1, length), F32)] + [turned_scratch(length)] * 2)

def state_back_kernel(core, low, high, k, v, dk_in, dv_in, dhv, kept, received, dk, dv, k_t, dk_t, line, turned, pulled, *, length):
    r, g = pl.program_id(0), pl.program_id(1)
    @pl.when(g == 0)
    def _():
        line[...] = owned_line(low, high, r, length)
        turn_all(k[...], k_t, turned, line[...])
    tail = length - WINDOW
    for n, (group, cols) in enumerate(groups()):
        st = state_for(r, core, kept, received, n)
        sb = st.astype(BF)
        vv = v[:, cols]
        total = dv_in[:, cols].astype(F32) + through_state(k_t, turned, st, group, line[...])
        dv[:tail, cols] = total[:tail].astype(BF)
        dv[tail:, cols] = (total[tail:] + dhv[:, cols].astype(F32)).astype(BF)
        gphi = nt(jnp.concatenate([sb * lane_mask(256, 64, h) for h in range(4)], axis=0), vv) * line[...]
        for h in range(4):
            at = head_rows(group, h)
            dk_t[at, :] = dk_in[0, at, :] + features_back_t(k_t, turned, at, gphi[h * ROWS_PHI:(h + 1) * ROWS_PHI], pulled)
    @pl.when(g == pl.num_programs(1) - 1)
    def _():
        dk[...] = (dk_t[...] + turned_back(pulled)).T.astype(BF)

def state_back(core, low, high, p, dk_in, dv_in, returned, state, rows, length, deps=()):
    total = rows * length
    tail = pl.BlockSpec((None, WINDOW, 256 * EACH), lambda r, g: (1, r, g))
    return call(functools.partial(state_back_kernel, length=length), "state_back", (rows, STEPS),
        [(core, SMEM), (low, SMEM), (high, SMEM), (p.k_lin, spec_all(length)), (p.v, spec_col(length)), (dk_in, spec_t(length)), (dv_in, spec_col(length)),
         (returned, tail), (state[0], SPEC_STATE), (state[1], SPEC_STATE)],
        [((total, 256), BF, spec_all(length)), ((total, 1024), BF, spec_col(length))],
        [pltpu.VMEM((256, length), BF), pltpu.VMEM((256, length), F32), pltpu.VMEM((1, length), F32)] + [turned_scratch(length)] * 2, deps=deps)

def tail_kernel(x, got, out):
    out[...] = (x[...].astype(F32) + got[...].astype(F32)).astype(BF)

def tail_added(x, returned, rows, length, deps=()):
    per_row = length // WINDOW
    end = pl.BlockSpec((WINDOW, x.shape[1]), lambda r: ((r + 1) * per_row - 1, 0))
    return call(tail_kernel, "tail", (rows,), [(x, end), (returned, pl.BlockSpec((None, WINDOW, x.shape[1]), lambda r: (0, r, 0)))],
        [(x.shape, BF, end)], flops=10, moved=MIB, alias={0: 0}, deps=deps)[0]


ONE = dict(pipeline_mode=pl.Buffered(1))
def resident(shape):
    return pl.BlockSpec(shape, lambda *s: (0,) * len(shape), **ONE)

class Projected:
    pass

def put_tails(tails, x, rows):
    length = x.shape[0] // rows
    for r in range(rows):
        tails[r * WINDOW:(r + 1) * WINDOW, :] = x[(r + 1) * length - WINDOW:(r + 1) * length, :]

def keys_kernel(tokens, gain, wk, wv, normed, k, v, tails, *, rows):
    @pl.when(pl.program_id(0) == 0)
    def _():
        x = tokens[...].astype(F32)
        normed[...] = (x * lax.rsqrt(jnp.mean(x * x, axis=-1, keepdims=True) + EPSILON) * gain[...]).astype(BF)
        k[...] = nn(normed[...], wk[...]).astype(BF)
    v[...] = nn(normed[...], wv[...]).astype(BF)
    put_tails(tails, v, rows)

def queries_kernel(normed, w, out):
    out[...] = nn(normed[...], w[...]).astype(BF)

def rest_kernel(normed, part, w, tails, out, normed_t, *, rows):
    normed_t[...] = part[...].T
    out[...] = nn(normed[...], w[...]).astype(BF)
    put_tails(tails, out, rows)

def project_keys(p, tokens, gain, w_in, rows):
    toks, width = tokens.shape
    lin = HEADS * FEAT
    first = (w_in.shape[1] - width) // 512
    p.normed, p.k_lin, p.v, p.tails = call(functools.partial(keys_kernel, rows=rows), "project_keys", (width // 512,),
        [(tokens, resident((toks, width))), (gain.reshape(1, width), resident((1, width))), (w_in, pl.BlockSpec((width, lin), lambda s: (0, 1), **ONE)),
         (w_in, pl.BlockSpec((width, 512), lambda s: (0, first + s)))],
        [((toks, width), BF, resident((toks, width))), ((toks, lin), BF, resident((toks, lin))), ((toks, width), BF, pl.BlockSpec((toks, 512), lambda s: (0, s))),
         ((2, rows * WINDOW, width), BF, pl.BlockSpec((None, rows * WINDOW, 512), lambda s: (1, 0, s)))])

def project_queries(p, w_in):
    toks, width = p.normed.shape
    lin = HEADS * FEAT
    p.q_lin, = call(queries_kernel, "project_queries", (1,),
        [(p.normed, resident((toks, width))), (w_in, pl.BlockSpec((width, lin), lambda s: (0, 0), **ONE))],
        [((toks, lin), BF, resident((toks, lin)))])

def project_rest(p, w_in, rows):
    toks, width = p.normed.shape
    lin = HEADS * FEAT
    count = 2 * width // 512
    piece = toks // count
    p.tails, p.qk_win, p.normed_t = call(functools.partial(rest_kernel, rows=rows), "project_rest", (count,),
        [(p.normed, resident((toks, width))), (p.normed, pl.BlockSpec((piece, width), lambda s: (s, 0))),
         (w_in, pl.BlockSpec((width, 512), lambda s: (0, 2 * lin // 512 + s)))],
        [((2, rows * WINDOW, width), BF, pl.BlockSpec((None, rows * WINDOW, 512), lambda s: (0, 0, jnp.maximum(s - count // 2, 0)))),
         ((toks, 2 * width), BF, pl.BlockSpec((toks, 512), lambda s: (0, s))), ((width, toks), BF, pl.BlockSpec((width, piece), lambda s: (0, s)))],
        into=(p.tails,))

def mlp(core, mixed, tokens, cot, w_out, gain, w_gate_up, w_down, count, tile=256, chunk=1024):
    toks, width = mixed.shape
    ff = w_down.shape[0]
    steps = ff // tile
    half = width // 2
    big = resident((toks, width))
    across = pl.BlockSpec((half, tile), lambda s: (0, s))
    down = pl.BlockSpec((tile, half), lambda s: (s, 0))
    return call(functools.partial(mlp_kernel, steps=steps, chunk=chunk, each=width // count), "mlp", (steps,),
        [(core, SMEM), (mixed, big), (tokens, big), (cot, big), (w_out, resident((width, width))), (gain.reshape(1, width), resident((1, width))),
         (w_gate_up, pl.BlockSpec((width, tile), lambda s: (0, s))), (w_gate_up, pl.BlockSpec((width, tile), lambda s: (0, s + steps))),
         (w_down, pl.BlockSpec((tile, width), lambda s: (s, 0)))],
        [((toks, width), BF, big), ((toks, width), F32, big), ((toks, width), BF, big)] + [((half, ff), BF, across)] * 4
        + [((ff, half), BF, down)] * 2 + [((half, width), BF, resident((half, width)))] * 2,
        [pltpu.VMEM((toks, width), F32)] * 3 + [pltpu.VMEM((toks, width), BF), pltpu.VMEM((width, toks), BF), pltpu.VMEM((toks, tile), BF),
         pltpu.VMEM((toks, 2 * tile), BF), pltpu.VMEM((width, 2 * tile), BF)],
        flops=2 * toks * width * (9 * ff + 3 * width), moved=60 * MIB)

def weight_kernel(core, normed_t, *refs, counts, each):
    parts, (keep, send) = refs[:len(counts)], refs[len(counts):]
    step = pl.program_id(0)
    first = core[0] == 0
    begin = 0
    for ref, count in zip(parts, counts):
        @pl.when((step >= begin) & (step < begin + count))
        def _(ref=ref):
            columns = ref.shape[1]
            keep[:, :columns], send[:, :columns] = parted(nn(normed_t[...], ref[...]), first, each)
        begin += count

def weight_grad(core, normed_t, parts, count, name, deps=()):
    width, toks = normed_t.shape
    counts = [max(p.shape[1] // 512, 1) for p in parts]
    begins = [sum(counts[:n]) for n in range(len(counts))]
    def spec(part, begin, size):
        return pl.BlockSpec((toks, min(part.shape[1], 512)), lambda s: (0, jnp.clip(s - begin, 0, size - 1)))
    half = width // 2
    out = ((half, 512 * sum(counts)), BF, pl.BlockSpec((half, 512), lambda s: (0, s)))
    return call(functools.partial(weight_kernel, counts=counts, each=width // count), name, (sum(counts),),
        [(core, SMEM), (normed_t, resident((width, toks)))] + [(p, spec(p, b, n)) for p, b, n in zip(parts, begins, counts)],
        [out, out], deps=deps)

def input_kernel(dq_lin, dk_lin, dq_win, dk_win, dv, w, tokens, gain, resid, out):
    begin, grad = 0, None
    for ref in (dq_lin, dk_lin, dq_win, dk_win, dv):
        size = ref.shape[1]
        term = nt(ref[...], w[:, begin:begin + size])
        grad = term if grad is None else grad + term
        begin += size
    x = tokens[...].astype(F32)
    scale = lax.rsqrt(jnp.mean(x * x, axis=-1, keepdims=True) + EPSILON)
    c = grad * gain[...]
    out[...] = resid[...] + scale * c - x * (scale * scale * scale * jnp.mean(c * x, axis=-1, keepdims=True))

def input_grad(parts, w_in, tokens, gain, resid, part, ways, name, deps=(), into=None):
    toks, width = tokens.shape
    piece = toks // ways
    by_rows = lambda columns: pl.BlockSpec((piece, columns), lambda s: (part, 0), **ONE)
    return call(input_kernel, name, (1,),
        [(p, by_rows(p.shape[1])) for p in parts] + [(w_in, resident(w_in.shape)), (tokens, by_rows(width)), (gain.reshape(1, width), resident((1, width))), (resid, by_rows(width))],
        [((toks, width), F32, by_rows(width))], flops=2 * piece * width * w_in.shape[1], deps=deps, into=into)

def swap(x, bit, count):
    return lax.ppermute(x, "seq", [(i, i ^ (1 << bit)) for i in range(count)])

def over(near, far):
    return near + (1.0 - near[FLAG_ROW:FLAG_ROW + 1, :]) * far

def begun_kernel(core, mine, received, total, *, backward):
    first = core[0] == 0
    for n in range(mine.shape[0]):
        m, r = mine[n], received[n].astype(F32)
        at0, at1 = jnp.where(first, m, r), jnp.where(first, r, m)
        total[n] = (over(at0, at1) if backward else over(at1, at0)).astype(BF)

def joined_kernel(ahead, total, received, new_total):
    here = ahead[0] == 1
    for n in range(total.shape[0]):
        t, r = total[n].astype(F32), received[n].astype(F32)
        new_total[n] = over(jnp.where(here, t, r), jnp.where(here, r, t)).astype(BF)

def ended_kernel(core, ahead, mine, *refs, backward):
    received, (kept, send) = refs[:-2], refs[-2:]
    first = core[0] == 0
    own = first ^ backward
    for n in range(mine.shape[0]):
        m, r = mine[n], received[0][n].astype(F32)
        base = jnp.where(own, m, r)
        e = jnp.zeros_like(m)
        for k, ref in enumerate(received[1:]):
            e = jnp.where(ahead[k] == 1, over(e, ref[n].astype(F32)), e)
        o = over(base, e)
        kept[n] = jnp.where(own, e, o).astype(BF)
        send[n] = jnp.where(own, o, e).astype(BF)

class Scan:
    def __init__(self, mine, send, me, count, backward):
        self.me, self.count, self.backward, self.mine = me, count, backward, mine
        self.received = [swap(send, 0, count)]
        self.bit, self.last = 0, count.bit_length() - 2
        self.core = (me % 2).reshape(1)
        self.ahead = ((me >> jnp.arange(1, self.last + 1, dtype=jnp.int32)) & 1) ^ (1 if backward else 0)
    def _call(self, kernel, name, flags, arrays, outs, through=()):
        shape = self.mine.shape
        whole = pl.BlockSpec(shape, lambda: (0, 0, 0))
        return call(kernel, name, (), [(f, SMEM) for f in flags] + [(a, whole) for a in arrays], [(shape, BF, whole)] * outs, flops=10, moved=MIB, through=through)
    def step(self, through=()):
        if self.bit == 0:
            self.total, *self.through = self._call(functools.partial(begun_kernel, backward=self.backward), "begun", [self.core], [self.mine, self.received[0]], 1, through)
        elif self.bit < self.last:
            self.total, *self.through = self._call(joined_kernel, "joined", [self.ahead[self.bit - 1:self.bit]], [self.total, self.received[-1]], 1, through)
        else:
            self.kept, self.total = self._call(functools.partial(ended_kernel, backward=self.backward), "ended", [self.core, self.ahead], [self.mine] + self.received, 2)
        self.bit += 1
        self.received.append(swap(self.total, self.bit if self.bit <= self.last else 0, self.count))
    def done(self):
        return self.kept, self.received[-1]

def padded(rows):
    return -(-rows // 16) * 16

class Piece:
    def __init__(self, arrays, first=0, size=None, rows=None):
        self.arrays = arrays
        self.first, self.size = first, size or arrays[0].shape[2]
        self.rows = rows or arrays[0].shape[1]
        self.height = self.size // 256 * padded(self.rows)

def add_kernel(*refs, plan, count, scalars):
    refs = refs[scalars:]
    ins, outs = refs[:-count], refs[-count:]
    for target, parts, at, height, rows, columns in plan:
        for k, sources in enumerate(parts):
            total = None
            for s in sources:
                term = ins[s][...].astype(F32)
                total = term if total is None else total + term
            total = total.astype(BF)
            pad = padded(rows)
            for c in range(columns // 256):
                outs[target + k][:, :, at + c * pad:at + c * pad + rows, :] = total[..., c * 256:(c + 1) * 256]

def add_up(groups, ways, name, most=4, deps=(), through=()):
    grid = min([most] + [outer for _, outer, _, _ in groups])
    ins, outs, plan = [], [], []
    for n, (pieces, outer, inner, own) in enumerate(groups):
        per = outer // grid
        at = 0
        for piece in pieces:
            parts = []
            for k in range(ways):
                sources = []
                for array in piece.arrays:
                    _, rows, columns = array.shape
                    def index(a, *own_refs, n=n, k=k, block=piece.first // piece.size):
                        return (a, own_refs[n][0] ^ k if ways > 1 else 0, 0, 0, block)
                    sources.append(len(ins))
                    ins.append((array.reshape(outer, ways, inner, rows, columns), pl.BlockSpec((per, None, inner, rows, piece.size), index)))
                parts.append(sources)
            plan.append((n * ways, parts, at, piece.height, piece.rows, piece.size))
            at += piece.height
        outs += [((outer, inner, at, 256), BF, pl.BlockSpec((per, inner, at, 256), lambda a, *own_refs: (a, 0, 0, 0)))] * ways
    got = call(functools.partial(add_kernel, plan=plan, count=len(outs), scalars=len(groups)), name, (grid,), ins, outs, flops=10, moved=20 * MIB,
        scalars=[own.reshape(1) for _, _, _, own in groups], deps=deps, through=through)
    sums = [x.reshape((-1,) + x.shape[2:]) for x in got[:len(outs)]]
    return [sums[n * ways:(n + 1) * ways] for n in range(len(groups))] + list(got[len(outs):])

def chips_first(x, chips):
    return x.reshape(chips, x.shape[0] // chips, x.shape[1])

class MlpSum:
    def __init__(self, pairs, me, count):
        self.me, self.count, self.chips = me, count, count // 2
        self.pairs = [(chips_first(k, self.chips), chips_first(swap(s, 0, count), self.chips)) for k, s in pairs]
        self.bit = 0
    def start(self, sends):
        self.a.append(swap(sends[0], 1, self.count))
        self.b.append(swap(sends[1], 2, self.count))
    def step(self, deps=()):
        me, chips = self.me, self.chips
        bits = self.count.bit_length() - 1
        self.bit += 1
        if self.bit == 1:
            g, u, d, o = self.pairs
            half = lambda x, n: Piece(x, n * (x[0].shape[2] // 2), x[0].shape[2] // 2)
            pieces = [Piece(g), half(d, 0), half(o, 0)], [Piece(u), half(d, 1), half(o, 1)]
            self.layout = [(p.rows, p.size) for ps in pieces for p in ps]
            (ka, sa), (kb, sb) = add_up([(pieces[0], chips // 2, 1, (me >> 1) & 1), (pieces[1], chips // 4, 2, (me >> 2) & 1)], 2, "sum_first", deps=deps)
            self.a, self.b, self.sends = [ka], [kb], (sa, sb)
        elif self.bit == 2:
            (ka, sa), (kb, sb) = add_up([([Piece(self.a)], chips // 4, 1, (me >> 2) & 1), ([Piece(self.b)], chips // 4, 1, (me >> 1) & 1)], 2, "sum_second")
            self.a, self.b = [ka, swap(sa, 2, self.count)], [kb, swap(sb, 1, self.count)]
        else:
            pieces = [Piece(self.a), Piece(self.b)] if self.bit == 3 else [Piece(self.all)]
            (k, s), = add_up([(pieces, chips >> self.bit, 1, (me >> self.bit) & 1)], 2, "sum_more")
            self.all = [k, swap(s, self.bit, self.count)]

def quarters(pieces, bit, me, count):
    flip = lambda x, k: lax.ppermute(x, "seq", [(i, i ^ (k << bit)) for i in range(count)])
    parts, = add_up([(pieces, (count // 2) >> (bit + 1), 1, (me >> bit) & 3)], 4, "quarters", 2)
    return [parts[0]] + [flip(parts[k], k) for k in (3, 2, 1)]

class InSum:
    def __init__(self, me, count):
        self.me, self.count, self.chips = me, count, count // 2
        self.bit = 1
    def first(self, keep, send, columns):
        arrays = chips_first(keep, self.chips), chips_first(swap(send, 0, self.count), self.chips)
        return arrays, columns
    def second(self, arrays, columns, through=()):
        me, chips = self.me, self.chips
        a, b = ([Piece(arrays, first, size) for first, size in c] for c in columns)
        (ka, sa), (kb, sb), *self.through = add_up([(a, chips // 2, 1, (me >> 1) & 1), (b, chips // 4, 2, (me >> 2) & 1)], 2, "in_first", through=through)
        return [ka, swap(sa, 1, self.count)], [kb, swap(sb, 2, self.count)]
    def third(self, *parts):
        me, chips = self.me, self.chips
        a, b = ([Piece(p[n]) for p in parts] for n in (0, 1))
        (ka, sa), (kb, sb) = add_up([(a, chips // 4, 1, (me >> 2) & 1), (b, chips // 4, 1, (me >> 1) & 1)], 2, "in_second")
        self.arrays = [Piece([ka, swap(sa, 2, self.count)]), Piece([kb, swap(sb, 1, self.count)])]
        self.bit = 3
    def rest(self):
        while self.bit < self.count.bit_length() - 1:
            got = quarters(self.arrays, self.bit, self.me, self.count)
            self.arrays = [Piece(got)]
            self.bit += 2
        return got

def gathered_kernel(place, weights, *refs, layout, rows):
    arrays, (out, gain_out) = refs[:-2], refs[-2:]
    total = None
    for n, at in enumerate(layout):
        g = None
        for ref in arrays:
            term = ref[0, at:at + rows, :].astype(F32)
            g = term if g is None else g + term
        out[:, n * 256:(n + 1) * 256] = g
        t = g * weights[:, n * 256:(n + 1) * 256].astype(F32)
        total = t if total is None else total + t
    gain_out[...] = jnp.sum(total, axis=1, keepdims=True)

def gathered(arrays, layout, weights, gain, me, count, through=()):
    each, columns = weights.shape[0] // count, weights.shape[1]
    own_gain = lax.dynamic_slice_in_dim(gain, me * each, each, 0)
    if each < 16:
        weights, me = lax.dynamic_slice_in_dim(weights, me * each, each, 0), jnp.zeros((), jnp.int32)
    mine = pl.BlockSpec((each, columns), lambda s, place: (place[0], 0))
    out, gain_out, *through = call(functools.partial(gathered_kernel, layout=layout, rows=each), "gathered", (1,),
        [(weights, mine)] + [(a, resident(a.shape)) for a in arrays],
        [((each, columns), F32, resident((each, columns))), ((each, 1), F32, resident((each, 1)))], scalars=[me.reshape(1)], through=through)
    return (out, gain_out.reshape(each) / own_gain, *through)

def plain_kernel(core, *refs, pieces, shapes):
    arrays, outs = refs[:-len(shapes)], refs[-len(shapes):]
    for out, first, rows, column in pieces:
        g = None
        for ref in arrays:
            term = ref[0, first:first + rows, :].astype(F32)
            g = term if g is None else g + term
        if out == 0:
            mine = core[0] == 0
            top, bottom = g[:rows // 2], g[rows // 2:]
            outs[0][:, column:column + 256] = jnp.where(mine, top, bottom)
            outs[1][:, column:column + 256] = jnp.where(mine, bottom, top)
        else:
            outs[2][:, column:column + 256] = g

def plain(core, arrays, pieces, shapes):
    return call(functools.partial(plain_kernel, pieces=pieces, shapes=shapes), "plain", (1,), [(core, SMEM)] + [(a, resident(a.shape)) for a in arrays],
        [(s, F32, resident(s)) for s in shapes])

def shards(tokens, seq_starts, seq_lengths, gain_in, gain_mlp, w_in, w_out, w_gate_up, w_down, cotangent):
    Order.last = None
    rows, length, width = tokens.shape
    count = lax.axis_size("seq")
    bits = count.bit_length() - 1
    order_a = list(range(1, bits))
    order_b = [2, 1] + list(range(3, bits))
    order_c = [3, 1, 2] + list(range(4, bits))
    me = lax.axis_index("seq")
    core = (me % 2).reshape(1)
    total = rows * length
    begin = me * length
    low = (seq_starts[:, ::WINDOW] - begin).reshape(-1)
    high = low + seq_lengths[:, ::WINDOW].reshape(-1)

    x = tokens.reshape(total, width)
    cot = cotangent.reshape(total, width)
    p = Projected()
    project_keys(p, x, gain_in, w_in, rows)
    scan = Scan(*local_states(core, low, high, p.k_lin, p.v, rows, length), me, count, False)
    project_queries(p, w_in)
    scan.step()
    project_rest(p, w_in, rows)
    forward = [(i, i + 1) for i in range(count - 1)]
    backward = [(i + 1, i) for i in range(count - 1)]
    halo = lax.ppermute(p.tails, "seq", forward)
    scan.step()
    local = intra(low, high, p, rows, length, 0)
    scan.step()
    local, = intra(low, high, p, rows, length, 1, into=local)
    scan.step()
    windowed, = window(low, high, p, halo, rows, length)
    while scan.bit < bits:
        scan.step()
    state_in = scan.done()
    numer, mixed = mix(core, low, p, state_in, local, windowed, rows, length)

    (result, grad_resid, grad_mixed, keep_g, send_g, keep_u, send_u, keep_d, send_d, keep_o, send_o) = mlp(
        core, mixed, x, cot, w_out, gain_mlp, w_gate_up, w_down, count)
    grad_numer, *grad_state_in = numer_back(core, low, p, numer, grad_mixed, rows, length)
    scan = Scan(*grad_state_in, me, count, True)

    mlp_sum = MlpSum([(keep_g, send_g), (keep_u, send_u), (keep_d, send_d), (keep_o, send_o)], me, count)
    scan.step()
    mlp_sum.step()
    scan.step(through=mlp_sum.sends)
    mlp_sum.start(scan.through)
    back, dh, kept = window_back_first(low, high, p, halo, grad_mixed, rows, length)
    scan.step()
    returned = lax.ppermute(dh, "seq", backward)
    dq_win, dk_win, dv_win = window_back_second(low, high, p, grad_mixed, back, kept, rows, length)
    scan.step()
    dq_lin, dk_t, dv_part = intra_back(core, low, high, p, grad_numer, dv_win, state_in, rows, length)
    while scan.bit < bits:
        scan.step()
    mlp_sum.step()
    dk_win = tail_added(dk_win, returned, rows, length, deps=(scan.received[-1],))
    lin = HEADS * FEAT
    in_sum = InSum(me, count)
    early = in_sum.first(*weight_grad(core, p.normed_t, [dq_win, dk_win, dq_lin], count, "weight_grad_early"), (((0, width), (2 * width, lin)), ((width, width),)))
    dk_lin, dv = state_back(core, low, high, p, dk_t, dv_part, returned, scan.done(), rows, length)
    mlp_sum.step()
    late = in_sum.first(*weight_grad(core, p.normed_t, [dv, dk_lin], count, "weight_grad_late"), (((0, width // 2),), ((width // 2, width // 2), (width, lin))))
    parts = [dq_lin, dk_lin, dq_win, dk_win, dv]
    early = in_sum.second(*early)
    grad_tokens = input_grad(parts, w_in, x, gain_in, grad_resid, 0, 2, "input_grad_first")
    late = in_sum.second(*late)
    while mlp_sum.bit < bits - 1:
        mlp_sum.step()
    in_sum.third(early, late)
    grad_tokens, = input_grad(parts, w_in, x, gain_in, grad_resid, 1, 2, "input_grad", into=grad_tokens)
    in_got = in_sum.rest()
    ff, each, chip = w_down.shape[0], width // count, w_down.shape[0] // (count // 2)
    pad = padded(each)
    height = ff // 256 * pad
    second = height + padded(chip) + 2 * pad
    part_gate_up, part_gain_mlp = gathered(mlp_sum.all, [n * pad for n in range(ff // 256)] + [second + n * pad for n in range(ff // 256)],
        w_gate_up, gain_mlp, me, count)
    own_down, send_down, part_out = plain(core, mlp_sum.all, [(0, height, chip, 0), (0, second + height, chip, 256)]
        + [(1, height + padded(chip) + n * pad + (second - 2 * pad if n >= 2 else 0), each, n * 256) for n in range(4)],
        [(chip // 2, width // 2), (chip // 2, width // 2), (each, width)])
    wide, piece = width // 256, list(range(3 * width // 256 + 2 * lin // 256))
    q_win, q_lin, v_a, k_win, v_b, k_lin = (piece[wide * n // 2 + m:wide * (n + c) // 2 + m + k] for n, m, c, k in
        ((0, 0, 2, 0), (2, 0, 0, 1), (2, 1, 1, 0), (3, 1, 2, 0), (5, 1, 1, 0), (6, 1, 0, 1)))
    part_in, part_gain_in, send_down = gathered(in_got, [n * pad for n in q_lin + k_lin + q_win + k_win + v_a + v_b], w_in, gain_in, me, count, through=(send_down,))
    got_down = swap(send_down, 0, count)
    first = me % 2 == 0
    part_down = jnp.concatenate([jnp.where(first, own_down, got_down), jnp.where(first, got_down, own_down)], axis=1)
    return (result.reshape(rows, length, width), grad_tokens.reshape(rows, length, width), part_gain_in, part_gain_mlp,
            part_in, part_out, part_gate_up, part_down)

def solution(mesh):
    split = P(None, "seq", None)
    placed = (split, P(None, "seq"), P(None, "seq"), P(), P(), P(), P(), P(), P(), split)
    return jax.shard_map(shards, mesh=mesh, in_specs=placed,
        out_specs=(split, split, P("seq"), P("seq"), P("seq", None), P("seq", None), P("seq", None), P("seq", None)),
        check_vma=False)
```

```python
import functools
import jax
import jax.numpy as jnp
from jax import lax
from jax.experimental import pallas as pl
from jax.experimental.pallas import tpu as pltpu
from jax.sharding import PartitionSpec as P
F32=jnp.float32; BF=jnp.bfloat16
EPSILON=1e-6
MIB=1<<20

def nn(a,b): return lax.dot_general(a,b,(((1,),(0,)),((),())),preferred_element_type=F32)
def nt(a,b): return lax.dot_general(a,b,(((1,),(1,)),((),())),preferred_element_type=F32)
def tn(a,b): return lax.dot_general(a,b,(((0,),(0,)),((),())),preferred_element_type=F32)

def parted(x, first, each):
    x = x.reshape(x.shape[0] // (2 * each), 2, each, x.shape[1])
    a, b = x[:, 0].reshape(-1, x.shape[3]), x[:, 1].reshape(-1, x.shape[3])
    return jnp.where(first, a, b).astype(BF), jnp.where(first, b, a).astype(BF)

def mlp_kernel(core_ref, mixed, tokens, cot, w_out, gain, wg, wu, wd,
               result, grad_resid, grad_mixed, keep_g, send_g, keep_u, send_u, keep_d, send_d, keep_o, send_o,
               resid, acc, dh, hn, hn_t, hid, dgu, wgu, *, steps, chunk, each):
    step = pl.program_id(0)
    toks = mixed.shape[0]
    width = mixed.shape[1]
    count = toks // chunk
    first = core_ref[0] == 0

    def rows(n):
        return pl.ds(pl.multiple_of(n * chunk, chunk), chunk)

    @pl.when(step == 0)
    def _():
        def one(n, carry):
            r = rows(n)
            res = tokens[r, :].astype(F32) + nn(mixed[r, :], w_out[...])
            scale = lax.rsqrt(jnp.mean(res * res, axis=-1, keepdims=True) + EPSILON)
            h = (res * scale * gain[...]).astype(BF)
            resid[r, :] = res
            acc[r, :] = res
            dh[r, :] = jnp.zeros((chunk, width), F32)
            hn[r, :] = h
            return carry
        lax.fori_loop(0, count, one, 0)
        for n in range(count):
            hn_t[:, n * chunk:(n + 1) * chunk] = hn[n * chunk:(n + 1) * chunk, :].T

    tile = wg.shape[1]
    wgu[:, :tile] = wg[...]
    wgu[:, tile:] = wu[...]

    def forward(n, carry):
        r = rows(n)
        h = hn[r, :]
        both = nn(h, wgu[...])
        gate, up = both[:, :tile], both[:, tile:]
        dhid = nt(cot[r, :], wd[...])
        sig = 1.0 / (1.0 + jnp.exp(-gate))
        silu = gate * sig
        hidden = (silu * up).astype(BF)
        d_gate = (dhid * up * (sig + silu * (1.0 - sig))).astype(BF)
        d_up = (dhid * silu).astype(BF)
        hid[r, :] = hidden
        dgu[r, :tile] = d_gate
        dgu[r, tile:] = d_up
        acc[r, :] += nn(hidden, wd[...])
        dh[r, :] += nt(dgu[r, :], wgu[...])
        return carry
    lax.fori_loop(0, count, forward, 0, unroll=2)

    half = width // 2
    grad_d = tn(hid[...], cot[...])
    left, right = grad_d[:, :half].astype(BF), grad_d[:, half:].astype(BF)
    keep_d[...] = jnp.where(first, left, right)
    send_d[...] = jnp.where(first, right, left)

    def weights(n, carry):
        r = rows(n)
        o = pl.ds(pl.multiple_of(n * (chunk // 2), chunk // 2), chunk // 2)
        grad = nn(hn_t[r, :], dgu[...])
        keep_g[o, :], send_g[o, :] = parted(grad[:, :tile], first, each)
        keep_u[o, :], send_u[o, :] = parted(grad[:, tile:], first, each)
        return carry
    lax.fori_loop(0, width // chunk, weights, 0, unroll=2)

    @pl.when(step == steps - 1)
    def _():
        def one(n, carry):
            r = rows(n)
            res = resid[r, :]
            scale = lax.rsqrt(jnp.mean(res * res, axis=-1, keepdims=True) + EPSILON)
            grad = dh[r, :]
            c = grad * gain[...]
            back = cot[r, :].astype(F32) + scale * c - res * (scale * scale * scale * jnp.mean(c * res, axis=-1, keepdims=True))
            result[r, :] = acc[r, :].astype(BF)
            grad_resid[r, :] = back
            b = back.astype(BF)
            hn[r, :] = b
            grad_mixed[r, :] = nt(b, w_out[...]).astype(BF)
            return carry
        lax.fori_loop(0, count, one, 0)
        for n in range(count):
            hn_t[:, n * chunk:(n + 1) * chunk] = mixed[n * chunk:(n + 1) * chunk, :].T
        def outer(n, carry):
            r = rows(n)
            o = pl.ds(pl.multiple_of(n * (chunk // 2), chunk // 2), chunk // 2)
            keep_o[o, :], send_o[o, :] = parted(nn(hn_t[r, :], hn[...]), first, each)
            return carry
        lax.fori_loop(0, width // chunk, outer, 0)


HEADS=16; FEAT=16; WINDOW=64; ROWS_PHI=160; FLAG_ROW=153
VMEM = 64 * MIB
GROUPS = HEADS // 4
EACH = 2
STEPS = GROUPS // EACH

def groups():
    return [(pl.program_id(1) * EACH + s, slice(s * 256, (s + 1) * 256)) for s in range(EACH)]

COST = dict(project_keys=6.8, state=7.4, project_rest=10, begun=2, joined=2.5, ended=3, intra=7.2, window=12, mix=10, mlp=88, numer_back=12,
    window_back=13, intra_back=25, sum_first=10.6, sum_second=6.4, state_back=0.1, weight_grad_early=0.1, weight_grad_late=0.1, input_grad_first=0.1, input_grad=0.1, in_first=3, in_second=3, quarters=3.5, tail=1.8, gathered=0.1, plain=0.1, sum_more=3)

class Order:
    last = None

def call(kernel, name, grid, ins, outs, scratch=(), flops=0, moved=10 * MIB, deps=(), into=None, alias=None, scalars=(), through=()):
    arrays, specs = [a for a, _ in ins], [s for _, s in ins]
    count, ahead = len(arrays), len(scalars)
    into = list(into or ())
    deps = list(deps)
    if Order.last is not None and not any(Order.last is a for a in into + deps + arrays):
        deps.append(Order.last)
    extra = deps + into + list(through)
    aliases = {ahead + count + len(deps) + n: n for n in range(len(into))}
    aliases.update({ahead + i: o for i, o in (alias or {}).items()})
    aliases.update({ahead + count + len(deps) + len(into) + n: len(outs) + n for n in range(len(through))})
    results = len(outs)
    outs = list(outs) + [(a.shape, a.dtype, pl.BlockSpec(memory_space=pl.ANY)) for a in through]
    def body(*refs):
        begin = ahead + count + len(extra)
        kernel(*refs[:ahead + count], *refs[begin:begin + results], *refs[begin + len(outs):])
    out = pl.pallas_call(
        body, grid_spec=pltpu.PrefetchScalarGridSpec(num_scalar_prefetch=ahead, grid=grid,
            in_specs=specs + [pl.BlockSpec(memory_space=pl.ANY)] * len(extra), out_specs=[s for _, _, s in outs], scratch_shapes=list(scratch)),
        out_shape=[jax.ShapeDtypeStruct(shape, dtype) for shape, dtype, _ in outs],
        input_output_aliases=aliases, name=name,
        compiler_params=pltpu.CompilerParams(vmem_limit_bytes=VMEM, dimension_semantics=("arbitrary",) * len(grid)),
        cost_estimate=pl.CostEstimate(flops=int(COST.get(name, 2.0) * 1e9), bytes_accessed=1000, transcendentals=0),
    )(*scalars, *arrays, *extra)
    Order.last = out[0]
    return out

def lane_mask(width, size, which, dtype=BF):
    lanes = lax.broadcasted_iota(jnp.int32, (1, width), 1)
    return ((lanes >> (size.bit_length() - 1)) == which).astype(dtype)

def spread(values, length):
    block = lax.broadcasted_iota(jnp.int32, (1, length), 1) >> 6
    out = jnp.zeros((1, length), jnp.int32)
    for n, value in enumerate(values):
        out = jnp.where(block == n, value, out)
    return out

def scalars(ref, row, length):
    per_row = length // WINDOW
    return [ref[row * per_row + n] for n in range(per_row)]

def early_line(low, row, length):
    return (spread(scalars(low, row, length), length) < 0).astype(F32)

def owned_line(low, high, row, length):
    lows = scalars(low, row, length)
    place = lax.broadcasted_iota(jnp.int32, (1, length), 1)
    same = spread(lows, length) == lows[-1]
    return (same & (place < spread(scalars(high, row, length), length))).astype(F32)

TURNS = FEAT // 2

def turn(d):
    row = lax.broadcasted_iota(jnp.int32, (HEADS * FEAT, HEADS * FEAT), 0)
    entry = lax.broadcasted_iota(jnp.int32, (HEADS * FEAT, HEADS * FEAT), 1)
    return (((row & -FEAT) | ((row + d) & (FEAT - 1))) == entry).astype(BF)

def turned_scratch(length):
    return pltpu.VMEM((TURNS, HEADS * FEAT, length), BF)

def turn_all(x, x_t, turned, line):
    flipped = x.astype(F32).T
    flat = (flipped if line is None else flipped * line).astype(BF)
    x_t[...] = flat
    for d in range(1, TURNS + 1):
        turned[d - 1] = nn(turn(d), flat).astype(BF)

def features_t(x_t, turned, at, line):
    half = FEAT // 2
    x = x_t[at, :]
    parts = [x * x * jnp.bfloat16((2.0 * FEAT) ** -0.5)]
    xs = x * jnp.bfloat16(FEAT ** -0.5)
    for d in range(1, half):
        parts.append(xs * turned[d - 1, at, :])
    parts.append(x * jnp.bfloat16(FEAT ** -0.25))
    row = lax.broadcasted_iota(jnp.int32, x.shape, 0)
    parts.append(jnp.where(row < half, xs * turned[half - 1, at, :], jnp.where(row == half, line, 0.0).astype(BF)))
    return jnp.concatenate(parts, axis=0)

def features_back_t(x_t, turned, at, g, pulled):
    half = FEAT // 2
    x = x_t[at, :]
    total = g[:FEAT] * x.astype(F32) * (2.0 * (2.0 * FEAT) ** -0.5) + g[half * FEAT:(half + 1) * FEAT] * FEAT ** -0.25
    mixed = jnp.zeros(x.shape, F32)
    xs = x * jnp.bfloat16(FEAT ** -0.5)
    row = lax.broadcasted_iota(jnp.int32, x.shape, 0)
    gb = g.astype(BF)
    for d in range(1, half + 1):
        if d < half:
            gd = gb[d * FEAT:(d + 1) * FEAT]
        else:
            gd = jnp.where(row < half, gb[(half + 1) * FEAT:(half + 2) * FEAT], jnp.bfloat16(0))
        mixed = mixed + (gd * turned[d - 1, at, :]).astype(F32)
        pulled[d - 1, at, :] = gd * xs
    return total + mixed * FEAT ** -0.5

def turned_back(pulled):
    total = None
    for d in range(1, TURNS + 1):
        term = nn(turn(-d), pulled[d - 1])
        total = term if total is None else total + term
    return total

def head_rows(group, h):
    return pl.ds(pl.multiple_of(group * 4 * FEAT + h * FEAT, FEAT), FEAT)

def states_of(x_t, turned, y, group, line, flag):
    row = lax.broadcasted_iota(jnp.int32, (ROWS_PHI, 256), 0)
    out = jnp.where(row == FLAG_ROW, flag, 0.0)
    phi = jnp.concatenate([features_t(x_t, turned, head_rows(group, h), line) for h in range(4)], axis=0)
    every = nn(phi, y)
    for h in range(4):
        out = out + every[h * ROWS_PHI:(h + 1) * ROWS_PHI] * lane_mask(256, 64, h, F32)
    return out

def put_state(g, state, core, mine, send):
    r = pl.program_id(0)
    @pl.when(r == core[0])
    def _():
        mine[g] = state
    @pl.when(r != core[0])
    def _():
        send[g] = state.astype(BF)

def state_outs():
    shape = (GROUPS, ROWS_PHI, 256)
    spec = pl.BlockSpec(shape, lambda r, g: (0, 0, 0))
    return [(shape, F32, spec), (shape, BF, spec)]

def state_kernel(core, low, high, k, v, mine, send, k_t, line, turned, *, length):
    r, g = pl.program_id(0), pl.program_id(1)
    @pl.when(g == 0)
    def _():
        line[...] = owned_line(low, high, r, length)
        turn_all(k[...], k_t, turned, line[...])
    flag = (low[(r + 1) * (length // WINDOW) - 1] >= 0).astype(F32)
    for g, at in groups():
        put_state(g, states_of(k_t, turned, v[:, at], g, line[...], flag), core, mine, send)

def spec_col(length, first=0, row=0):
    return pl.BlockSpec((length, 256 * EACH), lambda r, g: (r + row, first // EACH + g))
def spec_all(length, row=0):
    return pl.BlockSpec((length, 256), lambda r, g: (r + row, 0))
SPEC_STATE = pl.BlockSpec((EACH, ROWS_PHI, 256), lambda r, g: (g, 0, 0))
def spec_t(length, row=0):
    return pl.BlockSpec((1, 256, length), lambda r, g: (r + row, 0, 0))
SMEM = pl.BlockSpec(memory_space=pltpu.SMEM)
def local_states(core, low, high, k, v, rows, length):
    return call(functools.partial(state_kernel, length=length), "state", (rows, STEPS),
        [(core, SMEM), (low, SMEM), (high, SMEM), (k, spec_all(length)), (v, spec_col(length))], state_outs(),
        [pltpu.VMEM((256, length), BF), pltpu.VMEM((1, length), F32), turned_scratch(length)])

def intra_kernel(low, high, q, k, v, out, mask, *, length, row):
    g = pl.program_id(1)
    half = length // 2
    @pl.when(g == 0)
    def _():
        lows, highs = scalars(low, row, length), scalars(high, row, length)
        for n in range(length // WINDOW):
            i = lax.broadcasted_iota(jnp.int32, (WINDOW, length), 0) + n * WINDOW
            j = lax.broadcasted_iota(jnp.int32, (WINDOW, length), 1)
            mask[n * WINDOW:(n + 1) * WINDOW, :] = ((j >= lows[n]) & (j <= i) & (j < highs[n])).astype(BF)
    qv, kv = q[...] * jnp.bfloat16(FEAT ** -0.5), k[...]
    for g, at in groups():
        vv = v[:, at] * jnp.bfloat16(0.5)
        top = bottom = None
        for h in range(4):
            km = kv * lane_mask(HEADS * FEAT, FEAT, g * 4 + h)
            vm = vv * lane_mask(256, 64, h)
            u0 = 1.0 + nt(qv[:half], km[:half])
            a0 = (1.0 + u0 * u0).astype(BF) * mask[:half, :half]
            u1 = 1.0 + nt(qv[half:], km)
            a1 = (1.0 + u1 * u1).astype(BF) * mask[half:, :]
            o0, o1 = nn(a0, vm[:half]), nn(a1, vm)
            top = o0 if top is None else top + o0
            bottom = o1 if bottom is None else bottom + o1
        out[:half, at] = top.astype(BF)
        out[half:, at] = bottom.astype(BF)

def intra(low, high, p, rows, length, row, deps=(), into=None):
    return call(functools.partial(intra_kernel, length=length, row=row), "intra", (1, STEPS),
        [(low, SMEM), (high, SMEM), (p.q_lin, spec_all(length, row)), (p.k_lin, spec_all(length, row)), (p.v, spec_col(length, 0, row))],
        [((rows * length, 1024), BF, spec_col(length, 0, row))],
        [pltpu.VMEM((length, length), BF)], flops=HEADS * 2 * 6 * 256 ** 3, deps=deps, into=into)

def stacked(x, scale=1.0):
    return jnp.concatenate([x * (lane_mask(256, 64, h) * jnp.bfloat16(scale)) for h in range(4)], axis=0)

def unstacked(x, scale=1.0):
    total = None
    for h in range(4):
        part = x[h * WINDOW:(h + 1) * WINDOW] * (lane_mask(256, 64, h, F32) * scale)
        total = part if total is None else total + part
    return total

def window_probs(low, high, at, shift, keys, qs):
    s = nt(keys, qs)
    key = lax.broadcasted_iota(jnp.int32, (2 * WINDOW, 4 * WINDOW), 0)
    query = lax.broadcasted_iota(jnp.int32, (2 * WINDOW, 4 * WINDOW), 1) & (WINDOW - 1)
    ok = (key >= jnp.maximum(query, low[at] + shift)) & (key < jnp.minimum(query + (WINDOW + 1), high[at] + shift))
    s = jnp.where(ok, s, -1e30)
    p = jnp.exp(s - jnp.max(s, axis=0, keepdims=True))
    return p * (1.0 / jnp.sum(p, axis=0, keepdims=True))

def window_kernel(low, high, q, k, v, hk, hv, out, ka, va, *, length):
    row = pl.program_id(0)
    per_row = length // WINDOW
    ka[:WINDOW, :] = hk[...]
    ka[WINDOW:, :] = k[...]
    va[:WINDOW, :] = hv[...]
    va[WINDOW:, :] = v[...]
    for g, at in groups():
        for n in range(per_row):
            own, both = slice(n * WINDOW, (n + 1) * WINDOW), slice(n * WINDOW, (n + 2) * WINDOW)
            p = window_probs(low, high, row * per_row + n, (1 - n) * WINDOW, ka[both, at], stacked(q[own, at], 64 ** -0.5))
            out[own, at] = unstacked(tn(p.astype(BF), va[both, at])).astype(BF)

def window_ins(low, high, p, halo, length, row):
    tail = lambda part: pl.BlockSpec((None, WINDOW, 256 * EACH), lambda r, g: (part, r + row, g))
    return [(low, SMEM), (high, SMEM), (p.qk_win, spec_col(length, 0, row)), (p.qk_win, spec_col(length, GROUPS, row)), (p.v, spec_col(length, 0, row)),
            (halo, tail(0)), (halo, tail(1))]

def window(low, high, p, halo, rows, length):
    return call(functools.partial(window_kernel, length=length), "window", (rows, STEPS), window_ins(low, high, p, halo, length, 0),
        [((rows * length, 1024), BF, spec_col(length))], [pltpu.VMEM((length + WINDOW, 256 * EACH), BF)] * 2)

def window_back_block(low, high, row, n, per_row, q, keys, vals, go):
    qs, gs = stacked(q, 64 ** -0.5), stacked(go)
    p = window_probs(low, high, row * per_row + n, (1 - n) * WINDOW, keys, qs)
    gp = nt(vals, gs)
    ds = (p * (gp - jnp.sum(p * gp, axis=0, keepdims=True))).astype(BF)
    return unstacked(tn(ds, keys), 64 ** -0.5).astype(BF), nn(ds, qs), nn(p.astype(BF), gs)

def window_back_first_kernel(low, high, q, k, v, hk, hv, go, q1, k1, v1, hk1, hv1, go1, dq, dk, dv, dh, q_kept, k_kept, v_kept, ka, va, *, length):
    per_row = length // WINDOW
    ka[:WINDOW, :] = hk[...]
    ka[WINDOW:, :] = k[...]
    va[:WINDOW, :] = hv[...]
    va[WINDOW:, :] = v[...]
    for _, at in groups():
        carry_k = carry_v = None
        for n in range(per_row):
            rows = slice(n * WINDOW, (n + 1) * WINDOW)
            both = slice(n * WINDOW, (n + 2) * WINDOW)
            dq[rows, at], dk_n, dv_n = window_back_block(low, high, 0, n, per_row, q[rows, at], ka[both, at], va[both, at], go[rows, at])
            if n == 0:
                dh[0, :WINDOW, at] = dk_n[:WINDOW].astype(BF)
                dh[1, :WINDOW, at] = dv_n[:WINDOW].astype(BF)
            else:
                dk[(n - 1) * WINDOW:n * WINDOW, at] = (carry_k + dk_n[:WINDOW]).astype(BF)
                dv[(n - 1) * WINDOW:n * WINDOW, at] = (carry_v + dv_n[:WINDOW]).astype(BF)
            carry_k, carry_v = dk_n[WINDOW:], dv_n[WINDOW:]
        dk[length - WINDOW:, at] = carry_k.astype(BF)
        dv[length - WINDOW:, at] = carry_v.astype(BF)
        keys = jnp.concatenate([hk1[:, at], k1[:, at]], axis=0)
        vals = jnp.concatenate([hv1[:, at], v1[:, at]], axis=0)
        q_kept[:, at], dk_n, dv_n = window_back_block(low, high, 1, 0, per_row, q1[:, at], keys, vals, go1[:, at])
        dh[0, WINDOW:, at] = dk_n[:WINDOW].astype(BF)
        dh[1, WINDOW:, at] = dv_n[:WINDOW].astype(BF)
        k_kept[:, at] = dk_n[WINDOW:]
        v_kept[:, at] = dv_n[WINDOW:]

def window_back_second_kernel(low, high, q, k, v, go, q_kept, k_kept, v_kept, dq, dk, dv, *, length):
    per_row = length // WINDOW
    dq[:WINDOW, :] = q_kept[...]
    for _, at in groups():
        carry_k, carry_v = k_kept[:, at], v_kept[:, at]
        for n in range(1, per_row):
            rows = slice(n * WINDOW, (n + 1) * WINDOW)
            both = slice((n - 1) * WINDOW, (n + 1) * WINDOW)
            dq[rows, at], dk_n, dv_n = window_back_block(low, high, 1, n, per_row, q[rows, at], k[both, at], v[both, at], go[rows, at])
            dk[(n - 1) * WINDOW:n * WINDOW, at] = (carry_k + dk_n[:WINDOW]).astype(BF)
            dv[(n - 1) * WINDOW:n * WINDOW, at] = (carry_v + dv_n[:WINDOW]).astype(BF)
            carry_k, carry_v = dk_n[WINDOW:], dv_n[WINDOW:]
        dk[length - WINDOW:, at] = carry_k.astype(BF)
        dv[length - WINDOW:, at] = carry_v.astype(BF)

def window_back_outs(total, length, row):
    spec = spec_col(length, 0, row)
    return [((total, 1024), BF, spec)] * 3

def window_back_first(low, high, p, halo, go, rows, length):
    total, per_row = rows * length, length // WINDOW
    block = lambda first=0: pl.BlockSpec((WINDOW, 256 * EACH), lambda r, g: (per_row, first // EACH + g))
    tail = lambda part: pl.BlockSpec((None, WINDOW, 256 * EACH), lambda r, g: (part, 1, g))
    small = spec_col(WINDOW)
    got = call(functools.partial(window_back_first_kernel, length=length), "window_back", (1, STEPS),
        window_ins(low, high, p, halo, length, 0) + [(go, spec_col(length)), (p.qk_win, block()), (p.qk_win, block(GROUPS)), (p.v, block()), (halo, tail(0)), (halo, tail(1)), (go, block())],
        window_back_outs(total, length, 0) + [((2, rows * WINDOW, 1024), BF, pl.BlockSpec((2, rows * WINDOW, 256 * EACH), lambda r, g: (0, 0, g))),
         ((WINDOW, 1024), BF, small), ((WINDOW, 1024), F32, small), ((WINDOW, 1024), F32, small)],
        [pltpu.VMEM((length + WINDOW, 256 * EACH), BF)] * 2)
    return got[:3], got[3], got[4:]

def window_back_second(low, high, p, go, into, kept, rows, length):
    small = spec_col(WINDOW)
    return call(functools.partial(window_back_second_kernel, length=length), "window_back", (1, STEPS),
        [(low, SMEM), (high, SMEM), (p.qk_win, spec_col(length, 0, 1)), (p.qk_win, spec_col(length, GROUPS, 1)), (p.v, spec_col(length, 0, 1)), (go, spec_col(length, 0, 1))]
        + [(k, small) for k in kept], window_back_outs(rows * length, length, 1), into=into)

def piece_mean(x):
    a = lax.broadcasted_iota(jnp.int32, (256, 256), 0) >> 6
    b = lax.broadcasted_iota(jnp.int32, (256, 256), 1) >> 6
    ones = jnp.where(a == b, 1.0 / 64, 0.0).astype(BF)
    high = x.astype(BF)
    return nn(high, ones)

def through_state(x_t, turned, state, group, line):
    state_t = state.T.astype(BF)
    parts = []
    for h in range(4):
        parts.append(nn(state_t[h * 64:(h + 1) * 64], features_t(x_t, turned, head_rows(group, h), line)))
    return jnp.concatenate(parts, axis=0).T

def state_for(row, core, kept, received, n):
    return jnp.where(row == core[0], kept[n].astype(F32), received[n].astype(F32))

def mix_kernel(core, low, q, kept, received, local, windowed, numer, mixed, q_t, line, turned, *, length):
    r, g = pl.program_id(0), pl.program_id(1)
    @pl.when(g == 0)
    def _():
        line[...] = early_line(low, r, length)
        turn_all(q[...], q_t, turned, line[...])
    for n, (group, at) in enumerate(groups()):
        num = local[:, at].astype(F32) + through_state(q_t, turned, state_for(r, core, kept, received, n), group, line[...])
        rho = lax.rsqrt(piece_mean(num * num) + EPSILON)
        numer[:, at] = num.astype(BF)
        mixed[:, at] = (num * rho + windowed[:, at].astype(F32)).astype(BF)

def mix(core, low, p, state, local, windowed, rows, length, deps=()):
    total = rows * length
    return call(functools.partial(mix_kernel, length=length), "mix", (rows, STEPS),
        [(core, SMEM), (low, SMEM), (p.q_lin, spec_all(length)), (state[0], SPEC_STATE), (state[1], SPEC_STATE), (local, spec_col(length)), (windowed, spec_col(length))],
        [((total, 1024), BF, spec_col(length)), ((total, 1024), BF, spec_col(length))],
        [pltpu.VMEM((256, length), BF), pltpu.VMEM((1, length), F32), turned_scratch(length)], deps=deps)

def numer_back_kernel(core, low, q, numer, gm, grad_numer, mine, send, q_t, line, turned, *, length):
    r, g = pl.program_id(0), pl.program_id(1)
    @pl.when(g == 0)
    def _():
        line[...] = early_line(low, r, length)
        turn_all(q[...], q_t, turned, line[...])
    flag = (low[(r + 1) * (length // WINDOW) - 1] >= 0).astype(F32)
    for group, at in groups():
        num = numer[:, at].astype(F32)
        rho = lax.rsqrt(piece_mean(num * num) + EPSILON)
        lin = num * rho
        gl = gm[:, at].astype(F32)
        gn = (rho * (gl - lin * piece_mean(gl * lin))).astype(BF)
        grad_numer[:, at] = gn
        put_state(group, states_of(q_t, turned, gn, group, line[...], flag), core, mine, send)

def numer_back(core, low, p, numer, gm, rows, length, deps=()):
    total = rows * length
    return call(functools.partial(numer_back_kernel, length=length), "numer_back", (rows, STEPS),
        [(core, SMEM), (low, SMEM), (p.q_lin, spec_all(length)), (numer, spec_col(length)), (gm, spec_col(length))],
        [((total, 1024), BF, spec_col(length))] + state_outs(),
        [pltpu.VMEM((256, length), BF), pltpu.VMEM((1, length), F32), turned_scratch(length)], deps=deps)

def intra_back_kernel(core, low, high, q, k, v, gn, dv_in, kept, received, dq, dk_t, dv, mask, q_t, k_t, dq_t, early, turned, pulled, *, length):
    row, g = pl.program_id(0), pl.program_id(1)
    half = length // 2
    @pl.when(g == 0)
    def _():
        lows, highs = spread(scalars(low, row, length), length), spread(scalars(high, row, length), length)
        j = lax.broadcasted_iota(jnp.int32, (length, length), 0)
        i = lax.broadcasted_iota(jnp.int32, (length, length), 1)
        mask[...] = ((j >= lows) & (j <= i) & (j < highs)).astype(BF)
        early[...] = (lows < 0).astype(F32)
        turn_all(q[...], q_t, turned, None)
        k_t[...] = k[...].astype(F32).T.astype(BF)
    quarter = FEAT ** -0.5
    qv, kv = q[...] * jnp.bfloat16(quarter), k[...]
    for n, (group, cols) in enumerate(groups()):
        vv, gv = v[:, cols], gn[:, cols]
        st = state_for(row, core, kept, received, n).astype(BF)
        top = dv_in[:half, cols].astype(F32)
        bottom = dv_in[half:, cols].astype(F32)
        km = [kv * lane_mask(HEADS * FEAT, FEAT, group * 4 + h) for h in range(4)]
        vm = [vv * lane_mask(256, 64, h) for h in range(4)]
        u0 = nt(jnp.concatenate([x[:half] for x in km], axis=0), qv)
        u1 = nt(jnp.concatenate([x[half:] for x in km], axis=0), qv[half:])
        ga0 = nt(jnp.concatenate([x[:half] for x in vm], axis=0), gv)
        ga1 = nt(jnp.concatenate([x[half:] for x in vm], axis=0), gv[half:])
        gphi = nt(jnp.concatenate([st * lane_mask(256, 64, h) for h in range(4)], axis=0), gv) * early[...]
        m0, m1 = mask[:half, :], mask[half:, half:]
        for h in range(4):
            at = head_rows(group, h)
            mine = slice(h * half, (h + 1) * half)
            gm = gv * (lane_mask(256, 64, h) * jnp.bfloat16(0.5))
            qb, kb = q_t[at, :] * jnp.bfloat16(quarter), k_t[at, :] * jnp.bfloat16(quarter)
            w0, w1 = 1.0 + u0[mine], 1.0 + u1[mine]
            a0 = (1.0 + w0 * w0).astype(BF) * m0
            a1 = (1.0 + w1 * w1).astype(BF) * m1
            ds0 = (ga0[mine] * w0).astype(BF) * m0
            ds1 = (ga1[mine] * w1).astype(BF) * m1
            top = top + nn(a0, gm)
            bottom = bottom + nn(a1, gm[half:])
            dk_t[0, at, :half] = nt(qb, ds0)
            dk_t[0, at, half:] = nt(qb[:, half:], ds1)
            d = nn(kb[:, :half], ds0)
            d = d + jnp.concatenate([jnp.zeros((FEAT, half), F32), nn(kb[:, half:], ds1)], axis=1)
            dq_t[at, :] = d + features_back_t(q_t, turned, at, gphi[h * ROWS_PHI:(h + 1) * ROWS_PHI], pulled)
        dv[:half, cols] = top.astype(BF)
        dv[half:, cols] = bottom.astype(BF)
    @pl.when(g == pl.num_programs(1) - 1)
    def _():
        dq[...] = (dq_t[...] + turned_back(pulled)).T.astype(BF)

def intra_back(core, low, high, p, gn, dv_in, state, rows, length):
    total = rows * length
    return call(functools.partial(intra_back_kernel, length=length), "intra_back", (rows, STEPS),
        [(core, SMEM), (low, SMEM), (high, SMEM), (p.q_lin, spec_all(length)), (p.k_lin, spec_all(length)), (p.v, spec_col(length)),
         (gn, spec_col(length)), (dv_in, spec_col(length)), (state[0], SPEC_STATE), (state[1], SPEC_STATE)],
        [((total, 256), BF, spec_all(length)), ((rows, 256, length), F32, spec_t(length)), ((total, 1024), BF, spec_col(length))],
        [pltpu.VMEM((length, length), BF)] + [pltpu.VMEM((256, length), BF)] * 2 + [pltpu.VMEM((256, length), F32), pltpu.VMEM((1, length), F32)] + [turned_scratch(length)] * 2)

def state_back_kernel(core, low, high, k, v, dk_in, dv_in, dhv, kept, received, dk, dv, k_t, dk_t, line, turned, pulled, *, length):
    r, g = pl.program_id(0), pl.program_id(1)
    @pl.when(g == 0)
    def _():
        line[...] = owned_line(low, high, r, length)
        turn_all(k[...], k_t, turned, line[...])
    tail = length - WINDOW
    for n, (group, cols) in enumerate(groups()):
        st = state_for(r, core, kept, received, n)
        sb = st.astype(BF)
        vv = v[:, cols]
        total = dv_in[:, cols].astype(F32) + through_state(k_t, turned, st, group, line[...])
        dv[:tail, cols] = total[:tail].astype(BF)
        dv[tail:, cols] = (total[tail:] + dhv[:, cols].astype(F32)).astype(BF)
        gphi = nt(jnp.concatenate([sb * lane_mask(256, 64, h) for h in range(4)], axis=0), vv) * line[...]
        for h in range(4):
            at = head_rows(group, h)
            dk_t[at, :] = dk_in[0, at, :] + features_back_t(k_t, turned, at, gphi[h * ROWS_PHI:(h + 1) * ROWS_PHI], pulled)
    @pl.when(g == pl.num_programs(1) - 1)
    def _():
        dk[...] = (dk_t[...] + turned_back(pulled)).T.astype(BF)

def state_back(core, low, high, p, dk_in, dv_in, returned, state, rows, length, deps=()):
    total = rows * length
    tail = pl.BlockSpec((None, WINDOW, 256 * EACH), lambda r, g: (1, r, g))
    return call(functools.partial(state_back_kernel, length=length), "state_back", (rows, STEPS),
        [(core, SMEM), (low, SMEM), (high, SMEM), (p.k_lin, spec_all(length)), (p.v, spec_col(length)), (dk_in, spec_t(length)), (dv_in, spec_col(length)),
         (returned, tail), (state[0], SPEC_STATE), (state[1], SPEC_STATE)],
        [((total, 256), BF, spec_all(length)), ((total, 1024), BF, spec_col(length))],
        [pltpu.VMEM((256, length), BF), pltpu.VMEM((256, length), F32), pltpu.VMEM((1, length), F32)] + [turned_scratch(length)] * 2, deps=deps)

def tail_kernel(x, got, out):
    out[...] = (x[...].astype(F32) + got[...].astype(F32)).astype(BF)

def tail_added(x, returned, rows, length, deps=()):
    per_row = length // WINDOW
    end = pl.BlockSpec((WINDOW, x.shape[1]), lambda r: ((r + 1) * per_row - 1, 0))
    return call(tail_kernel, "tail", (rows,), [(x, end), (returned, pl.BlockSpec((None, WINDOW, x.shape[1]), lambda r: (0, r, 0)))],
        [(x.shape, BF, end)], flops=10, moved=MIB, alias={0: 0}, deps=deps)[0]


ONE = dict(pipeline_mode=pl.Buffered(1))
def resident(shape):
    return pl.BlockSpec(shape, lambda *s: (0,) * len(shape), **ONE)

class Projected:
    pass

def put_tails(tails, x, rows):
    length = x.shape[0] // rows
    for r in range(rows):
        tails[r * WINDOW:(r + 1) * WINDOW, :] = x[(r + 1) * length - WINDOW:(r + 1) * length, :]

def keys_kernel(tokens, gain, wk, wv, normed, k, v, tails, *, rows):
    @pl.when(pl.program_id(0) == 0)
    def _():
        x = tokens[...].astype(F32)
        normed[...] = (x * lax.rsqrt(jnp.mean(x * x, axis=-1, keepdims=True) + EPSILON) * gain[...]).astype(BF)
        k[...] = nn(normed[...], wk[...]).astype(BF)
    v[...] = nn(normed[...], wv[...]).astype(BF)
    put_tails(tails, v, rows)

def queries_kernel(normed, w, out):
    out[...] = nn(normed[...], w[...]).astype(BF)

def rest_kernel(normed, part, w, tails, out, normed_t, *, rows):
    normed_t[...] = part[...].T
    out[...] = nn(normed[...], w[...]).astype(BF)
    put_tails(tails, out, rows)

def project_keys(p, tokens, gain, w_in, rows):
    toks, width = tokens.shape
    lin = HEADS * FEAT
    first = (w_in.shape[1] - width) // 512
    p.normed, p.k_lin, p.v, p.tails = call(functools.partial(keys_kernel, rows=rows), "project_keys", (width // 512,),
        [(tokens, resident((toks, width))), (gain.reshape(1, width), resident((1, width))), (w_in, pl.BlockSpec((width, lin), lambda s: (0, 1), **ONE)),
         (w_in, pl.BlockSpec((width, 512), lambda s: (0, first + s)))],
        [((toks, width), BF, resident((toks, width))), ((toks, lin), BF, resident((toks, lin))), ((toks, width), BF, pl.BlockSpec((toks, 512), lambda s: (0, s))),
         ((2, rows * WINDOW, width), BF, pl.BlockSpec((None, rows * WINDOW, 512), lambda s: (1, 0, s)))])

def project_queries(p, w_in):
    toks, width = p.normed.shape
    lin = HEADS * FEAT
    p.q_lin, = call(queries_kernel, "project_queries", (1,),
        [(p.normed, resident((toks, width))), (w_in, pl.BlockSpec((width, lin), lambda s: (0, 0), **ONE))],
        [((toks, lin), BF, resident((toks, lin)))])

def project_rest(p, w_in, rows):
    toks, width = p.normed.shape
    lin = HEADS * FEAT
    count = 2 * width // 512
    piece = toks // count
    p.tails, p.qk_win, p.normed_t = call(functools.partial(rest_kernel, rows=rows), "project_rest", (count,),
        [(p.normed, resident((toks, width))), (p.normed, pl.BlockSpec((piece, width), lambda s: (s, 0))),
         (w_in, pl.BlockSpec((width, 512), lambda s: (0, 2 * lin // 512 + s)))],
        [((2, rows * WINDOW, width), BF, pl.BlockSpec((None, rows * WINDOW, 512), lambda s: (0, 0, jnp.maximum(s - count // 2, 0)))),
         ((toks, 2 * width), BF, pl.BlockSpec((toks, 512), lambda s: (0, s))), ((width, toks), BF, pl.BlockSpec((width, piece), lambda s: (0, s)))],
        into=(p.tails,))

def mlp(core, mixed, tokens, cot, w_out, gain, w_gate_up, w_down, count, tile=256, chunk=1024):
    toks, width = mixed.shape
    ff = w_down.shape[0]
    steps = ff // tile
    half = width // 2
    big = resident((toks, width))
    across = pl.BlockSpec((half, tile), lambda s: (0, s))
    down = pl.BlockSpec((tile, half), lambda s: (s, 0))
    return call(functools.partial(mlp_kernel, steps=steps, chunk=chunk, each=width // count), "mlp", (steps,),
        [(core, SMEM), (mixed, big), (tokens, big), (cot, big), (w_out, resident((width, width))), (gain.reshape(1, width), resident((1, width))),
         (w_gate_up, pl.BlockSpec((width, tile), lambda s: (0, s))), (w_gate_up, pl.BlockSpec((width, tile), lambda s: (0, s + steps))),
         (w_down, pl.BlockSpec((tile, width), lambda s: (s, 0)))],
        [((toks, width), BF, big), ((toks, width), F32, big), ((toks, width), BF, big)] + [((half, ff), BF, across)] * 4
        + [((ff, half), BF, down)] * 2 + [((half, width), BF, resident((half, width)))] * 2,
        [pltpu.VMEM((toks, width), F32)] * 3 + [pltpu.VMEM((toks, width), BF), pltpu.VMEM((width, toks), BF), pltpu.VMEM((toks, tile), BF),
         pltpu.VMEM((toks, 2 * tile), BF), pltpu.VMEM((width, 2 * tile), BF)],
        flops=2 * toks * width * (9 * ff + 3 * width), moved=60 * MIB)

def weight_kernel(core, normed_t, *refs, counts, each):
    parts, (keep, send) = refs[:len(counts)], refs[len(counts):]
    step = pl.program_id(0)
    first = core[0] == 0
    begin = 0
    for ref, count in zip(parts, counts):
        @pl.when((step >= begin) & (step < begin + count))
        def _(ref=ref):
            columns = ref.shape[1]
            keep[:, :columns], send[:, :columns] = parted(nn(normed_t[...], ref[...]), first, each)
        begin += count

def weight_grad(core, normed_t, parts, count, name, deps=()):
    width, toks = normed_t.shape
    counts = [max(p.shape[1] // 512, 1) for p in parts]
    begins = [sum(counts[:n]) for n in range(len(counts))]
    def spec(part, begin, size):
        return pl.BlockSpec((toks, min(part.shape[1], 512)), lambda s: (0, jnp.clip(s - begin, 0, size - 1)))
    half = width // 2
    out = ((half, 512 * sum(counts)), BF, pl.BlockSpec((half, 512), lambda s: (0, s)))
    return call(functools.partial(weight_kernel, counts=counts, each=width // count), name, (sum(counts),),
        [(core, SMEM), (normed_t, resident((width, toks)))] + [(p, spec(p, b, n)) for p, b, n in zip(parts, begins, counts)],
        [out, out], deps=deps)

def input_kernel(dq_lin, dk_lin, dq_win, dk_win, dv, w, tokens, gain, resid, out):
    begin, grad = 0, None
    for ref in (dq_lin, dk_lin, dq_win, dk_win, dv):
        size = ref.shape[1]
        term = nt(ref[...], w[:, begin:begin + size])
        grad = term if grad is None else grad + term
        begin += size
    x = tokens[...].astype(F32)
    scale = lax.rsqrt(jnp.mean(x * x, axis=-1, keepdims=True) + EPSILON)
    c = grad * gain[...]
    out[...] = resid[...] + scale * c - x * (scale * scale * scale * jnp.mean(c * x, axis=-1, keepdims=True))

def input_grad(parts, w_in, tokens, gain, resid, piece=512):
    toks, width = tokens.shape
    by_rows = lambda columns: pl.BlockSpec((piece, columns), lambda s: (s, 0))
    return call(input_kernel, "input_grad", (toks // piece,),
        [(p, by_rows(p.shape[1])) for p in parts] + [(w_in, resident(w_in.shape)), (tokens, by_rows(width)), (gain.reshape(1, width), resident((1, width))), (resid, by_rows(width))],
        [((toks, width), F32, by_rows(width))])[0]

def swap(x, bit, count):
    return lax.ppermute(x, "seq", [(i, i ^ (1 << bit)) for i in range(count)])

def over(near, far):
    return near + (1.0 - near[FLAG_ROW:FLAG_ROW + 1, :]) * far

def begun_kernel(core, mine, received, total, *, backward):
    first = core[0] == 0
    for n in range(mine.shape[0]):
        m, r = mine[n], received[n].astype(F32)
        at0, at1 = jnp.where(first, m, r), jnp.where(first, r, m)
        total[n] = (over(at0, at1) if backward else over(at1, at0)).astype(BF)

def joined_kernel(ahead, total, received, new_total):
    here = ahead[0] == 1
    for n in range(total.shape[0]):
        t, r = total[n].astype(F32), received[n].astype(F32)
        new_total[n] = over(jnp.where(here, t, r), jnp.where(here, r, t)).astype(BF)

def ended_kernel(core, ahead, mine, *refs, backward):
    received, (kept, send) = refs[:-2], refs[-2:]
    first = core[0] == 0
    own = first ^ backward
    for n in range(mine.shape[0]):
        m, r = mine[n], received[0][n].astype(F32)
        base = jnp.where(own, m, r)
        e = jnp.zeros_like(m)
        for k, ref in enumerate(received[1:]):
            e = jnp.where(ahead[k] == 1, over(e, ref[n].astype(F32)), e)
        o = over(base, e)
        kept[n] = jnp.where(own, e, o).astype(BF)
        send[n] = jnp.where(own, o, e).astype(BF)

class Scan:
    def __init__(self, mine, send, me, count, backward):
        self.me, self.count, self.backward, self.mine = me, count, backward, mine
        self.received = [swap(send, 0, count)]
        self.bit, self.last = 0, count.bit_length() - 2
        self.core = (me % 2).reshape(1)
        self.ahead = ((me >> jnp.arange(1, self.last + 1, dtype=jnp.int32)) & 1) ^ (1 if backward else 0)
    def _call(self, kernel, name, flags, arrays, outs, through=()):
        shape = self.mine.shape
        whole = pl.BlockSpec(shape, lambda: (0, 0, 0))
        return call(kernel, name, (), [(f, SMEM) for f in flags] + [(a, whole) for a in arrays], [(shape, BF, whole)] * outs, flops=10, moved=MIB, through=through)
    def step(self, through=()):
        if self.bit == 0:
            self.total, *self.through = self._call(functools.partial(begun_kernel, backward=self.backward), "begun", [self.core], [self.mine, self.received[0]], 1, through)
        elif self.bit < self.last:
            self.total, *self.through = self._call(joined_kernel, "joined", [self.ahead[self.bit - 1:self.bit]], [self.total, self.received[-1]], 1, through)
        else:
            self.kept, self.total = self._call(functools.partial(ended_kernel, backward=self.backward), "ended", [self.core, self.ahead], [self.mine] + self.received, 2)
        self.bit += 1
        self.received.append(swap(self.total, self.bit if self.bit <= self.last else 0, self.count))
    def done(self):
        return self.kept, self.received[-1]

def padded(rows):
    return -(-rows // 16) * 16

class Piece:
    def __init__(self, arrays, first=0, size=None, rows=None):
        self.arrays = arrays
        self.first, self.size = first, size or arrays[0].shape[2]
        self.rows = rows or arrays[0].shape[1]
        self.height = self.size // 256 * padded(self.rows)

def add_kernel(*refs, plan, count, scalars):
    refs = refs[scalars:]
    ins, outs = refs[:-count], refs[-count:]
    for target, parts, at, height, rows, columns in plan:
        for k, sources in enumerate(parts):
            total = None
            for s in sources:
                term = ins[s][...].astype(F32)
                total = term if total is None else total + term
            total = total.astype(BF)
            pad = padded(rows)
            for c in range(columns // 256):
                outs[target + k][:, :, at + c * pad:at + c * pad + rows, :] = total[..., c * 256:(c + 1) * 256]

def add_up(groups, ways, name, most=4, deps=(), through=()):
    grid = min([most] + [outer for _, outer, _, _ in groups])
    ins, outs, plan = [], [], []
    for n, (pieces, outer, inner, own) in enumerate(groups):
        per = outer // grid
        at = 0
        for piece in pieces:
            parts = []
            for k in range(ways):
                sources = []
                for array in piece.arrays:
                    _, rows, columns = array.shape
                    def index(a, *own_refs, n=n, k=k, block=piece.first // piece.size):
                        return (a, own_refs[n][0] ^ k if ways > 1 else 0, 0, 0, block)
                    sources.append(len(ins))
                    ins.append((array.reshape(outer, ways, inner, rows, columns), pl.BlockSpec((per, None, inner, rows, piece.size), index)))
                parts.append(sources)
            plan.append((n * ways, parts, at, piece.height, piece.rows, piece.size))
            at += piece.height
        outs += [((outer, inner, at, 256), BF, pl.BlockSpec((per, inner, at, 256), lambda a, *own_refs: (a, 0, 0, 0)))] * ways
    got = call(functools.partial(add_kernel, plan=plan, count=len(outs), scalars=len(groups)), name, (grid,), ins, outs, flops=10, moved=20 * MIB,
        scalars=[own.reshape(1) for _, _, _, own in groups], deps=deps, through=through)
    sums = [x.reshape((-1,) + x.shape[2:]) for x in got[:len(outs)]]
    return [sums[n * ways:(n + 1) * ways] for n in range(len(groups))] + list(got[len(outs):])

def chips_first(x, chips):
    return x.reshape(chips, x.shape[0] // chips, x.shape[1])

class MlpSum:
    def __init__(self, pairs, me, count):
        self.me, self.count, self.chips = me, count, count // 2
        self.pairs = [(chips_first(k, self.chips), chips_first(swap(s, 0, count), self.chips)) for k, s in pairs]
        self.bit = 0
    def start(self, sends):
        self.a.append(swap(sends[0], 1, self.count))
        self.b.append(swap(sends[1], 2, self.count))
    def step(self, deps=()):
        me, chips = self.me, self.chips
        bits = self.count.bit_length() - 1
        self.bit += 1
        if self.bit == 1:
            g, u, d, o = self.pairs
            half = lambda x, n: Piece(x, n * (x[0].shape[2] // 2), x[0].shape[2] // 2)
            pieces = [Piece(g), half(d, 0), half(o, 0)], [Piece(u), half(d, 1), half(o, 1)]
            self.layout = [(p.rows, p.size) for ps in pieces for p in ps]
            (ka, sa), (kb, sb) = add_up([(pieces[0], chips // 2, 1, (me >> 1) & 1), (pieces[1], chips // 4, 2, (me >> 2) & 1)], 2, "sum_first", deps=deps)
            self.a, self.b, self.sends = [ka], [kb], (sa, sb)
        elif self.bit == 2:
            (ka, sa), (kb, sb) = add_up([([Piece(self.a)], chips // 4, 1, (me >> 2) & 1), ([Piece(self.b)], chips // 4, 1, (me >> 1) & 1)], 2, "sum_second")
            self.a, self.b = [ka, swap(sa, 2, self.count)], [kb, swap(sb, 1, self.count)]
        else:
            got, = add_up([self.group()], 2, "sum_more")
            self.send(got)
    def group(self):
        pieces = [Piece(self.a), Piece(self.b)] if self.bit == 3 else [Piece(self.all)]
        return pieces, self.chips >> self.bit, 1, (self.me >> self.bit) & 1
    def send(self, got):
        self.all = [got[0], swap(got[1], self.bit, self.count)]

def quarters(pieces, bit, me, count):
    flip = lambda x, k: lax.ppermute(x, "seq", [(i, i ^ (k << bit)) for i in range(count)])
    parts, = add_up([(pieces, (count // 2) >> (bit + 1), 1, (me >> bit) & 3)], 4, "quarters", 2)
    return [parts[0]] + [flip(parts[k], k) for k in (3, 2, 1)]

class InSum:
    def __init__(self, me, count):
        self.me, self.count, self.chips = me, count, count // 2
        self.bit = 1
    def first(self, keep, send, columns):
        arrays = chips_first(keep, self.chips), chips_first(swap(send, 0, self.count), self.chips)
        return arrays, columns
    def second(self, arrays, columns, through=()):
        me, chips = self.me, self.chips
        a, b = ([Piece(arrays, first, size) for first, size in c] for c in columns)
        (ka, sa), (kb, sb), *self.through = add_up([(a, chips // 2, 1, (me >> 1) & 1), (b, chips // 4, 2, (me >> 2) & 1)], 2, "in_first", through=through)
        return [ka, swap(sa, 1, self.count)], [kb, swap(sb, 2, self.count)]
    def third(self, mlp_sum, *parts):
        me, chips = self.me, self.chips
        a, b = ([Piece(p[n]) for p in parts] for n in (0, 1))
        mlp_sum.bit += 1
        (ka, sa), (kb, sb), got = add_up([(a, chips // 4, 1, (me >> 2) & 1), (b, chips // 4, 1, (me >> 1) & 1), mlp_sum.group()], 2, "in_second")
        mlp_sum.send(got)
        self.arrays = [Piece([ka, swap(sa, 2, self.count)]), Piece([kb, swap(sb, 1, self.count)])]
        self.bit = 3
    def rest(self):
        while self.bit < self.count.bit_length() - 1:
            got = quarters(self.arrays, self.bit, self.me, self.count)
            self.arrays = [Piece(got)]
            self.bit += 2
        return got

def gathered_kernel(place, weights, *refs, layout, rows):
    arrays, (out, gain_out) = refs[:-2], refs[-2:]
    total = None
    for n, at in enumerate(layout):
        g = None
        for ref in arrays:
            term = ref[0, at:at + rows, :].astype(F32)
            g = term if g is None else g + term
        out[:, n * 256:(n + 1) * 256] = g
        t = g * weights[:, n * 256:(n + 1) * 256].astype(F32)
        total = t if total is None else total + t
    gain_out[...] = jnp.sum(total, axis=1, keepdims=True)

def gathered(arrays, layout, weights, gain, me, count, through=()):
    each, columns = weights.shape[0] // count, weights.shape[1]
    own_gain = lax.dynamic_slice_in_dim(gain, me * each, each, 0)
    if each < 16:
        weights, me = lax.dynamic_slice_in_dim(weights, me * each, each, 0), jnp.zeros((), jnp.int32)
    mine = pl.BlockSpec((each, columns), lambda s, place: (place[0], 0))
    out, gain_out, *through = call(functools.partial(gathered_kernel, layout=layout, rows=each), "gathered", (1,),
        [(weights, mine)] + [(a, resident(a.shape)) for a in arrays],
        [((each, columns), F32, resident((each, columns))), ((each, 1), F32, resident((each, 1)))], scalars=[me.reshape(1)], through=through)
    return (out, gain_out.reshape(each) / own_gain, *through)

def plain_kernel(core, *refs, pieces, shapes):
    arrays, outs = refs[:-len(shapes)], refs[-len(shapes):]
    for out, first, rows, column in pieces:
        g = None
        for ref in arrays:
            term = ref[0, first:first + rows, :].astype(F32)
            g = term if g is None else g + term
        if out == 0:
            mine = core[0] == 0
            top, bottom = g[:rows // 2], g[rows // 2:]
            outs[0][:, column:column + 256] = jnp.where(mine, top, bottom)
            outs[1][:, column:column + 256] = jnp.where(mine, bottom, top)
        else:
            outs[2][:, column:column + 256] = g

def plain(core, arrays, pieces, shapes):
    return call(functools.partial(plain_kernel, pieces=pieces, shapes=shapes), "plain", (1,), [(core, SMEM)] + [(a, resident(a.shape)) for a in arrays],
        [(s, F32, resident(s)) for s in shapes])

def shards(tokens, seq_starts, seq_lengths, gain_in, gain_mlp, w_in, w_out, w_gate_up, w_down, cotangent):
    Order.last = None
    rows, length, width = tokens.shape
    count = lax.axis_size("seq")
    bits = count.bit_length() - 1
    order_a = list(range(1, bits))
    order_b = [2, 1] + list(range(3, bits))
    order_c = [3, 1, 2] + list(range(4, bits))
    me = lax.axis_index("seq")
    core = (me % 2).reshape(1)
    total = rows * length
    begin = me * length
    low = (seq_starts[:, ::WINDOW] - begin).reshape(-1)
    high = low + seq_lengths[:, ::WINDOW].reshape(-1)

    x = tokens.reshape(total, width)
    cot = cotangent.reshape(total, width)
    p = Projected()
    project_keys(p, x, gain_in, w_in, rows)
    scan = Scan(*local_states(core, low, high, p.k_lin, p.v, rows, length), me, count, False)
    project_queries(p, w_in)
    scan.step()
    project_rest(p, w_in, rows)
    forward = [(i, i + 1) for i in range(count - 1)]
    backward = [(i + 1, i) for i in range(count - 1)]
    halo = lax.ppermute(p.tails, "seq", forward)
    scan.step()
    local = intra(low, high, p, rows, length, 0)
    scan.step()
    local, = intra(low, high, p, rows, length, 1, into=local)
    scan.step()
    windowed, = window(low, high, p, halo, rows, length)
    while scan.bit < bits:
        scan.step()
    state_in = scan.done()
    numer, mixed = mix(core, low, p, state_in, local, windowed, rows, length)

    (result, grad_resid, grad_mixed, keep_g, send_g, keep_u, send_u, keep_d, send_d, keep_o, send_o) = mlp(
        core, mixed, x, cot, w_out, gain_mlp, w_gate_up, w_down, count)
    grad_numer, *grad_state_in = numer_back(core, low, p, numer, grad_mixed, rows, length)
    scan = Scan(*grad_state_in, me, count, True)

    mlp_sum = MlpSum([(keep_g, send_g), (keep_u, send_u), (keep_d, send_d), (keep_o, send_o)], me, count)
    scan.step()
    mlp_sum.step()
    scan.step(through=mlp_sum.sends)
    mlp_sum.start(scan.through)
    back, dh, kept = window_back_first(low, high, p, halo, grad_mixed, rows, length)
    scan.step()
    returned = lax.ppermute(dh, "seq", backward)
    dq_win, dk_win, dv_win = window_back_second(low, high, p, grad_mixed, back, kept, rows, length)
    scan.step()
    dq_lin, dk_t, dv_part = intra_back(core, low, high, p, grad_numer, dv_win, state_in, rows, length)
    while scan.bit < bits:
        scan.step()
    mlp_sum.step()
    dk_win = tail_added(dk_win, returned, rows, length, deps=(scan.received[-1],))
    lin = HEADS * FEAT
    in_sum = InSum(me, count)
    early = in_sum.first(*weight_grad(core, p.normed_t, [dq_win, dk_win, dq_lin], count, "weight_grad_early"), (((0, width), (2 * width, lin)), ((width, width),)))
    dk_lin, dv = state_back(core, low, high, p, dk_t, dv_part, returned, scan.done(), rows, length)
    mlp_sum.step()
    late = in_sum.first(*weight_grad(core, p.normed_t, [dv, dk_lin], count, "weight_grad_late"), (((0, width // 2),), ((width // 2, width // 2), (width, lin))))
    parts = [dq_lin, dk_lin, dq_win, dk_win, dv]
    early = in_sum.second(*early)
    late = in_sum.second(*late)
    while mlp_sum.bit < bits - 2:
        mlp_sum.step()
    in_sum.third(mlp_sum, early, late)
    grad_tokens = input_grad(parts, w_in, x, gain_in, grad_resid)
    in_got = in_sum.rest()
    ff, each, chip = w_down.shape[0], width // count, w_down.shape[0] // (count // 2)
    pad = padded(each)
    height = ff // 256 * pad
    second = height + padded(chip) + 2 * pad
    part_gate_up, part_gain_mlp = gathered(mlp_sum.all, [n * pad for n in range(ff // 256)] + [second + n * pad for n in range(ff // 256)],
        w_gate_up, gain_mlp, me, count)
    own_down, send_down, part_out = plain(core, mlp_sum.all, [(0, height, chip, 0), (0, second + height, chip, 256)]
        + [(1, height + padded(chip) + n * pad + (second - 2 * pad if n >= 2 else 0), each, n * 256) for n in range(4)],
        [(chip // 2, width // 2), (chip // 2, width // 2), (each, width)])
    wide, piece = width // 256, list(range(3 * width // 256 + 2 * lin // 256))
    q_win, q_lin, v_a, k_win, v_b, k_lin = (piece[wide * n // 2 + m:wide * (n + c) // 2 + m + k] for n, m, c, k in
        ((0, 0, 2, 0), (2, 0, 0, 1), (2, 1, 1, 0), (3, 1, 2, 0), (5, 1, 1, 0), (6, 1, 0, 1)))
    part_in, part_gain_in, send_down = gathered(in_got, [n * pad for n in q_lin + k_lin + q_win + k_win + v_a + v_b], w_in, gain_in, me, count, through=(send_down,))
    got_down = swap(send_down, 0, count)
    first = me % 2 == 0
    part_down = jnp.concatenate([jnp.where(first, own_down, got_down), jnp.where(first, got_down, own_down)], axis=1)
    return (result.reshape(rows, length, width), grad_tokens.reshape(rows, length, width), part_gain_in, part_gain_mlp,
            part_in, part_out, part_gate_up, part_down)

def solution(mesh):
    split = P(None, "seq", None)
    placed = (split, P(None, "seq"), P(None, "seq"), P(), P(), P(), P(), P(), P(), split)
    return jax.shard_map(shards, mesh=mesh, in_specs=placed,
        out_specs=(split, split, P("seq"), P("seq"), P("seq", None), P("seq", None), P("seq", None), P("seq", None)),
        check_vma=False)
```

```python
import functools
import jax
import jax.numpy as jnp
from jax import lax
from jax.experimental import pallas as pl
from jax.experimental.pallas import tpu as pltpu
from jax.sharding import PartitionSpec as P
F32=jnp.float32; BF=jnp.bfloat16
EPSILON=1e-6
MIB=1<<20

def nn(a,b): return lax.dot_general(a,b,(((1,),(0,)),((),())),preferred_element_type=F32)
def nt(a,b): return lax.dot_general(a,b,(((1,),(1,)),((),())),preferred_element_type=F32)
def tn(a,b): return lax.dot_general(a,b,(((0,),(0,)),((),())),preferred_element_type=F32)

def parted(x, first, each):
    x = x.reshape(x.shape[0] // (2 * each), 2, each, x.shape[1])
    a, b = x[:, 0].reshape(-1, x.shape[3]), x[:, 1].reshape(-1, x.shape[3])
    return jnp.where(first, a, b).astype(BF), jnp.where(first, b, a).astype(BF)

def mlp_kernel(core_ref, mixed, tokens, cot, w_out, gain, wg, wu, wd,
               result, grad_resid, grad_mixed, keep_g, send_g, keep_u, send_u, keep_d, send_d, keep_o, send_o,
               resid, acc, dh, hn, hn_t, hid, dgu, wgu, *, steps, chunk, each):
    step = pl.program_id(0)
    toks = mixed.shape[0]
    width = mixed.shape[1]
    count = toks // chunk
    first = core_ref[0] == 0

    def rows(n):
        return pl.ds(pl.multiple_of(n * chunk, chunk), chunk)

    @pl.when(step == 0)
    def _():
        def one(n, carry):
            r = rows(n)
            res = tokens[r, :].astype(F32) + nn(mixed[r, :], w_out[...])
            scale = lax.rsqrt(jnp.mean(res * res, axis=-1, keepdims=True) + EPSILON)
            h = (res * scale * gain[...]).astype(BF)
            resid[r, :] = res
            acc[r, :] = res
            dh[r, :] = jnp.zeros((chunk, width), F32)
            hn[r, :] = h
            return carry
        lax.fori_loop(0, count, one, 0)
        for n in range(count):
            hn_t[:, n * chunk:(n + 1) * chunk] = hn[n * chunk:(n + 1) * chunk, :].T

    tile = wg.shape[1]
    wgu[:, :tile] = wg[...]
    wgu[:, tile:] = wu[...]

    def forward(n, carry):
        r = rows(n)
        h = hn[r, :]
        both = nn(h, wgu[...])
        gate, up = both[:, :tile], both[:, tile:]
        dhid = nt(cot[r, :], wd[...])
        sig = 1.0 / (1.0 + jnp.exp(-gate))
        silu = gate * sig
        hidden = (silu * up).astype(BF)
        d_gate = (dhid * up * (sig + silu * (1.0 - sig))).astype(BF)
        d_up = (dhid * silu).astype(BF)
        hid[r, :] = hidden
        dgu[r, :tile] = d_gate
        dgu[r, tile:] = d_up
        acc[r, :] += nn(hidden, wd[...])
        dh[r, :] += nt(dgu[r, :], wgu[...])
        return carry
    lax.fori_loop(0, count, forward, 0, unroll=2)

    half = width // 2
    grad_d = tn(hid[...], cot[...])
    left, right = grad_d[:, :half].astype(BF), grad_d[:, half:].astype(BF)
    keep_d[...] = jnp.where(first, left, right)
    send_d[...] = jnp.where(first, right, left)

    def weights(n, carry):
        r = rows(n)
        o = pl.ds(pl.multiple_of(n * (chunk // 2), chunk // 2), chunk // 2)
        grad = nn(hn_t[r, :], dgu[...])
        keep_g[o, :], send_g[o, :] = parted(grad[:, :tile], first, each)
        keep_u[o, :], send_u[o, :] = parted(grad[:, tile:], first, each)
        return carry
    lax.fori_loop(0, width // chunk, weights, 0, unroll=2)

    @pl.when(step == steps - 1)
    def _():
        def one(n, carry):
            r = rows(n)
            res = resid[r, :]
            scale = lax.rsqrt(jnp.mean(res * res, axis=-1, keepdims=True) + EPSILON)
            grad = dh[r, :]
            c = grad * gain[...]
            back = cot[r, :].astype(F32) + scale * c - res * (scale * scale * scale * jnp.mean(c * res, axis=-1, keepdims=True))
            result[r, :] = acc[r, :].astype(BF)
            grad_resid[r, :] = back
            b = back.astype(BF)
            hn[r, :] = b
            grad_mixed[r, :] = nt(b, w_out[...]).astype(BF)
            return carry
        lax.fori_loop(0, count, one, 0)
        for n in range(count):
            hn_t[:, n * chunk:(n + 1) * chunk] = mixed[n * chunk:(n + 1) * chunk, :].T
        def outer(n, carry):
            r = rows(n)
            o = pl.ds(pl.multiple_of(n * (chunk // 2), chunk // 2), chunk // 2)
            keep_o[o, :], send_o[o, :] = parted(nn(hn_t[r, :], hn[...]), first, each)
            return carry
        lax.fori_loop(0, width // chunk, outer, 0)


HEADS=16; FEAT=16; WINDOW=64; ROWS_PHI=160; FLAG_ROW=153
VMEM = 64 * MIB
GROUPS = HEADS // 4
EACH = 2
STEPS = GROUPS // EACH

def groups():
    return [(pl.program_id(1) * EACH + s, slice(s * 256, (s + 1) * 256)) for s in range(EACH)]

COST = dict(project_keys=6.8, state=7.4, project_rest=10, begun=2, joined=2.5, ended=3, intra=7.2, window=12, mix=10, mlp=88, numer_back=12,
    window_back=13, intra_back=25, sum_first=10.6, sum_second=6.4, state_back=0.1, weight_grad_early=0.1, weight_grad_late=0.1, input_grad_first=0.1, input_grad=0.1, in_first=3, in_second=3, quarters=3.5, tail=1.8, gathered=0.1, plain=0.1, sum_more=3)

class Order:
    last = None

def call(kernel, name, grid, ins, outs, scratch=(), flops=0, moved=10 * MIB, deps=(), into=None, alias=None, scalars=(), through=()):
    arrays, specs = [a for a, _ in ins], [s for _, s in ins]
    count, ahead = len(arrays), len(scalars)
    into = list(into or ())
    deps = list(deps)
    if Order.last is not None and not any(Order.last is a for a in into + deps + arrays + list(through)):
        deps.append(Order.last)
    extra = deps + into + list(through)
    aliases = {ahead + count + len(deps) + n: n for n in range(len(into))}
    aliases.update({ahead + i: o for i, o in (alias or {}).items()})
    aliases.update({ahead + count + len(deps) + len(into) + n: len(outs) + n for n in range(len(through))})
    results = len(outs)
    outs = list(outs) + [(a.shape, a.dtype, pl.BlockSpec(memory_space=pl.ANY)) for a in through]
    def body(*refs):
        begin = ahead + count + len(extra)
        kernel(*refs[:ahead + count], *refs[begin:begin + results], *refs[begin + len(outs):])
    out = pl.pallas_call(
        body, grid_spec=pltpu.PrefetchScalarGridSpec(num_scalar_prefetch=ahead, grid=grid,
            in_specs=specs + [pl.BlockSpec(memory_space=pl.ANY)] * len(extra), out_specs=[s for _, _, s in outs], scratch_shapes=list(scratch)),
        out_shape=[jax.ShapeDtypeStruct(shape, dtype) for shape, dtype, _ in outs],
        input_output_aliases=aliases, name=name,
        compiler_params=pltpu.CompilerParams(vmem_limit_bytes=VMEM, dimension_semantics=("arbitrary",) * len(grid)),
        cost_estimate=pl.CostEstimate(flops=int(COST.get(name, 2.0) * 1e9), bytes_accessed=1000, transcendentals=0),
    )(*scalars, *arrays, *extra)
    Order.last = out[0]
    return out

def lane_mask(width, size, which, dtype=BF):
    lanes = lax.broadcasted_iota(jnp.int32, (1, width), 1)
    return ((lanes >> (size.bit_length() - 1)) == which).astype(dtype)

def spread(values, length):
    block = lax.broadcasted_iota(jnp.int32, (1, length), 1) >> 6
    out = jnp.zeros((1, length), jnp.int32)
    for n, value in enumerate(values):
        out = jnp.where(block == n, value, out)
    return out

def scalars(ref, row, length):
    per_row = length // WINDOW
    return [ref[row * per_row + n] for n in range(per_row)]

def early_line(low, row, length):
    return (spread(scalars(low, row, length), length) < 0).astype(F32)

def owned_line(low, high, row, length):
    lows = scalars(low, row, length)
    place = lax.broadcasted_iota(jnp.int32, (1, length), 1)
    same = spread(lows, length) == lows[-1]
    return (same & (place < spread(scalars(high, row, length), length))).astype(F32)

TURNS = FEAT // 2

def turn(d):
    row = lax.broadcasted_iota(jnp.int32, (HEADS * FEAT, HEADS * FEAT), 0)
    entry = lax.broadcasted_iota(jnp.int32, (HEADS * FEAT, HEADS * FEAT), 1)
    return (((row & -FEAT) | ((row + d) & (FEAT - 1))) == entry).astype(BF)

def turned_scratch(length):
    return pltpu.VMEM((TURNS, HEADS * FEAT, length), BF)

def turn_all(x, x_t, turned, line):
    flipped = x.astype(F32).T
    flat = (flipped if line is None else flipped * line).astype(BF)
    x_t[...] = flat
    for d in range(1, TURNS + 1):
        turned[d - 1] = nn(turn(d), flat).astype(BF)

def features_t(x_t, turned, at, line):
    half = FEAT // 2
    x = x_t[at, :]
    parts = [x * x * jnp.bfloat16((2.0 * FEAT) ** -0.5)]
    xs = x * jnp.bfloat16(FEAT ** -0.5)
    for d in range(1, half):
        parts.append(xs * turned[d - 1, at, :])
    parts.append(x * jnp.bfloat16(FEAT ** -0.25))
    row = lax.broadcasted_iota(jnp.int32, x.shape, 0)
    parts.append(jnp.where(row < half, xs * turned[half - 1, at, :], jnp.where(row == half, line, 0.0).astype(BF)))
    return jnp.concatenate(parts, axis=0)

def features_back_t(x_t, turned, at, g, pulled):
    half = FEAT // 2
    x = x_t[at, :]
    total = g[:FEAT] * x.astype(F32) * (2.0 * (2.0 * FEAT) ** -0.5) + g[half * FEAT:(half + 1) * FEAT] * FEAT ** -0.25
    mixed = jnp.zeros(x.shape, F32)
    xs = x * jnp.bfloat16(FEAT ** -0.5)
    row = lax.broadcasted_iota(jnp.int32, x.shape, 0)
    gb = g.astype(BF)
    for d in range(1, half + 1):
        if d < half:
            gd = gb[d * FEAT:(d + 1) * FEAT]
        else:
            gd = jnp.where(row < half, gb[(half + 1) * FEAT:(half + 2) * FEAT], jnp.bfloat16(0))
        mixed = mixed + (gd * turned[d - 1, at, :]).astype(F32)
        pulled[d - 1, at, :] = gd * xs
    return total + mixed * FEAT ** -0.5

def turned_back(pulled):
    total = None
    for d in range(1, TURNS + 1):
        term = nn(turn(-d), pulled[d - 1])
        total = term if total is None else total + term
    return total

def head_rows(group, h):
    return pl.ds(pl.multiple_of(group * 4 * FEAT + h * FEAT, FEAT), FEAT)

def states_of(x_t, turned, y, group, line, flag):
    row = lax.broadcasted_iota(jnp.int32, (ROWS_PHI, 256), 0)
    out = jnp.where(row == FLAG_ROW, flag, 0.0)
    phi = jnp.concatenate([features_t(x_t, turned, head_rows(group, h), line) for h in range(4)], axis=0)
    every = nn(phi, y)
    for h in range(4):
        out = out + every[h * ROWS_PHI:(h + 1) * ROWS_PHI] * lane_mask(256, 64, h, F32)
    return out

def put_state(g, state, core, mine, send):
    r = pl.program_id(0)
    @pl.when(r == core[0])
    def _():
        mine[g] = state
    @pl.when(r != core[0])
    def _():
        send[g] = state.astype(BF)

def state_outs():
    shape = (GROUPS, ROWS_PHI, 256)
    spec = pl.BlockSpec(shape, lambda r, g: (0, 0, 0))
    return [(shape, F32, spec), (shape, BF, spec)]

def state_kernel(core, low, high, k, v, mine, send, k_t, line, turned, *, length):
    r, g = pl.program_id(0), pl.program_id(1)
    @pl.when(g == 0)
    def _():
        line[...] = owned_line(low, high, r, length)
        turn_all(k[...], k_t, turned, line[...])
    flag = (low[(r + 1) * (length // WINDOW) - 1] >= 0).astype(F32)
    for g, at in groups():
        put_state(g, states_of(k_t, turned, v[:, at], g, line[...], flag), core, mine, send)

def spec_col(length, first=0, row=0):
    return pl.BlockSpec((length, 256 * EACH), lambda r, g: (r + row, first // EACH + g))
def spec_all(length, row=0):
    return pl.BlockSpec((length, 256), lambda r, g: (r + row, 0))
SPEC_STATE = pl.BlockSpec((EACH, ROWS_PHI, 256), lambda r, g: (g, 0, 0))
def spec_t(length, row=0):
    return pl.BlockSpec((1, 256, length), lambda r, g: (r + row, 0, 0))
SMEM = pl.BlockSpec(memory_space=pltpu.SMEM)
def local_states(core, low, high, k, v, rows, length):
    return call(functools.partial(state_kernel, length=length), "state", (rows, STEPS),
        [(core, SMEM), (low, SMEM), (high, SMEM), (k, spec_all(length)), (v, spec_col(length))], state_outs(),
        [pltpu.VMEM((256, length), BF), pltpu.VMEM((1, length), F32), turned_scratch(length)])

def intra_kernel(low, high, q, k, v, out, mask, *, length, row):
    g = pl.program_id(1)
    half = length // 2
    @pl.when(g == 0)
    def _():
        lows, highs = scalars(low, row, length), scalars(high, row, length)
        for n in range(length // WINDOW):
            i = lax.broadcasted_iota(jnp.int32, (WINDOW, length), 0) + n * WINDOW
            j = lax.broadcasted_iota(jnp.int32, (WINDOW, length), 1)
            mask[n * WINDOW:(n + 1) * WINDOW, :] = ((j >= lows[n]) & (j <= i) & (j < highs[n])).astype(BF)
    qv, kv = q[...] * jnp.bfloat16(FEAT ** -0.5), k[...]
    for g, at in groups():
        vv = v[:, at] * jnp.bfloat16(0.5)
        top = bottom = None
        for h in range(4):
            km = kv * lane_mask(HEADS * FEAT, FEAT, g * 4 + h)
            vm = vv * lane_mask(256, 64, h)
            u0 = 1.0 + nt(qv[:half], km[:half])
            a0 = (1.0 + u0 * u0).astype(BF) * mask[:half, :half]
            u1 = 1.0 + nt(qv[half:], km)
            a1 = (1.0 + u1 * u1).astype(BF) * mask[half:, :]
            o0, o1 = nn(a0, vm[:half]), nn(a1, vm)
            top = o0 if top is None else top + o0
            bottom = o1 if bottom is None else bottom + o1
        out[:half, at] = top.astype(BF)
        out[half:, at] = bottom.astype(BF)

def intra(low, high, p, rows, length, row, deps=(), into=None):
    return call(functools.partial(intra_kernel, length=length, row=row), "intra", (1, STEPS),
        [(low, SMEM), (high, SMEM), (p.q_lin, spec_all(length, row)), (p.k_lin, spec_all(length, row)), (p.v, spec_col(length, 0, row))],
        [((rows * length, 1024), BF, spec_col(length, 0, row))],
        [pltpu.VMEM((length, length), BF)], flops=HEADS * 2 * 6 * 256 ** 3, deps=deps, into=into)

def stacked(x, scale=1.0):
    return jnp.concatenate([x * (lane_mask(256, 64, h) * jnp.bfloat16(scale)) for h in range(4)], axis=0)

def unstacked(x, scale=1.0):
    total = None
    for h in range(4):
        part = x[h * WINDOW:(h + 1) * WINDOW] * (lane_mask(256, 64, h, F32) * scale)
        total = part if total is None else total + part
    return total

def window_probs(low, high, at, shift, keys, qs):
    s = nt(keys, qs)
    key = lax.broadcasted_iota(jnp.int32, (2 * WINDOW, 4 * WINDOW), 0)
    query = lax.broadcasted_iota(jnp.int32, (2 * WINDOW, 4 * WINDOW), 1) & (WINDOW - 1)
    ok = (key >= jnp.maximum(query, low[at] + shift)) & (key < jnp.minimum(query + (WINDOW + 1), high[at] + shift))
    s = jnp.where(ok, s, -1e30)
    p = jnp.exp(s - jnp.max(s, axis=0, keepdims=True))
    return p * (1.0 / jnp.sum(p, axis=0, keepdims=True))

def window_kernel(low, high, q, k, v, hk, hv, out, ka, va, *, length):
    row = pl.program_id(0)
    per_row = length // WINDOW
    ka[:WINDOW, :] = hk[...]
    ka[WINDOW:, :] = k[...]
    va[:WINDOW, :] = hv[...]
    va[WINDOW:, :] = v[...]
    for g, at in groups():
        for n in range(per_row):
            own, both = slice(n * WINDOW, (n + 1) * WINDOW), slice(n * WINDOW, (n + 2) * WINDOW)
            p = window_probs(low, high, row * per_row + n, (1 - n) * WINDOW, ka[both, at], stacked(q[own, at], 64 ** -0.5))
            out[own, at] = unstacked(tn(p.astype(BF), va[both, at])).astype(BF)

def window_ins(low, high, p, halo, length, row):
    tail = lambda part: pl.BlockSpec((None, WINDOW, 256 * EACH), lambda r, g: (part, r + row, g))
    return [(low, SMEM), (high, SMEM), (p.qk_win, spec_col(length, 0, row)), (p.qk_win, spec_col(length, GROUPS, row)), (p.v, spec_col(length, 0, row)),
            (halo, tail(0)), (halo, tail(1))]

def window(low, high, p, halo, rows, length):
    return call(functools.partial(window_kernel, length=length), "window", (rows, STEPS), window_ins(low, high, p, halo, length, 0),
        [((rows * length, 1024), BF, spec_col(length))], [pltpu.VMEM((length + WINDOW, 256 * EACH), BF)] * 2)

def window_back_block(low, high, row, n, per_row, q, keys, vals, go):
    qs, gs = stacked(q, 64 ** -0.5), stacked(go)
    p = window_probs(low, high, row * per_row + n, (1 - n) * WINDOW, keys, qs)
    gp = nt(vals, gs)
    ds = (p * (gp - jnp.sum(p * gp, axis=0, keepdims=True))).astype(BF)
    return unstacked(tn(ds, keys), 64 ** -0.5).astype(BF), nn(ds, qs), nn(p.astype(BF), gs)

def window_back_first_kernel(low, high, q, k, v, hk, hv, go, q1, k1, v1, hk1, hv1, go1, dq, dk, dv, dh, q_kept, k_kept, v_kept, ka, va, *, length):
    per_row = length // WINDOW
    ka[:WINDOW, :] = hk[...]
    ka[WINDOW:, :] = k[...]
    va[:WINDOW, :] = hv[...]
    va[WINDOW:, :] = v[...]
    for _, at in groups():
        carry_k = carry_v = None
        for n in range(per_row):
            rows = slice(n * WINDOW, (n + 1) * WINDOW)
            both = slice(n * WINDOW, (n + 2) * WINDOW)
            dq[rows, at], dk_n, dv_n = window_back_block(low, high, 0, n, per_row, q[rows, at], ka[both, at], va[both, at], go[rows, at])
            if n == 0:
                dh[0, :WINDOW, at] = dk_n[:WINDOW].astype(BF)
                dh[1, :WINDOW, at] = dv_n[:WINDOW].astype(BF)
            else:
                dk[(n - 1) * WINDOW:n * WINDOW, at] = (carry_k + dk_n[:WINDOW]).astype(BF)
                dv[(n - 1) * WINDOW:n * WINDOW, at] = (carry_v + dv_n[:WINDOW]).astype(BF)
            carry_k, carry_v = dk_n[WINDOW:], dv_n[WINDOW:]
        dk[length - WINDOW:, at] = carry_k.astype(BF)
        dv[length - WINDOW:, at] = carry_v.astype(BF)
        keys = jnp.concatenate([hk1[:, at], k1[:, at]], axis=0)
        vals = jnp.concatenate([hv1[:, at], v1[:, at]], axis=0)
        q_kept[:, at], dk_n, dv_n = window_back_block(low, high, 1, 0, per_row, q1[:, at], keys, vals, go1[:, at])
        dh[0, WINDOW:, at] = dk_n[:WINDOW].astype(BF)
        dh[1, WINDOW:, at] = dv_n[:WINDOW].astype(BF)
        k_kept[:, at] = dk_n[WINDOW:]
        v_kept[:, at] = dv_n[WINDOW:]

def window_back_second_kernel(low, high, q, k, v, go, q_kept, k_kept, v_kept, dq, dk, dv, *, length):
    per_row = length // WINDOW
    dq[:WINDOW, :] = q_kept[...]
    for _, at in groups():
        carry_k, carry_v = k_kept[:, at], v_kept[:, at]
        for n in range(1, per_row):
            rows = slice(n * WINDOW, (n + 1) * WINDOW)
            both = slice((n - 1) * WINDOW, (n + 1) * WINDOW)
            dq[rows, at], dk_n, dv_n = window_back_block(low, high, 1, n, per_row, q[rows, at], k[both, at], v[both, at], go[rows, at])
            dk[(n - 1) * WINDOW:n * WINDOW, at] = (carry_k + dk_n[:WINDOW]).astype(BF)
            dv[(n - 1) * WINDOW:n * WINDOW, at] = (carry_v + dv_n[:WINDOW]).astype(BF)
            carry_k, carry_v = dk_n[WINDOW:], dv_n[WINDOW:]
        dk[length - WINDOW:, at] = carry_k.astype(BF)
        dv[length - WINDOW:, at] = carry_v.astype(BF)

def window_back_outs(total, length, row):
    spec = spec_col(length, 0, row)
    return [((total, 1024), BF, spec)] * 3

def window_back_first(low, high, p, halo, go, rows, length):
    total, per_row = rows * length, length // WINDOW
    block = lambda first=0: pl.BlockSpec((WINDOW, 256 * EACH), lambda r, g: (per_row, first // EACH + g))
    tail = lambda part: pl.BlockSpec((None, WINDOW, 256 * EACH), lambda r, g: (part, 1, g))
    small = spec_col(WINDOW)
    got = call(functools.partial(window_back_first_kernel, length=length), "window_back", (1, STEPS),
        window_ins(low, high, p, halo, length, 0) + [(go, spec_col(length)), (p.qk_win, block()), (p.qk_win, block(GROUPS)), (p.v, block()), (halo, tail(0)), (halo, tail(1)), (go, block())],
        window_back_outs(total, length, 0) + [((2, rows * WINDOW, 1024), BF, pl.BlockSpec((2, rows * WINDOW, 256 * EACH), lambda r, g: (0, 0, g))),
         ((WINDOW, 1024), BF, small), ((WINDOW, 1024), F32, small), ((WINDOW, 1024), F32, small)],
        [pltpu.VMEM((length + WINDOW, 256 * EACH), BF)] * 2)
    return got[:3], got[3], got[4:]

def window_back_second(low, high, p, go, into, kept, rows, length):
    small = spec_col(WINDOW)
    return call(functools.partial(window_back_second_kernel, length=length), "window_back", (1, STEPS),
        [(low, SMEM), (high, SMEM), (p.qk_win, spec_col(length, 0, 1)), (p.qk_win, spec_col(length, GROUPS, 1)), (p.v, spec_col(length, 0, 1)), (go, spec_col(length, 0, 1))]
        + [(k, small) for k in kept], window_back_outs(rows * length, length, 1), into=into)

def piece_mean(x):
    a = lax.broadcasted_iota(jnp.int32, (256, 256), 0) >> 6
    b = lax.broadcasted_iota(jnp.int32, (256, 256), 1) >> 6
    ones = jnp.where(a == b, 1.0 / 64, 0.0).astype(BF)
    high = x.astype(BF)
    return nn(high, ones)

def through_state(x_t, turned, state, group, line):
    state_t = state.T.astype(BF)
    parts = []
    for h in range(4):
        parts.append(nn(state_t[h * 64:(h + 1) * 64], features_t(x_t, turned, head_rows(group, h), line)))
    return jnp.concatenate(parts, axis=0).T

def state_for(row, core, kept, received, n):
    return jnp.where(row == core[0], kept[n].astype(F32), received[n].astype(F32))

def mix_kernel(core, low, q, kept, received, local, windowed, numer, mixed, q_t, line, turned, *, length):
    r, g = pl.program_id(0), pl.program_id(1)
    @pl.when(g == 0)
    def _():
        line[...] = early_line(low, r, length)
        turn_all(q[...], q_t, turned, line[...])
    for n, (group, at) in enumerate(groups()):
        num = local[:, at].astype(F32) + through_state(q_t, turned, state_for(r, core, kept, received, n), group, line[...])
        rho = lax.rsqrt(piece_mean(num * num) + EPSILON)
        numer[:, at] = num.astype(BF)
        mixed[:, at] = (num * rho + windowed[:, at].astype(F32)).astype(BF)

def mix(core, low, p, state, local, windowed, rows, length, deps=()):
    total = rows * length
    return call(functools.partial(mix_kernel, length=length), "mix", (rows, STEPS),
        [(core, SMEM), (low, SMEM), (p.q_lin, spec_all(length)), (state[0], SPEC_STATE), (state[1], SPEC_STATE), (local, spec_col(length)), (windowed, spec_col(length))],
        [((total, 1024), BF, spec_col(length)), ((total, 1024), BF, spec_col(length))],
        [pltpu.VMEM((256, length), BF), pltpu.VMEM((1, length), F32), turned_scratch(length)], deps=deps)

def numer_back_kernel(core, low, q, numer, gm, grad_numer, mine, send, q_t, line, turned, *, length):
    r, g = pl.program_id(0), pl.program_id(1)
    @pl.when(g == 0)
    def _():
        line[...] = early_line(low, r, length)
        turn_all(q[...], q_t, turned, line[...])
    flag = (low[(r + 1) * (length // WINDOW) - 1] >= 0).astype(F32)
    for group, at in groups():
        num = numer[:, at].astype(F32)
        rho = lax.rsqrt(piece_mean(num * num) + EPSILON)
        lin = num * rho
        gl = gm[:, at].astype(F32)
        gn = (rho * (gl - lin * piece_mean(gl * lin))).astype(BF)
        grad_numer[:, at] = gn
        put_state(group, states_of(q_t, turned, gn, group, line[...], flag), core, mine, send)

def numer_back(core, low, p, numer, gm, rows, length, deps=()):
    total = rows * length
    return call(functools.partial(numer_back_kernel, length=length), "numer_back", (rows, STEPS),
        [(core, SMEM), (low, SMEM), (p.q_lin, spec_all(length)), (numer, spec_col(length)), (gm, spec_col(length))],
        [((total, 1024), BF, spec_col(length))] + state_outs(),
        [pltpu.VMEM((256, length), BF), pltpu.VMEM((1, length), F32), turned_scratch(length)], deps=deps)

def intra_back_kernel(core, low, high, q, k, v, gn, dv_in, kept, received, dq, dk_t, dv, mask, q_t, k_t, dq_t, early, turned, pulled, *, length):
    row, g = pl.program_id(0), pl.program_id(1)
    half = length // 2
    @pl.when(g == 0)
    def _():
        lows, highs = spread(scalars(low, row, length), length), spread(scalars(high, row, length), length)
        j = lax.broadcasted_iota(jnp.int32, (length, length), 0)
        i = lax.broadcasted_iota(jnp.int32, (length, length), 1)
        mask[...] = ((j >= lows) & (j <= i) & (j < highs)).astype(BF)
        early[...] = (lows < 0).astype(F32)
        turn_all(q[...], q_t, turned, None)
        k_t[...] = k[...].astype(F32).T.astype(BF)
    quarter = FEAT ** -0.5
    qv, kv = q[...] * jnp.bfloat16(quarter), k[...]
    for n, (group, cols) in enumerate(groups()):
        vv, gv = v[:, cols], gn[:, cols]
        st = state_for(row, core, kept, received, n).astype(BF)
        top = dv_in[:half, cols].astype(F32)
        bottom = dv_in[half:, cols].astype(F32)
        km = [kv * lane_mask(HEADS * FEAT, FEAT, group * 4 + h) for h in range(4)]
        vm = [vv * lane_mask(256, 64, h) for h in range(4)]
        u0 = nt(jnp.concatenate([x[:half] for x in km], axis=0), qv)
        u1 = nt(jnp.concatenate([x[half:] for x in km], axis=0), qv[half:])
        ga0 = nt(jnp.concatenate([x[:half] for x in vm], axis=0), gv)
        ga1 = nt(jnp.concatenate([x[half:] for x in vm], axis=0), gv[half:])
        gphi = nt(jnp.concatenate([st * lane_mask(256, 64, h) for h in range(4)], axis=0), gv) * early[...]
        m0, m1 = mask[:half, :], mask[half:, half:]
        for h in range(4):
            at = head_rows(group, h)
            mine = slice(h * half, (h + 1) * half)
            gm = gv * (lane_mask(256, 64, h) * jnp.bfloat16(0.5))
            qb, kb = q_t[at, :] * jnp.bfloat16(quarter), k_t[at, :] * jnp.bfloat16(quarter)
            w0, w1 = 1.0 + u0[mine], 1.0 + u1[mine]
            a0 = (1.0 + w0 * w0).astype(BF) * m0
            a1 = (1.0 + w1 * w1).astype(BF) * m1
            ds0 = (ga0[mine] * w0).astype(BF) * m0
            ds1 = (ga1[mine] * w1).astype(BF) * m1
            top = top + nn(a0, gm)
            bottom = bottom + nn(a1, gm[half:])
            dk_t[0, at, :half] = nt(qb, ds0)
            dk_t[0, at, half:] = nt(qb[:, half:], ds1)
            d = nn(kb[:, :half], ds0)
            d = d + jnp.concatenate([jnp.zeros((FEAT, half), F32), nn(kb[:, half:], ds1)], axis=1)
            dq_t[at, :] = d + features_back_t(q_t, turned, at, gphi[h * ROWS_PHI:(h + 1) * ROWS_PHI], pulled)
        dv[:half, cols] = top.astype(BF)
        dv[half:, cols] = bottom.astype(BF)
    @pl.when(g == pl.num_programs(1) - 1)
    def _():
        dq[...] = (dq_t[...] + turned_back(pulled)).T.astype(BF)

def intra_back(core, low, high, p, gn, dv_in, state, rows, length):
    total = rows * length
    return call(functools.partial(intra_back_kernel, length=length), "intra_back", (rows, STEPS),
        [(core, SMEM), (low, SMEM), (high, SMEM), (p.q_lin, spec_all(length)), (p.k_lin, spec_all(length)), (p.v, spec_col(length)),
         (gn, spec_col(length)), (dv_in, spec_col(length)), (state[0], SPEC_STATE), (state[1], SPEC_STATE)],
        [((total, 256), BF, spec_all(length)), ((rows, 256, length), F32, spec_t(length)), ((total, 1024), BF, spec_col(length))],
        [pltpu.VMEM((length, length), BF)] + [pltpu.VMEM((256, length), BF)] * 2 + [pltpu.VMEM((256, length), F32), pltpu.VMEM((1, length), F32)] + [turned_scratch(length)] * 2)

def state_back_kernel(core, low, high, k, v, dk_in, dv_in, dhv, kept, received, dk, dv, k_t, dk_t, line, turned, pulled, *, length):
    r, g = pl.program_id(0), pl.program_id(1)
    @pl.when(g == 0)
    def _():
        line[...] = owned_line(low, high, r, length)
        turn_all(k[...], k_t, turned, line[...])
    tail = length - WINDOW
    for n, (group, cols) in enumerate(groups()):
        st = state_for(r, core, kept, received, n)
        sb = st.astype(BF)
        vv = v[:, cols]
        total = dv_in[:, cols].astype(F32) + through_state(k_t, turned, st, group, line[...])
        dv[:tail, cols] = total[:tail].astype(BF)
        dv[tail:, cols] = (total[tail:] + dhv[:, cols].astype(F32)).astype(BF)
        gphi = nt(jnp.concatenate([sb * lane_mask(256, 64, h) for h in range(4)], axis=0), vv) * line[...]
        for h in range(4):
            at = head_rows(group, h)
            dk_t[at, :] = dk_in[0, at, :] + features_back_t(k_t, turned, at, gphi[h * ROWS_PHI:(h + 1) * ROWS_PHI], pulled)
    @pl.when(g == pl.num_programs(1) - 1)
    def _():
        dk[...] = (dk_t[...] + turned_back(pulled)).T.astype(BF)

def state_back(core, low, high, p, dk_in, dv_in, returned, state, rows, length, deps=()):
    total = rows * length
    tail = pl.BlockSpec((None, WINDOW, 256 * EACH), lambda r, g: (1, r, g))
    return call(functools.partial(state_back_kernel, length=length), "state_back", (rows, STEPS),
        [(core, SMEM), (low, SMEM), (high, SMEM), (p.k_lin, spec_all(length)), (p.v, spec_col(length)), (dk_in, spec_t(length)), (dv_in, spec_col(length)),
         (returned, tail), (state[0], SPEC_STATE), (state[1], SPEC_STATE)],
        [((total, 256), BF, spec_all(length)), ((total, 1024), BF, spec_col(length))],
        [pltpu.VMEM((256, length), BF), pltpu.VMEM((256, length), F32), pltpu.VMEM((1, length), F32)] + [turned_scratch(length)] * 2, deps=deps)

def tail_kernel(x, got, out):
    out[...] = (x[...].astype(F32) + got[...].astype(F32)).astype(BF)

def tail_added(x, returned, rows, length, deps=()):
    per_row = length // WINDOW
    end = pl.BlockSpec((WINDOW, x.shape[1]), lambda r: ((r + 1) * per_row - 1, 0))
    return call(tail_kernel, "tail", (rows,), [(x, end), (returned, pl.BlockSpec((None, WINDOW, x.shape[1]), lambda r: (0, r, 0)))],
        [(x.shape, BF, end)], flops=10, moved=MIB, alias={0: 0}, deps=deps)[0]


ONE = dict(pipeline_mode=pl.Buffered(1))
def resident(shape):
    return pl.BlockSpec(shape, lambda *s: (0,) * len(shape), **ONE)

class Projected:
    pass

def put_tails(tails, x, rows):
    length = x.shape[0] // rows
    for r in range(rows):
        tails[r * WINDOW:(r + 1) * WINDOW, :] = x[(r + 1) * length - WINDOW:(r + 1) * length, :]

def keys_kernel(tokens, gain, wk, wv, normed, k, v, tails, *, rows):
    @pl.when(pl.program_id(0) == 0)
    def _():
        x = tokens[...].astype(F32)
        normed[...] = (x * lax.rsqrt(jnp.mean(x * x, axis=-1, keepdims=True) + EPSILON) * gain[...]).astype(BF)
        k[...] = nn(normed[...], wk[...]).astype(BF)
    v[...] = nn(normed[...], wv[...]).astype(BF)
    put_tails(tails, v, rows)

def queries_kernel(normed, w, out):
    out[...] = nn(normed[...], w[...]).astype(BF)

def rest_kernel(normed, part, w, tails, out, normed_t, *, rows):
    normed_t[...] = part[...].T
    out[...] = nn(normed[...], w[...]).astype(BF)
    put_tails(tails, out, rows)

def project_keys(p, tokens, gain, w_in, rows):
    toks, width = tokens.shape
    lin = HEADS * FEAT
    first = (w_in.shape[1] - width) // 512
    p.normed, p.k_lin, p.v, p.tails = call(functools.partial(keys_kernel, rows=rows), "project_keys", (width // 512,),
        [(tokens, resident((toks, width))), (gain.reshape(1, width), resident((1, width))), (w_in, pl.BlockSpec((width, lin), lambda s: (0, 1), **ONE)),
         (w_in, pl.BlockSpec((width, 512), lambda s: (0, first + s)))],
        [((toks, width), BF, resident((toks, width))), ((toks, lin), BF, resident((toks, lin))), ((toks, width), BF, pl.BlockSpec((toks, 512), lambda s: (0, s))),
         ((2, rows * WINDOW, width), BF, pl.BlockSpec((None, rows * WINDOW, 512), lambda s: (1, 0, s)))])

def project_queries(p, w_in):
    toks, width = p.normed.shape
    lin = HEADS * FEAT
    p.q_lin, = call(queries_kernel, "project_queries", (1,),
        [(p.normed, resident((toks, width))), (w_in, pl.BlockSpec((width, lin), lambda s: (0, 0), **ONE))],
        [((toks, lin), BF, resident((toks, lin)))])

def project_rest(p, w_in, rows):
    toks, width = p.normed.shape
    lin = HEADS * FEAT
    count = 2 * width // 512
    piece = toks // count
    p.tails, p.qk_win, p.normed_t = call(functools.partial(rest_kernel, rows=rows), "project_rest", (count,),
        [(p.normed, resident((toks, width))), (p.normed, pl.BlockSpec((piece, width), lambda s: (s, 0))),
         (w_in, pl.BlockSpec((width, 512), lambda s: (0, 2 * lin // 512 + s)))],
        [((2, rows * WINDOW, width), BF, pl.BlockSpec((None, rows * WINDOW, 512), lambda s: (0, 0, jnp.maximum(s - count // 2, 0)))),
         ((toks, 2 * width), BF, pl.BlockSpec((toks, 512), lambda s: (0, s))), ((width, toks), BF, pl.BlockSpec((width, piece), lambda s: (0, s)))],
        into=(p.tails,))

def mlp(core, mixed, tokens, cot, w_out, gain, w_gate_up, w_down, count, tile=256, chunk=1024):
    toks, width = mixed.shape
    ff = w_down.shape[0]
    steps = ff // tile
    half = width // 2
    big = resident((toks, width))
    across = pl.BlockSpec((half, tile), lambda s: (0, s))
    down = pl.BlockSpec((tile, half), lambda s: (s, 0))
    return call(functools.partial(mlp_kernel, steps=steps, chunk=chunk, each=width // count), "mlp", (steps,),
        [(core, SMEM), (mixed, big), (tokens, big), (cot, big), (w_out, resident((width, width))), (gain.reshape(1, width), resident((1, width))),
         (w_gate_up, pl.BlockSpec((width, tile), lambda s: (0, s))), (w_gate_up, pl.BlockSpec((width, tile), lambda s: (0, s + steps))),
         (w_down, pl.BlockSpec((tile, width), lambda s: (s, 0)))],
        [((toks, width), BF, big), ((toks, width), F32, big), ((toks, width), BF, big)] + [((half, ff), BF, across)] * 4
        + [((ff, half), BF, down)] * 2 + [((half, width), BF, resident((half, width)))] * 2,
        [pltpu.VMEM((toks, width), F32)] * 3 + [pltpu.VMEM((toks, width), BF), pltpu.VMEM((width, toks), BF), pltpu.VMEM((toks, tile), BF),
         pltpu.VMEM((toks, 2 * tile), BF), pltpu.VMEM((width, 2 * tile), BF)],
        flops=2 * toks * width * (9 * ff + 3 * width), moved=60 * MIB)

def weight_kernel(core, normed_t, *refs, counts, each):
    parts, (keep, send) = refs[:len(counts)], refs[len(counts):]
    step = pl.program_id(0)
    first = core[0] == 0
    begin = 0
    for ref, count in zip(parts, counts):
        @pl.when((step >= begin) & (step < begin + count))
        def _(ref=ref):
            columns = ref.shape[1]
            keep[:, :columns], send[:, :columns] = parted(nn(normed_t[...], ref[...]), first, each)
        begin += count

def weight_grad(core, normed_t, parts, count, name, deps=()):
    width, toks = normed_t.shape
    counts = [max(p.shape[1] // 512, 1) for p in parts]
    begins = [sum(counts[:n]) for n in range(len(counts))]
    def spec(part, begin, size):
        return pl.BlockSpec((toks, min(part.shape[1], 512)), lambda s: (0, jnp.clip(s - begin, 0, size - 1)))
    half = width // 2
    out = ((half, 512 * sum(counts)), BF, pl.BlockSpec((half, 512), lambda s: (0, s)))
    return call(functools.partial(weight_kernel, counts=counts, each=width // count), name, (sum(counts),),
        [(core, SMEM), (normed_t, resident((width, toks)))] + [(p, spec(p, b, n)) for p, b, n in zip(parts, begins, counts)],
        [out, out], deps=deps)

def input_kernel(dq_lin, dk_lin, dq_win, dk_win, dv, w, tokens, gain, resid, out):
    begin, grad = 0, None
    for ref in (dq_lin, dk_lin, dq_win, dk_win, dv):
        size = ref.shape[1]
        term = nt(ref[...], w[:, begin:begin + size])
        grad = term if grad is None else grad + term
        begin += size
    x = tokens[...].astype(F32)
    scale = lax.rsqrt(jnp.mean(x * x, axis=-1, keepdims=True) + EPSILON)
    c = grad * gain[...]
    out[...] = resid[...] + scale * c - x * (scale * scale * scale * jnp.mean(c * x, axis=-1, keepdims=True))

def input_grad(parts, w_in, tokens, gain, resid, piece=512):
    toks, width = tokens.shape
    by_rows = lambda columns: pl.BlockSpec((piece, columns), lambda s: (s, 0))
    return call(input_kernel, "input_grad", (toks // piece,),
        [(p, by_rows(p.shape[1])) for p in parts] + [(w_in, resident(w_in.shape)), (tokens, by_rows(width)), (gain.reshape(1, width), resident((1, width))), (resid, by_rows(width))],
        [((toks, width), F32, by_rows(width))])[0]

def swap(x, bit, count):
    return lax.ppermute(x, "seq", [(i, i ^ (1 << bit)) for i in range(count)])

def over(near, far):
    return near + (1.0 - near[FLAG_ROW:FLAG_ROW + 1, :]) * far

def begun_kernel(core, mine, received, total, *, backward):
    first = core[0] == 0
    for n in range(mine.shape[0]):
        m, r = mine[n], received[n].astype(F32)
        at0, at1 = jnp.where(first, m, r), jnp.where(first, r, m)
        total[n] = (over(at0, at1) if backward else over(at1, at0)).astype(BF)

def joined_kernel(ahead, total, received, new_total):
    here = ahead[0] == 1
    for n in range(total.shape[0]):
        t, r = total[n].astype(F32), received[n].astype(F32)
        new_total[n] = over(jnp.where(here, t, r), jnp.where(here, r, t)).astype(BF)

def ended_kernel(core, ahead, mine, *refs, backward):
    received, (kept, send) = refs[:-2], refs[-2:]
    first = core[0] == 0
    own = first ^ backward
    for n in range(mine.shape[0]):
        m, r = mine[n], received[0][n].astype(F32)
        base = jnp.where(own, m, r)
        e = jnp.zeros_like(m)
        for k, ref in enumerate(received[1:]):
            e = jnp.where(ahead[k] == 1, over(e, ref[n].astype(F32)), e)
        o = over(base, e)
        kept[n] = jnp.where(own, e, o).astype(BF)
        send[n] = jnp.where(own, o, e).astype(BF)

class Scan:
    def __init__(self, mine, send, me, count, backward):
        self.me, self.count, self.backward, self.mine = me, count, backward, mine
        self.received = [swap(send, 0, count)]
        self.bit, self.last = 0, count.bit_length() - 2
        self.core = (me % 2).reshape(1)
        self.ahead = ((me >> jnp.arange(1, self.last + 1, dtype=jnp.int32)) & 1) ^ (1 if backward else 0)
    def _call(self, kernel, name, flags, arrays, outs, through=()):
        shape = self.mine.shape
        whole = pl.BlockSpec(shape, lambda: (0, 0, 0))
        return call(kernel, name, (), [(f, SMEM) for f in flags] + [(a, whole) for a in arrays], [(shape, BF, whole)] * outs, flops=10, moved=MIB, through=through)
    def step(self, through=()):
        if self.bit == 0:
            self.total, *self.through = self._call(functools.partial(begun_kernel, backward=self.backward), "begun", [self.core], [self.mine, self.received[0]], 1, through)
        elif self.bit < self.last:
            self.total, *self.through = self._call(joined_kernel, "joined", [self.ahead[self.bit - 1:self.bit]], [self.total, self.received[-1]], 1, through)
        else:
            self.kept, self.total = self._call(functools.partial(ended_kernel, backward=self.backward), "ended", [self.core, self.ahead], [self.mine] + self.received, 2)
        self.bit += 1
        self.received.append(swap(self.total, self.bit if self.bit <= self.last else 0, self.count))
    def done(self):
        return self.kept, self.received[-1]

def padded(rows):
    return -(-rows // 16) * 16

class Piece:
    def __init__(self, arrays, first=0, size=None, rows=None):
        self.arrays = arrays
        self.first, self.size = first, size or arrays[0].shape[2]
        self.rows = rows or arrays[0].shape[1]
        self.height = self.size // 256 * padded(self.rows)

def add_kernel(*refs, plan, count, scalars):
    refs = refs[scalars:]
    ins, outs = refs[:-count], refs[-count:]
    for target, parts, at, height, rows, columns in plan:
        for k, sources in enumerate(parts):
            total = None
            for s in sources:
                term = ins[s][...].astype(F32)
                total = term if total is None else total + term
            total = total.astype(BF)
            pad = padded(rows)
            for c in range(columns // 256):
                outs[target + k][:, :, at + c * pad:at + c * pad + rows, :] = total[..., c * 256:(c + 1) * 256]

def add_up(groups, ways, name, most=4, deps=(), through=()):
    grid = min([most] + [outer for _, outer, _, _ in groups])
    ins, outs, plan = [], [], []
    for n, (pieces, outer, inner, own) in enumerate(groups):
        per = outer // grid
        at = 0
        for piece in pieces:
            parts = []
            for k in range(ways):
                sources = []
                for array in piece.arrays:
                    _, rows, columns = array.shape
                    def index(a, *own_refs, n=n, k=k, block=piece.first // piece.size):
                        return (a, own_refs[n][0] ^ k if ways > 1 else 0, 0, 0, block)
                    sources.append(len(ins))
                    ins.append((array.reshape(outer, ways, inner, rows, columns), pl.BlockSpec((per, None, inner, rows, piece.size), index)))
                parts.append(sources)
            plan.append((n * ways, parts, at, piece.height, piece.rows, piece.size))
            at += piece.height
        outs += [((outer, inner, at, 256), BF, pl.BlockSpec((per, inner, at, 256), lambda a, *own_refs: (a, 0, 0, 0)))] * ways
    got = call(functools.partial(add_kernel, plan=plan, count=len(outs), scalars=len(groups)), name, (grid,), ins, outs, flops=10, moved=20 * MIB,
        scalars=[own.reshape(1) for _, _, _, own in groups], deps=deps, through=through)
    sums = [x.reshape((-1,) + x.shape[2:]) for x in got[:len(outs)]]
    return [sums[n * ways:(n + 1) * ways] for n in range(len(groups))] + list(got[len(outs):])

def chips_first(x, chips):
    return x.reshape(chips, x.shape[0] // chips, x.shape[1])

class MlpSum:
    def __init__(self, pairs, me, count):
        self.me, self.count, self.chips = me, count, count // 2
        self.pairs = [(chips_first(k, self.chips), chips_first(swap(s, 0, count), self.chips)) for k, s in pairs]
        self.bit = 0
    def start(self, sends):
        self.a.append(swap(sends[0], 1, self.count))
        self.b.append(swap(sends[1], 2, self.count))
    def step(self, deps=()):
        me, chips = self.me, self.chips
        bits = self.count.bit_length() - 1
        self.bit += 1
        if self.bit == 1:
            g, u, d, o = self.pairs
            half = lambda x, n: Piece(x, n * (x[0].shape[2] // 2), x[0].shape[2] // 2)
            pieces = [Piece(g), half(d, 0), half(o, 0)], [Piece(u), half(d, 1), half(o, 1)]
            self.layout = [(p.rows, p.size) for ps in pieces for p in ps]
            (ka, sa), (kb, sb) = add_up([(pieces[0], chips // 2, 1, (me >> 1) & 1), (pieces[1], chips // 4, 2, (me >> 2) & 1)], 2, "sum_first", deps=deps)
            self.a, self.b, self.sends = [ka], [kb], (sa, sb)
        elif self.bit == 2:
            (ka, sa), (kb, sb) = add_up([([Piece(self.a)], chips // 4, 1, (me >> 2) & 1), ([Piece(self.b)], chips // 4, 1, (me >> 1) & 1)], 2, "sum_second")
            self.a, self.b = [ka, swap(sa, 2, self.count)], [kb, swap(sb, 1, self.count)]
        else:
            got, = add_up([self.group()], 2, "sum_more")
            self.send(got)
    def group(self):
        pieces = [Piece(self.a), Piece(self.b)] if self.bit == 3 else [Piece(self.all)]
        return pieces, self.chips >> self.bit, 1, (self.me >> self.bit) & 1
    def send(self, got):
        self.all = [got[0], swap(got[1], self.bit, self.count)]

def quarters(pieces, bit, me, count):
    flip = lambda x, k: lax.ppermute(x, "seq", [(i, i ^ (k << bit)) for i in range(count)])
    parts, = add_up([(pieces, (count // 2) >> (bit + 1), 1, (me >> bit) & 3)], 4, "quarters", 2)
    return [parts[0]] + [flip(parts[k], k) for k in (3, 2, 1)]

class InSum:
    def __init__(self, me, count):
        self.me, self.count, self.chips = me, count, count // 2
        self.bit = 1
    def first(self, keep, send, columns):
        arrays = chips_first(keep, self.chips), chips_first(swap(send, 0, self.count), self.chips)
        return arrays, columns
    def second(self, arrays, columns, through=()):
        me, chips = self.me, self.chips
        a, b = ([Piece(arrays, first, size) for first, size in c] for c in columns)
        (ka, sa), (kb, sb), *self.through = add_up([(a, chips // 2, 1, (me >> 1) & 1), (b, chips // 4, 2, (me >> 2) & 1)], 2, "in_first", through=through)
        return [ka, swap(sa, 1, self.count)], [kb, swap(sb, 2, self.count)]
    def third(self, mlp_sum, *parts):
        me, chips = self.me, self.chips
        a, b = ([Piece(p[n]) for p in parts] for n in (0, 1))
        mlp_sum.bit += 1
        (ka, sa), (kb, sb), got = add_up([(a, chips // 4, 1, (me >> 2) & 1), (b, chips // 4, 1, (me >> 1) & 1), mlp_sum.group()], 2, "in_second")
        mlp_sum.send(got)
        self.arrays = [Piece([ka, swap(sa, 2, self.count)]), Piece([kb, swap(sb, 1, self.count)])]
        self.bit = 3
    def rest(self):
        while self.bit < self.count.bit_length() - 1:
            got = quarters(self.arrays, self.bit, self.me, self.count)
            self.arrays = [Piece(got)]
            self.bit += 2
        return got

def gathered_kernel(place, weights, *refs, layout, rows):
    arrays, (out, gain_out) = refs[:-2], refs[-2:]
    total = None
    for n, at in enumerate(layout):
        g = None
        for ref in arrays:
            term = ref[0, at:at + rows, :].astype(F32)
            g = term if g is None else g + term
        out[:, n * 256:(n + 1) * 256] = g
        t = g * weights[:, n * 256:(n + 1) * 256].astype(F32)
        total = t if total is None else total + t
    gain_out[...] = jnp.sum(total, axis=1, keepdims=True)

def gathered(arrays, layout, weights, gain, me, count, through=()):
    each, columns = weights.shape[0] // count, weights.shape[1]
    own_gain = lax.dynamic_slice_in_dim(gain, me * each, each, 0)
    if each < 16:
        weights, me = lax.dynamic_slice_in_dim(weights, me * each, each, 0), jnp.zeros((), jnp.int32)
    mine = pl.BlockSpec((each, columns), lambda s, place: (place[0], 0))
    out, gain_out, *through = call(functools.partial(gathered_kernel, layout=layout, rows=each), "gathered", (1,),
        [(weights, mine)] + [(a, resident(a.shape)) for a in arrays],
        [((each, columns), F32, resident((each, columns))), ((each, 1), F32, resident((each, 1)))], scalars=[me.reshape(1)], through=through)
    return (out, gain_out.reshape(each) / own_gain, *through)

def plain_kernel(core, *refs, pieces, shapes):
    arrays, outs = refs[:-len(shapes)], refs[-len(shapes):]
    for out, first, rows, column in pieces:
        g = None
        for ref in arrays:
            term = ref[0, first:first + rows, :].astype(F32)
            g = term if g is None else g + term
        if out == 0:
            mine = core[0] == 0
            top, bottom = g[:rows // 2], g[rows // 2:]
            outs[0][:, column:column + 256] = jnp.where(mine, top, bottom)
            outs[1][:, column:column + 256] = jnp.where(mine, bottom, top)
        else:
            outs[2][:, column:column + 256] = g

def plain(core, arrays, pieces, shapes):
    return call(functools.partial(plain_kernel, pieces=pieces, shapes=shapes), "plain", (1,), [(core, SMEM)] + [(a, resident(a.shape)) for a in arrays],
        [(s, F32, resident(s)) for s in shapes])

def shards(tokens, seq_starts, seq_lengths, gain_in, gain_mlp, w_in, w_out, w_gate_up, w_down, cotangent):
    Order.last = None
    rows, length, width = tokens.shape
    count = lax.axis_size("seq")
    bits = count.bit_length() - 1
    order_a = list(range(1, bits))
    order_b = [2, 1] + list(range(3, bits))
    order_c = [3, 1, 2] + list(range(4, bits))
    me = lax.axis_index("seq")
    core = (me % 2).reshape(1)
    total = rows * length
    begin = me * length
    low = (seq_starts[:, ::WINDOW] - begin).reshape(-1)
    high = low + seq_lengths[:, ::WINDOW].reshape(-1)

    x = tokens.reshape(total, width)
    cot = cotangent.reshape(total, width)
    p = Projected()
    project_keys(p, x, gain_in, w_in, rows)
    scan = Scan(*local_states(core, low, high, p.k_lin, p.v, rows, length), me, count, False)
    project_queries(p, w_in)
    scan.step()
    project_rest(p, w_in, rows)
    forward = [(i, i + 1) for i in range(count - 1)]
    backward = [(i + 1, i) for i in range(count - 1)]
    scan.step(through=(p.tails,))
    halo = lax.ppermute(scan.through[0], "seq", forward)
    local = intra(low, high, p, rows, length, 0)
    scan.step()
    local, = intra(low, high, p, rows, length, 1, into=local)
    scan.step()
    windowed, = window(low, high, p, halo, rows, length)
    while scan.bit < bits:
        scan.step()
    state_in = scan.done()
    numer, mixed = mix(core, low, p, state_in, local, windowed, rows, length)

    (result, grad_resid, grad_mixed, keep_g, send_g, keep_u, send_u, keep_d, send_d, keep_o, send_o) = mlp(
        core, mixed, x, cot, w_out, gain_mlp, w_gate_up, w_down, count)
    grad_numer, *grad_state_in = numer_back(core, low, p, numer, grad_mixed, rows, length)
    scan = Scan(*grad_state_in, me, count, True)

    mlp_sum = MlpSum([(keep_g, send_g), (keep_u, send_u), (keep_d, send_d), (keep_o, send_o)], me, count)
    scan.step()
    mlp_sum.step()
    scan.step(through=mlp_sum.sends)
    mlp_sum.start(scan.through)
    back, dh, kept = window_back_first(low, high, p, halo, grad_mixed, rows, length)
    scan.step()
    returned = lax.ppermute(dh, "seq", backward)
    dq_win, dk_win, dv_win = window_back_second(low, high, p, grad_mixed, back, kept, rows, length)
    scan.step()
    dq_lin, dk_t, dv_part = intra_back(core, low, high, p, grad_numer, dv_win, state_in, rows, length)
    while scan.bit < bits:
        scan.step()
    mlp_sum.step()
    dk_win = tail_added(dk_win, returned, rows, length, deps=(scan.received[-1],))
    lin = HEADS * FEAT
    in_sum = InSum(me, count)
    early = in_sum.first(*weight_grad(core, p.normed_t, [dq_win, dk_win, dq_lin], count, "weight_grad_early"), (((0, width), (2 * width, lin)), ((width, width),)))
    dk_lin, dv = state_back(core, low, high, p, dk_t, dv_part, returned, scan.done(), rows, length)
    mlp_sum.step()
    late = in_sum.first(*weight_grad(core, p.normed_t, [dv, dk_lin], count, "weight_grad_late"), (((0, width // 2),), ((width // 2, width // 2), (width, lin))))
    parts = [dq_lin, dk_lin, dq_win, dk_win, dv]
    early = in_sum.second(*early)
    late = in_sum.second(*late)
    while mlp_sum.bit < bits - 2:
        mlp_sum.step()
    in_sum.third(mlp_sum, early, late)
    grad_tokens = input_grad(parts, w_in, x, gain_in, grad_resid)
    in_got = in_sum.rest()
    ff, each, chip = w_down.shape[0], width // count, w_down.shape[0] // (count // 2)
    pad = padded(each)
    height = ff // 256 * pad
    second = height + padded(chip) + 2 * pad
    part_gate_up, part_gain_mlp = gathered(mlp_sum.all, [n * pad for n in range(ff // 256)] + [second + n * pad for n in range(ff // 256)],
        w_gate_up, gain_mlp, me, count)
    own_down, send_down, part_out = plain(core, mlp_sum.all, [(0, height, chip, 0), (0, second + height, chip, 256)]
        + [(1, height + padded(chip) + n * pad + (second - 2 * pad if n >= 2 else 0), each, n * 256) for n in range(4)],
        [(chip // 2, width // 2), (chip // 2, width // 2), (each, width)])
    wide, piece = width // 256, list(range(3 * width // 256 + 2 * lin // 256))
    q_win, q_lin, v_a, k_win, v_b, k_lin = (piece[wide * n // 2 + m:wide * (n + c) // 2 + m + k] for n, m, c, k in
        ((0, 0, 2, 0), (2, 0, 0, 1), (2, 1, 1, 0), (3, 1, 2, 0), (5, 1, 1, 0), (6, 1, 0, 1)))
    part_in, part_gain_in, send_down = gathered(in_got, [n * pad for n in q_lin + k_lin + q_win + k_win + v_a + v_b], w_in, gain_in, me, count, through=(send_down,))
    got_down = swap(send_down, 0, count)
    first = me % 2 == 0
    part_down = jnp.concatenate([jnp.where(first, own_down, got_down), jnp.where(first, got_down, own_down)], axis=1)
    return (result.reshape(rows, length, width), grad_tokens.reshape(rows, length, width), part_gain_in, part_gain_mlp,
            part_in, part_out, part_gate_up, part_down)

def solution(mesh):
    split = P(None, "seq", None)
    placed = (split, P(None, "seq"), P(None, "seq"), P(), P(), P(), P(), P(), P(), split)
    return jax.shard_map(shards, mesh=mesh, in_specs=placed,
        out_specs=(split, split, P("seq"), P("seq"), P("seq", None), P("seq", None), P("seq", None), P("seq", None)),
        check_vma=False)
```
